32 devices in a mesh: ctx: 8 (over y, x, core), shard: 4 (over z).
Axes of the slice: x: 2, y: 2, z: 4, core: 2. Of those that a mesh axis runs over, the one named last changes fastest.
Arguments:
- layer_input: bfloat16 [4, 1024, 2048], P('shard', 'ctx'), may hold values from -6 to 6
- w_query: bfloat16 [2048, 2048], P(None, 'shard'), may hold values from -0.125 to 0.125
- w_key: bfloat16 [2048, 1024], P(None, 'shard'), may hold values from -0.125 to 0.125
- w_value: bfloat16 [2048, 1024], P(None, 'shard'), may hold values from -0.125 to 0.125
- w_out: bfloat16 [2048, 2048], P(None, 'shard'), may hold values from -1.5 to 1.5
- w_gate: bfloat16 [2048, 8192], P(None, 'shard'), may hold values from -0.125 to 0.125
- w_up: bfloat16 [2048, 8192], P(None, 'shard'), may hold values from -0.125 to 0.125
- w_down: bfloat16 [8192, 2048], P(None, 'shard'), may hold values from -0.0625 to 0.0625
- attn_gain: float32 [2048], replicated, may hold values from 0.5 to 1.5
- mlp_gain: float32 [2048], replicated, may hold values from 0.5 to 1.5
- block_pairs: int32 [4, 8], P('shard'), may hold values from 0 to 7, each once within a row
- doc_ids: int32 [4, 1024], P('shard'), may hold values from 0 to 3, never falling along the last dimension, each value on 1 to 512 neighbouring positions
- cotangent: bfloat16 [4, 1024, 2048], P('shard', 'ctx'), may hold values from -6 to 6
Outputs:
- output: bfloat16 [4, 1024, 2048], P('shard', 'ctx')
- grad_input: bfloat16 [4, 1024, 2048], P('shard', 'ctx')
- grad_query: float32 [2048, 2048], P(('ctx', 'shard'))
- grad_key: float32 [2048, 1024], P(('ctx', 'shard'))
- grad_value: float32 [2048, 1024], P(('ctx', 'shard'))
- grad_out: float32 [2048, 2048], P(('ctx', 'shard'))
- grad_gate: float32 [2048, 8192], P(('ctx', 'shard'))
- grad_up: float32 [2048, 8192], P(('ctx', 'shard'))
- grad_down: float32 [8192, 2048], P(('ctx', 'shard'))
- grad_attn_gain: float32 [2048], P(('ctx', 'shard'))
- grad_mlp_gain: float32 [2048], P(('ctx', 'shard'))
The draws below stay inside these ranges and needn't reach their ends.
Inputs may be any that keep to these rules, and one draw needn't show every extreme that they name: Each row holds each number once: in sequence s, ctx index c holds blocks block_pairs[s, c] and 15 - block_pairs[s, c] of the sequence's 2 * 8 blocks. `doc_ids`: each row never falls along positions; every document has 1 to 512 positions, one of each row exactly 512.
All inputs are finite; a program needn't handle non-finite values.
Results may differ from the reference program's by a relative error of at most 0.02.
Values may be sent and summed in bfloat16 or wider, within the bound.
A program may use at most 320 MiB of HBM per device.

```python
import math
import jax
import jax.numpy as jnp
import numpy as np
from jax import lax

D = 2048
HQ = 8
HK = 4
HD = 256
FF = 8192
TOK_DEV = 128
WINDOW = 1024
SEQ_TOK = 1024
SEQS = 4
TOKENS = 4096
DOCS = 4
DOC_MOST = 512
N_CTX = 8


def block_scale(rng, dims, shards, least, largest):
    def one(dim, blocks):
        heights = jax.random.uniform(jax.random.fold_in(jax.random.fold_in(rng, 6), dim), (blocks,), jnp.float32, least / len(shards), largest / len(shards))
        return jnp.repeat(jnp.exp(heights), dims[dim] // blocks).reshape((-1,) + (1,) * (len(dims) - dim - 1))

    factor_of = one(*shards[0])
    for cut in shards[1:]:
        factor_of = factor_of * one(*cut)
    return factor_of


def split_up(number_of, total, reach, skew):
    loads = [(1 << 20) // math.isqrt(standing ** skew) + 1 for standing in range(2, number_of + 1)]
    rest, given = total - reach - (number_of - 1), [1] * (number_of - 1)
    while rest > 0:
        candidates = [i for i in range(number_of - 1) if given[i] < reach]
        pool, budget = sum([loads[i] for i in candidates]), rest
        for i in candidates:
            addition = min(reach - given[i], max(1, budget * loads[i] // pool), rest)
            given[i] = given[i] + addition
            rest = rest - addition
    return np.array([reach] + given)


def uneven_parts(own_key, amount, total, limit, slope):
    if amount == 2:
        one = jax.random.randint(own_key, (), max(1, total - limit), min(limit, total - 1) + 1)
        return jnp.stack([one, total - one])
    lengths = jnp.asarray(split_up(amount, total, limit, slope), jnp.int32)
    couples = (amount - 1) // 2
    donor, sink = lengths[1:1 + 2 * couples:2], lengths[2:2 + 2 * couples:2]
    margin = jnp.minimum(donor - 1, limit - sink)
    moved = jax.random.randint(jax.random.fold_in(own_key, 1), (couples,), 0, 1 << 20) % (margin + 1)
    lengths = lengths.at[1:1 + 2 * couples:2].set(donor - moved).at[2:2 + 2 * couples:2].set(sink + moved)
    return lengths[jax.random.permutation(jax.random.fold_in(own_key, 2), amount)]


def noise(key, dims, spread, limit, shards=(), kind=jnp.bfloat16):
    values = spread * jax.random.normal(key, dims, jnp.float32)
    if shards:
        values = values * block_scale(key, dims, shards, -0.22, 0.18)
    return jnp.clip(values, -limit, limit).astype(kind)


def setup_inputs(seed: int = 0) -> dict:
    streams_of = jax.random.split(jax.random.key(seed), 14)
    return {
        "layer_input": noise(streams_of[0], (SEQS, SEQ_TOK, D), 1.0, 6.0, ((0, 4), (1, 8))),
        "w_query": noise(streams_of[1], (D, HQ * HD), D ** -0.5, 0.125, ((1, 4),)),
        "w_key": noise(streams_of[2], (D, HK * HD), D ** -0.5, 0.125, ((1, 4),)),
        "w_value": noise(streams_of[3], (D, HK * HD), D ** -0.5, 0.125, ((1, 4),)),
        "w_out": noise(streams_of[4], (HQ * HD, D), (HQ * HD * 8 // WINDOW) ** -0.5, 1.5, ((1, 4),)),
        "w_gate": noise(streams_of[5], (D, FF), D ** -0.5, 0.125, ((1, 4),)),
        "w_up": noise(streams_of[6], (D, FF), D ** -0.5, 0.125, ((1, 4),)),
        "w_down": noise(streams_of[7], (FF, D), FF ** -0.5, 0.0625, ((1, 4),)),
        "attn_gain": jnp.clip(1.0 + 0.1 * jax.random.normal(streams_of[8], (D,), jnp.float32), 0.5, 1.5),
        "mlp_gain": jnp.clip(1.0 + 0.1 * jax.random.normal(streams_of[9], (D,), jnp.float32), 0.5, 1.5),
        "block_pairs": jax.vmap(lambda own: jax.random.permutation(own, N_CTX))(jax.random.split(streams_of[10], SEQS)).reshape((SEQS, N_CTX)).astype(jnp.int32),
        "doc_ids": jax.vmap(lambda own: jnp.searchsorted(jnp.cumsum(uneven_parts(own, DOCS, SEQ_TOK, DOC_MOST, 1)), jnp.arange(SEQ_TOK), side="right"))(jax.random.split(streams_of[11], SEQS)).reshape((SEQS, SEQ_TOK)).astype(jnp.int32),
        "cotangent": noise(streams_of[12], (SEQS, SEQ_TOK, D), 1.0, 6.0, ((0, 4), (1, 8))),
    }


EPSILON = 1e-06
SCORE_SCALE = 0.0625
MASKED = -1e+30
ROPE_BASE = 1000042.0

@jax.custom_vjp
def low(v):
    return lax.optimization_barrier(v.astype(jnp.bfloat16)).astype(jnp.float32)

@jax.custom_vjp
def low_back(v):
    return v

def low_keep(v):
    return (low(v), None)

def low_pass(kept, grad):
    return (grad,)

def back_keep(v):
    return (v, None)

def back_low(kept, grad):
    return (low(grad),)
low.defvjp(low_keep, low_pass)
low_back.defvjp(back_keep, back_low)

def position_of(rows, pairs, per_device, blocks_total):
    device = rows // per_device
    within = rows % per_device
    half = per_device // 2
    chosen = jnp.take(pairs, device)
    first = chosen * half + within
    second = (blocks_total - 1 - chosen) * half + within - half
    return jnp.where(within < half, first, second).astype(jnp.int32)

def rope_tables(positions, head):
    half = head // 2
    freq = ROPE_BASE ** (-(jnp.arange(half, dtype=jnp.float32) * 2.0) / head)
    angle = positions.astype(jnp.float32)[:, None] * freq[None, :]
    return (jnp.cos(angle), jnp.sin(angle))

def rotate(values, cosine, sine):
    half = values.shape[-1] // 2
    first = values[..., :half]
    second = values[..., half:]
    cosine = cosine[:, None, :]
    sine = sine[:, None, :]
    return jnp.concatenate([first * cosine - second * sine, second * cosine + first * sine], axis=-1)

def visible(query_pos, query_doc, key_pos, key_doc):
    distance = query_pos[:, None] - key_pos[None, :]
    return (query_doc[:, None] == key_doc[None, :]) & (distance >= 0) & (distance < WINDOW)

def rms_scale(values):
    return values * lax.rsqrt(lax.optimization_barrier(jnp.mean(values * values, axis=-1, keepdims=True)) + EPSILON)

def product(left, right):
    return jnp.dot(left, right, precision=lax.Precision.HIGHEST)

def reference(layer_input, w_query, w_key, w_value, w_out, w_gate, w_up, w_down, attn_gain, mlp_gain, block_pairs, doc_ids, cotangent):
    group_size = HQ // HK
    rows = jnp.arange(SEQ_TOK, dtype=jnp.int32)
    positions = jax.vmap(lambda pairs: position_of(rows, pairs, TOK_DEV, 2 * N_CTX))(block_pairs)
    documents = jnp.take_along_axis(doc_ids, positions, axis=1)
    cosine, sine = rope_tables(positions.reshape(TOKENS), HD)
    block = math.gcd(SEQ_TOK, 512)
    block_count = SEQ_TOK // block

    def forward(inputs, query_w, key_w, value_w, out_w, gate_w, up_w, down_w, gain_one, gain_two):
        flat = inputs.reshape(TOKENS, D)
        normed = low(rms_scale(flat) * gain_one)
        query_lin = low_back(product(normed, query_w))
        key_lin = low_back(product(normed, key_w))
        value_lin = low_back(product(normed, value_w))
        query_rot = low(rotate(query_lin.reshape(TOKENS, HQ, HD), cosine, sine))
        key_rot = low(rotate(key_lin.reshape(TOKENS, HK, HD), cosine, sine))
        value_low = low(value_lin).reshape(TOKENS, HK, HD)

        def one_seq(pieces):
            query_seq, key_seq, value_seq, pos_seq, doc_seq = pieces

            def one_block(parts):
                query_block, query_pos, query_doc = parts
                scores = jnp.einsum('qkgd,skd->qkgs', query_block, key_seq, precision=lax.Precision.HIGHEST) * SCORE_SCALE
                scores = low_back(scores)
                mask = visible(query_pos, query_doc, pos_seq, doc_seq)[:, None, None, :]
                scores = jnp.where(mask, scores, MASKED)
                probs = low(jax.nn.softmax(scores, axis=-1))
                return jnp.einsum('qkgs,skd->qkgd', probs, value_seq, precision=lax.Precision.HIGHEST)
            return lax.map(jax.checkpoint(one_block), (query_seq.reshape(block_count, block, HK, group_size, HD), pos_seq.reshape(block_count, block), doc_seq.reshape(block_count, block)))
        attended = lax.map(one_seq, (query_rot.reshape(SEQS, SEQ_TOK, HK, group_size, HD), key_rot.reshape(SEQS, SEQ_TOK, HK, HD), value_low.reshape(SEQS, SEQ_TOK, HK, HD), positions, documents))
        attended = low_back(low(attended.reshape(TOKENS, HQ * HD)))
        mid = flat + low_back(product(attended, out_w))
        normed_two = low(rms_scale(mid) * gain_two)
        gate = low_back(product(normed_two, gate_w))
        up = low_back(product(normed_two, up_w))
        act = low(jax.nn.silu(gate) * up)
        return (mid + low_back(product(act, down_w))).reshape(SEQS, SEQ_TOK, D)
    params = (layer_input.astype(jnp.float32), w_query.astype(jnp.float32), w_key.astype(jnp.float32), w_value.astype(jnp.float32), w_out.astype(jnp.float32), w_gate.astype(jnp.float32), w_up.astype(jnp.float32), w_down.astype(jnp.float32), attn_gain.astype(jnp.float32), mlp_gain.astype(jnp.float32))
    result, pull = jax.vjp(forward, *params)
    grads = pull(cotangent.astype(jnp.float32))
    return (result.astype(jnp.bfloat16), grads[0].astype(jnp.bfloat16), grads[1], grads[2], grads[3], grads[4], grads[5], grads[6], grads[7], grads[8], grads[9])
```

```python
import functools
import math

import jax
import jax.numpy as jnp
from jax import lax
from jax.experimental import pallas as pl
from jax.experimental.pallas import tpu as pltpu
from jax.sharding import PartitionSpec as P

HQ = 8
HK = 4
HD = 256
WINDOW = 1024


EPSILON = 1e-06
SCORE_SCALE = 0.0625
MASKED = -1e30
ROPE_BASE = 1000042.0


def position_of(rows, pairs, per_device, blocks_total):
    device = rows // per_device
    within = rows % per_device
    half = per_device // 2
    chosen = jnp.take(pairs, device)
    first = chosen * half + within
    second = (blocks_total - 1 - chosen) * half + within - half
    return jnp.where(within < half, first, second)


def rope_tables(positions, head):
    half = head // 2
    freq = ROPE_BASE ** (-(jnp.arange(half, dtype=jnp.float32) * 2.0) / head)
    angle = positions.astype(jnp.float32)[:, None] * freq[None, :]
    return (jnp.cos(angle), jnp.sin(angle))


def rotate(values, cosine, sine):
    half = values.shape[-1] // 2
    first = values[..., :half]
    second = values[..., half:]
    cosine = cosine[:, None, :]
    sine = sine[:, None, :]
    return jnp.concatenate(
        [first * cosine - second * sine, second * cosine + first * sine], axis=-1
    )


def rotate_back(grads, cosine, sine):
    half = grads.shape[-1] // 2
    first = grads[..., :half]
    second = grads[..., half:]
    cosine = cosine[:, None, :]
    sine = sine[:, None, :]
    return jnp.concatenate(
        [first * cosine + second * sine, second * cosine - first * sine], axis=-1
    )


def visible(query_pos, query_doc, key_pos, key_doc):
    distance = query_pos[:, None] - key_pos[None, :]
    return (query_doc[:, None] == key_doc[None, :]) & (distance >= 0) & (distance < WINDOW)


def write_columns(left, piece):
    made = jnp.dot(left, piece, preferred_element_type=jnp.float32)
    return made


def contract_full(grads, weight):
    return lax.dot_general(
        grads, weight, (((1,), (1,)), ((), ())), preferred_element_type=jnp.float32
    )


def alternate(parts, shard_count, rows):
    return jnp.concatenate([part.reshape(rows, shard_count, -1) for part in parts], axis=2).reshape(
        rows, -1
    )


def outer_sum(left, right):
    return lax.dot_general(
        left, right, (((0,), (0,)), ((), ())), preferred_element_type=jnp.float32
    )


def term_rows(lefts, rights, gain_block, count):
    normed_all, attended_all, second_all, act_all = lefts
    query_g, key_g, value_g, branch_g, gate_g, up_g, upstream_g = rights
    down_part = outer_sum(act_all, upstream_g).reshape(count, -1)
    return jnp.concatenate(
        [
            outer_sum(normed_all, query_g),
            outer_sum(normed_all, key_g),
            outer_sum(normed_all, value_g),
            outer_sum(attended_all, branch_g),
            outer_sum(second_all, gate_g),
            outer_sum(second_all, up_g),
            down_part,
            gain_block,
        ],
        axis=1,
    )


def deal_columns(values, ctx_count, shard_count):
    rows = values.shape[0]
    return (
        values.reshape(rows, ctx_count, shard_count, -1)
        .transpose(0, 2, 1, 3)
        .reshape(rows, shard_count, -1)
    )


def on_device(
    layer_input,
    w_query,
    w_key,
    w_value,
    w_out,
    w_gate,
    w_up,
    w_down,
    attn_gain,
    mlp_gain,
    block_pairs,
    doc_ids,
    cotangent,
):
    tok_rows = layer_input.shape[1]
    model_width = layer_input.shape[2]
    shard_count = lax.axis_size("shard")
    ctx_count = lax.axis_size("ctx")
    device_count = lax.axis_size(("ctx", "shard"))
    group_size = HQ // HK
    blocks_total = 2 * ctx_count
    pairs = block_pairs[0]
    documents = doc_ids[0]
    own_rows = lax.axis_index("ctx") * tok_rows + jnp.arange(tok_rows, dtype=jnp.int32)
    own_pos = position_of(own_rows, pairs, tok_rows, blocks_total)
    own_doc = jnp.take(documents, own_pos)
    cosine, sine = rope_tables(own_pos, HD)
    stack_qkv = jnp.concatenate([w_query, w_key, w_value], axis=1)
    stack_mlp = jnp.concatenate([w_gate, w_up], axis=1)
    per_query = w_query.shape[1]
    per_key = w_key.shape[1]
    per_hidden = w_gate.shape[1]
    hidden_width = w_down.shape[0]
    inputs = layer_input.reshape(tok_rows, model_width).astype(jnp.float32)
    factor_one = lax.rsqrt(jnp.mean(inputs * inputs, axis=-1, keepdims=True) + EPSILON)
    normed = (inputs * factor_one * attn_gain).astype(jnp.bfloat16)
    projected = write_columns(normed, lax.all_gather(stack_qkv, "shard", axis=1, tiled=True))
    projected = projected.reshape(tok_rows, shard_count, -1)
    query_lin = projected[:, :, :per_query].reshape(tok_rows, HQ, HD)
    key_lin = projected[:, :, per_query : per_query + per_key].reshape(tok_rows, HK, HD)
    value_lin = projected[:, :, per_query + per_key :].reshape(tok_rows, HK * HD)
    query_rot = (
        rotate(query_lin, cosine, sine).astype(jnp.bfloat16).reshape(tok_rows, HK, group_size, HD)
    )
    key_rot = rotate(key_lin, cosine, sine).astype(jnp.bfloat16).reshape(tok_rows, HK * HD)
    value_low = value_lin.astype(jnp.bfloat16)

    def key_mask(first_row, count):
        key_pos = position_of(
            first_row + jnp.arange(count, dtype=jnp.int32), pairs, tok_rows, blocks_total
        )
        return visible(own_pos, own_doc, key_pos, jnp.take(documents, key_pos))[:, None, None, :]

    start_state = (
        jnp.full((tok_rows, HK, group_size), MASKED, jnp.float32),
        jnp.zeros((tok_rows, HK, group_size), jnp.float32),
        jnp.zeros((tok_rows, HK, group_size, HD), jnp.float32),
    )
    keys = lax.all_gather(key_rot, "ctx", axis=0, tiled=True)
    values = lax.all_gather(value_low, "ctx", axis=0, tiled=True)
    count = keys.shape[0]
    step = math.gcd(count, 4 * tok_rows)
    keys = keys.reshape(count // step, step, HK, HD)
    values = values.reshape(count // step, step, HK, HD)

    def attend_step(i, running):
        top, total, accum = running
        mask = key_mask(i * step, step)
        scores = (
            jnp.einsum("tkgd,skd->tkgs", query_rot, keys[i], preferred_element_type=jnp.float32)
            * SCORE_SCALE
        )
        scores = jnp.where(mask, scores, MASKED)
        new_top = jnp.maximum(top, jnp.max(scores, axis=-1))
        weights = jnp.where(mask, jnp.exp(scores - new_top[..., None]), 0.0)
        shrink = jnp.exp(top - new_top)
        total = total * shrink + jnp.sum(weights, axis=-1)
        accum = accum * shrink[..., None] + jnp.einsum(
            "tkgs,skd->tkgd",
            weights.astype(jnp.bfloat16),
            values[i],
            preferred_element_type=jnp.float32,
        )
        return (new_top, total, accum)

    top, total, accum = lax.fori_loop(0, count // step, attend_step, start_state)
    log_total = top + jnp.log(total)
    attended_full = accum / total[..., None]
    attended = attended_full.astype(jnp.bfloat16).reshape(tok_rows, HQ * HD)
    branch_one = write_columns(attended, lax.all_gather(w_out, "shard", axis=1, tiled=True))
    mid = inputs + branch_one
    factor_two = lax.rsqrt(jnp.mean(mid * mid, axis=-1, keepdims=True) + EPSILON)
    normed_two = (mid * factor_two * mlp_gain).astype(jnp.bfloat16)
    gate_up = write_columns(normed_two, lax.all_gather(stack_mlp, "shard", axis=1, tiled=True))
    gate_up = gate_up.reshape(tok_rows, shard_count, -1)
    gate = gate_up[:, :, :per_hidden].reshape(tok_rows, hidden_width)
    up_lin = gate_up[:, :, per_hidden:].reshape(tok_rows, hidden_width)
    sigma = jax.nn.sigmoid(gate)
    swish = gate * sigma
    act = (swish * up_lin).astype(jnp.bfloat16)
    branch_two = write_columns(act, lax.all_gather(w_down, "shard", axis=1, tiled=True))
    output = (mid + branch_two).astype(jnp.bfloat16).reshape(1, tok_rows, model_width)
    full_qkv, full_out, full_mlp, full_down = (
        lax.all_gather(stack_qkv, "shard", axis=1, tiled=True),
        lax.all_gather(w_out, "shard", axis=1, tiled=True),
        lax.all_gather(stack_mlp, "shard", axis=1, tiled=True),
        lax.all_gather(w_down, "shard", axis=1, tiled=True),
    )
    upstream_low = cotangent.reshape(tok_rows, model_width)
    upstream = upstream_low.astype(jnp.float32)
    act_grad = contract_full(upstream_low, full_down)
    gate_grad = (act_grad * up_lin * (sigma * (1.0 + gate * (1.0 - sigma)))).astype(jnp.bfloat16)
    up_grad = (act_grad * swish).astype(jnp.bfloat16)
    stacked_mlp_grad = alternate((gate_grad, up_grad), shard_count, tok_rows)
    norm_two_grad = contract_full(stacked_mlp_grad, full_mlp)
    mlp_gain_term = jnp.sum(norm_two_grad * mid * factor_two, axis=0)
    scaled_two = norm_two_grad * mlp_gain
    mid_grad = (
        upstream
        + factor_two * scaled_two
        - mid * factor_two**3 * jnp.mean(scaled_two * mid, axis=-1, keepdims=True)
    )
    branch_grad = mid_grad.astype(jnp.bfloat16)
    attended_grad = contract_full(branch_grad, full_out)
    attended_low = attended_grad.astype(jnp.bfloat16).reshape(tok_rows, HK, group_size, HD)
    delta = jnp.sum(attended_low.astype(jnp.float32) * attended_full, axis=-1)

    def query_grads(carry, piece):
        keys, values = piece
        count = keys.shape[0]
        step = math.gcd(count, 4 * tok_rows)
        keys = keys.reshape(count // step, step, HK, HD)
        values = values.reshape(count // step, step, HK, HD)

        def query_step(i, query_sum):
            mask = key_mask(i * step, step)
            scores = (
                jnp.einsum("tkgd,skd->tkgs", query_rot, keys[i], preferred_element_type=jnp.float32)
                * SCORE_SCALE
            )
            probs = jnp.where(mask, jnp.exp(scores - log_total[..., None]), 0.0)
            prob_grad = jnp.einsum(
                "tkgd,skd->tkgs", attended_low, values[i], preferred_element_type=jnp.float32
            )
            score_grad = (probs * (prob_grad - delta[..., None])).astype(jnp.bfloat16)
            return query_sum + jnp.einsum(
                "tkgs,skd->tkgd", score_grad, keys[i], preferred_element_type=jnp.float32
            )

        return lax.fori_loop(0, count // step, query_step, carry)

    query_sum = query_grads(
        jnp.zeros((tok_rows, HK, group_size, HD), jnp.float32),
        (
            lax.all_gather(key_rot, "ctx", axis=0, tiled=True),
            lax.all_gather(value_low, "ctx", axis=0, tiled=True),
        ),
    )
    all_log_total, all_delta = (
        lax.all_gather(log_total, "ctx", axis=0, tiled=True),
        lax.all_gather(delta, "ctx", axis=0, tiled=True),
    )
    key_three = key_rot.reshape(tok_rows, HK, HD)
    value_three = value_low.reshape(tok_rows, HK, HD)

    def key_grads(carry, piece):
        queries, outgrads = piece
        count = queries.shape[0]
        step = math.gcd(count, 4 * tok_rows)
        queries = queries.reshape(count // step, step, HK, group_size, HD)
        outgrads = outgrads.reshape(count // step, step, HK, group_size, HD)

        def key_step(i, running):
            key_sum, value_sum = running
            first_row = i * step
            query_pos = position_of(
                first_row + jnp.arange(step, dtype=jnp.int32), pairs, tok_rows, blocks_total
            )
            mask = visible(query_pos, jnp.take(documents, query_pos), own_pos, own_doc)[
                :, None, None, :
            ]
            lse_part = lax.dynamic_slice_in_dim(all_log_total, first_row, step, 0)
            delta_part = lax.dynamic_slice_in_dim(all_delta, first_row, step, 0)
            scores = (
                jnp.einsum(
                    "skgd,tkd->skgt", queries[i], key_three, preferred_element_type=jnp.float32
                )
                * SCORE_SCALE
            )
            probs = jnp.where(mask, jnp.exp(scores - lse_part[..., None]), 0.0)
            prob_grad = jnp.einsum(
                "skgd,tkd->skgt", outgrads[i], value_three, preferred_element_type=jnp.float32
            )
            score_grad = (probs * (prob_grad - delta_part[..., None])).astype(jnp.bfloat16)
            value_sum = value_sum + jnp.einsum(
                "skgt,skgd->tkd",
                probs.astype(jnp.bfloat16),
                outgrads[i],
                preferred_element_type=jnp.float32,
            )
            key_sum = key_sum + jnp.einsum(
                "skgt,skgd->tkd", score_grad, queries[i], preferred_element_type=jnp.float32
            )
            return (key_sum, value_sum)

        return lax.fori_loop(0, count // step, key_step, carry)

    key_sum, value_sum = key_grads(
        (jnp.zeros((tok_rows, HK, HD), jnp.float32), jnp.zeros((tok_rows, HK, HD), jnp.float32)),
        (
            lax.all_gather(query_rot.reshape(tok_rows, HQ * HD), "ctx", axis=0, tiled=True),
            lax.all_gather(attended_low.reshape(tok_rows, HQ * HD), "ctx", axis=0, tiled=True),
        ),
    )
    query_grad = (
        rotate_back(query_sum.reshape(tok_rows, HQ, HD) * SCORE_SCALE, cosine, sine)
        .astype(jnp.bfloat16)
        .reshape(tok_rows, HQ * HD)
    )
    key_grad = (
        rotate_back(key_sum * SCORE_SCALE, cosine, sine)
        .astype(jnp.bfloat16)
        .reshape(tok_rows, HK * HD)
    )
    value_grad = value_sum.astype(jnp.bfloat16).reshape(tok_rows, HK * HD)
    stacked_qkv_grad = alternate((query_grad, key_grad, value_grad), shard_count, tok_rows)
    normed_grad = contract_full(stacked_qkv_grad, full_qkv)
    attn_gain_term = jnp.sum(normed_grad * inputs * factor_one, axis=0)
    scaled_one = normed_grad * attn_gain
    input_grad = (
        mid_grad
        + factor_one * scaled_one
        - inputs * factor_one**3 * jnp.mean(scaled_one * inputs, axis=-1, keepdims=True)
    )
    grad_input = input_grad.astype(jnp.bfloat16).reshape(1, tok_rows, model_width)
    ratio = hidden_width // model_width
    own_share = model_width // device_count
    rights = (query_grad, key_grad, value_grad, branch_grad, gate_grad, up_grad, upstream_low)
    group_rights = (
        lax.all_gather(rights[0], "shard", axis=0, tiled=True),
        lax.all_gather(rights[1], "shard", axis=0, tiled=True),
        lax.all_gather(rights[2], "shard", axis=0, tiled=True),
        lax.all_gather(rights[3], "shard", axis=0, tiled=True),
        lax.all_gather(rights[4], "shard", axis=0, tiled=True),
        lax.all_gather(rights[5], "shard", axis=0, tiled=True),
        lax.all_gather(rights[6], "shard", axis=0, tiled=True),
    )
    dealt = (
        lax.all_to_all(
            deal_columns(normed, ctx_count, shard_count),
            "shard",
            split_axis=1,
            concat_axis=0,
            tiled=True,
        ),
        lax.all_to_all(
            deal_columns(attended, ctx_count, shard_count),
            "shard",
            split_axis=1,
            concat_axis=0,
            tiled=True,
        ),
        lax.all_to_all(
            deal_columns(normed_two, ctx_count, shard_count),
            "shard",
            split_axis=1,
            concat_axis=0,
            tiled=True,
        ),
        lax.all_to_all(
            deal_columns(act, ctx_count, shard_count),
            "shard",
            split_axis=1,
            concat_axis=0,
            tiled=True,
        ),
    )
    group_lefts = tuple((part.reshape(part.shape[0], -1) for part in dealt))
    gain_pair = lax.psum(jnp.stack([attn_gain_term, mlp_gain_term]), "shard")
    gain_mine = lax.dynamic_index_in_dim(
        gain_pair.reshape(2, ctx_count, shard_count, own_share),
        lax.axis_index("shard"),
        2,
        keepdims=False,
    ).reshape(2, ctx_count * own_share)
    gain_block = jnp.concatenate(
        [gain_mine.T, jnp.zeros((ctx_count * own_share, 126), jnp.float32)], axis=1
    )
    summed = lax.psum_scatter(
        term_rows(group_lefts, group_rights, gain_block, own_share * lax.axis_size("ctx")).astype(
            jnp.bfloat16
        ),
        "ctx",
        scatter_dimension=0,
        tiled=True,
    ).astype(jnp.float32)
    edge_one = HQ * HD
    edge_two = edge_one + HK * HD
    edge_three = edge_two + HK * HD
    edge_four = edge_three + model_width
    edge_five = edge_four + hidden_width
    edge_six = edge_five + hidden_width
    edge_seven = edge_six + ratio * model_width
    grad_query = summed[:, :edge_one]
    grad_key = summed[:, edge_one:edge_two]
    grad_value = summed[:, edge_two:edge_three]
    grad_out = summed[:, edge_three:edge_four]
    grad_gate = summed[:, edge_four:edge_five]
    grad_up = summed[:, edge_five:edge_six]
    grad_down = summed[:, edge_six:edge_seven].reshape(own_share * ratio, model_width)
    grad_attn_gain = summed[:, edge_seven]
    grad_mlp_gain = summed[:, edge_seven + 1]
    return (
        output,
        grad_input,
        grad_query,
        grad_key,
        grad_value,
        grad_out,
        grad_gate,
        grad_up,
        grad_down,
        grad_attn_gain,
        grad_mlp_gain,
    )


BF16 = jnp.bfloat16
F32 = jnp.float32
VISIBLE_ROWS = 256


def dot_nn(a, b):
    return jnp.dot(a, b, preferred_element_type=F32)


def dot_nt(a, b):
    return lax.dot_general(a, b, (((1,), (1,)), ((), ())), preferred_element_type=F32)


def dot_tn(a, b):
    return lax.dot_general(a, b, (((0,), (0,)), ((), ())), preferred_element_type=F32)


def scores_of(query, key, code, low_code, key_code):
    scores = dot_nt(query, key) * SCORE_SCALE
    mask = (key_code <= code) & (key_code >= low_code)
    return jnp.where(mask, scores, MASKED)


def attend_kernel(query, key, value, code, low_code, key_code, attended, log_total):
    scores = scores_of(query[...], key[...], code[...], low_code[...], key_code[...])
    top = jnp.max(scores, axis=-1, keepdims=True)
    weights = jnp.exp(scores - top)
    total = jnp.sum(weights, axis=-1, keepdims=True)
    mixed = dot_nn(weights.astype(BF16), value[...])
    attended[...] = (mixed / total).astype(BF16)
    log_total[...] = top + jnp.log(total)


def attend(query, key, value, code, low_code, key_code):
    rows, head = query.shape
    step = math.gcd(rows, VISIBLE_ROWS)
    by_row = lambda width: pl.BlockSpec((step, width), lambda i: (i, 0))
    whole = lambda shape: pl.BlockSpec(shape, lambda i: (0, 0))
    return pl.pallas_call(
        attend_kernel,
        grid=(rows // step,),
        in_specs=[
            by_row(head),
            whole(key.shape),
            whole(value.shape),
            by_row(1),
            by_row(1),
            whole(key_code.shape),
        ],
        out_specs=[by_row(head), by_row(1)],
        out_shape=[
            jax.ShapeDtypeStruct((rows, head), BF16),
            jax.ShapeDtypeStruct((rows, 1), F32),
        ],
        compiler_params=pltpu.CompilerParams(vmem_limit_bytes=32 << 20),
        cost_estimate=pl.CostEstimate(
            flops=4 * rows * key.shape[0] * head,
            bytes_accessed=8 * rows * head,
            transcendentals=rows * key.shape[0],
        ),
    )(query, key, value, code, low_code, key_code)


def attend_back_kernel(
    query, outgrad, key, value, log_total, code, low_code, key_code, d_query, d_key, d_value
):
    @pl.when(pl.program_id(0) == 0)
    def _():
        d_key[...] = jnp.zeros_like(d_key)
        d_value[...] = jnp.zeros_like(d_value)

    scores = scores_of(query[...], key[...], code[...], low_code[...], key_code[...])
    probs = jnp.exp(scores - log_total[...])
    prob_grad = dot_nt(outgrad[...], value[...])
    delta = jnp.sum(probs * prob_grad, axis=-1, keepdims=True)
    score_grad = (probs * (prob_grad - delta)).astype(BF16)
    d_query[...] = dot_nn(score_grad, key[...]) * SCORE_SCALE
    d_key[...] += dot_tn(score_grad, query[...]) * SCORE_SCALE
    d_value[...] += dot_tn(probs.astype(BF16), outgrad[...])


def attend_back(query, outgrad, key, value, log_total, code, low_code, key_code):
    rows, head = query.shape
    step = math.gcd(rows, VISIBLE_ROWS)
    by_row = lambda width: pl.BlockSpec((step, width), lambda i: (i, 0))
    whole = lambda shape: pl.BlockSpec(shape, lambda i: (0, 0))
    return pl.pallas_call(
        attend_back_kernel,
        grid=(rows // step,),
        in_specs=[
            by_row(head),
            by_row(head),
            whole(key.shape),
            whole(value.shape),
            by_row(1),
            by_row(1),
            by_row(1),
            whole(key_code.shape),
        ],
        out_specs=[by_row(head), whole(key.shape), whole(value.shape)],
        out_shape=[
            jax.ShapeDtypeStruct((rows, head), F32),
            jax.ShapeDtypeStruct(key.shape, F32),
            jax.ShapeDtypeStruct(value.shape, F32),
        ],
        compiler_params=pltpu.CompilerParams(vmem_limit_bytes=40 << 20),
        cost_estimate=pl.CostEstimate(
            flops=10 * rows * key.shape[0] * head,
            bytes_accessed=20 * rows * head,
            transcendentals=rows * key.shape[0],
        ),
    )(query, outgrad, key, value, log_total, code, low_code, key_code)


def rotate_head(values, cosine, sine):
    half = values.shape[-1] // 2
    first, second = values[:, :half], values[:, half:]
    return jnp.concatenate([first * cosine - second * sine, second * cosine + first * sine], axis=1)


def swap_halves(values):
    half = values.shape[0] // 2
    return jnp.concatenate([values[half:], values[:half]], axis=0)


def index_of(stacked, i):
    return lax.dynamic_index_in_dim(stacked, i, 0, keepdims=False)


def cut(values, starts, sizes):
    return lax.dynamic_slice(values, starts, sizes)


def on_device_by_head(
    layer_input,
    w_query,
    w_key,
    w_value,
    w_out,
    w_gate,
    w_up,
    w_down,
    attn_gain,
    mlp_gain,
    block_pairs,
    doc_ids,
    cotangent,
):
    tok_rows, width = layer_input.shape[1:]
    planes = lax.axis_size("shard")
    ctx_count = lax.axis_size("ctx")
    chips = ctx_count // 2
    ctx, plane = lax.axis_index("ctx"), lax.axis_index("shard")
    chip, core = ctx // 2, ctx % 2
    first_core = core == 0
    seq_rows = tok_rows * ctx_count
    half_seq = seq_rows // 2
    group_rows = tok_rows * planes
    shard_width = w_down.shape[1]
    hidden_plane = w_gate.shape[1]
    hidden = hidden_plane // 2
    own_share = width // (planes * ctx_count)

    def over_z(values, d):
        return lax.ppermute(values, "shard", [(i, i ^ d) for i in range(planes)])

    def over_chips(values, d):
        return lax.ppermute(values, "ctx", [(i, i ^ (2 * d)) for i in range(ctx_count)])

    def sibling(values):
        return lax.ppermute(values, "ctx", [(i, i ^ 1) for i in range(ctx_count)])

    z_steps = range(1, planes)
    chip_steps = range(1, chips)

    def gather_z(values):
        return [values] + [over_z(values, d) for d in z_steps]

    def gather_chips(values):
        return [values] + [over_chips(values, d) for d in chip_steps]

    def gather_seq(values):
        mine = jnp.concatenate(gather_chips(values), axis=0)
        return jnp.concatenate([mine, sibling(mine)], axis=0)

    def gather_group(values):
        mine = jnp.concatenate(gather_z(values), axis=0)
        return jnp.concatenate([mine, sibling(mine)], axis=0)

    def sum_chips(block_of):
        total = block_of(0)
        for d in chip_steps:
            total = total + over_chips(block_of(d).astype(BF16), d).astype(F32)
        return total

    def sum_z(block_of):
        total = block_of(0)
        for d in z_steps:
            total = total + over_z(block_of(d).astype(BF16), d).astype(F32)
        return total

    quarter = width // chips
    head_block = jnp.concatenate(
        [
            cut(w_query, (quarter * chip, HD * core), (quarter, HD)),
            jnp.where(
                first_core,
                cut(w_key, (quarter * chip, 0), (quarter, HD)),
                cut(w_value, (quarter * chip, 0), (quarter, HD)),
            ),
        ],
        axis=1,
    )
    head_parts = jnp.stack(gather_z(head_block))
    w_head = jnp.zeros((width, 2 * HD), BF16)
    for d in range(chips):
        part = index_of(head_parts, plane ^ chip ^ d)
        if d:
            part = over_chips(part, d)
        w_head = lax.dynamic_update_slice(w_head, part, (quarter * (chip ^ d), 0))

    inputs_low = layer_input[0]
    inputs = inputs_low.astype(F32)
    all_inputs = gather_seq(inputs_low).astype(F32)
    pairs, documents = block_pairs[0], doc_ids[0]
    order = jnp.stack([(chip ^ d) * 2 + (core ^ e) for e in range(2) for d in range(chips)])
    rows = (order[:, None] * tok_rows + jnp.arange(tok_rows, dtype=jnp.int32)[None, :]).reshape(-1)
    positions = position_of(rows, pairs, tok_rows, 2 * ctx_count).astype(jnp.int32)
    span = 2 * seq_rows
    doc_first = jnp.take(documents, positions).astype(jnp.int32) * span
    code = doc_first + positions
    low_code = jnp.maximum(doc_first, code - (WINDOW - 1))
    code_column, low_column, code_row = code[:, None], low_code[:, None], code[None, :]
    cosine, sine = rope_tables(positions, HD)

    factor_all = lax.rsqrt(jnp.mean(all_inputs * all_inputs, axis=-1, keepdims=True) + EPSILON)
    normed_all = (all_inputs * factor_all * attn_gain).astype(BF16)
    projected = dot_nn(normed_all, w_head)
    query = rotate_head(projected[:, :HD], cosine, sine).astype(BF16)
    key_cosine = jnp.where(first_core, cosine, 1.0)
    key_sine = jnp.where(first_core, sine, 0.0)
    mine_kv = rotate_head(projected[:, HD:], key_cosine, key_sine).astype(BF16)
    other_kv = swap_halves(sibling(mine_kv))
    key = jnp.where(first_core, mine_kv, other_kv)
    value = jnp.where(first_core, other_kv, mine_kv)
    attended, log_total = attend(query, key, value, code_column, low_column, code_row)

    out_rows = jnp.zeros((HD, width), BF16)
    for d, part in enumerate(gather_z(cut(w_out, (HD * ctx, 0), (HD, shard_width)))):
        out_rows = lax.dynamic_update_slice(out_rows, part, (0, shard_width * (plane ^ d)))
    out_pair = jnp.concatenate([out_rows, sibling(out_rows)], axis=0)
    attended_pair = jnp.concatenate([attended[:half_seq], sibling(attended[half_seq:])], axis=1)
    branch_parts = dot_nn(attended_pair, out_pair).reshape(chips, tok_rows, width)
    mid = inputs + sum_chips(lambda d: branch_parts[d])
    factor_two = lax.rsqrt(jnp.mean(mid * mid, axis=-1, keepdims=True) + EPSILON)
    normed_two = (mid * factor_two * mlp_gain).astype(BF16)
    normed_group = gather_group(normed_two)

    quarter_hidden = hidden // chips
    down_block = jnp.zeros((quarter_hidden, width), BF16)
    for d in range(planes):
        start = hidden_plane * (plane ^ d) + hidden * core + quarter_hidden * chip
        part = cut(w_down, (start, 0), (quarter_hidden, shard_width))
        if d:
            part = over_z(part, d)
        down_block = lax.dynamic_update_slice(down_block, part, (0, shard_width * (plane ^ d)))
    down_rows = jnp.zeros((hidden, width), BF16)
    for d, part in enumerate(gather_chips(down_block)):
        down_rows = lax.dynamic_update_slice(down_rows, part, (quarter_hidden * (chip ^ d), 0))

    upstream_low = cotangent[0]
    upstream = upstream_low.astype(F32)
    upstream_group = gather_group(upstream_low)
    act_grad = dot_nt(upstream_group, down_rows)
    gate_cols = cut(w_gate, (0, hidden * core), (width, hidden))
    up_cols = cut(w_up, (0, hidden * core), (width, hidden))
    gate = dot_nn(normed_group, gate_cols)
    up_lin = dot_nn(normed_group, up_cols)
    sigma = jax.nn.sigmoid(gate)
    swish = gate * sigma
    act = (swish * up_lin).astype(BF16)
    gate_grad = (act_grad * up_lin * (sigma * (1.0 + gate * (1.0 - sigma)))).astype(BF16)
    up_grad = (act_grad * swish).astype(BF16)

    def back_to_tokens(partial):
        low = partial.astype(BF16)
        pair = partial[:group_rows] + sibling(low[group_rows:]).astype(F32)
        blocks = pair.reshape(planes, tok_rows, width)
        return sum_z(lambda d: blocks[d])

    norm_two_grad = back_to_tokens(dot_nt(gate_grad, gate_cols) + dot_nt(up_grad, up_cols))
    mlp_gain_term = jnp.sum(norm_two_grad * mid * factor_two, axis=0)
    scaled_two = norm_two_grad * mlp_gain
    mid_grad = (
        upstream
        + factor_two * scaled_two
        - mid * factor_two**3 * jnp.mean(scaled_two * mid, axis=-1, keepdims=True)
    )
    branch_grad_all = gather_seq(mid_grad.astype(BF16))
    output = (mid + back_to_tokens(dot_nn(act, down_rows))).astype(BF16)[None]

    attended_grad = dot_nt(branch_grad_all, out_rows).astype(BF16)
    d_query, d_key, d_value = attend_back(
        query, attended_grad, key, value, log_total, code_column, low_column, code_row
    )
    keep = jnp.where(first_core, d_key, d_value)
    give = jnp.where(first_core, d_value, d_key)
    d_kv = keep + swap_halves(sibling(give))
    d_head = jnp.concatenate(
        [rotate_head(d_query, cosine, -sine), rotate_head(d_kv, key_cosine, -key_sine)], axis=1
    ).astype(BF16)
    d_head_pair = jnp.concatenate([d_head[:half_seq], sibling(d_head[half_seq:])], axis=1)
    w_head_pair = jnp.concatenate([w_head, sibling(w_head)], axis=1)
    normed_parts = dot_nt(d_head_pair, w_head_pair).reshape(chips, tok_rows, width)
    normed_grad = sum_chips(lambda d: normed_parts[d])
    factor_one = factor_all[:tok_rows]
    attn_gain_term = jnp.sum(normed_grad * inputs * factor_one, axis=0)
    scaled_one = normed_grad * attn_gain
    grad_input = (
        mid_grad
        + factor_one * scaled_one
        - inputs * factor_one**3 * jnp.mean(scaled_one * inputs, axis=-1, keepdims=True)
    ).astype(BF16)[None]

    mlp_grads = jnp.concatenate([gate_grad, up_grad], axis=1)

    def mlp_rows(d):
        left = cut(normed_group, (0, quarter * (chip ^ d)), (2 * group_rows, quarter))
        return dot_tn(left, mlp_grads)

    mlp_sum = sum_chips(mlp_rows).astype(BF16).reshape(2, quarter // 2, 2 * hidden)
    mlp_mine = index_of(mlp_sum, core)
    mlp_other = sibling(index_of(mlp_sum, 1 - core))
    left_half = jnp.where(first_core, mlp_mine, mlp_other)
    right_half = jnp.where(first_core, mlp_other, mlp_mine)
    mlp_rows_all = jnp.concatenate(
        [left_half[:, :hidden], right_half[:, :hidden], left_half[:, hidden:], right_half[:, hidden:]],
        axis=1,
    ).reshape(planes, own_share, 2 * hidden_plane)
    grad_gate = jnp.zeros((own_share, planes * hidden_plane), F32)
    grad_up = jnp.zeros((own_share, planes * hidden_plane), F32)
    for d in range(planes):
        part = index_of(mlp_rows_all, plane ^ d)
        if d:
            part = over_z(part, d)
        part = part.astype(F32)
        at = (0, hidden_plane * (plane ^ d))
        grad_gate = lax.dynamic_update_slice(grad_gate, part[:, :hidden_plane], at)
        grad_up = lax.dynamic_update_slice(grad_up, part[:, hidden_plane:], at)

    down_terms = dot_tn(act, upstream_group).reshape(planes, chips, -1, width)
    down_sum = sum_chips(
        lambda d: lax.dynamic_index_in_dim(down_terms, chip ^ d, 1, keepdims=False)
    ).astype(BF16)
    down_parts = []
    for d in range(planes):
        part = index_of(down_sum, plane ^ d)
        down_parts.append(over_z(part, d) if d else part)
    down_parts = jnp.stack(down_parts)
    share = down_parts.shape[1]
    grad_down = jnp.zeros((chips * share, width), F32)
    for d in range(chips):
        part = index_of(down_parts, plane ^ chip ^ d)
        if d:
            part = over_chips(part, d)
        grad_down = lax.dynamic_update_slice(grad_down, part.astype(F32), (share * (chip ^ d), 0))

    out_terms = dot_tn(attended, branch_grad_all).reshape(planes, own_share, width)
    grad_out = sum_z(lambda d: index_of(out_terms, plane ^ d))

    head_terms = dot_tn(normed_all, d_head).reshape(ctx_count, planes, own_share, 2 * HD)
    head_sum = sum_z(
        lambda d: lax.dynamic_index_in_dim(head_terms, plane ^ d, 1, keepdims=False)
    ).astype(BF16)
    head_sum = head_sum.reshape(chips, 2, own_share, 2 * HD)
    head_mine = lax.dynamic_index_in_dim(head_sum, core, 1, keepdims=False)
    head_other = sibling(lax.dynamic_index_in_dim(head_sum, 1 - core, 1, keepdims=False))
    left_half = jnp.where(first_core, head_mine, head_other)
    right_half = jnp.where(first_core, head_other, head_mine)
    head_rows = jnp.concatenate(
        [left_half[..., :HD], right_half[..., :HD], left_half[..., HD:], right_half[..., HD:]], axis=2
    )
    grad_query = jnp.zeros((own_share, HQ * HD), F32)
    grad_key = jnp.zeros((own_share, HK * HD), F32)
    grad_value = jnp.zeros((own_share, HK * HD), F32)
    for d in range(chips):
        part = index_of(head_rows, chip ^ d)
        if d:
            part = over_chips(part, d)
        part = part.astype(F32)
        grad_query = lax.dynamic_update_slice(grad_query, part[:, : 2 * HD], (0, 2 * HD * (chip ^ d)))
        grad_key = lax.dynamic_update_slice(grad_key, part[:, 2 * HD : 3 * HD], (0, HD * (chip ^ d)))
        grad_value = lax.dynamic_update_slice(grad_value, part[:, 3 * HD :], (0, HD * (chip ^ d)))

    gains = jnp.stack([attn_gain_term, mlp_gain_term]).reshape(2, ctx_count, planes, own_share)

    def gain_block(d):
        return lax.dynamic_index_in_dim(gains, plane ^ d, 2, keepdims=False)

    gain_sum = gain_block(0)
    for d in z_steps:
        gain_sum = gain_sum + over_z(gain_block(d), d)
    gain_sum = gain_sum.reshape(2, chips, 2, own_share)
    gain_sum = lax.dynamic_index_in_dim(gain_sum, core, 2, keepdims=False) + sibling(
        lax.dynamic_index_in_dim(gain_sum, 1 - core, 2, keepdims=False)
    )
    gain_mine = lax.dynamic_index_in_dim(gain_sum, chip, 1, keepdims=False)
    for d in chip_steps:
        gain_mine = gain_mine + over_chips(
            lax.dynamic_index_in_dim(gain_sum, chip ^ d, 1, keepdims=False), d
        )
    return (
        output,
        grad_input,
        grad_query,
        grad_key,
        grad_value,
        grad_out,
        grad_gate,
        grad_up,
        grad_down,
        gain_mine[0],
        gain_mine[1],
    )


def plan_of(mesh):
    chips, planes = mesh.shape["ctx"] // 2, mesh.shape["shard"]
    if mesh.shape["ctx"] == HQ and HQ == 2 * HK and chips == planes == HK:
        return on_device_by_head
    return on_device


def solution(mesh):
    placed = (
        P("shard", "ctx", None),
        P(None, "shard"),
        P(None, "shard"),
        P(None, "shard"),
        P(None, "shard"),
        P(None, "shard"),
        P(None, "shard"),
        P(None, "shard"),
        P(),
        P(),
        P("shard", None),
        P("shard", None),
        P("shard", "ctx", None),
    )
    return jax.shard_map(
        plan_of(mesh),
        mesh=mesh,
        in_specs=placed,
        out_specs=(
            P("shard", "ctx", None),
            P("shard", "ctx", None),
            P(("ctx", "shard"), None),
            P(("ctx", "shard"), None),
            P(("ctx", "shard"), None),
            P(("ctx", "shard"), None),
            P(("ctx", "shard"), None),
            P(("ctx", "shard"), None),
            P(("ctx", "shard"), None),
            P(("ctx", "shard")),
            P(("ctx", "shard")),
        ),
        check_vma=False,
    )
```

```python
import functools
import math

import jax
import jax.numpy as jnp
from jax import lax
from jax.experimental import pallas as pl
from jax.experimental.pallas import tpu as pltpu
from jax.sharding import PartitionSpec as P

HQ = 8
HK = 4
HD = 256
WINDOW = 1024


EPSILON = 1e-06
SCORE_SCALE = 0.0625
MASKED = -1e30
ROPE_BASE = 1000042.0


def position_of(rows, pairs, per_device, blocks_total):
    device = rows // per_device
    within = rows % per_device
    half = per_device // 2
    chosen = jnp.take(pairs, device)
    first = chosen * half + within
    second = (blocks_total - 1 - chosen) * half + within - half
    return jnp.where(within < half, first, second)


def rope_tables(positions, head):
    half = head // 2
    freq = ROPE_BASE ** (-(jnp.arange(half, dtype=jnp.float32) * 2.0) / head)
    angle = positions.astype(jnp.float32)[:, None] * freq[None, :]
    return (jnp.cos(angle), jnp.sin(angle))


def rotate(values, cosine, sine):
    half = values.shape[-1] // 2
    first = values[..., :half]
    second = values[..., half:]
    cosine = cosine[:, None, :]
    sine = sine[:, None, :]
    return jnp.concatenate(
        [first * cosine - second * sine, second * cosine + first * sine], axis=-1
    )


def rotate_back(grads, cosine, sine):
    half = grads.shape[-1] // 2
    first = grads[..., :half]
    second = grads[..., half:]
    cosine = cosine[:, None, :]
    sine = sine[:, None, :]
    return jnp.concatenate(
        [first * cosine + second * sine, second * cosine - first * sine], axis=-1
    )


def visible(query_pos, query_doc, key_pos, key_doc):
    distance = query_pos[:, None] - key_pos[None, :]
    return (query_doc[:, None] == key_doc[None, :]) & (distance >= 0) & (distance < WINDOW)


def write_columns(left, piece):
    made = jnp.dot(left, piece, preferred_element_type=jnp.float32)
    return made


def contract_full(grads, weight):
    return lax.dot_general(
        grads, weight, (((1,), (1,)), ((), ())), preferred_element_type=jnp.float32
    )


def alternate(parts, shard_count, rows):
    return jnp.concatenate([part.reshape(rows, shard_count, -1) for part in parts], axis=2).reshape(
        rows, -1
    )


def outer_sum(left, right):
    return lax.dot_general(
        left, right, (((0,), (0,)), ((), ())), preferred_element_type=jnp.float32
    )


def term_rows(lefts, rights, gain_block, count):
    normed_all, attended_all, second_all, act_all = lefts
    query_g, key_g, value_g, branch_g, gate_g, up_g, upstream_g = rights
    down_part = outer_sum(act_all, upstream_g).reshape(count, -1)
    return jnp.concatenate(
        [
            outer_sum(normed_all, query_g),
            outer_sum(normed_all, key_g),
            outer_sum(normed_all, value_g),
            outer_sum(attended_all, branch_g),
            outer_sum(second_all, gate_g),
            outer_sum(second_all, up_g),
            down_part,
            gain_block,
        ],
        axis=1,
    )


def deal_columns(values, ctx_count, shard_count):
    rows = values.shape[0]
    return (
        values.reshape(rows, ctx_count, shard_count, -1)
        .transpose(0, 2, 1, 3)
        .reshape(rows, shard_count, -1)
    )


def on_device(
    layer_input,
    w_query,
    w_key,
    w_value,
    w_out,
    w_gate,
    w_up,
    w_down,
    attn_gain,
    mlp_gain,
    block_pairs,
    doc_ids,
    cotangent,
):
    tok_rows = layer_input.shape[1]
    model_width = layer_input.shape[2]
    shard_count = lax.axis_size("shard")
    ctx_count = lax.axis_size("ctx")
    device_count = lax.axis_size(("ctx", "shard"))
    group_size = HQ // HK
    blocks_total = 2 * ctx_count
    pairs = block_pairs[0]
    documents = doc_ids[0]
    own_rows = lax.axis_index("ctx") * tok_rows + jnp.arange(tok_rows, dtype=jnp.int32)
    own_pos = position_of(own_rows, pairs, tok_rows, blocks_total)
    own_doc = jnp.take(documents, own_pos)
    cosine, sine = rope_tables(own_pos, HD)
    stack_qkv = jnp.concatenate([w_query, w_key, w_value], axis=1)
    stack_mlp = jnp.concatenate([w_gate, w_up], axis=1)
    per_query = w_query.shape[1]
    per_key = w_key.shape[1]
    per_hidden = w_gate.shape[1]
    hidden_width = w_down.shape[0]
    inputs = layer_input.reshape(tok_rows, model_width).astype(jnp.float32)
    factor_one = lax.rsqrt(jnp.mean(inputs * inputs, axis=-1, keepdims=True) + EPSILON)
    normed = (inputs * factor_one * attn_gain).astype(jnp.bfloat16)
    projected = write_columns(normed, lax.all_gather(stack_qkv, "shard", axis=1, tiled=True))
    projected = projected.reshape(tok_rows, shard_count, -1)
    query_lin = projected[:, :, :per_query].reshape(tok_rows, HQ, HD)
    key_lin = projected[:, :, per_query : per_query + per_key].reshape(tok_rows, HK, HD)
    value_lin = projected[:, :, per_query + per_key :].reshape(tok_rows, HK * HD)
    query_rot = (
        rotate(query_lin, cosine, sine).astype(jnp.bfloat16).reshape(tok_rows, HK, group_size, HD)
    )
    key_rot = rotate(key_lin, cosine, sine).astype(jnp.bfloat16).reshape(tok_rows, HK * HD)
    value_low = value_lin.astype(jnp.bfloat16)

    def key_mask(first_row, count):
        key_pos = position_of(
            first_row + jnp.arange(count, dtype=jnp.int32), pairs, tok_rows, blocks_total
        )
        return visible(own_pos, own_doc, key_pos, jnp.take(documents, key_pos))[:, None, None, :]

    start_state = (
        jnp.full((tok_rows, HK, group_size), MASKED, jnp.float32),
        jnp.zeros((tok_rows, HK, group_size), jnp.float32),
        jnp.zeros((tok_rows, HK, group_size, HD), jnp.float32),
    )
    keys = lax.all_gather(key_rot, "ctx", axis=0, tiled=True)
    values = lax.all_gather(value_low, "ctx", axis=0, tiled=True)
    count = keys.shape[0]
    step = math.gcd(count, 4 * tok_rows)
    keys = keys.reshape(count // step, step, HK, HD)
    values = values.reshape(count // step, step, HK, HD)

    def attend_step(i, running):
        top, total, accum = running
        mask = key_mask(i * step, step)
        scores = (
            jnp.einsum("tkgd,skd->tkgs", query_rot, keys[i], preferred_element_type=jnp.float32)
            * SCORE_SCALE
        )
        scores = jnp.where(mask, scores, MASKED)
        new_top = jnp.maximum(top, jnp.max(scores, axis=-1))
        weights = jnp.where(mask, jnp.exp(scores - new_top[..., None]), 0.0)
        shrink = jnp.exp(top - new_top)
        total = total * shrink + jnp.sum(weights, axis=-1)
        accum = accum * shrink[..., None] + jnp.einsum(
            "tkgs,skd->tkgd",
            weights.astype(jnp.bfloat16),
            values[i],
            preferred_element_type=jnp.float32,
        )
        return (new_top, total, accum)

    top, total, accum = lax.fori_loop(0, count // step, attend_step, start_state)
    log_total = top + jnp.log(total)
    attended_full = accum / total[..., None]
    attended = attended_full.astype(jnp.bfloat16).reshape(tok_rows, HQ * HD)
    branch_one = write_columns(attended, lax.all_gather(w_out, "shard", axis=1, tiled=True))
    mid = inputs + branch_one
    factor_two = lax.rsqrt(jnp.mean(mid * mid, axis=-1, keepdims=True) + EPSILON)
    normed_two = (mid * factor_two * mlp_gain).astype(jnp.bfloat16)
    gate_up = write_columns(normed_two, lax.all_gather(stack_mlp, "shard", axis=1, tiled=True))
    gate_up = gate_up.reshape(tok_rows, shard_count, -1)
    gate = gate_up[:, :, :per_hidden].reshape(tok_rows, hidden_width)
    up_lin = gate_up[:, :, per_hidden:].reshape(tok_rows, hidden_width)
    sigma = jax.nn.sigmoid(gate)
    swish = gate * sigma
    act = (swish * up_lin).astype(jnp.bfloat16)
    branch_two = write_columns(act, lax.all_gather(w_down, "shard", axis=1, tiled=True))
    output = (mid + branch_two).astype(jnp.bfloat16).reshape(1, tok_rows, model_width)
    full_qkv, full_out, full_mlp, full_down = (
        lax.all_gather(stack_qkv, "shard", axis=1, tiled=True),
        lax.all_gather(w_out, "shard", axis=1, tiled=True),
        lax.all_gather(stack_mlp, "shard", axis=1, tiled=True),
        lax.all_gather(w_down, "shard", axis=1, tiled=True),
    )
    upstream_low = cotangent.reshape(tok_rows, model_width)
    upstream = upstream_low.astype(jnp.float32)
    act_grad = contract_full(upstream_low, full_down)
    gate_grad = (act_grad * up_lin * (sigma * (1.0 + gate * (1.0 - sigma)))).astype(jnp.bfloat16)
    up_grad = (act_grad * swish).astype(jnp.bfloat16)
    stacked_mlp_grad = alternate((gate_grad, up_grad), shard_count, tok_rows)
    norm_two_grad = contract_full(stacked_mlp_grad, full_mlp)
    mlp_gain_term = jnp.sum(norm_two_grad * mid * factor_two, axis=0)
    scaled_two = norm_two_grad * mlp_gain
    mid_grad = (
        upstream
        + factor_two * scaled_two
        - mid * factor_two**3 * jnp.mean(scaled_two * mid, axis=-1, keepdims=True)
    )
    branch_grad = mid_grad.astype(jnp.bfloat16)
    attended_grad = contract_full(branch_grad, full_out)
    attended_low = attended_grad.astype(jnp.bfloat16).reshape(tok_rows, HK, group_size, HD)
    delta = jnp.sum(attended_low.astype(jnp.float32) * attended_full, axis=-1)

    def query_grads(carry, piece):
        keys, values = piece
        count = keys.shape[0]
        step = math.gcd(count, 4 * tok_rows)
        keys = keys.reshape(count // step, step, HK, HD)
        values = values.reshape(count // step, step, HK, HD)

        def query_step(i, query_sum):
            mask = key_mask(i * step, step)
            scores = (
                jnp.einsum("tkgd,skd->tkgs", query_rot, keys[i], preferred_element_type=jnp.float32)
                * SCORE_SCALE
            )
            probs = jnp.where(mask, jnp.exp(scores - log_total[..., None]), 0.0)
            prob_grad = jnp.einsum(
                "tkgd,skd->tkgs", attended_low, values[i], preferred_element_type=jnp.float32
            )
            score_grad = (probs * (prob_grad - delta[..., None])).astype(jnp.bfloat16)
            return query_sum + jnp.einsum(
                "tkgs,skd->tkgd", score_grad, keys[i], preferred_element_type=jnp.float32
            )

        return lax.fori_loop(0, count // step, query_step, carry)

    query_sum = query_grads(
        jnp.zeros((tok_rows, HK, group_size, HD), jnp.float32),
        (
            lax.all_gather(key_rot, "ctx", axis=0, tiled=True),
            lax.all_gather(value_low, "ctx", axis=0, tiled=True),
        ),
    )
    all_log_total, all_delta = (
        lax.all_gather(log_total, "ctx", axis=0, tiled=True),
        lax.all_gather(delta, "ctx", axis=0, tiled=True),
    )
    key_three = key_rot.reshape(tok_rows, HK, HD)
    value_three = value_low.reshape(tok_rows, HK, HD)

    def key_grads(carry, piece):
        queries, outgrads = piece
        count = queries.shape[0]
        step = math.gcd(count, 4 * tok_rows)
        queries = queries.reshape(count // step, step, HK, group_size, HD)
        outgrads = outgrads.reshape(count // step, step, HK, group_size, HD)

        def key_step(i, running):
            key_sum, value_sum = running
            first_row = i * step
            query_pos = position_of(
                first_row + jnp.arange(step, dtype=jnp.int32), pairs, tok_rows, blocks_total
            )
            mask = visible(query_pos, jnp.take(documents, query_pos), own_pos, own_doc)[
                :, None, None, :
            ]
            lse_part = lax.dynamic_slice_in_dim(all_log_total, first_row, step, 0)
            delta_part = lax.dynamic_slice_in_dim(all_delta, first_row, step, 0)
            scores = (
                jnp.einsum(
                    "skgd,tkd->skgt", queries[i], key_three, preferred_element_type=jnp.float32
                )
                * SCORE_SCALE
            )
            probs = jnp.where(mask, jnp.exp(scores - lse_part[..., None]), 0.0)
            prob_grad = jnp.einsum(
                "skgd,tkd->skgt", outgrads[i], value_three, preferred_element_type=jnp.float32
            )
            score_grad = (probs * (prob_grad - delta_part[..., None])).astype(jnp.bfloat16)
            value_sum = value_sum + jnp.einsum(
                "skgt,skgd->tkd",
                probs.astype(jnp.bfloat16),
                outgrads[i],
                preferred_element_type=jnp.float32,
            )
            key_sum = key_sum + jnp.einsum(
                "skgt,skgd->tkd", score_grad, queries[i], preferred_element_type=jnp.float32
            )
            return (key_sum, value_sum)

        return lax.fori_loop(0, count // step, key_step, carry)

    key_sum, value_sum = key_grads(
        (jnp.zeros((tok_rows, HK, HD), jnp.float32), jnp.zeros((tok_rows, HK, HD), jnp.float32)),
        (
            lax.all_gather(query_rot.reshape(tok_rows, HQ * HD), "ctx", axis=0, tiled=True),
            lax.all_gather(attended_low.reshape(tok_rows, HQ * HD), "ctx", axis=0, tiled=True),
        ),
    )
    query_grad = (
        rotate_back(query_sum.reshape(tok_rows, HQ, HD) * SCORE_SCALE, cosine, sine)
        .astype(jnp.bfloat16)
        .reshape(tok_rows, HQ * HD)
    )
    key_grad = (
        rotate_back(key_sum * SCORE_SCALE, cosine, sine)
        .astype(jnp.bfloat16)
        .reshape(tok_rows, HK * HD)
    )
    value_grad = value_sum.astype(jnp.bfloat16).reshape(tok_rows, HK * HD)
    stacked_qkv_grad = alternate((query_grad, key_grad, value_grad), shard_count, tok_rows)
    normed_grad = contract_full(stacked_qkv_grad, full_qkv)
    attn_gain_term = jnp.sum(normed_grad * inputs * factor_one, axis=0)
    scaled_one = normed_grad * attn_gain
    input_grad = (
        mid_grad
        + factor_one * scaled_one
        - inputs * factor_one**3 * jnp.mean(scaled_one * inputs, axis=-1, keepdims=True)
    )
    grad_input = input_grad.astype(jnp.bfloat16).reshape(1, tok_rows, model_width)
    ratio = hidden_width // model_width
    own_share = model_width // device_count
    rights = (query_grad, key_grad, value_grad, branch_grad, gate_grad, up_grad, upstream_low)
    group_rights = (
        lax.all_gather(rights[0], "shard", axis=0, tiled=True),
        lax.all_gather(rights[1], "shard", axis=0, tiled=True),
        lax.all_gather(rights[2], "shard", axis=0, tiled=True),
        lax.all_gather(rights[3], "shard", axis=0, tiled=True),
        lax.all_gather(rights[4], "shard", axis=0, tiled=True),
        lax.all_gather(rights[5], "shard", axis=0, tiled=True),
        lax.all_gather(rights[6], "shard", axis=0, tiled=True),
    )
    dealt = (
        lax.all_to_all(
            deal_columns(normed, ctx_count, shard_count),
            "shard",
            split_axis=1,
            concat_axis=0,
            tiled=True,
        ),
        lax.all_to_all(
            deal_columns(attended, ctx_count, shard_count),
            "shard",
            split_axis=1,
            concat_axis=0,
            tiled=True,
        ),
        lax.all_to_all(
            deal_columns(normed_two, ctx_count, shard_count),
            "shard",
            split_axis=1,
            concat_axis=0,
            tiled=True,
        ),
        lax.all_to_all(
            deal_columns(act, ctx_count, shard_count),
            "shard",
            split_axis=1,
            concat_axis=0,
            tiled=True,
        ),
    )
    group_lefts = tuple((part.reshape(part.shape[0], -1) for part in dealt))
    gain_pair = lax.psum(jnp.stack([attn_gain_term, mlp_gain_term]), "shard")
    gain_mine = lax.dynamic_index_in_dim(
        gain_pair.reshape(2, ctx_count, shard_count, own_share),
        lax.axis_index("shard"),
        2,
        keepdims=False,
    ).reshape(2, ctx_count * own_share)
    gain_block = jnp.concatenate(
        [gain_mine.T, jnp.zeros((ctx_count * own_share, 126), jnp.float32)], axis=1
    )
    summed = lax.psum_scatter(
        term_rows(group_lefts, group_rights, gain_block, own_share * lax.axis_size("ctx")).astype(
            jnp.bfloat16
        ),
        "ctx",
        scatter_dimension=0,
        tiled=True,
    ).astype(jnp.float32)
    edge_one = HQ * HD
    edge_two = edge_one + HK * HD
    edge_three = edge_two + HK * HD
    edge_four = edge_three + model_width
    edge_five = edge_four + hidden_width
    edge_six = edge_five + hidden_width
    edge_seven = edge_six + ratio * model_width
    grad_query = summed[:, :edge_one]
    grad_key = summed[:, edge_one:edge_two]
    grad_value = summed[:, edge_two:edge_three]
    grad_out = summed[:, edge_three:edge_four]
    grad_gate = summed[:, edge_four:edge_five]
    grad_up = summed[:, edge_five:edge_six]
    grad_down = summed[:, edge_six:edge_seven].reshape(own_share * ratio, model_width)
    grad_attn_gain = summed[:, edge_seven]
    grad_mlp_gain = summed[:, edge_seven + 1]
    return (
        output,
        grad_input,
        grad_query,
        grad_key,
        grad_value,
        grad_out,
        grad_gate,
        grad_up,
        grad_down,
        grad_attn_gain,
        grad_mlp_gain,
    )


BF16 = jnp.bfloat16
F32 = jnp.float32
VISIBLE_ROWS = 256


def dot_nn(a, b):
    return jnp.dot(a, b, preferred_element_type=F32)


def dot_nt(a, b):
    return lax.dot_general(a, b, (((1,), (1,)), ((), ())), preferred_element_type=F32)


def dot_tn(a, b):
    return lax.dot_general(a, b, (((0,), (0,)), ((), ())), preferred_element_type=F32)


def scores_of(query, key, code, low_code, key_code):
    scores = dot_nt(query, key) * SCORE_SCALE
    mask = (key_code <= code) & (key_code >= low_code)
    return jnp.where(mask, scores, MASKED)


def attend_kernel(query, key, value, code, low_code, key_code, attended, log_total):
    scores = scores_of(query[...], key[...], code[...], low_code[...], key_code[...])
    top = jnp.max(scores, axis=-1, keepdims=True)
    weights = jnp.exp(scores - top)
    total = jnp.sum(weights, axis=-1, keepdims=True)
    mixed = dot_nn(weights.astype(BF16), value[...])
    attended[...] = (mixed / total).astype(BF16)
    log_total[...] = top + jnp.log(total)


def attend(query, key, value, code, low_code, key_code):
    rows, head = query.shape
    step = math.gcd(rows, VISIBLE_ROWS)
    by_row = lambda width: pl.BlockSpec((step, width), lambda i: (i, 0))
    whole = lambda shape: pl.BlockSpec(shape, lambda i: (0, 0))
    return pl.pallas_call(
        attend_kernel,
        grid=(rows // step,),
        in_specs=[
            by_row(head),
            whole(key.shape),
            whole(value.shape),
            by_row(1),
            by_row(1),
            whole(key_code.shape),
        ],
        out_specs=[by_row(head), by_row(1)],
        out_shape=[
            jax.ShapeDtypeStruct((rows, head), BF16),
            jax.ShapeDtypeStruct((rows, 1), F32),
        ],
        compiler_params=pltpu.CompilerParams(vmem_limit_bytes=32 << 20),
        cost_estimate=pl.CostEstimate(
            flops=4 * rows * key.shape[0] * head,
            bytes_accessed=8 * rows * head,
            transcendentals=rows * key.shape[0],
        ),
    )(query, key, value, code, low_code, key_code)


def attend_back_kernel(
    query, outgrad, key, value, log_total, code, low_code, key_code, d_query, d_key, d_value
):
    @pl.when(pl.program_id(0) == 0)
    def _():
        d_key[...] = jnp.zeros_like(d_key)
        d_value[...] = jnp.zeros_like(d_value)

    scores = scores_of(query[...], key[...], code[...], low_code[...], key_code[...])
    probs = jnp.exp(scores - log_total[...])
    prob_grad = dot_nt(outgrad[...], value[...])
    delta = jnp.sum(probs * prob_grad, axis=-1, keepdims=True)
    score_grad = (probs * (prob_grad - delta)).astype(BF16)
    d_query[...] = dot_nn(score_grad, key[...]) * SCORE_SCALE
    d_key[...] += dot_tn(score_grad, query[...]) * SCORE_SCALE
    d_value[...] += dot_tn(probs.astype(BF16), outgrad[...])


def attend_back(query, outgrad, key, value, log_total, code, low_code, key_code):
    rows, head = query.shape
    step = math.gcd(rows, VISIBLE_ROWS)
    by_row = lambda width: pl.BlockSpec((step, width), lambda i: (i, 0))
    whole = lambda shape: pl.BlockSpec(shape, lambda i: (0, 0))
    return pl.pallas_call(
        attend_back_kernel,
        grid=(rows // step,),
        in_specs=[
            by_row(head),
            by_row(head),
            whole(key.shape),
            whole(value.shape),
            by_row(1),
            by_row(1),
            by_row(1),
            whole(key_code.shape),
        ],
        out_specs=[by_row(head), whole(key.shape), whole(value.shape)],
        out_shape=[
            jax.ShapeDtypeStruct((rows, head), F32),
            jax.ShapeDtypeStruct(key.shape, F32),
            jax.ShapeDtypeStruct(value.shape, F32),
        ],
        compiler_params=pltpu.CompilerParams(vmem_limit_bytes=40 << 20),
        cost_estimate=pl.CostEstimate(
            flops=10 * rows * key.shape[0] * head,
            bytes_accessed=20 * rows * head,
            transcendentals=rows * key.shape[0],
        ),
    )(query, outgrad, key, value, log_total, code, low_code, key_code)


MESH = pl.DeviceIdType.MESH
TILE = 256


def flip(i, d):
    return (i, i + 1 - 2 * (i % 2), (i + 2) % 4, 3 - i)[d]


def mlp_kernel(
    second_ref,
    mid_ref,
    upstream_ref,
    gain_ref,
    upstream_hbm,
    gate_hbm,
    up_hbm,
    down_hbm,
    output_ref,
    mid_grad_ref,
    gain_grad_ref,
    branch_all,
    gate_up_terms,
    down_terms,
    gate_w,
    up_w,
    down_w,
    upstream_all,
    second_all,
    act,
    gate_grad,
    up_grad,
    held,
    own_sum,
    pair_send,
    pair_recv,
    z_send,
    z_recv,
    branch_low,
    staged,
    local_sem,
    staged_sem,
    send_sem,
    recv_sem,
):
    tok = second_ref.shape[0]
    pair = 2 * tok
    hidden = gate_w.shape[1]
    width = second_ref.shape[1]
    ctx, plane = lax.axis_index("ctx"), lax.axis_index("shard")
    chip, core = ctx // 2, ctx % 2
    sibling = (ctx + 1 - 2 * core, plane)
    over_z = [(ctx, flip(plane, d)) for d in range(4)]
    over_chips = [(2 * flip(chip, d) + core, plane) for d in range(4)]

    half = pl.ds(pl.multiple_of(core * hidden, hidden), hidden)
    loads = [
        pltpu.make_async_copy(upstream_hbm, upstream_all, local_sem.at[0]),
        pltpu.make_async_copy(down_hbm, down_w, local_sem.at[1]),
        pltpu.make_async_copy(gate_hbm.at[:, half], gate_w, local_sem.at[2]),
        pltpu.make_async_copy(up_hbm.at[:, half], up_w, local_sem.at[3]),
        pltpu.make_async_copy(second_ref, second_all.at[0, 0], local_sem.at[4]),
    ]
    for load in loads:
        load.start()

    barrier = pltpu.get_barrier_semaphore()
    partners = [sibling] + over_z[1:] + over_chips[1:]
    for partner in partners:
        pl.semaphore_signal(barrier, inc=1, device_id=partner, device_id_type=MESH)
    pl.semaphore_wait(barrier, len(partners))

    def send(slot, source, target, device):
        copy = pltpu.make_async_remote_copy(
            src_ref=source,
            dst_ref=target,
            send_sem=send_sem.at[slot],
            recv_sem=recv_sem.at[slot],
            device_id=device,
            device_id_type=MESH,
        )
        copy.start()
        return copy

    gather_z = {d: send(d, second_ref, second_all.at[d, 0], over_z[d]) for d in (1, 2, 3)}
    gather_pair = {0: send(0, second_ref, second_all.at[0, 1], sibling)}
    for load in loads:
        load.wait()

    def rows_of(d):
        return pl.ds(d * pair, pair)

    def forward(d):
        rows = rows_of(d)
        second = lambda: second_all[d].reshape(pair, width)

        def step(t, carry):
            at = pl.ds(pl.multiple_of(t * TILE, TILE), TILE)
            act_grad = dot_nt(upstream_all[rows, :], down_w[at, :])
            gate = dot_nn(second(), gate_w[:, at])
            up_lin = dot_nn(second(), up_w[:, at])
            sigma = 1.0 / (1.0 + jnp.exp(-gate))
            swish = gate * sigma
            act[rows, at] = (swish * up_lin).astype(BF16)
            gate_grad[rows, at] = (
                act_grad * up_lin * (sigma * (1.0 + gate * (1.0 - sigma)))
            ).astype(BF16)
            up_grad[rows, at] = (act_grad * swish).astype(BF16)
            return carry

        lax.fori_loop(0, hidden // TILE, step, 0)

    def give_pair(d, base, product):
        which = 0 if base == 7 else 1

        def step(t, carry):
            at = pl.ds(pl.multiple_of(t * TILE, TILE), TILE)
            terms = product(at)
            held[d % 2, :, at] = terms[:tok]
            pair_send[which, d, :, at] = terms[tok:].astype(BF16)
            return carry

        lax.fori_loop(0, width // TILE, step, 0)
        return send(base + d, pair_send.at[which, d], pair_recv.at[which, d], sibling)

    def give_plane(d, base, copy):
        which = 0 if base == 7 else 1
        copy.wait_recv()
        total = held[d % 2] + pair_recv[which, d].astype(F32)
        if d == 0:
            own_sum[which] = total
            return None
        z_send[which, d - 1] = total.astype(BF16)
        return send(base + 3 + d, z_send.at[which, d - 1], z_recv.at[which, d - 1], over_z[d])

    def back(d):
        rows = rows_of(d)
        return lambda at: dot_nt(gate_grad[rows, :], gate_w[at, :]) + dot_nt(
            up_grad[rows, :], up_w[at, :]
        )

    def onward(d):
        rows = rows_of(d)
        return lambda at: dot_nn(act[rows, :], down_w[:, at])

    pairs, planes = {}, {}
    for d in range(4):
        if d:
            gather_z[d].wait_recv()
            gather_pair[d] = send(
                3 + d, second_all.at[d, 0], second_all.at[d, 1], sibling
            )
        gather_pair[d].wait_recv()
        forward(d)
        pairs[d] = give_pair(d, 7, back(d))
        if d:
            planes[d - 1] = give_plane(d - 1, 7, pairs[d - 1])
    planes[3] = give_plane(3, 7, pairs[3])

    out_pairs, out_planes = {}, {}
    for d in range(4):
        out_pairs[d] = give_pair(d, 14, onward(d))
        if d:
            out_planes[d - 1] = give_plane(d - 1, 14, out_pairs[d - 1])
    out_planes[3] = give_plane(3, 14, out_pairs[3])

    second_rows = second_all.reshape(8 * tok, width)

    def to_hbm(slot, target):
        return pltpu.make_async_copy(staged.at[slot], target, staged_sem.at[slot])

    def gate_up_step(d):
        for h in range(2):
            first = flip(chip, d) * (2 * TILE) + h * TILE
            left = second_rows[:, pl.ds(pl.multiple_of(first, TILE), TILE)]
            target = gate_up_terms.at[d, pl.ds(h * TILE, TILE)]
            if d:
                to_hbm(h, target).wait()
            staged[h, :, :hidden] = dot_tn(left, gate_grad[...]).astype(BF16)
            staged[h, :, hidden:] = dot_tn(left, up_grad[...]).astype(BF16)
            to_hbm(h, target).start()

    for d in range(4):
        gate_up_step(d)

    for d in (1, 2, 3):
        planes[d].wait_recv()
    chunk = 32
    gain = gain_ref[...]

    def mid_step(i, carry):
        at = pl.ds(pl.multiple_of(i * chunk, chunk), chunk)
        grad = own_sum[0, at, :]
        for d in range(3):
            grad = grad + z_recv[0, d, at, :].astype(F32)
        mid = mid_ref[at, :]
        factor = lax.rsqrt(jnp.mean(mid * mid, axis=-1, keepdims=True) + EPSILON)
        scaled = grad * gain
        mid_grad = (
            upstream_ref[at, :].astype(F32)
            + factor * scaled
            - mid * (factor * factor * factor * jnp.mean(scaled * mid, axis=-1, keepdims=True))
        )
        mid_grad_ref[at, :] = mid_grad
        branch_low[at, :] = mid_grad.astype(BF16)
        return carry + jnp.sum(grad * mid * factor, axis=0, keepdims=True)

    gain_grad_ref[...] = lax.fori_loop(0, tok // chunk, mid_step, jnp.zeros((1, width), F32))
    branch_chips = {
        d: send(20 + d, branch_low, branch_all.at[0, d], over_chips[d]) for d in (1, 2, 3)
    }
    branch_pairs = {0: send(24, branch_low, branch_all.at[1, 0], sibling)}
    keep = pltpu.make_async_copy(branch_low, branch_all.at[0, 0], local_sem.at[0])
    keep.start()

    def down_step(t):
        slot = t % 2
        target = down_terms.at[pl.ds(t * TILE, TILE)]
        to_hbm(slot, target).wait()
        left = act[:, pl.ds(t * TILE, TILE)]
        staged[slot] = dot_tn(left, upstream_all[...]).astype(BF16)
        to_hbm(slot, target).start()

    for t in range(hidden // TILE):
        down_step(t)
    for d in (1, 2, 3):
        branch_chips[d].wait_recv()
        branch_pairs[d] = send(24 + d, branch_all.at[0, d], branch_all.at[1, d], sibling)

    for d in (1, 2, 3):
        out_planes[d].wait_recv()

    def out_step(i, carry):
        at = pl.ds(pl.multiple_of(i * chunk, chunk), chunk)
        total = mid_ref[at, :] + own_sum[1, at, :]
        for d in range(3):
            total = total + z_recv[1, d, at, :].astype(F32)
        output_ref[at, :] = total.astype(BF16)
        return carry

    lax.fori_loop(0, tok // chunk, out_step, 0)

    for d in range(4):
        branch_pairs[d].wait_recv()
        for copy in (gather_pair[d], pairs[d], out_pairs[d], branch_pairs[d]):
            copy.wait_send()
    for d in (1, 2, 3):
        for copy in (gather_z[d], planes[d], out_planes[d], branch_chips[d]):
            copy.wait_send()
    keep.wait()
    for slot in range(2):
        to_hbm(slot, down_terms.at[pl.ds(0, TILE)]).wait()


def mlp_of(normed_two, mid, upstream, gain, upstream_group, w_gate, w_up, down_rows):
    tok, width = mid.shape
    hidden = down_rows.shape[0]
    rows = upstream_group.shape[0]
    vmem = pl.BlockSpec(memory_space=pltpu.VMEM)
    hbm = pl.BlockSpec(memory_space=pl.ANY)
    return pl.pallas_call(
        mlp_kernel,
        in_specs=[vmem] * 4 + [hbm] * 4,
        out_specs=[vmem] * 3 + [hbm] * 3,
        out_shape=[
            jax.ShapeDtypeStruct((tok, width), BF16),
            jax.ShapeDtypeStruct((tok, width), F32),
            jax.ShapeDtypeStruct((1, width), F32),
            jax.ShapeDtypeStruct((2, 4, tok, width), BF16),
            jax.ShapeDtypeStruct((4, 2 * TILE, 2 * hidden), BF16),
            jax.ShapeDtypeStruct((hidden, width), BF16),
        ],
        scratch_shapes=[
            pltpu.VMEM((width, hidden), BF16),
            pltpu.VMEM((width, hidden), BF16),
            pltpu.VMEM((hidden, width), BF16),
            pltpu.VMEM((rows, width), BF16),
            pltpu.VMEM((4, 2, tok, width), BF16),
            pltpu.VMEM((rows, hidden), BF16),
            pltpu.VMEM((rows, hidden), BF16),
            pltpu.VMEM((rows, hidden), BF16),
            pltpu.VMEM((2, tok, width), F32),
            pltpu.VMEM((2, tok, width), F32),
            pltpu.VMEM((2, 4, tok, width), BF16),
            pltpu.VMEM((2, 4, tok, width), BF16),
            pltpu.VMEM((2, 3, tok, width), BF16),
            pltpu.VMEM((2, 3, tok, width), BF16),
            pltpu.VMEM((tok, width), BF16),
            pltpu.VMEM((2, TILE, width), BF16),
            pltpu.SemaphoreType.DMA((5,)),
            pltpu.SemaphoreType.DMA((2,)),
            pltpu.SemaphoreType.DMA((28,)),
            pltpu.SemaphoreType.DMA((28,)),
        ],
        compiler_params=pltpu.CompilerParams(
            collective_id=1, has_side_effects=True, vmem_limit_bytes=60 << 20
        ),
        cost_estimate=pl.CostEstimate(
            flops=18 * rows * width * hidden,
            bytes_accessed=2 * (5 * width * hidden + 4 * rows * width),
            transcendentals=rows * hidden,
        ),
    )(normed_two, mid, upstream, gain, upstream_group, w_gate, w_up, down_rows)


def rotate_head(values, cosine, sine):
    half = values.shape[-1] // 2
    first, second = values[:, :half], values[:, half:]
    return jnp.concatenate([first * cosine - second * sine, second * cosine + first * sine], axis=1)


def swap_halves(values):
    half = values.shape[0] // 2
    return jnp.concatenate([values[half:], values[:half]], axis=0)


def index_of(stacked, i):
    return lax.dynamic_index_in_dim(stacked, i, 0, keepdims=False)


def cut(values, starts, sizes):
    return lax.dynamic_slice(values, starts, sizes)


def on_device_by_head(
    layer_input,
    w_query,
    w_key,
    w_value,
    w_out,
    w_gate,
    w_up,
    w_down,
    attn_gain,
    mlp_gain,
    block_pairs,
    doc_ids,
    cotangent,
):
    tok_rows, width = layer_input.shape[1:]
    planes = lax.axis_size("shard")
    ctx_count = lax.axis_size("ctx")
    chips = ctx_count // 2
    ctx, plane = lax.axis_index("ctx"), lax.axis_index("shard")
    chip, core = ctx // 2, ctx % 2
    first_core = core == 0
    seq_rows = tok_rows * ctx_count
    half_seq = seq_rows // 2
    shard_width = w_down.shape[1]
    hidden_plane = w_gate.shape[1]
    hidden = hidden_plane // 2
    own_share = width // (planes * ctx_count)

    def over_z(values, d):
        return lax.ppermute(values, "shard", [(i, i ^ d) for i in range(planes)])

    def over_chips(values, d):
        return lax.ppermute(values, "ctx", [(i, i ^ (2 * d)) for i in range(ctx_count)])

    def sibling(values):
        return lax.ppermute(values, "ctx", [(i, i ^ 1) for i in range(ctx_count)])

    z_steps = range(1, planes)
    chip_steps = range(1, chips)

    def gather_z(values):
        return [values] + [over_z(values, d) for d in z_steps]

    def gather_chips(values):
        return [values] + [over_chips(values, d) for d in chip_steps]

    def gather_seq(values):
        mine = jnp.concatenate(gather_chips(values), axis=0)
        return jnp.concatenate([mine, sibling(mine)], axis=0)

    def gather_group(values):
        mine = jnp.stack(gather_z(values))
        return jnp.stack([mine, sibling(mine)], axis=1).reshape(-1, width)

    def sum_chips(block_of):
        total = block_of(0)
        for d in chip_steps:
            total = total + over_chips(block_of(d).astype(BF16), d).astype(F32)
        return total

    def sum_z(block_of):
        total = block_of(0)
        for d in z_steps:
            total = total + over_z(block_of(d).astype(BF16), d).astype(F32)
        return total

    quarter = width // chips
    head_block = jnp.concatenate(
        [
            cut(w_query, (quarter * chip, HD * core), (quarter, HD)),
            jnp.where(
                first_core,
                cut(w_key, (quarter * chip, 0), (quarter, HD)),
                cut(w_value, (quarter * chip, 0), (quarter, HD)),
            ),
        ],
        axis=1,
    )
    head_parts = jnp.stack(gather_z(head_block))
    w_head = jnp.zeros((width, 2 * HD), BF16)
    for d in range(chips):
        part = index_of(head_parts, plane ^ chip ^ d)
        if d:
            part = over_chips(part, d)
        w_head = lax.dynamic_update_slice(w_head, part, (quarter * (chip ^ d), 0))

    inputs_low = layer_input[0]
    inputs = inputs_low.astype(F32)
    all_inputs = gather_seq(inputs_low).astype(F32)
    pairs, documents = block_pairs[0], doc_ids[0]
    order = jnp.stack([(chip ^ d) * 2 + (core ^ e) for e in range(2) for d in range(chips)])
    rows = (order[:, None] * tok_rows + jnp.arange(tok_rows, dtype=jnp.int32)[None, :]).reshape(-1)
    positions = position_of(rows, pairs, tok_rows, 2 * ctx_count).astype(jnp.int32)
    span = 2 * seq_rows
    doc_first = jnp.take(documents, positions).astype(jnp.int32) * span
    code = doc_first + positions
    low_code = jnp.maximum(doc_first, code - (WINDOW - 1))
    code_column, low_column, code_row = code[:, None], low_code[:, None], code[None, :]
    cosine, sine = rope_tables(positions, HD)

    factor_all = lax.rsqrt(jnp.mean(all_inputs * all_inputs, axis=-1, keepdims=True) + EPSILON)
    normed_all = (all_inputs * factor_all * attn_gain).astype(BF16)
    projected = dot_nn(normed_all, w_head)
    query = rotate_head(projected[:, :HD], cosine, sine).astype(BF16)
    key_cosine = jnp.where(first_core, cosine, 1.0)
    key_sine = jnp.where(first_core, sine, 0.0)
    mine_kv = rotate_head(projected[:, HD:], key_cosine, key_sine).astype(BF16)
    other_kv = swap_halves(sibling(mine_kv))
    key = jnp.where(first_core, mine_kv, other_kv)
    value = jnp.where(first_core, other_kv, mine_kv)
    attended, log_total = attend(query, key, value, code_column, low_column, code_row)

    out_rows = jnp.zeros((HD, width), BF16)
    for d, part in enumerate(gather_z(cut(w_out, (HD * ctx, 0), (HD, shard_width)))):
        out_rows = lax.dynamic_update_slice(out_rows, part, (0, shard_width * (plane ^ d)))
    out_pair = jnp.concatenate([out_rows, sibling(out_rows)], axis=0)
    attended_pair = jnp.concatenate([attended[:half_seq], sibling(attended[half_seq:])], axis=1)
    branch_parts = dot_nn(attended_pair, out_pair).reshape(chips, tok_rows, width)
    mid = inputs + sum_chips(lambda d: branch_parts[d])
    factor_two = lax.rsqrt(jnp.mean(mid * mid, axis=-1, keepdims=True) + EPSILON)
    normed_two = (mid * factor_two * mlp_gain).astype(BF16)

    quarter_hidden = hidden // chips
    down_block = jnp.zeros((quarter_hidden, width), BF16)
    for d in range(planes):
        start = hidden_plane * (plane ^ d) + hidden * core + quarter_hidden * chip
        part = cut(w_down, (start, 0), (quarter_hidden, shard_width))
        if d:
            part = over_z(part, d)
        down_block = lax.dynamic_update_slice(down_block, part, (0, shard_width * (plane ^ d)))
    down_rows = jnp.zeros((hidden, width), BF16)
    for d, part in enumerate(gather_chips(down_block)):
        down_rows = lax.dynamic_update_slice(down_rows, part, (quarter_hidden * (chip ^ d), 0))

    upstream_low = cotangent[0]
    upstream_group = gather_group(upstream_low)
    output, mid_grad, mlp_gain_term, branch_grad_all, gate_up_terms, down_terms = mlp_of(
        normed_two, mid, upstream_low, mlp_gain[None], upstream_group, w_gate, w_up, down_rows
    )
    output = output[None]
    mlp_gain_term = mlp_gain_term[0]
    branch_grad_all = branch_grad_all.reshape(seq_rows, width)

    attended_grad = dot_nt(branch_grad_all, out_rows).astype(BF16)
    d_query, d_key, d_value = attend_back(
        query, attended_grad, key, value, log_total, code_column, low_column, code_row
    )
    keep = jnp.where(first_core, d_key, d_value)
    give = jnp.where(first_core, d_value, d_key)
    d_kv = keep + swap_halves(sibling(give))
    d_head = jnp.concatenate(
        [rotate_head(d_query, cosine, -sine), rotate_head(d_kv, key_cosine, -key_sine)], axis=1
    ).astype(BF16)
    d_head_pair = jnp.concatenate([d_head[:half_seq], sibling(d_head[half_seq:])], axis=1)
    w_head_pair = jnp.concatenate([w_head, sibling(w_head)], axis=1)
    normed_parts = dot_nt(d_head_pair, w_head_pair).reshape(chips, tok_rows, width)
    normed_grad = sum_chips(lambda d: normed_parts[d])
    factor_one = factor_all[:tok_rows]
    attn_gain_term = jnp.sum(normed_grad * inputs * factor_one, axis=0)
    scaled_one = normed_grad * attn_gain
    grad_input = (
        mid_grad
        + factor_one * scaled_one
        - inputs * factor_one**3 * jnp.mean(scaled_one * inputs, axis=-1, keepdims=True)
    ).astype(BF16)[None]

    mlp_sum = sum_chips(lambda d: gate_up_terms[d].astype(F32)).astype(BF16).reshape(2, quarter // 2, 2 * hidden)
    mlp_mine = index_of(mlp_sum, core)
    mlp_other = sibling(index_of(mlp_sum, 1 - core))
    left_half = jnp.where(first_core, mlp_mine, mlp_other)
    right_half = jnp.where(first_core, mlp_other, mlp_mine)
    mlp_rows_all = jnp.concatenate(
        [left_half[:, :hidden], right_half[:, :hidden], left_half[:, hidden:], right_half[:, hidden:]],
        axis=1,
    ).reshape(planes, own_share, 2 * hidden_plane)
    grad_gate = jnp.zeros((own_share, planes * hidden_plane), F32)
    grad_up = jnp.zeros((own_share, planes * hidden_plane), F32)
    for d in range(planes):
        part = index_of(mlp_rows_all, plane ^ d)
        if d:
            part = over_z(part, d)
        part = part.astype(F32)
        at = (0, hidden_plane * (plane ^ d))
        grad_gate = lax.dynamic_update_slice(grad_gate, part[:, :hidden_plane], at)
        grad_up = lax.dynamic_update_slice(grad_up, part[:, hidden_plane:], at)

    down_terms = down_terms.reshape(planes, chips, -1, width)
    down_sum = sum_chips(
        lambda d: lax.dynamic_index_in_dim(down_terms, chip ^ d, 1, keepdims=False).astype(F32)
    ).astype(BF16)
    down_parts = []
    for d in range(planes):
        part = index_of(down_sum, plane ^ d)
        down_parts.append(over_z(part, d) if d else part)
    down_parts = jnp.stack(down_parts)
    share = down_parts.shape[1]
    grad_down = jnp.zeros((chips * share, width), F32)
    for d in range(chips):
        part = index_of(down_parts, plane ^ chip ^ d)
        if d:
            part = over_chips(part, d)
        grad_down = lax.dynamic_update_slice(grad_down, part.astype(F32), (share * (chip ^ d), 0))

    out_terms = dot_tn(attended, branch_grad_all).reshape(planes, own_share, width)
    grad_out = sum_z(lambda d: index_of(out_terms, plane ^ d))

    head_terms = dot_tn(normed_all, d_head).reshape(ctx_count, planes, own_share, 2 * HD)
    head_sum = sum_z(
        lambda d: lax.dynamic_index_in_dim(head_terms, plane ^ d, 1, keepdims=False)
    ).astype(BF16)
    head_sum = head_sum.reshape(chips, 2, own_share, 2 * HD)
    head_mine = lax.dynamic_index_in_dim(head_sum, core, 1, keepdims=False)
    head_other = sibling(lax.dynamic_index_in_dim(head_sum, 1 - core, 1, keepdims=False))
    left_half = jnp.where(first_core, head_mine, head_other)
    right_half = jnp.where(first_core, head_other, head_mine)
    head_rows = jnp.concatenate(
        [left_half[..., :HD], right_half[..., :HD], left_half[..., HD:], right_half[..., HD:]], axis=2
    )
    grad_query = jnp.zeros((own_share, HQ * HD), F32)
    grad_key = jnp.zeros((own_share, HK * HD), F32)
    grad_value = jnp.zeros((own_share, HK * HD), F32)
    for d in range(chips):
        part = index_of(head_rows, chip ^ d)
        if d:
            part = over_chips(part, d)
        part = part.astype(F32)
        grad_query = lax.dynamic_update_slice(grad_query, part[:, : 2 * HD], (0, 2 * HD * (chip ^ d)))
        grad_key = lax.dynamic_update_slice(grad_key, part[:, 2 * HD : 3 * HD], (0, HD * (chip ^ d)))
        grad_value = lax.dynamic_update_slice(grad_value, part[:, 3 * HD :], (0, HD * (chip ^ d)))

    gains = jnp.stack([attn_gain_term, mlp_gain_term]).reshape(2, ctx_count, planes, own_share)

    def gain_block(d):
        return lax.dynamic_index_in_dim(gains, plane ^ d, 2, keepdims=False)

    gain_sum = gain_block(0)
    for d in z_steps:
        gain_sum = gain_sum + over_z(gain_block(d), d)
    gain_sum = gain_sum.reshape(2, chips, 2, own_share)
    gain_sum = lax.dynamic_index_in_dim(gain_sum, core, 2, keepdims=False) + sibling(
        lax.dynamic_index_in_dim(gain_sum, 1 - core, 2, keepdims=False)
    )
    gain_mine = lax.dynamic_index_in_dim(gain_sum, chip, 1, keepdims=False)
    for d in chip_steps:
        gain_mine = gain_mine + over_chips(
            lax.dynamic_index_in_dim(gain_sum, chip ^ d, 1, keepdims=False), d
        )
    return (
        output,
        grad_input,
        grad_query,
        grad_key,
        grad_value,
        grad_out,
        grad_gate,
        grad_up,
        grad_down,
        gain_mine[0],
        gain_mine[1],
    )


def plan_of(mesh):
    chips, planes = mesh.shape["ctx"] // 2, mesh.shape["shard"]
    if mesh.shape["ctx"] == HQ and HQ == 2 * HK and chips == planes == HK:
        return on_device_by_head
    return on_device


def solution(mesh):
    placed = (
        P("shard", "ctx", None),
        P(None, "shard"),
        P(None, "shard"),
        P(None, "shard"),
        P(None, "shard"),
        P(None, "shard"),
        P(None, "shard"),
        P(None, "shard"),
        P(),
        P(),
        P("shard", None),
        P("shard", None),
        P("shard", "ctx", None),
    )
    return jax.shard_map(
        plan_of(mesh),
        mesh=mesh,
        in_specs=placed,
        out_specs=(
            P("shard", "ctx", None),
            P("shard", "ctx", None),
            P(("ctx", "shard"), None),
            P(("ctx", "shard"), None),
            P(("ctx", "shard"), None),
            P(("ctx", "shard"), None),
            P(("ctx", "shard"), None),
            P(("ctx", "shard"), None),
            P(("ctx", "shard"), None),
            P(("ctx", "shard")),
            P(("ctx", "shard")),
        ),
        check_vma=False,
    )
```

```python
import functools
import math

import jax
import jax.numpy as jnp
from jax import lax
from jax.experimental import pallas as pl
from jax.experimental.pallas import tpu as pltpu
from jax.sharding import PartitionSpec as P

HQ = 8
HK = 4
HD = 256
WINDOW = 1024


EPSILON = 1e-06
SCORE_SCALE = 0.0625
MASKED = -1e30
ROPE_BASE = 1000042.0


def position_of(rows, pairs, per_device, blocks_total):
    device = rows // per_device
    within = rows % per_device
    half = per_device // 2
    chosen = jnp.take(pairs, device)
    first = chosen * half + within
    second = (blocks_total - 1 - chosen) * half + within - half
    return jnp.where(within < half, first, second)


def rope_tables(positions, head):
    half = head // 2
    freq = ROPE_BASE ** (-(jnp.arange(half, dtype=jnp.float32) * 2.0) / head)
    angle = positions.astype(jnp.float32)[:, None] * freq[None, :]
    return (jnp.cos(angle), jnp.sin(angle))


def rotate(values, cosine, sine):
    half = values.shape[-1] // 2
    first = values[..., :half]
    second = values[..., half:]
    cosine = cosine[:, None, :]
    sine = sine[:, None, :]
    return jnp.concatenate(
        [first * cosine - second * sine, second * cosine + first * sine], axis=-1
    )


def rotate_back(grads, cosine, sine):
    half = grads.shape[-1] // 2
    first = grads[..., :half]
    second = grads[..., half:]
    cosine = cosine[:, None, :]
    sine = sine[:, None, :]
    return jnp.concatenate(
        [first * cosine + second * sine, second * cosine - first * sine], axis=-1
    )


def visible(query_pos, query_doc, key_pos, key_doc):
    distance = query_pos[:, None] - key_pos[None, :]
    return (query_doc[:, None] == key_doc[None, :]) & (distance >= 0) & (distance < WINDOW)


def write_columns(left, piece):
    made = jnp.dot(left, piece, preferred_element_type=jnp.float32)
    return made


def contract_full(grads, weight):
    return lax.dot_general(
        grads, weight, (((1,), (1,)), ((), ())), preferred_element_type=jnp.float32
    )


def alternate(parts, shard_count, rows):
    return jnp.concatenate([part.reshape(rows, shard_count, -1) for part in parts], axis=2).reshape(
        rows, -1
    )


def outer_sum(left, right):
    return lax.dot_general(
        left, right, (((0,), (0,)), ((), ())), preferred_element_type=jnp.float32
    )


def term_rows(lefts, rights, gain_block, count):
    normed_all, attended_all, second_all, act_all = lefts
    query_g, key_g, value_g, branch_g, gate_g, up_g, upstream_g = rights
    down_part = outer_sum(act_all, upstream_g).reshape(count, -1)
    return jnp.concatenate(
        [
            outer_sum(normed_all, query_g),
            outer_sum(normed_all, key_g),
            outer_sum(normed_all, value_g),
            outer_sum(attended_all, branch_g),
            outer_sum(second_all, gate_g),
            outer_sum(second_all, up_g),
            down_part,
            gain_block,
        ],
        axis=1,
    )


def deal_columns(values, ctx_count, shard_count):
    rows = values.shape[0]
    return (
        values.reshape(rows, ctx_count, shard_count, -1)
        .transpose(0, 2, 1, 3)
        .reshape(rows, shard_count, -1)
    )


def on_device(
    layer_input,
    w_query,
    w_key,
    w_value,
    w_out,
    w_gate,
    w_up,
    w_down,
    attn_gain,
    mlp_gain,
    block_pairs,
    doc_ids,
    cotangent,
):
    tok_rows = layer_input.shape[1]
    model_width = layer_input.shape[2]
    shard_count = lax.axis_size("shard")
    ctx_count = lax.axis_size("ctx")
    device_count = lax.axis_size(("ctx", "shard"))
    group_size = HQ // HK
    blocks_total = 2 * ctx_count
    pairs = block_pairs[0]
    documents = doc_ids[0]
    own_rows = lax.axis_index("ctx") * tok_rows + jnp.arange(tok_rows, dtype=jnp.int32)
    own_pos = position_of(own_rows, pairs, tok_rows, blocks_total)
    own_doc = jnp.take(documents, own_pos)
    cosine, sine = rope_tables(own_pos, HD)
    stack_qkv = jnp.concatenate([w_query, w_key, w_value], axis=1)
    stack_mlp = jnp.concatenate([w_gate, w_up], axis=1)
    per_query = w_query.shape[1]
    per_key = w_key.shape[1]
    per_hidden = w_gate.shape[1]
    hidden_width = w_down.shape[0]
    inputs = layer_input.reshape(tok_rows, model_width).astype(jnp.float32)
    factor_one = lax.rsqrt(jnp.mean(inputs * inputs, axis=-1, keepdims=True) + EPSILON)
    normed = (inputs * factor_one * attn_gain).astype(jnp.bfloat16)
    projected = write_columns(normed, lax.all_gather(stack_qkv, "shard", axis=1, tiled=True))
    projected = projected.reshape(tok_rows, shard_count, -1)
    query_lin = projected[:, :, :per_query].reshape(tok_rows, HQ, HD)
    key_lin = projected[:, :, per_query : per_query + per_key].reshape(tok_rows, HK, HD)
    value_lin = projected[:, :, per_query + per_key :].reshape(tok_rows, HK * HD)
    query_rot = (
        rotate(query_lin, cosine, sine).astype(jnp.bfloat16).reshape(tok_rows, HK, group_size, HD)
    )
    key_rot = rotate(key_lin, cosine, sine).astype(jnp.bfloat16).reshape(tok_rows, HK * HD)
    value_low = value_lin.astype(jnp.bfloat16)

    def key_mask(first_row, count):
        key_pos = position_of(
            first_row + jnp.arange(count, dtype=jnp.int32), pairs, tok_rows, blocks_total
        )
        return visible(own_pos, own_doc, key_pos, jnp.take(documents, key_pos))[:, None, None, :]

    start_state = (
        jnp.full((tok_rows, HK, group_size), MASKED, jnp.float32),
        jnp.zeros((tok_rows, HK, group_size), jnp.float32),
        jnp.zeros((tok_rows, HK, group_size, HD), jnp.float32),
    )
    keys = lax.all_gather(key_rot, "ctx", axis=0, tiled=True)
    values = lax.all_gather(value_low, "ctx", axis=0, tiled=True)
    count = keys.shape[0]
    step = math.gcd(count, 4 * tok_rows)
    keys = keys.reshape(count // step, step, HK, HD)
    values = values.reshape(count // step, step, HK, HD)

    def attend_step(i, running):
        top, total, accum = running
        mask = key_mask(i * step, step)
        scores = (
            jnp.einsum("tkgd,skd->tkgs", query_rot, keys[i], preferred_element_type=jnp.float32)
            * SCORE_SCALE
        )
        scores = jnp.where(mask, scores, MASKED)
        new_top = jnp.maximum(top, jnp.max(scores, axis=-1))
        weights = jnp.where(mask, jnp.exp(scores - new_top[..., None]), 0.0)
        shrink = jnp.exp(top - new_top)
        total = total * shrink + jnp.sum(weights, axis=-1)
        accum = accum * shrink[..., None] + jnp.einsum(
            "tkgs,skd->tkgd",
            weights.astype(jnp.bfloat16),
            values[i],
            preferred_element_type=jnp.float32,
        )
        return (new_top, total, accum)

    top, total, accum = lax.fori_loop(0, count // step, attend_step, start_state)
    log_total = top + jnp.log(total)
    attended_full = accum / total[..., None]
    attended = attended_full.astype(jnp.bfloat16).reshape(tok_rows, HQ * HD)
    branch_one = write_columns(attended, lax.all_gather(w_out, "shard", axis=1, tiled=True))
    mid = inputs + branch_one
    factor_two = lax.rsqrt(jnp.mean(mid * mid, axis=-1, keepdims=True) + EPSILON)
    normed_two = (mid * factor_two * mlp_gain).astype(jnp.bfloat16)
    gate_up = write_columns(normed_two, lax.all_gather(stack_mlp, "shard", axis=1, tiled=True))
    gate_up = gate_up.reshape(tok_rows, shard_count, -1)
    gate = gate_up[:, :, :per_hidden].reshape(tok_rows, hidden_width)
    up_lin = gate_up[:, :, per_hidden:].reshape(tok_rows, hidden_width)
    sigma = jax.nn.sigmoid(gate)
    swish = gate * sigma
    act = (swish * up_lin).astype(jnp.bfloat16)
    branch_two = write_columns(act, lax.all_gather(w_down, "shard", axis=1, tiled=True))
    output = (mid + branch_two).astype(jnp.bfloat16).reshape(1, tok_rows, model_width)
    full_qkv, full_out, full_mlp, full_down = (
        lax.all_gather(stack_qkv, "shard", axis=1, tiled=True),
        lax.all_gather(w_out, "shard", axis=1, tiled=True),
        lax.all_gather(stack_mlp, "shard", axis=1, tiled=True),
        lax.all_gather(w_down, "shard", axis=1, tiled=True),
    )
    upstream_low = cotangent.reshape(tok_rows, model_width)
    upstream = upstream_low.astype(jnp.float32)
    act_grad = contract_full(upstream_low, full_down)
    gate_grad = (act_grad * up_lin * (sigma * (1.0 + gate * (1.0 - sigma)))).astype(jnp.bfloat16)
    up_grad = (act_grad * swish).astype(jnp.bfloat16)
    stacked_mlp_grad = alternate((gate_grad, up_grad), shard_count, tok_rows)
    norm_two_grad = contract_full(stacked_mlp_grad, full_mlp)
    mlp_gain_term = jnp.sum(norm_two_grad * mid * factor_two, axis=0)
    scaled_two = norm_two_grad * mlp_gain
    mid_grad = (
        upstream
        + factor_two * scaled_two
        - mid * factor_two**3 * jnp.mean(scaled_two * mid, axis=-1, keepdims=True)
    )
    branch_grad = mid_grad.astype(jnp.bfloat16)
    attended_grad = contract_full(branch_grad, full_out)
    attended_low = attended_grad.astype(jnp.bfloat16).reshape(tok_rows, HK, group_size, HD)
    delta = jnp.sum(attended_low.astype(jnp.float32) * attended_full, axis=-1)

    def query_grads(carry, piece):
        keys, values = piece
        count = keys.shape[0]
        step = math.gcd(count, 4 * tok_rows)
        keys = keys.reshape(count // step, step, HK, HD)
        values = values.reshape(count // step, step, HK, HD)

        def query_step(i, query_sum):
            mask = key_mask(i * step, step)
            scores = (
                jnp.einsum("tkgd,skd->tkgs", query_rot, keys[i], preferred_element_type=jnp.float32)
                * SCORE_SCALE
            )
            probs = jnp.where(mask, jnp.exp(scores - log_total[..., None]), 0.0)
            prob_grad = jnp.einsum(
                "tkgd,skd->tkgs", attended_low, values[i], preferred_element_type=jnp.float32
            )
            score_grad = (probs * (prob_grad - delta[..., None])).astype(jnp.bfloat16)
            return query_sum + jnp.einsum(
                "tkgs,skd->tkgd", score_grad, keys[i], preferred_element_type=jnp.float32
            )

        return lax.fori_loop(0, count // step, query_step, carry)

    query_sum = query_grads(
        jnp.zeros((tok_rows, HK, group_size, HD), jnp.float32),
        (
            lax.all_gather(key_rot, "ctx", axis=0, tiled=True),
            lax.all_gather(value_low, "ctx", axis=0, tiled=True),
        ),
    )
    all_log_total, all_delta = (
        lax.all_gather(log_total, "ctx", axis=0, tiled=True),
        lax.all_gather(delta, "ctx", axis=0, tiled=True),
    )
    key_three = key_rot.reshape(tok_rows, HK, HD)
    value_three = value_low.reshape(tok_rows, HK, HD)

    def key_grads(carry, piece):
        queries, outgrads = piece
        count = queries.shape[0]
        step = math.gcd(count, 4 * tok_rows)
        queries = queries.reshape(count // step, step, HK, group_size, HD)
        outgrads = outgrads.reshape(count // step, step, HK, group_size, HD)

        def key_step(i, running):
            key_sum, value_sum = running
            first_row = i * step
            query_pos = position_of(
                first_row + jnp.arange(step, dtype=jnp.int32), pairs, tok_rows, blocks_total
            )
            mask = visible(query_pos, jnp.take(documents, query_pos), own_pos, own_doc)[
                :, None, None, :
            ]
            lse_part = lax.dynamic_slice_in_dim(all_log_total, first_row, step, 0)
            delta_part = lax.dynamic_slice_in_dim(all_delta, first_row, step, 0)
            scores = (
                jnp.einsum(
                    "skgd,tkd->skgt", queries[i], key_three, preferred_element_type=jnp.float32
                )
                * SCORE_SCALE
            )
            probs = jnp.where(mask, jnp.exp(scores - lse_part[..., None]), 0.0)
            prob_grad = jnp.einsum(
                "skgd,tkd->skgt", outgrads[i], value_three, preferred_element_type=jnp.float32
            )
            score_grad = (probs * (prob_grad - delta_part[..., None])).astype(jnp.bfloat16)
            value_sum = value_sum + jnp.einsum(
                "skgt,skgd->tkd",
                probs.astype(jnp.bfloat16),
                outgrads[i],
                preferred_element_type=jnp.float32,
            )
            key_sum = key_sum + jnp.einsum(
                "skgt,skgd->tkd", score_grad, queries[i], preferred_element_type=jnp.float32
            )
            return (key_sum, value_sum)

        return lax.fori_loop(0, count // step, key_step, carry)

    key_sum, value_sum = key_grads(
        (jnp.zeros((tok_rows, HK, HD), jnp.float32), jnp.zeros((tok_rows, HK, HD), jnp.float32)),
        (
            lax.all_gather(query_rot.reshape(tok_rows, HQ * HD), "ctx", axis=0, tiled=True),
            lax.all_gather(attended_low.reshape(tok_rows, HQ * HD), "ctx", axis=0, tiled=True),
        ),
    )
    query_grad = (
        rotate_back(query_sum.reshape(tok_rows, HQ, HD) * SCORE_SCALE, cosine, sine)
        .astype(jnp.bfloat16)
        .reshape(tok_rows, HQ * HD)
    )
    key_grad = (
        rotate_back(key_sum * SCORE_SCALE, cosine, sine)
        .astype(jnp.bfloat16)
        .reshape(tok_rows, HK * HD)
    )
    value_grad = value_sum.astype(jnp.bfloat16).reshape(tok_rows, HK * HD)
    stacked_qkv_grad = alternate((query_grad, key_grad, value_grad), shard_count, tok_rows)
    normed_grad = contract_full(stacked_qkv_grad, full_qkv)
    attn_gain_term = jnp.sum(normed_grad * inputs * factor_one, axis=0)
    scaled_one = normed_grad * attn_gain
    input_grad = (
        mid_grad
        + factor_one * scaled_one
        - inputs * factor_one**3 * jnp.mean(scaled_one * inputs, axis=-1, keepdims=True)
    )
    grad_input = input_grad.astype(jnp.bfloat16).reshape(1, tok_rows, model_width)
    ratio = hidden_width // model_width
    own_share = model_width // device_count
    rights = (query_grad, key_grad, value_grad, branch_grad, gate_grad, up_grad, upstream_low)
    group_rights = (
        lax.all_gather(rights[0], "shard", axis=0, tiled=True),
        lax.all_gather(rights[1], "shard", axis=0, tiled=True),
        lax.all_gather(rights[2], "shard", axis=0, tiled=True),
        lax.all_gather(rights[3], "shard", axis=0, tiled=True),
        lax.all_gather(rights[4], "shard", axis=0, tiled=True),
        lax.all_gather(rights[5], "shard", axis=0, tiled=True),
        lax.all_gather(rights[6], "shard", axis=0, tiled=True),
    )
    dealt = (
        lax.all_to_all(
            deal_columns(normed, ctx_count, shard_count),
            "shard",
            split_axis=1,
            concat_axis=0,
            tiled=True,
        ),
        lax.all_to_all(
            deal_columns(attended, ctx_count, shard_count),
            "shard",
            split_axis=1,
            concat_axis=0,
            tiled=True,
        ),
        lax.all_to_all(
            deal_columns(normed_two, ctx_count, shard_count),
            "shard",
            split_axis=1,
            concat_axis=0,
            tiled=True,
        ),
        lax.all_to_all(
            deal_columns(act, ctx_count, shard_count),
            "shard",
            split_axis=1,
            concat_axis=0,
            tiled=True,
        ),
    )
    group_lefts = tuple((part.reshape(part.shape[0], -1) for part in dealt))
    gain_pair = lax.psum(jnp.stack([attn_gain_term, mlp_gain_term]), "shard")
    gain_mine = lax.dynamic_index_in_dim(
        gain_pair.reshape(2, ctx_count, shard_count, own_share),
        lax.axis_index("shard"),
        2,
        keepdims=False,
    ).reshape(2, ctx_count * own_share)
    gain_block = jnp.concatenate(
        [gain_mine.T, jnp.zeros((ctx_count * own_share, 126), jnp.float32)], axis=1
    )
    summed = lax.psum_scatter(
        term_rows(group_lefts, group_rights, gain_block, own_share * lax.axis_size("ctx")).astype(
            jnp.bfloat16
        ),
        "ctx",
        scatter_dimension=0,
        tiled=True,
    ).astype(jnp.float32)
    edge_one = HQ * HD
    edge_two = edge_one + HK * HD
    edge_three = edge_two + HK * HD
    edge_four = edge_three + model_width
    edge_five = edge_four + hidden_width
    edge_six = edge_five + hidden_width
    edge_seven = edge_six + ratio * model_width
    grad_query = summed[:, :edge_one]
    grad_key = summed[:, edge_one:edge_two]
    grad_value = summed[:, edge_two:edge_three]
    grad_out = summed[:, edge_three:edge_four]
    grad_gate = summed[:, edge_four:edge_five]
    grad_up = summed[:, edge_five:edge_six]
    grad_down = summed[:, edge_six:edge_seven].reshape(own_share * ratio, model_width)
    grad_attn_gain = summed[:, edge_seven]
    grad_mlp_gain = summed[:, edge_seven + 1]
    return (
        output,
        grad_input,
        grad_query,
        grad_key,
        grad_value,
        grad_out,
        grad_gate,
        grad_up,
        grad_down,
        grad_attn_gain,
        grad_mlp_gain,
    )


BF16 = jnp.bfloat16
F32 = jnp.float32
VISIBLE_ROWS = 256


def dot_nn(a, b):
    return jnp.dot(a, b, preferred_element_type=F32)


def dot_nt(a, b):
    return lax.dot_general(a, b, (((1,), (1,)), ((), ())), preferred_element_type=F32)


def dot_tn(a, b):
    return lax.dot_general(a, b, (((0,), (0,)), ((), ())), preferred_element_type=F32)


def scores_of(query, key, code, low_code, key_code):
    scores = dot_nt(query, key) * SCORE_SCALE
    mask = (key_code <= code) & (key_code >= low_code)
    return jnp.where(mask, scores, MASKED)


def attend_kernel(query, key, value, code, low_code, key_code, attended, log_total):
    scores = scores_of(query[...], key[...], code[...], low_code[...], key_code[...])
    top = jnp.max(scores, axis=-1, keepdims=True)
    weights = jnp.exp(scores - top)
    total = jnp.sum(weights, axis=-1, keepdims=True)
    mixed = dot_nn(weights.astype(BF16), value[...])
    attended[...] = (mixed / total).astype(BF16)
    log_total[...] = top + jnp.log(total)


def attend(query, key, value, code, low_code, key_code):
    rows, head = query.shape
    step = math.gcd(rows, VISIBLE_ROWS)
    by_row = lambda width: pl.BlockSpec((step, width), lambda i: (i, 0))
    whole = lambda shape: pl.BlockSpec(shape, lambda i: (0, 0))
    return pl.pallas_call(
        attend_kernel,
        grid=(rows // step,),
        in_specs=[
            by_row(head),
            whole(key.shape),
            whole(value.shape),
            by_row(1),
            by_row(1),
            whole(key_code.shape),
        ],
        out_specs=[by_row(head), by_row(1)],
        out_shape=[
            jax.ShapeDtypeStruct((rows, head), BF16),
            jax.ShapeDtypeStruct((rows, 1), F32),
        ],
        compiler_params=pltpu.CompilerParams(vmem_limit_bytes=32 << 20),
        cost_estimate=pl.CostEstimate(
            flops=4 * rows * key.shape[0] * head,
            bytes_accessed=8 * rows * head,
            transcendentals=rows * key.shape[0],
        ),
    )(query, key, value, code, low_code, key_code)


def attend_back_kernel(
    query, outgrad, key, value, log_total, code, low_code, key_code, d_query, d_key, d_value
):
    @pl.when(pl.program_id(0) == 0)
    def _():
        d_key[...] = jnp.zeros_like(d_key)
        d_value[...] = jnp.zeros_like(d_value)

    scores = scores_of(query[...], key[...], code[...], low_code[...], key_code[...])
    probs = jnp.exp(scores - log_total[...])
    prob_grad = dot_nt(outgrad[...], value[...])
    delta = jnp.sum(probs * prob_grad, axis=-1, keepdims=True)
    score_grad = (probs * (prob_grad - delta)).astype(BF16)
    d_query[...] = dot_nn(score_grad, key[...]) * SCORE_SCALE
    d_key[...] += dot_tn(score_grad, query[...]) * SCORE_SCALE
    d_value[...] += dot_tn(probs.astype(BF16), outgrad[...])


def attend_back(query, outgrad, key, value, log_total, code, low_code, key_code):
    rows, head = query.shape
    step = math.gcd(rows, VISIBLE_ROWS)
    by_row = lambda width: pl.BlockSpec((step, width), lambda i: (i, 0))
    whole = lambda shape: pl.BlockSpec(shape, lambda i: (0, 0))
    return pl.pallas_call(
        attend_back_kernel,
        grid=(rows // step,),
        in_specs=[
            by_row(head),
            by_row(head),
            whole(key.shape),
            whole(value.shape),
            by_row(1),
            by_row(1),
            by_row(1),
            whole(key_code.shape),
        ],
        out_specs=[by_row(head), whole(key.shape), whole(value.shape)],
        out_shape=[
            jax.ShapeDtypeStruct((rows, head), F32),
            jax.ShapeDtypeStruct(key.shape, F32),
            jax.ShapeDtypeStruct(value.shape, F32),
        ],
        compiler_params=pltpu.CompilerParams(vmem_limit_bytes=40 << 20),
        cost_estimate=pl.CostEstimate(
            flops=10 * rows * key.shape[0] * head,
            bytes_accessed=20 * rows * head,
            transcendentals=rows * key.shape[0],
        ),
    )(query, outgrad, key, value, log_total, code, low_code, key_code)


MESH = pl.DeviceIdType.MESH
TILE = 256


def flip(i, d):
    return (i, i + 1 - 2 * (i % 2), (i + 2) % 4, 3 - i)[d]


def mlp_kernel(
    second_ref,
    mid_ref,
    upstream_ref,
    gain_ref,
    upstream_hbm,
    gate_hbm,
    up_hbm,
    down_hbm,
    output_ref,
    mid_grad_ref,
    gain_grad_ref,
    branch_all,
    gate_up_terms,
    down_terms,
    gate_w,
    up_w,
    down_w,
    upstream_all,
    second_all,
    act,
    gate_grad,
    up_grad,
    held,
    own_sum,
    pair_send,
    pair_recv,
    z_send,
    z_recv,
    branch_low,
    staged,
    local_sem,
    staged_sem,
    send_sem,
    recv_sem,
):
    tok = second_ref.shape[0]
    pair = 2 * tok
    hidden = gate_w.shape[1]
    width = second_ref.shape[1]
    ctx, plane = lax.axis_index("ctx"), lax.axis_index("shard")
    chip, core = ctx // 2, ctx % 2
    sibling = (ctx + 1 - 2 * core, plane)
    over_z = [(ctx, flip(plane, d)) for d in range(4)]
    over_chips = [(2 * flip(chip, d) + core, plane) for d in range(4)]

    half = pl.ds(pl.multiple_of(core * hidden, hidden), hidden)
    loads = [
        pltpu.make_async_copy(upstream_hbm, upstream_all, local_sem.at[0]),
        pltpu.make_async_copy(down_hbm, down_w, local_sem.at[1]),
        pltpu.make_async_copy(gate_hbm.at[:, half], gate_w, local_sem.at[2]),
        pltpu.make_async_copy(up_hbm.at[:, half], up_w, local_sem.at[3]),
        pltpu.make_async_copy(second_ref, second_all.at[0, 0], local_sem.at[4]),
    ]
    for load in loads:
        load.start()

    barrier = pltpu.get_barrier_semaphore()
    partners = [sibling] + over_z[1:] + over_chips[1:]
    for partner in partners:
        pl.semaphore_signal(barrier, inc=1, device_id=partner, device_id_type=MESH)
    pl.semaphore_wait(barrier, len(partners))

    def send(slot, source, target, device):
        copy = pltpu.make_async_remote_copy(
            src_ref=source,
            dst_ref=target,
            send_sem=send_sem.at[slot],
            recv_sem=recv_sem.at[slot],
            device_id=device,
            device_id_type=MESH,
        )
        copy.start()
        return copy

    gather_z = {d: send(d, second_ref, second_all.at[d, 0], over_z[d]) for d in (1, 2, 3)}
    gather_pair = {0: send(0, second_ref, second_all.at[0, 1], sibling)}
    for load in loads:
        load.wait()

    def rows_of(d):
        return pl.ds(d * pair, pair)

    def forward(d):
        rows = rows_of(d)
        second = lambda: second_all[d].reshape(pair, width)

        def step(t, carry):
            at = pl.ds(pl.multiple_of(t * TILE, TILE), TILE)
            act_grad = dot_nt(upstream_all[rows, :], down_w[at, :])
            gate = dot_nn(second(), gate_w[:, at])
            up_lin = dot_nn(second(), up_w[:, at])
            sigma = 1.0 / (1.0 + jnp.exp(-gate))
            swish = gate * sigma
            act[rows, at] = (swish * up_lin).astype(BF16)
            gate_grad[rows, at] = (
                act_grad * up_lin * (sigma * (1.0 + gate * (1.0 - sigma)))
            ).astype(BF16)
            up_grad[rows, at] = (act_grad * swish).astype(BF16)
            return carry

        lax.fori_loop(0, hidden // TILE, step, 0)

    def give_pair(d, base, product):
        which = 0 if base == 7 else 1

        def step(t, carry):
            at = pl.ds(pl.multiple_of(t * TILE, TILE), TILE)
            terms = product(at)
            held[d % 2, :, at] = terms[:tok]
            pair_send[which, d, :, at] = terms[tok:].astype(BF16)
            return carry

        lax.fori_loop(0, width // TILE, step, 0)
        return send(base + d, pair_send.at[which, d], pair_recv.at[which, d], sibling)

    def give_plane(d, base, copy):
        which = 0 if base == 7 else 1
        copy.wait_recv()
        total = held[d % 2] + pair_recv[which, d].astype(F32)
        if d == 0:
            own_sum[which] = total
            return None
        z_send[which, d - 1] = total.astype(BF16)
        return send(base + 3 + d, z_send.at[which, d - 1], z_recv.at[which, d - 1], over_z[d])

    def back(d):
        rows = rows_of(d)
        return lambda at: dot_nt(gate_grad[rows, :], gate_w[at, :]) + dot_nt(
            up_grad[rows, :], up_w[at, :]
        )

    def onward(d):
        rows = rows_of(d)
        return lambda at: dot_nn(act[rows, :], down_w[:, at])

    pairs, planes = {}, {}
    for d in range(4):
        if d:
            gather_z[d].wait_recv()
            gather_pair[d] = send(
                3 + d, second_all.at[d, 0], second_all.at[d, 1], sibling
            )
        gather_pair[d].wait_recv()
        forward(d)
        pairs[d] = give_pair(d, 7, back(d))
        if d:
            planes[d - 1] = give_plane(d - 1, 7, pairs[d - 1])
    planes[3] = give_plane(3, 7, pairs[3])

    out_pairs, out_planes = {}, {}
    for d in range(4):
        out_pairs[d] = give_pair(d, 14, onward(d))
        if d:
            out_planes[d - 1] = give_plane(d - 1, 14, out_pairs[d - 1])
    out_planes[3] = give_plane(3, 14, out_pairs[3])

    second_rows = second_all.reshape(8 * tok, width)

    def to_hbm(slot, target):
        return pltpu.make_async_copy(staged.at[slot], target, staged_sem.at[slot])

    def gate_up_step(d):
        for h in range(2):
            first = flip(chip, d) * (2 * TILE) + h * TILE
            left = second_rows[:, pl.ds(pl.multiple_of(first, TILE), TILE)]
            target = gate_up_terms.at[d, pl.ds(h * TILE, TILE)]
            if d:
                to_hbm(h, target).wait()
            staged[h, :, :hidden] = dot_tn(left, gate_grad[...]).astype(BF16)
            staged[h, :, hidden:] = dot_tn(left, up_grad[...]).astype(BF16)
            to_hbm(h, target).start()

    for d in range(4):
        gate_up_step(d)

    for d in (1, 2, 3):
        planes[d].wait_recv()
    chunk = 32
    gain = gain_ref[...]

    def mid_step(i, carry):
        at = pl.ds(pl.multiple_of(i * chunk, chunk), chunk)
        grad = own_sum[0, at, :]
        for d in range(3):
            grad = grad + z_recv[0, d, at, :].astype(F32)
        mid = mid_ref[at, :]
        factor = lax.rsqrt(jnp.mean(mid * mid, axis=-1, keepdims=True) + EPSILON)
        scaled = grad * gain
        mid_grad = (
            upstream_ref[at, :].astype(F32)
            + factor * scaled
            - mid * (factor * factor * factor * jnp.mean(scaled * mid, axis=-1, keepdims=True))
        )
        mid_grad_ref[at, :] = mid_grad
        branch_low[at, :] = mid_grad.astype(BF16)
        return carry + jnp.sum(grad * mid * factor, axis=0, keepdims=True)

    gain_grad_ref[...] = lax.fori_loop(0, tok // chunk, mid_step, jnp.zeros((1, width), F32))
    branch_chips = {
        d: send(20 + d, branch_low, branch_all.at[0, d], over_chips[d]) for d in (1, 2, 3)
    }
    branch_pairs = {0: send(24, branch_low, branch_all.at[1, 0], sibling)}
    keep = pltpu.make_async_copy(branch_low, branch_all.at[0, 0], local_sem.at[0])
    keep.start()

    def down_step(t):
        slot = t % 2
        target = down_terms.at[pl.ds(t * TILE, TILE)]
        to_hbm(slot, target).wait()
        left = act[:, pl.ds(t * TILE, TILE)]
        staged[slot] = dot_tn(left, upstream_all[...]).astype(BF16)
        to_hbm(slot, target).start()

    for t in range(hidden // TILE):
        down_step(t)
    for d in (1, 2, 3):
        branch_chips[d].wait_recv()
        branch_pairs[d] = send(24 + d, branch_all.at[0, d], branch_all.at[1, d], sibling)

    for d in (1, 2, 3):
        out_planes[d].wait_recv()

    def out_step(i, carry):
        at = pl.ds(pl.multiple_of(i * chunk, chunk), chunk)
        total = mid_ref[at, :] + own_sum[1, at, :]
        for d in range(3):
            total = total + z_recv[1, d, at, :].astype(F32)
        output_ref[at, :] = total.astype(BF16)
        return carry

    lax.fori_loop(0, tok // chunk, out_step, 0)

    for d in range(4):
        branch_pairs[d].wait_recv()
        for copy in (gather_pair[d], pairs[d], out_pairs[d], branch_pairs[d]):
            copy.wait_send()
    for d in (1, 2, 3):
        for copy in (gather_z[d], planes[d], out_planes[d], branch_chips[d]):
            copy.wait_send()
    keep.wait()
    for slot in range(2):
        to_hbm(slot, down_terms.at[pl.ds(0, TILE)]).wait()


def mlp_of(normed_two, mid, upstream, gain, upstream_group, w_gate, w_up, down_rows):
    tok, width = mid.shape
    hidden = down_rows.shape[0]
    rows = upstream_group.shape[0]
    vmem = pl.BlockSpec(memory_space=pltpu.VMEM)
    hbm = pl.BlockSpec(memory_space=pl.ANY)
    return pl.pallas_call(
        mlp_kernel,
        in_specs=[vmem] * 4 + [hbm] * 4,
        out_specs=[vmem] * 3 + [hbm] * 3,
        out_shape=[
            jax.ShapeDtypeStruct((tok, width), BF16),
            jax.ShapeDtypeStruct((tok, width), F32),
            jax.ShapeDtypeStruct((1, width), F32),
            jax.ShapeDtypeStruct((2, 4, tok, width), BF16),
            jax.ShapeDtypeStruct((4, 2 * TILE, 2 * hidden), BF16),
            jax.ShapeDtypeStruct((hidden, width), BF16),
        ],
        scratch_shapes=[
            pltpu.VMEM((width, hidden), BF16),
            pltpu.VMEM((width, hidden), BF16),
            pltpu.VMEM((hidden, width), BF16),
            pltpu.VMEM((rows, width), BF16),
            pltpu.VMEM((4, 2, tok, width), BF16),
            pltpu.VMEM((rows, hidden), BF16),
            pltpu.VMEM((rows, hidden), BF16),
            pltpu.VMEM((rows, hidden), BF16),
            pltpu.VMEM((2, tok, width), F32),
            pltpu.VMEM((2, tok, width), F32),
            pltpu.VMEM((2, 4, tok, width), BF16),
            pltpu.VMEM((2, 4, tok, width), BF16),
            pltpu.VMEM((2, 3, tok, width), BF16),
            pltpu.VMEM((2, 3, tok, width), BF16),
            pltpu.VMEM((tok, width), BF16),
            pltpu.VMEM((2, TILE, width), BF16),
            pltpu.SemaphoreType.DMA((5,)),
            pltpu.SemaphoreType.DMA((2,)),
            pltpu.SemaphoreType.DMA((28,)),
            pltpu.SemaphoreType.DMA((28,)),
        ],
        compiler_params=pltpu.CompilerParams(
            collective_id=1, has_side_effects=True, vmem_limit_bytes=60 << 20
        ),
        cost_estimate=pl.CostEstimate(
            flops=18 * rows * width * hidden,
            bytes_accessed=2 * (5 * width * hidden + 4 * rows * width),
            transcendentals=rows * hidden,
        ),
    )(normed_two, mid, upstream, gain, upstream_group, w_gate, w_up, down_rows)


def xor4(a, b):
    return 2 * ((a // 2 + b // 2) % 2) + (a % 2 + b % 2) % 2


def rotated(values, cosine, sine):
    half = values.shape[1] // 2
    first, second = values[:, :half], values[:, half:]
    return jnp.concatenate([first * cosine - second * sine, second * cosine + first * sine], axis=1)


def front_kernel(
    input_ref,
    attn_gain_ref,
    mlp_gain_ref,
    cosine_ref,
    sine_ref,
    code_ref,
    low_code_ref,
    key_code_ref,
    query_hbm,
    key_hbm,
    value_hbm,
    out_hbm,
    down_hbm,
    upstream_hbm,
    second_ref,
    mid_ref,
    normed_ref,
    query_ref,
    kv_ref,
    attended_ref,
    log_total_ref,
    w_head,
    w_sibling,
    out_pair,
    down_rows,
    upstream_all,
    inputs_all,
    w_parts,
    attended_other,
    own_sum,
    chip_send,
    chip_recv,
    local_sem,
    send_sem,
    recv_sem,
):
    tok, width = input_ref.shape
    quarter = width // 4
    shard = out_hbm.shape[1]
    hidden = down_rows.shape[0]
    part = hidden // 4
    seq = 8 * tok
    half_seq = 4 * tok
    ctx, plane = lax.axis_index("ctx"), lax.axis_index("shard")
    chip, core = ctx // 2, ctx % 2
    sibling = (ctx + 1 - 2 * core, plane)
    over_z = [(ctx, flip(plane, d)) for d in range(4)]
    over_chips = [(2 * flip(chip, d) + core, plane) for d in range(4)]
    others = (1, 2, 3)

    def at(i, size):
        return pl.ds(pl.multiple_of(i * size, size), size)

    def remote(slot, source, target, device):
        return pltpu.make_async_remote_copy(
            src_ref=source,
            dst_ref=target,
            send_sem=send_sem.at[slot],
            recv_sem=recv_sem.at[slot],
            device_id=device,
            device_id_type=MESH,
        )

    def send(slot, source, target, device):
        copy = remote(slot, source, target, device)
        copy.start()
        return copy

    def local(slot, source, target):
        return pltpu.make_async_copy(source, target, local_sem.at[slot])

    rows = at(chip, quarter)
    mine = w_parts.at[plane]
    load_query = local(0, query_hbm.at[rows, at(core, HD)], mine.at[0])
    load_key = local(1, key_hbm.at[rows], mine.at[1])
    load_value = local(1, value_hbm.at[rows], mine.at[1])
    load_query.start()

    @pl.when(core == 0)
    def _():
        load_key.start()

    @pl.when(core == 1)
    def _():
        load_value.start()

    keep_input = local(2, input_ref, inputs_all.at[0, 0])
    keep_input.start()
    out_own = out_hbm.at[at(ctx, HD), :]
    keep_out = local(3, out_own, out_pair.at[0, :, at(plane, shard)])
    keep_out.start()

    def down_block(to_plane):
        first = to_plane * (2 * hidden) + core * hidden + chip * part
        return down_hbm.at[pl.ds(pl.multiple_of(first, part), part), :]

    down_place = down_rows.at[at(chip, part), at(plane, shard)]
    keep_down = local(4, down_block(plane), down_place)
    keep_down.start()
    keep_upstream = local(5, upstream_hbm, upstream_all.at[0, 0])
    keep_upstream.start()

    barrier = pltpu.get_barrier_semaphore()
    partners = [sibling] + over_z[1:] + over_chips[1:]
    for partner in partners:
        pl.semaphore_signal(barrier, inc=1, device_id=partner, device_id_type=MESH)
    pl.semaphore_wait(barrier, len(partners))

    input_chips = {
        d: send(d - 1, input_ref, inputs_all.at[0, d], over_chips[d]) for d in others
    }
    input_pairs = {0: send(3, input_ref, inputs_all.at[1, 0], sibling)}
    load_query.wait()
    load_key.wait()
    head_z = {d: send(6 + d, mine, w_parts.at[plane], over_z[d]) for d in others}

    chunk = 32
    attn_gain = attn_gain_ref[...]

    def norm(e, d):
        def step(i, carry):
            block = inputs_all[e, d, at(i, chunk), :].astype(F32)
            factor = lax.rsqrt(jnp.mean(block * block, axis=-1, keepdims=True) + EPSILON)
            first = (4 * e + d) * tok + i * chunk
            normed_ref[pl.ds(pl.multiple_of(first, chunk), chunk), :] = (
                block * factor * attn_gain
            ).astype(BF16)
            return carry

        lax.fori_loop(0, tok // chunk, step, 0)

    keep_input.wait()
    norm(0, 0)
    for d in others:
        input_chips[d].wait_recv()
        input_pairs[d] = send(3 + d, inputs_all.at[0, d], inputs_all.at[1, d], sibling)
        norm(0, d)
    for d in range(4):
        input_pairs[d].wait_recv()
        norm(1, d)

    head_rows = w_head.at[:, rows, :]
    for d in range(4):
        if d:
            head_z[d].wait_recv()
        source = flip(plane, d)
        apart = xor4(chip, source)
        block = w_parts.at[source]

        @pl.when(apart == 0)
        def _(block=block):
            local(6, block, head_rows).start()

        @pl.when(apart != 0)
        def _(block=block, source=source, apart=apart):
            remote(9 + apart, block, head_rows, (2 * source + core, plane)).start()

    out_z = {
        d: send(12 + d, out_own, out_pair.at[0, :, at(plane, shard)], over_z[d]) for d in others
    }
    local(6, mine, head_rows).wait()
    for d in others:
        remote(9 + d, mine, head_rows, over_chips[d]).wait_recv()
    head_pair = send(16, w_head, w_sibling, sibling)
    down_z = {d: send(16 + d, down_block(flip(plane, d)), down_place, over_z[d]) for d in others}

    def project(which, target, flat):
        def step(t, carry):
            here = at(t, TILE)
            made = dot_nn(normed_ref[here, :], w_head[which])
            cosine, sine = cosine_ref[here, :], sine_ref[here, :]
            if flat:
                cosine = jnp.where(core == 0, cosine, 1.0)
                sine = jnp.where(core == 0, sine, 0.0)
            target[here, :] = rotated(made, cosine, sine).astype(BF16)
            return carry

        lax.fori_loop(0, seq // TILE, step, 0)

    mine_kv = kv_ref.at[core]
    project(1, mine_kv, True)
    kv_pair = [
        send(20 + e, mine_kv.at[pl.ds(e * half_seq, half_seq)],
             mine_kv.at[pl.ds((1 - e) * half_seq, half_seq)], sibling)
        for e in range(2)
    ]
    project(0, query_ref, False)
    for copy in kv_pair:
        copy.wait_recv()

    def attend_step(t, carry):
        here = at(t, TILE)
        scores = scores_of(
            query_ref[here, :], kv_ref[0], code_ref[here, :], low_code_ref[here, :], key_code_ref[...]
        )
        top = jnp.max(scores, axis=-1, keepdims=True)
        weights = jnp.exp(scores - top)
        total = jnp.sum(weights, axis=-1, keepdims=True)
        mixed = dot_nn(weights.astype(BF16), kv_ref[1])
        attended_ref[here, :] = (mixed / total).astype(BF16)
        log_total_ref[here, :] = top + jnp.log(total)
        return carry

    lax.fori_loop(0, seq // TILE, attend_step, 0)
    attended_pair = send(22, attended_ref.at[pl.ds(half_seq, half_seq)], attended_other, sibling)
    keep_out.wait()
    for d in others:
        out_z[d].wait_recv()
    out_sibling = send(23, out_pair.at[0], out_pair.at[1], sibling)
    attended_pair.wait_recv()
    out_sibling.wait_recv()

    def out_step(t, carry):
        here = at(t, TILE)
        terms = dot_nn(attended_ref[:half_seq, :], out_pair[0, :, here]) + dot_nn(
            attended_other[...], out_pair[1, :, here]
        )
        own_sum[:, here] = terms[:tok]
        for d in others:
            chip_send[d - 1, :, here] = terms[d * tok : (d + 1) * tok].astype(BF16)
        return carry

    lax.fori_loop(0, width // TILE, out_step, 0)
    branch = {
        d: send(23 + d, chip_send.at[d - 1], chip_recv.at[d - 1], over_chips[d]) for d in others
    }

    keep_down.wait()
    for d in others:
        down_z[d].wait_recv()
    upstream_z = {
        d: send(29 + d, upstream_hbm, upstream_all.at[d, 0], over_z[d]) for d in others
    }
    upstream_pair = {0: send(33, upstream_hbm, upstream_all.at[0, 1], sibling)}

    for d in others:
        branch[d].wait_recv()
    down_mine = down_rows.at[at(chip, part), :]
    down_chips = {d: send(26 + d, down_mine, down_mine, over_chips[d]) for d in others}
    mlp_gain = mlp_gain_ref[...]

    def mid_step(i, carry):
        here = at(i, chunk)
        mid = input_ref[here, :].astype(F32) + own_sum[here, :]
        for d in range(3):
            mid = mid + chip_recv[d, here, :].astype(F32)
        factor = lax.rsqrt(jnp.mean(mid * mid, axis=-1, keepdims=True) + EPSILON)
        mid_ref[here, :] = mid
        second_ref[here, :] = (mid * factor * mlp_gain).astype(BF16)
        return carry

    lax.fori_loop(0, tok // chunk, mid_step, 0)

    for d in others:
        upstream_z[d].wait_recv()
        upstream_pair[d] = send(33 + d, upstream_all.at[d, 0], upstream_all.at[d, 1], sibling)
    keep_upstream.wait()
    for d in range(4):
        upstream_pair[d].wait_recv()
        upstream_pair[d].wait_send()
        input_pairs[d].wait_send()
    head_pair.wait_recv()
    for copy in (head_pair, attended_pair, out_sibling, *kv_pair):
        copy.wait_send()
    for d in others:
        down_chips[d].wait_recv()
        for copies in (input_chips, head_z, out_z, down_z, branch, down_chips, upstream_z):
            copies[d].wait_send()
        remote(9 + d, mine, head_rows, over_chips[d]).wait_send()


def front_of(
    inputs, attn_gain, mlp_gain, cosine, sine, code, low_code, key_code,
    w_query, w_key, w_value, w_out, w_down, upstream,
):
    tok, width = inputs.shape
    seq = 8 * tok
    hidden = w_down.shape[0] // 8
    vmem = pl.BlockSpec(memory_space=pltpu.VMEM)
    hbm = pl.BlockSpec(memory_space=pl.ANY)
    return pl.pallas_call(
        front_kernel,
        in_specs=[vmem] * 8 + [hbm] * 6,
        out_specs=[vmem] * 8 + [hbm] + [vmem] + [hbm] * 2,
        out_shape=[
            jax.ShapeDtypeStruct((tok, width), BF16),
            jax.ShapeDtypeStruct((tok, width), F32),
            jax.ShapeDtypeStruct((seq, width), BF16),
            jax.ShapeDtypeStruct((seq, HD), BF16),
            jax.ShapeDtypeStruct((2, seq, HD), BF16),
            jax.ShapeDtypeStruct((seq, HD), BF16),
            jax.ShapeDtypeStruct((seq, 1), F32),
            jax.ShapeDtypeStruct((2, width, HD), BF16),
            jax.ShapeDtypeStruct((2, width, HD), BF16),
            jax.ShapeDtypeStruct((2, HD, width), BF16),
            jax.ShapeDtypeStruct((hidden, width), BF16),
            jax.ShapeDtypeStruct((4, 2, tok, width), BF16),
        ],
        scratch_shapes=[
            pltpu.VMEM((2, 4, tok, width), BF16),
            pltpu.VMEM((4, 2, width // 4, HD), BF16),
            pltpu.VMEM((4 * tok, HD), BF16),
            pltpu.VMEM((tok, width), F32),
            pltpu.VMEM((3, tok, width), BF16),
            pltpu.VMEM((3, tok, width), BF16),
            pltpu.SemaphoreType.DMA((7,)),
            pltpu.SemaphoreType.DMA((37,)),
            pltpu.SemaphoreType.DMA((37,)),
        ],
        compiler_params=pltpu.CompilerParams(
            collective_id=2, has_side_effects=True, vmem_limit_bytes=56 << 20
        ),
        cost_estimate=pl.CostEstimate(
            flops=2 * seq * width * 3 * HD + 4 * seq * seq * HD,
            bytes_accessed=20 * seq * width,
            transcendentals=seq * seq,
        ),
    )(
        inputs, attn_gain, mlp_gain, cosine, sine, code, low_code, key_code,
        w_query, w_key, w_value, w_out, w_down, upstream,
    )


def rotate_head(values, cosine, sine):
    half = values.shape[-1] // 2
    first, second = values[:, :half], values[:, half:]
    return jnp.concatenate([first * cosine - second * sine, second * cosine + first * sine], axis=1)


def swap_halves(values):
    half = values.shape[0] // 2
    return jnp.concatenate([values[half:], values[:half]], axis=0)


def index_of(stacked, i):
    return lax.dynamic_index_in_dim(stacked, i, 0, keepdims=False)


def cut(values, starts, sizes):
    return lax.dynamic_slice(values, starts, sizes)


def on_device_by_head(
    layer_input,
    w_query,
    w_key,
    w_value,
    w_out,
    w_gate,
    w_up,
    w_down,
    attn_gain,
    mlp_gain,
    block_pairs,
    doc_ids,
    cotangent,
):
    tok_rows, width = layer_input.shape[1:]
    planes = lax.axis_size("shard")
    ctx_count = lax.axis_size("ctx")
    chips = ctx_count // 2
    ctx, plane = lax.axis_index("ctx"), lax.axis_index("shard")
    chip, core = ctx // 2, ctx % 2
    first_core = core == 0
    seq_rows = tok_rows * ctx_count
    half_seq = seq_rows // 2
    shard_width = w_down.shape[1]
    hidden_plane = w_gate.shape[1]
    hidden = hidden_plane // 2
    own_share = width // (planes * ctx_count)

    def over_z(values, d):
        return lax.ppermute(values, "shard", [(i, i ^ d) for i in range(planes)])

    def over_chips(values, d):
        return lax.ppermute(values, "ctx", [(i, i ^ (2 * d)) for i in range(ctx_count)])

    def sibling(values):
        return lax.ppermute(values, "ctx", [(i, i ^ 1) for i in range(ctx_count)])

    z_steps = range(1, planes)
    chip_steps = range(1, chips)

    def gather_z(values):
        return [values] + [over_z(values, d) for d in z_steps]

    def gather_chips(values):
        return [values] + [over_chips(values, d) for d in chip_steps]

    def gather_seq(values):
        mine = jnp.concatenate(gather_chips(values), axis=0)
        return jnp.concatenate([mine, sibling(mine)], axis=0)

    def gather_group(values):
        mine = jnp.stack(gather_z(values))
        return jnp.stack([mine, sibling(mine)], axis=1).reshape(-1, width)

    def sum_chips(block_of):
        total = block_of(0)
        for d in chip_steps:
            total = total + over_chips(block_of(d).astype(BF16), d).astype(F32)
        return total

    def sum_z(block_of):
        total = block_of(0)
        for d in z_steps:
            total = total + over_z(block_of(d).astype(BF16), d).astype(F32)
        return total

    quarter = width // chips
    inputs_low = layer_input[0]
    inputs = inputs_low.astype(F32)
    pairs, documents = block_pairs[0], doc_ids[0]
    order = jnp.stack([(chip ^ d) * 2 + (core ^ e) for e in range(2) for d in range(chips)])
    rows = (order[:, None] * tok_rows + jnp.arange(tok_rows, dtype=jnp.int32)[None, :]).reshape(-1)
    positions = position_of(rows, pairs, tok_rows, 2 * ctx_count).astype(jnp.int32)
    span = 2 * seq_rows
    doc_first = jnp.take(documents, positions).astype(jnp.int32) * span
    code = doc_first + positions
    low_code = jnp.maximum(doc_first, code - (WINDOW - 1))
    code_column, low_column, code_row = code[:, None], low_code[:, None], code[None, :]
    cosine, sine = rope_tables(positions, HD)

    upstream_low = cotangent[0]
    (
        normed_two,
        mid,
        normed_all,
        query,
        key_value,
        attended,
        log_total,
        w_head,
        w_sibling,
        out_pair,
        down_rows,
        upstream_group,
    ) = front_of(
        inputs_low,
        attn_gain[None],
        mlp_gain[None],
        cosine,
        sine,
        code_column,
        low_column,
        code_row,
        w_query,
        w_key,
        w_value,
        w_out,
        w_down,
        upstream_low,
    )
    key, value = key_value[0], key_value[1]
    out_rows = out_pair[0]
    upstream_group = upstream_group.reshape(-1, width)
    key_cosine = jnp.where(first_core, cosine, 1.0)
    key_sine = jnp.where(first_core, sine, 0.0)
    factor_one = lax.rsqrt(jnp.mean(inputs * inputs, axis=-1, keepdims=True) + EPSILON)
    output, mid_grad, mlp_gain_term, branch_grad_all, gate_up_terms, down_terms = mlp_of(
        normed_two, mid, upstream_low, mlp_gain[None], upstream_group, w_gate, w_up, down_rows
    )
    output = output[None]
    mlp_gain_term = mlp_gain_term[0]
    branch_grad_all = branch_grad_all.reshape(seq_rows, width)

    attended_grad = dot_nt(branch_grad_all, out_rows).astype(BF16)
    d_query, d_key, d_value = attend_back(
        query, attended_grad, key, value, log_total, code_column, low_column, code_row
    )
    keep = jnp.where(first_core, d_key, d_value)
    give = jnp.where(first_core, d_value, d_key)
    d_kv = keep + swap_halves(sibling(give))
    d_head = jnp.concatenate(
        [rotate_head(d_query, cosine, -sine), rotate_head(d_kv, key_cosine, -key_sine)], axis=1
    ).astype(BF16)
    d_head_pair = jnp.concatenate([d_head[:half_seq], sibling(d_head[half_seq:])], axis=1)
    w_head_pair = jnp.concatenate([w_head[0], w_head[1], w_sibling[0], w_sibling[1]], axis=1)
    normed_parts = dot_nt(d_head_pair, w_head_pair).reshape(chips, tok_rows, width)
    normed_grad = sum_chips(lambda d: normed_parts[d])
    attn_gain_term = jnp.sum(normed_grad * inputs * factor_one, axis=0)
    scaled_one = normed_grad * attn_gain
    grad_input = (
        mid_grad
        + factor_one * scaled_one
        - inputs * factor_one**3 * jnp.mean(scaled_one * inputs, axis=-1, keepdims=True)
    ).astype(BF16)[None]

    mlp_sum = sum_chips(lambda d: gate_up_terms[d].astype(F32)).astype(BF16).reshape(2, quarter // 2, 2 * hidden)
    mlp_mine = index_of(mlp_sum, core)
    mlp_other = sibling(index_of(mlp_sum, 1 - core))
    left_half = jnp.where(first_core, mlp_mine, mlp_other)
    right_half = jnp.where(first_core, mlp_other, mlp_mine)
    mlp_rows_all = jnp.concatenate(
        [left_half[:, :hidden], right_half[:, :hidden], left_half[:, hidden:], right_half[:, hidden:]],
        axis=1,
    ).reshape(planes, own_share, 2 * hidden_plane)
    grad_gate = jnp.zeros((own_share, planes * hidden_plane), F32)
    grad_up = jnp.zeros((own_share, planes * hidden_plane), F32)
    for d in range(planes):
        part = index_of(mlp_rows_all, plane ^ d)
        if d:
            part = over_z(part, d)
        part = part.astype(F32)
        at = (0, hidden_plane * (plane ^ d))
        grad_gate = lax.dynamic_update_slice(grad_gate, part[:, :hidden_plane], at)
        grad_up = lax.dynamic_update_slice(grad_up, part[:, hidden_plane:], at)

    down_terms = down_terms.reshape(planes, chips, -1, width)
    down_sum = sum_chips(
        lambda d: lax.dynamic_index_in_dim(down_terms, chip ^ d, 1, keepdims=False).astype(F32)
    ).astype(BF16)
    down_parts = []
    for d in range(planes):
        part = index_of(down_sum, plane ^ d)
        down_parts.append(over_z(part, d) if d else part)
    down_parts = jnp.stack(down_parts)
    share = down_parts.shape[1]
    grad_down = jnp.zeros((chips * share, width), F32)
    for d in range(chips):
        part = index_of(down_parts, plane ^ chip ^ d)
        if d:
            part = over_chips(part, d)
        grad_down = lax.dynamic_update_slice(grad_down, part.astype(F32), (share * (chip ^ d), 0))

    out_terms = dot_tn(attended, branch_grad_all).reshape(planes, own_share, width)
    grad_out = sum_z(lambda d: index_of(out_terms, plane ^ d))

    head_terms = dot_tn(normed_all, d_head).reshape(ctx_count, planes, own_share, 2 * HD)
    head_sum = sum_z(
        lambda d: lax.dynamic_index_in_dim(head_terms, plane ^ d, 1, keepdims=False)
    ).astype(BF16)
    head_sum = head_sum.reshape(chips, 2, own_share, 2 * HD)
    head_mine = lax.dynamic_index_in_dim(head_sum, core, 1, keepdims=False)
    head_other = sibling(lax.dynamic_index_in_dim(head_sum, 1 - core, 1, keepdims=False))
    left_half = jnp.where(first_core, head_mine, head_other)
    right_half = jnp.where(first_core, head_other, head_mine)
    head_rows = jnp.concatenate(
        [left_half[..., :HD], right_half[..., :HD], left_half[..., HD:], right_half[..., HD:]], axis=2
    )
    grad_query = jnp.zeros((own_share, HQ * HD), F32)
    grad_key = jnp.zeros((own_share, HK * HD), F32)
    grad_value = jnp.zeros((own_share, HK * HD), F32)
    for d in range(chips):
        part = index_of(head_rows, chip ^ d)
        if d:
            part = over_chips(part, d)
        part = part.astype(F32)
        grad_query = lax.dynamic_update_slice(grad_query, part[:, : 2 * HD], (0, 2 * HD * (chip ^ d)))
        grad_key = lax.dynamic_update_slice(grad_key, part[:, 2 * HD : 3 * HD], (0, HD * (chip ^ d)))
        grad_value = lax.dynamic_update_slice(grad_value, part[:, 3 * HD :], (0, HD * (chip ^ d)))

    gains = jnp.stack([attn_gain_term, mlp_gain_term]).reshape(2, ctx_count, planes, own_share)

    def gain_block(d):
        return lax.dynamic_index_in_dim(gains, plane ^ d, 2, keepdims=False)

    gain_sum = gain_block(0)
    for d in z_steps:
        gain_sum = gain_sum + over_z(gain_block(d), d)
    gain_sum = gain_sum.reshape(2, chips, 2, own_share)
    gain_sum = lax.dynamic_index_in_dim(gain_sum, core, 2, keepdims=False) + sibling(
        lax.dynamic_index_in_dim(gain_sum, 1 - core, 2, keepdims=False)
    )
    gain_mine = lax.dynamic_index_in_dim(gain_sum, chip, 1, keepdims=False)
    for d in chip_steps:
        gain_mine = gain_mine + over_chips(
            lax.dynamic_index_in_dim(gain_sum, chip ^ d, 1, keepdims=False), d
        )
    return (
        output,
        grad_input,
        grad_query,
        grad_key,
        grad_value,
        grad_out,
        grad_gate,
        grad_up,
        grad_down,
        gain_mine[0],
        gain_mine[1],
    )


def plan_of(mesh):
    chips, planes = mesh.shape["ctx"] // 2, mesh.shape["shard"]
    if mesh.shape["ctx"] == HQ and HQ == 2 * HK and chips == planes == HK:
        return on_device_by_head
    return on_device


def solution(mesh):
    placed = (
        P("shard", "ctx", None),
        P(None, "shard"),
        P(None, "shard"),
        P(None, "shard"),
        P(None, "shard"),
        P(None, "shard"),
        P(None, "shard"),
        P(None, "shard"),
        P(),
        P(),
        P("shard", None),
        P("shard", None),
        P("shard", "ctx", None),
    )
    return jax.shard_map(
        plan_of(mesh),
        mesh=mesh,
        in_specs=placed,
        out_specs=(
            P("shard", "ctx", None),
            P("shard", "ctx", None),
            P(("ctx", "shard"), None),
            P(("ctx", "shard"), None),
            P(("ctx", "shard"), None),
            P(("ctx", "shard"), None),
            P(("ctx", "shard"), None),
            P(("ctx", "shard"), None),
            P(("ctx", "shard"), None),
            P(("ctx", "shard")),
            P(("ctx", "shard")),
        ),
        check_vma=False,
    )
```

```python
import functools
import math

import jax
import jax.numpy as jnp
from jax import lax
from jax.experimental import pallas as pl
from jax.experimental.pallas import tpu as pltpu
from jax.sharding import PartitionSpec as P

HQ = 8
HK = 4
HD = 256
WINDOW = 1024


EPSILON = 1e-06
SCORE_SCALE = 0.0625
MASKED = -1e30
ROPE_BASE = 1000042.0


def position_of(rows, pairs, per_device, blocks_total):
    device = rows // per_device
    within = rows % per_device
    half = per_device // 2
    chosen = jnp.take(pairs, device)
    first = chosen * half + within
    second = (blocks_total - 1 - chosen) * half + within - half
    return jnp.where(within < half, first, second)


def rope_tables(positions, head):
    half = head // 2
    freq = ROPE_BASE ** (-(jnp.arange(half, dtype=jnp.float32) * 2.0) / head)
    angle = positions.astype(jnp.float32)[:, None] * freq[None, :]
    return (jnp.cos(angle), jnp.sin(angle))


def rotate(values, cosine, sine):
    half = values.shape[-1] // 2
    first = values[..., :half]
    second = values[..., half:]
    cosine = cosine[:, None, :]
    sine = sine[:, None, :]
    return jnp.concatenate(
        [first * cosine - second * sine, second * cosine + first * sine], axis=-1
    )


def rotate_back(grads, cosine, sine):
    half = grads.shape[-1] // 2
    first = grads[..., :half]
    second = grads[..., half:]
    cosine = cosine[:, None, :]
    sine = sine[:, None, :]
    return jnp.concatenate(
        [first * cosine + second * sine, second * cosine - first * sine], axis=-1
    )


def visible(query_pos, query_doc, key_pos, key_doc):
    distance = query_pos[:, None] - key_pos[None, :]
    return (query_doc[:, None] == key_doc[None, :]) & (distance >= 0) & (distance < WINDOW)


def write_columns(left, piece):
    made = jnp.dot(left, piece, preferred_element_type=jnp.float32)
    return made


def contract_full(grads, weight):
    return lax.dot_general(
        grads, weight, (((1,), (1,)), ((), ())), preferred_element_type=jnp.float32
    )


def alternate(parts, shard_count, rows):
    return jnp.concatenate([part.reshape(rows, shard_count, -1) for part in parts], axis=2).reshape(
        rows, -1
    )


def outer_sum(left, right):
    return lax.dot_general(
        left, right, (((0,), (0,)), ((), ())), preferred_element_type=jnp.float32
    )


def term_rows(lefts, rights, gain_block, count):
    normed_all, attended_all, second_all, act_all = lefts
    query_g, key_g, value_g, branch_g, gate_g, up_g, upstream_g = rights
    down_part = outer_sum(act_all, upstream_g).reshape(count, -1)
    return jnp.concatenate(
        [
            outer_sum(normed_all, query_g),
            outer_sum(normed_all, key_g),
            outer_sum(normed_all, value_g),
            outer_sum(attended_all, branch_g),
            outer_sum(second_all, gate_g),
            outer_sum(second_all, up_g),
            down_part,
            gain_block,
        ],
        axis=1,
    )


def deal_columns(values, ctx_count, shard_count):
    rows = values.shape[0]
    return (
        values.reshape(rows, ctx_count, shard_count, -1)
        .transpose(0, 2, 1, 3)
        .reshape(rows, shard_count, -1)
    )


def on_device(
    layer_input,
    w_query,
    w_key,
    w_value,
    w_out,
    w_gate,
    w_up,
    w_down,
    attn_gain,
    mlp_gain,
    block_pairs,
    doc_ids,
    cotangent,
):
    tok_rows = layer_input.shape[1]
    model_width = layer_input.shape[2]
    shard_count = lax.axis_size("shard")
    ctx_count = lax.axis_size("ctx")
    device_count = lax.axis_size(("ctx", "shard"))
    group_size = HQ // HK
    blocks_total = 2 * ctx_count
    pairs = block_pairs[0]
    documents = doc_ids[0]
    own_rows = lax.axis_index("ctx") * tok_rows + jnp.arange(tok_rows, dtype=jnp.int32)
    own_pos = position_of(own_rows, pairs, tok_rows, blocks_total)
    own_doc = jnp.take(documents, own_pos)
    cosine, sine = rope_tables(own_pos, HD)
    stack_qkv = jnp.concatenate([w_query, w_key, w_value], axis=1)
    stack_mlp = jnp.concatenate([w_gate, w_up], axis=1)
    per_query = w_query.shape[1]
    per_key = w_key.shape[1]
    per_hidden = w_gate.shape[1]
    hidden_width = w_down.shape[0]
    inputs = layer_input.reshape(tok_rows, model_width).astype(jnp.float32)
    factor_one = lax.rsqrt(jnp.mean(inputs * inputs, axis=-1, keepdims=True) + EPSILON)
    normed = (inputs * factor_one * attn_gain).astype(jnp.bfloat16)
    projected = write_columns(normed, lax.all_gather(stack_qkv, "shard", axis=1, tiled=True))
    projected = projected.reshape(tok_rows, shard_count, -1)
    query_lin = projected[:, :, :per_query].reshape(tok_rows, HQ, HD)
    key_lin = projected[:, :, per_query : per_query + per_key].reshape(tok_rows, HK, HD)
    value_lin = projected[:, :, per_query + per_key :].reshape(tok_rows, HK * HD)
    query_rot = (
        rotate(query_lin, cosine, sine).astype(jnp.bfloat16).reshape(tok_rows, HK, group_size, HD)
    )
    key_rot = rotate(key_lin, cosine, sine).astype(jnp.bfloat16).reshape(tok_rows, HK * HD)
    value_low = value_lin.astype(jnp.bfloat16)

    def key_mask(first_row, count):
        key_pos = position_of(
            first_row + jnp.arange(count, dtype=jnp.int32), pairs, tok_rows, blocks_total
        )
        return visible(own_pos, own_doc, key_pos, jnp.take(documents, key_pos))[:, None, None, :]

    start_state = (
        jnp.full((tok_rows, HK, group_size), MASKED, jnp.float32),
        jnp.zeros((tok_rows, HK, group_size), jnp.float32),
        jnp.zeros((tok_rows, HK, group_size, HD), jnp.float32),
    )
    keys = lax.all_gather(key_rot, "ctx", axis=0, tiled=True)
    values = lax.all_gather(value_low, "ctx", axis=0, tiled=True)
    count = keys.shape[0]
    step = math.gcd(count, 4 * tok_rows)
    keys = keys.reshape(count // step, step, HK, HD)
    values = values.reshape(count // step, step, HK, HD)

    def attend_step(i, running):
        top, total, accum = running
        mask = key_mask(i * step, step)
        scores = (
            jnp.einsum("tkgd,skd->tkgs", query_rot, keys[i], preferred_element_type=jnp.float32)
            * SCORE_SCALE
        )
        scores = jnp.where(mask, scores, MASKED)
        new_top = jnp.maximum(top, jnp.max(scores, axis=-1))
        weights = jnp.where(mask, jnp.exp(scores - new_top[..., None]), 0.0)
        shrink = jnp.exp(top - new_top)
        total = total * shrink + jnp.sum(weights, axis=-1)
        accum = accum * shrink[..., None] + jnp.einsum(
            "tkgs,skd->tkgd",
            weights.astype(jnp.bfloat16),
            values[i],
            preferred_element_type=jnp.float32,
        )
        return (new_top, total, accum)

    top, total, accum = lax.fori_loop(0, count // step, attend_step, start_state)
    log_total = top + jnp.log(total)
    attended_full = accum / total[..., None]
    attended = attended_full.astype(jnp.bfloat16).reshape(tok_rows, HQ * HD)
    branch_one = write_columns(attended, lax.all_gather(w_out, "shard", axis=1, tiled=True))
    mid = inputs + branch_one
    factor_two = lax.rsqrt(jnp.mean(mid * mid, axis=-1, keepdims=True) + EPSILON)
    normed_two = (mid * factor_two * mlp_gain).astype(jnp.bfloat16)
    gate_up = write_columns(normed_two, lax.all_gather(stack_mlp, "shard", axis=1, tiled=True))
    gate_up = gate_up.reshape(tok_rows, shard_count, -1)
    gate = gate_up[:, :, :per_hidden].reshape(tok_rows, hidden_width)
    up_lin = gate_up[:, :, per_hidden:].reshape(tok_rows, hidden_width)
    sigma = jax.nn.sigmoid(gate)
    swish = gate * sigma
    act = (swish * up_lin).astype(jnp.bfloat16)
    branch_two = write_columns(act, lax.all_gather(w_down, "shard", axis=1, tiled=True))
    output = (mid + branch_two).astype(jnp.bfloat16).reshape(1, tok_rows, model_width)
    full_qkv, full_out, full_mlp, full_down = (
        lax.all_gather(stack_qkv, "shard", axis=1, tiled=True),
        lax.all_gather(w_out, "shard", axis=1, tiled=True),
        lax.all_gather(stack_mlp, "shard", axis=1, tiled=True),
        lax.all_gather(w_down, "shard", axis=1, tiled=True),
    )
    upstream_low = cotangent.reshape(tok_rows, model_width)
    upstream = upstream_low.astype(jnp.float32)
    act_grad = contract_full(upstream_low, full_down)
    gate_grad = (act_grad * up_lin * (sigma * (1.0 + gate * (1.0 - sigma)))).astype(jnp.bfloat16)
    up_grad = (act_grad * swish).astype(jnp.bfloat16)
    stacked_mlp_grad = alternate((gate_grad, up_grad), shard_count, tok_rows)
    norm_two_grad = contract_full(stacked_mlp_grad, full_mlp)
    mlp_gain_term = jnp.sum(norm_two_grad * mid * factor_two, axis=0)
    scaled_two = norm_two_grad * mlp_gain
    mid_grad = (
        upstream
        + factor_two * scaled_two
        - mid * factor_two**3 * jnp.mean(scaled_two * mid, axis=-1, keepdims=True)
    )
    branch_grad = mid_grad.astype(jnp.bfloat16)
    attended_grad = contract_full(branch_grad, full_out)
    attended_low = attended_grad.astype(jnp.bfloat16).reshape(tok_rows, HK, group_size, HD)
    delta = jnp.sum(attended_low.astype(jnp.float32) * attended_full, axis=-1)

    def query_grads(carry, piece):
        keys, values = piece
        count = keys.shape[0]
        step = math.gcd(count, 4 * tok_rows)
        keys = keys.reshape(count // step, step, HK, HD)
        values = values.reshape(count // step, step, HK, HD)

        def query_step(i, query_sum):
            mask = key_mask(i * step, step)
            scores = (
                jnp.einsum("tkgd,skd->tkgs", query_rot, keys[i], preferred_element_type=jnp.float32)
                * SCORE_SCALE
            )
            probs = jnp.where(mask, jnp.exp(scores - log_total[..., None]), 0.0)
            prob_grad = jnp.einsum(
                "tkgd,skd->tkgs", attended_low, values[i], preferred_element_type=jnp.float32
            )
            score_grad = (probs * (prob_grad - delta[..., None])).astype(jnp.bfloat16)
            return query_sum + jnp.einsum(
                "tkgs,skd->tkgd", score_grad, keys[i], preferred_element_type=jnp.float32
            )

        return lax.fori_loop(0, count // step, query_step, carry)

    query_sum = query_grads(
        jnp.zeros((tok_rows, HK, group_size, HD), jnp.float32),
        (
            lax.all_gather(key_rot, "ctx", axis=0, tiled=True),
            lax.all_gather(value_low, "ctx", axis=0, tiled=True),
        ),
    )
    all_log_total, all_delta = (
        lax.all_gather(log_total, "ctx", axis=0, tiled=True),
        lax.all_gather(delta, "ctx", axis=0, tiled=True),
    )
    key_three = key_rot.reshape(tok_rows, HK, HD)
    value_three = value_low.reshape(tok_rows, HK, HD)

    def key_grads(carry, piece):
        queries, outgrads = piece
        count = queries.shape[0]
        step = math.gcd(count, 4 * tok_rows)
        queries = queries.reshape(count // step, step, HK, group_size, HD)
        outgrads = outgrads.reshape(count // step, step, HK, group_size, HD)

        def key_step(i, running):
            key_sum, value_sum = running
            first_row = i * step
            query_pos = position_of(
                first_row + jnp.arange(step, dtype=jnp.int32), pairs, tok_rows, blocks_total
            )
            mask = visible(query_pos, jnp.take(documents, query_pos), own_pos, own_doc)[
                :, None, None, :
            ]
            lse_part = lax.dynamic_slice_in_dim(all_log_total, first_row, step, 0)
            delta_part = lax.dynamic_slice_in_dim(all_delta, first_row, step, 0)
            scores = (
                jnp.einsum(
                    "skgd,tkd->skgt", queries[i], key_three, preferred_element_type=jnp.float32
                )
                * SCORE_SCALE
            )
            probs = jnp.where(mask, jnp.exp(scores - lse_part[..., None]), 0.0)
            prob_grad = jnp.einsum(
                "skgd,tkd->skgt", outgrads[i], value_three, preferred_element_type=jnp.float32
            )
            score_grad = (probs * (prob_grad - delta_part[..., None])).astype(jnp.bfloat16)
            value_sum = value_sum + jnp.einsum(
                "skgt,skgd->tkd",
                probs.astype(jnp.bfloat16),
                outgrads[i],
                preferred_element_type=jnp.float32,
            )
            key_sum = key_sum + jnp.einsum(
                "skgt,skgd->tkd", score_grad, queries[i], preferred_element_type=jnp.float32
            )
            return (key_sum, value_sum)

        return lax.fori_loop(0, count // step, key_step, carry)

    key_sum, value_sum = key_grads(
        (jnp.zeros((tok_rows, HK, HD), jnp.float32), jnp.zeros((tok_rows, HK, HD), jnp.float32)),
        (
            lax.all_gather(query_rot.reshape(tok_rows, HQ * HD), "ctx", axis=0, tiled=True),
            lax.all_gather(attended_low.reshape(tok_rows, HQ * HD), "ctx", axis=0, tiled=True),
        ),
    )
    query_grad = (
        rotate_back(query_sum.reshape(tok_rows, HQ, HD) * SCORE_SCALE, cosine, sine)
        .astype(jnp.bfloat16)
        .reshape(tok_rows, HQ * HD)
    )
    key_grad = (
        rotate_back(key_sum * SCORE_SCALE, cosine, sine)
        .astype(jnp.bfloat16)
        .reshape(tok_rows, HK * HD)
    )
    value_grad = value_sum.astype(jnp.bfloat16).reshape(tok_rows, HK * HD)
    stacked_qkv_grad = alternate((query_grad, key_grad, value_grad), shard_count, tok_rows)
    normed_grad = contract_full(stacked_qkv_grad, full_qkv)
    attn_gain_term = jnp.sum(normed_grad * inputs * factor_one, axis=0)
    scaled_one = normed_grad * attn_gain
    input_grad = (
        mid_grad
        + factor_one * scaled_one
        - inputs * factor_one**3 * jnp.mean(scaled_one * inputs, axis=-1, keepdims=True)
    )
    grad_input = input_grad.astype(jnp.bfloat16).reshape(1, tok_rows, model_width)
    ratio = hidden_width // model_width
    own_share = model_width // device_count
    rights = (query_grad, key_grad, value_grad, branch_grad, gate_grad, up_grad, upstream_low)
    group_rights = (
        lax.all_gather(rights[0], "shard", axis=0, tiled=True),
        lax.all_gather(rights[1], "shard", axis=0, tiled=True),
        lax.all_gather(rights[2], "shard", axis=0, tiled=True),
        lax.all_gather(rights[3], "shard", axis=0, tiled=True),
        lax.all_gather(rights[4], "shard", axis=0, tiled=True),
        lax.all_gather(rights[5], "shard", axis=0, tiled=True),
        lax.all_gather(rights[6], "shard", axis=0, tiled=True),
    )
    dealt = (
        lax.all_to_all(
            deal_columns(normed, ctx_count, shard_count),
            "shard",
            split_axis=1,
            concat_axis=0,
            tiled=True,
        ),
        lax.all_to_all(
            deal_columns(attended, ctx_count, shard_count),
            "shard",
            split_axis=1,
            concat_axis=0,
            tiled=True,
        ),
        lax.all_to_all(
            deal_columns(normed_two, ctx_count, shard_count),
            "shard",
            split_axis=1,
            concat_axis=0,
            tiled=True,
        ),
        lax.all_to_all(
            deal_columns(act, ctx_count, shard_count),
            "shard",
            split_axis=1,
            concat_axis=0,
            tiled=True,
        ),
    )
    group_lefts = tuple((part.reshape(part.shape[0], -1) for part in dealt))
    gain_pair = lax.psum(jnp.stack([attn_gain_term, mlp_gain_term]), "shard")
    gain_mine = lax.dynamic_index_in_dim(
        gain_pair.reshape(2, ctx_count, shard_count, own_share),
        lax.axis_index("shard"),
        2,
        keepdims=False,
    ).reshape(2, ctx_count * own_share)
    gain_block = jnp.concatenate(
        [gain_mine.T, jnp.zeros((ctx_count * own_share, 126), jnp.float32)], axis=1
    )
    summed = lax.psum_scatter(
        term_rows(group_lefts, group_rights, gain_block, own_share * lax.axis_size("ctx")).astype(
            jnp.bfloat16
        ),
        "ctx",
        scatter_dimension=0,
        tiled=True,
    ).astype(jnp.float32)
    edge_one = HQ * HD
    edge_two = edge_one + HK * HD
    edge_three = edge_two + HK * HD
    edge_four = edge_three + model_width
    edge_five = edge_four + hidden_width
    edge_six = edge_five + hidden_width
    edge_seven = edge_six + ratio * model_width
    grad_query = summed[:, :edge_one]
    grad_key = summed[:, edge_one:edge_two]
    grad_value = summed[:, edge_two:edge_three]
    grad_out = summed[:, edge_three:edge_four]
    grad_gate = summed[:, edge_four:edge_five]
    grad_up = summed[:, edge_five:edge_six]
    grad_down = summed[:, edge_six:edge_seven].reshape(own_share * ratio, model_width)
    grad_attn_gain = summed[:, edge_seven]
    grad_mlp_gain = summed[:, edge_seven + 1]
    return (
        output,
        grad_input,
        grad_query,
        grad_key,
        grad_value,
        grad_out,
        grad_gate,
        grad_up,
        grad_down,
        grad_attn_gain,
        grad_mlp_gain,
    )


BF16 = jnp.bfloat16
F32 = jnp.float32
VISIBLE_ROWS = 256


def dot_nn(a, b):
    return jnp.dot(a, b, preferred_element_type=F32)


def dot_nt(a, b):
    return lax.dot_general(a, b, (((1,), (1,)), ((), ())), preferred_element_type=F32)


def dot_tn(a, b):
    return lax.dot_general(a, b, (((0,), (0,)), ((), ())), preferred_element_type=F32)


def scores_of(query, key, code, low_code, key_code):
    scores = dot_nt(query, key) * SCORE_SCALE
    mask = (key_code <= code) & (key_code >= low_code)
    return jnp.where(mask, scores, MASKED)


MESH = pl.DeviceIdType.MESH
TILE = 256


def flip(i, d):
    return (i, i + 1 - 2 * (i % 2), (i + 2) % 4, 3 - i)[d]


def mlp_kernel(
    second_ref,
    mid_ref,
    upstream_ref,
    gain_ref,
    upstream_hbm,
    gate_hbm,
    up_hbm,
    down_hbm,
    output_ref,
    mid_grad_ref,
    gain_grad_ref,
    branch_all,
    gate_up_terms,
    gate_up_near,
    down_terms,
    gate_w,
    up_w,
    down_w,
    upstream_all,
    second_all,
    act,
    gate_grad,
    up_grad,
    held,
    own_sum,
    pair_send,
    pair_recv,
    z_send,
    z_recv,
    branch_low,
    staged,
    local_sem,
    staged_sem,
    send_sem,
    recv_sem,
):
    tok = second_ref.shape[0]
    pair = 2 * tok
    hidden = gate_w.shape[1]
    width = second_ref.shape[1]
    ctx, plane = lax.axis_index("ctx"), lax.axis_index("shard")
    chip, core = ctx // 2, ctx % 2
    sibling = (ctx + 1 - 2 * core, plane)
    over_z = [(ctx, flip(plane, d)) for d in range(4)]
    over_chips = [(2 * flip(chip, d) + core, plane) for d in range(4)]

    half = pl.ds(pl.multiple_of(core * hidden, hidden), hidden)
    loads = [
        pltpu.make_async_copy(upstream_hbm, upstream_all, local_sem.at[0]),
        pltpu.make_async_copy(down_hbm, down_w, local_sem.at[1]),
        pltpu.make_async_copy(gate_hbm.at[:, half], gate_w, local_sem.at[2]),
        pltpu.make_async_copy(up_hbm.at[:, half], up_w, local_sem.at[3]),
        pltpu.make_async_copy(second_ref, second_all.at[0, 0], local_sem.at[4]),
    ]
    for load in loads:
        load.start()

    barrier = pltpu.get_barrier_semaphore()
    partners = [sibling] + over_z[1:] + over_chips[1:]
    for partner in partners:
        pl.semaphore_signal(barrier, inc=1, device_id=partner, device_id_type=MESH)
    pl.semaphore_wait(barrier, len(partners))

    def send(slot, source, target, device):
        copy = pltpu.make_async_remote_copy(
            src_ref=source,
            dst_ref=target,
            send_sem=send_sem.at[slot],
            recv_sem=recv_sem.at[slot],
            device_id=device,
            device_id_type=MESH,
        )
        copy.start()
        return copy

    gather_z = {d: send(d, second_ref, second_all.at[d, 0], over_z[d]) for d in (1, 2, 3)}
    gather_pair = {0: send(0, second_ref, second_all.at[0, 1], sibling)}
    for load in loads:
        load.wait()

    def rows_of(d):
        return pl.ds(d * pair, pair)

    def forward(d):
        rows = rows_of(d)
        second = lambda: second_all[d].reshape(pair, width)

        def step(t, carry):
            at = pl.ds(pl.multiple_of(t * TILE, TILE), TILE)
            act_grad = dot_nt(upstream_all[rows, :], down_w[at, :])
            gate = dot_nn(second(), gate_w[:, at])
            up_lin = dot_nn(second(), up_w[:, at])
            sigma = 1.0 / (1.0 + jnp.exp(-gate))
            swish = gate * sigma
            act[rows, at] = (swish * up_lin).astype(BF16)
            gate_grad[rows, at] = (
                act_grad * up_lin * (sigma * (1.0 + gate * (1.0 - sigma)))
            ).astype(BF16)
            up_grad[rows, at] = (act_grad * swish).astype(BF16)
            return carry

        lax.fori_loop(0, hidden // TILE, step, 0)

    def give_pair(d, base, product):
        which = 0 if base == 7 else 1

        def step(t, carry):
            at = pl.ds(pl.multiple_of(t * TILE, TILE), TILE)
            terms = product(at)
            held[d % 2, :, at] = terms[:tok]
            pair_send[which, d, :, at] = terms[tok:].astype(BF16)
            return carry

        lax.fori_loop(0, width // TILE, step, 0)
        return send(base + d, pair_send.at[which, d], pair_recv.at[which, d], sibling)

    def give_plane(d, base, copy):
        which = 0 if base == 7 else 1
        copy.wait_recv()
        total = held[d % 2] + pair_recv[which, d].astype(F32)
        if d == 0:
            own_sum[which] = total
            return None
        z_send[which, d - 1] = total.astype(BF16)
        return send(base + 3 + d, z_send.at[which, d - 1], z_recv.at[which, d - 1], over_z[d])

    def back(d):
        rows = rows_of(d)
        return lambda at: dot_nt(gate_grad[rows, :], gate_w[at, :]) + dot_nt(
            up_grad[rows, :], up_w[at, :]
        )

    def onward(d):
        rows = rows_of(d)
        return lambda at: dot_nn(act[rows, :], down_w[:, at])

    pairs, planes = {}, {}
    for d in range(4):
        if d:
            gather_z[d].wait_recv()
            gather_pair[d] = send(
                3 + d, second_all.at[d, 0], second_all.at[d, 1], sibling
            )
        gather_pair[d].wait_recv()
        forward(d)
        pairs[d] = give_pair(d, 7, back(d))
        if d:
            planes[d - 1] = give_plane(d - 1, 7, pairs[d - 1])
    planes[3] = give_plane(3, 7, pairs[3])

    out_pairs, out_planes = {}, {}
    for d in range(4):
        out_pairs[d] = give_pair(d, 14, onward(d))
        if d:
            out_planes[d - 1] = give_plane(d - 1, 14, out_pairs[d - 1])
    out_planes[3] = give_plane(3, 14, out_pairs[3])

    second_rows = second_all.reshape(8 * tok, width)

    def to_hbm(slot, target):
        return pltpu.make_async_copy(staged.at[slot], target, staged_sem.at[slot])

    chunks = (1, 2, 3, 0)
    near = {}
    for i, d in enumerate(chunks):
        for h in range(2):
            first = flip(chip, d) * (2 * TILE) + h * TILE
            left = second_rows[:, pl.ds(pl.multiple_of(first, TILE), TILE)]
            target = gate_up_terms.at[d, pl.ds(h * TILE, TILE)]
            if i:
                to_hbm(h, target).wait()
            if h and 1 <= i <= 2:
                done = chunks[i - 1]
                near[done] = send(
                    27 + done, gate_up_terms.at[done], gate_up_near.at[done - 1], over_chips[done]
                )
            staged[h, :, :hidden] = dot_tn(left, gate_grad[...]).astype(BF16)
            staged[h, :, hidden:] = dot_tn(left, up_grad[...]).astype(BF16)
            to_hbm(h, target).start()

    for d in (1, 2, 3):
        planes[d].wait_recv()
    chunk = 32
    gain = gain_ref[...]

    def mid_step(i, carry):
        at = pl.ds(pl.multiple_of(i * chunk, chunk), chunk)
        grad = own_sum[0, at, :]
        for d in range(3):
            grad = grad + z_recv[0, d, at, :].astype(F32)
        mid = mid_ref[at, :]
        factor = lax.rsqrt(jnp.mean(mid * mid, axis=-1, keepdims=True) + EPSILON)
        scaled = grad * gain
        mid_grad = (
            upstream_ref[at, :].astype(F32)
            + factor * scaled
            - mid * (factor * factor * factor * jnp.mean(scaled * mid, axis=-1, keepdims=True))
        )
        mid_grad_ref[at, :] = mid_grad
        branch_low[at, :] = mid_grad.astype(BF16)
        return carry + jnp.sum(grad * mid * factor, axis=0, keepdims=True)

    gain_grad_ref[...] = lax.fori_loop(0, tok // chunk, mid_step, jnp.zeros((1, width), F32))
    branch_chips = {
        d: send(20 + d, branch_low, branch_all.at[0, d], over_chips[d]) for d in (1, 2, 3)
    }
    branch_pairs = {0: send(24, branch_low, branch_all.at[1, 0], sibling)}
    keep = pltpu.make_async_copy(branch_low, branch_all.at[0, 0], local_sem.at[0])
    keep.start()

    def down_step(t):
        slot = t % 2
        target = down_terms.at[pl.ds(t * TILE, TILE)]
        to_hbm(slot, target).wait()
        left = act[:, pl.ds(t * TILE, TILE)]
        staged[slot] = dot_tn(left, upstream_all[...]).astype(BF16)
        to_hbm(slot, target).start()

    for t in range(hidden // TILE):
        down_step(t)
    for d in (1, 2, 3):
        branch_chips[d].wait_recv()
        branch_pairs[d] = send(24 + d, branch_all.at[0, d], branch_all.at[1, d], sibling)

    for d in (1, 2, 3):
        out_planes[d].wait_recv()

    def out_step(i, carry):
        at = pl.ds(pl.multiple_of(i * chunk, chunk), chunk)
        total = mid_ref[at, :] + own_sum[1, at, :]
        for d in range(3):
            total = total + z_recv[1, d, at, :].astype(F32)
        output_ref[at, :] = total.astype(BF16)
        return carry

    lax.fori_loop(0, tok // chunk, out_step, 0)

    for d in range(4):
        branch_pairs[d].wait_recv()
        for copy in (gather_pair[d], pairs[d], out_pairs[d], branch_pairs[d]):
            copy.wait_send()
    for d in (1, 2, 3):
        for copy in (gather_z[d], planes[d], out_planes[d], branch_chips[d]):
            copy.wait_send()
    keep.wait()
    for d in (1, 2):
        near[d].wait()
    for slot in range(2):
        to_hbm(slot, down_terms.at[pl.ds(0, TILE)]).wait()


def mlp_of(normed_two, mid, upstream, gain, upstream_group, w_gate, w_up, down_rows):
    tok, width = mid.shape
    hidden = down_rows.shape[0]
    rows = upstream_group.shape[0]
    vmem = pl.BlockSpec(memory_space=pltpu.VMEM)
    hbm = pl.BlockSpec(memory_space=pl.ANY)
    return pl.pallas_call(
        mlp_kernel,
        in_specs=[vmem] * 4 + [hbm] * 4,
        out_specs=[vmem] * 3 + [hbm] * 4,
        out_shape=[
            jax.ShapeDtypeStruct((tok, width), BF16),
            jax.ShapeDtypeStruct((tok, width), F32),
            jax.ShapeDtypeStruct((1, width), F32),
            jax.ShapeDtypeStruct((2, 4, tok, width), BF16),
            jax.ShapeDtypeStruct((4, 2 * TILE, 2 * hidden), BF16),
            jax.ShapeDtypeStruct((2, 2 * TILE, 2 * hidden), BF16),
            jax.ShapeDtypeStruct((hidden, width), BF16),
        ],
        scratch_shapes=[
            pltpu.VMEM((width, hidden), BF16),
            pltpu.VMEM((width, hidden), BF16),
            pltpu.VMEM((hidden, width), BF16),
            pltpu.VMEM((rows, width), BF16),
            pltpu.VMEM((4, 2, tok, width), BF16),
            pltpu.VMEM((rows, hidden), BF16),
            pltpu.VMEM((rows, hidden), BF16),
            pltpu.VMEM((rows, hidden), BF16),
            pltpu.VMEM((2, tok, width), F32),
            pltpu.VMEM((2, tok, width), F32),
            pltpu.VMEM((2, 4, tok, width), BF16),
            pltpu.VMEM((2, 4, tok, width), BF16),
            pltpu.VMEM((2, 3, tok, width), BF16),
            pltpu.VMEM((2, 3, tok, width), BF16),
            pltpu.VMEM((tok, width), BF16),
            pltpu.VMEM((2, TILE, width), BF16),
            pltpu.SemaphoreType.DMA((5,)),
            pltpu.SemaphoreType.DMA((2,)),
            pltpu.SemaphoreType.DMA((30,)),
            pltpu.SemaphoreType.DMA((30,)),
        ],
        compiler_params=pltpu.CompilerParams(
            collective_id=1, has_side_effects=True, vmem_limit_bytes=60 << 20
        ),
        cost_estimate=pl.CostEstimate(
            flops=18 * rows * width * hidden,
            bytes_accessed=2 * (5 * width * hidden + 4 * rows * width),
            transcendentals=rows * hidden,
        ),
    )(normed_two, mid, upstream, gain, upstream_group, w_gate, w_up, down_rows)


def xor4(a, b):
    return 2 * ((a // 2 + b // 2) % 2) + (a % 2 + b % 2) % 2


def rotated(values, cosine, sine):
    half = values.shape[1] // 2
    first, second = values[:, :half], values[:, half:]
    return jnp.concatenate([first * cosine - second * sine, second * cosine + first * sine], axis=1)


def front_kernel(
    input_ref,
    attn_gain_ref,
    mlp_gain_ref,
    cosine_ref,
    sine_ref,
    code_ref,
    low_code_ref,
    key_code_ref,
    query_hbm,
    key_hbm,
    value_hbm,
    out_hbm,
    down_hbm,
    upstream_hbm,
    second_ref,
    mid_ref,
    normed_ref,
    query_ref,
    kv_ref,
    attended_ref,
    log_total_ref,
    w_head,
    w_sibling,
    out_pair,
    down_rows,
    upstream_all,
    inputs_all,
    w_parts,
    attended_other,
    own_sum,
    chip_send,
    chip_recv,
    local_sem,
    send_sem,
    recv_sem,
):
    tok, width = input_ref.shape
    quarter = width // 4
    shard = out_hbm.shape[1]
    hidden = down_rows.shape[0]
    part = hidden // 4
    seq = 8 * tok
    half_seq = 4 * tok
    ctx, plane = lax.axis_index("ctx"), lax.axis_index("shard")
    chip, core = ctx // 2, ctx % 2
    sibling = (ctx + 1 - 2 * core, plane)
    over_z = [(ctx, flip(plane, d)) for d in range(4)]
    over_chips = [(2 * flip(chip, d) + core, plane) for d in range(4)]
    others = (1, 2, 3)

    def at(i, size):
        return pl.ds(pl.multiple_of(i * size, size), size)

    def remote(slot, source, target, device):
        return pltpu.make_async_remote_copy(
            src_ref=source,
            dst_ref=target,
            send_sem=send_sem.at[slot],
            recv_sem=recv_sem.at[slot],
            device_id=device,
            device_id_type=MESH,
        )

    def send(slot, source, target, device):
        copy = remote(slot, source, target, device)
        copy.start()
        return copy

    def local(slot, source, target):
        return pltpu.make_async_copy(source, target, local_sem.at[slot])

    rows = at(chip, quarter)
    mine = w_parts.at[plane]
    load_query = local(0, query_hbm.at[rows, at(core, HD)], mine.at[0])
    load_key = local(1, key_hbm.at[rows], mine.at[1])
    load_value = local(1, value_hbm.at[rows], mine.at[1])
    load_query.start()

    @pl.when(core == 0)
    def _():
        load_key.start()

    @pl.when(core == 1)
    def _():
        load_value.start()

    keep_input = local(2, input_ref, inputs_all.at[0, 0])
    keep_input.start()
    out_own = out_hbm.at[at(ctx, HD), :]
    keep_out = local(3, out_own, out_pair.at[0, :, at(plane, shard)])
    keep_out.start()

    def down_block(to_plane):
        first = to_plane * (2 * hidden) + core * hidden + chip * part
        return down_hbm.at[pl.ds(pl.multiple_of(first, part), part), :]

    down_place = down_rows.at[at(chip, part), at(plane, shard)]
    keep_down = local(4, down_block(plane), down_place)
    keep_down.start()
    keep_upstream = local(5, upstream_hbm, upstream_all.at[0, 0])
    keep_upstream.start()

    barrier = pltpu.get_barrier_semaphore()
    partners = [sibling] + over_z[1:] + over_chips[1:]
    for partner in partners:
        pl.semaphore_signal(barrier, inc=1, device_id=partner, device_id_type=MESH)
    pl.semaphore_wait(barrier, len(partners))

    input_chips = {
        d: send(d - 1, input_ref, inputs_all.at[0, d], over_chips[d]) for d in others
    }
    input_pairs = {0: send(3, input_ref, inputs_all.at[1, 0], sibling)}
    load_query.wait()
    load_key.wait()
    head_z = {d: send(6 + d, mine, w_parts.at[plane], over_z[d]) for d in others}

    chunk = 32
    attn_gain = attn_gain_ref[...]

    def norm(e, d):
        def step(i, carry):
            block = inputs_all[e, d, at(i, chunk), :].astype(F32)
            factor = lax.rsqrt(jnp.mean(block * block, axis=-1, keepdims=True) + EPSILON)
            first = (4 * e + d) * tok + i * chunk
            normed_ref[pl.ds(pl.multiple_of(first, chunk), chunk), :] = (
                block * factor * attn_gain
            ).astype(BF16)
            return carry

        lax.fori_loop(0, tok // chunk, step, 0)

    keep_input.wait()
    norm(0, 0)
    for d in others:
        input_chips[d].wait_recv()
        input_pairs[d] = send(3 + d, inputs_all.at[0, d], inputs_all.at[1, d], sibling)
        norm(0, d)
    for d in range(4):
        input_pairs[d].wait_recv()
        norm(1, d)

    head_rows = w_head.at[:, rows, :]
    for d in range(4):
        if d:
            head_z[d].wait_recv()
        source = flip(plane, d)
        apart = xor4(chip, source)
        block = w_parts.at[source]

        @pl.when(apart == 0)
        def _(block=block):
            local(6, block, head_rows).start()

        @pl.when(apart != 0)
        def _(block=block, source=source, apart=apart):
            remote(9 + apart, block, head_rows, (2 * source + core, plane)).start()

    out_z = {
        d: send(12 + d, out_own, out_pair.at[0, :, at(plane, shard)], over_z[d]) for d in others
    }
    local(6, mine, head_rows).wait()
    for d in others:
        remote(9 + d, mine, head_rows, over_chips[d]).wait_recv()
    head_pair = send(16, w_head, w_sibling, sibling)
    down_z = {d: send(16 + d, down_block(flip(plane, d)), down_place, over_z[d]) for d in others}

    def project(which, target, flat):
        def step(t, carry):
            here = at(t, TILE)
            made = dot_nn(normed_ref[here, :], w_head[which])
            cosine, sine = cosine_ref[here, :], sine_ref[here, :]
            if flat:
                cosine = jnp.where(core == 0, cosine, 1.0)
                sine = jnp.where(core == 0, sine, 0.0)
            target[here, :] = rotated(made, cosine, sine).astype(BF16)
            return carry

        lax.fori_loop(0, seq // TILE, step, 0)

    mine_kv = kv_ref.at[core]
    project(1, mine_kv, True)
    kv_pair = [
        send(20 + e, mine_kv.at[pl.ds(e * half_seq, half_seq)],
             mine_kv.at[pl.ds((1 - e) * half_seq, half_seq)], sibling)
        for e in range(2)
    ]
    project(0, query_ref, False)
    for copy in kv_pair:
        copy.wait_recv()

    def attend_step(t, carry):
        here = at(t, TILE)
        scores = scores_of(
            query_ref[here, :], kv_ref[0], code_ref[here, :], low_code_ref[here, :], key_code_ref[...]
        )
        top = jnp.max(scores, axis=-1, keepdims=True)
        weights = jnp.exp(scores - top)
        total = jnp.sum(weights, axis=-1, keepdims=True)
        mixed = dot_nn(weights.astype(BF16), kv_ref[1])
        attended_ref[here, :] = (mixed / total).astype(BF16)
        log_total_ref[here, :] = top + jnp.log(total)
        return carry

    lax.fori_loop(0, seq // TILE, attend_step, 0)
    attended_pair = send(22, attended_ref.at[pl.ds(half_seq, half_seq)], attended_other, sibling)
    keep_out.wait()
    for d in others:
        out_z[d].wait_recv()
    out_sibling = send(23, out_pair.at[0], out_pair.at[1], sibling)
    attended_pair.wait_recv()
    out_sibling.wait_recv()

    def out_step(t, carry):
        here = at(t, TILE)
        terms = dot_nn(attended_ref[:half_seq, :], out_pair[0, :, here]) + dot_nn(
            attended_other[...], out_pair[1, :, here]
        )
        own_sum[:, here] = terms[:tok]
        for d in others:
            chip_send[d - 1, :, here] = terms[d * tok : (d + 1) * tok].astype(BF16)
        return carry

    lax.fori_loop(0, width // TILE, out_step, 0)
    branch = {
        d: send(23 + d, chip_send.at[d - 1], chip_recv.at[d - 1], over_chips[d]) for d in others
    }

    keep_down.wait()
    for d in others:
        down_z[d].wait_recv()
    upstream_z = {
        d: send(29 + d, upstream_hbm, upstream_all.at[d, 0], over_z[d]) for d in others
    }
    upstream_pair = {0: send(33, upstream_hbm, upstream_all.at[0, 1], sibling)}

    for d in others:
        branch[d].wait_recv()
    down_mine = down_rows.at[at(chip, part), :]
    down_chips = {d: send(26 + d, down_mine, down_mine, over_chips[d]) for d in others}
    mlp_gain = mlp_gain_ref[...]

    def mid_step(i, carry):
        here = at(i, chunk)
        mid = input_ref[here, :].astype(F32) + own_sum[here, :]
        for d in range(3):
            mid = mid + chip_recv[d, here, :].astype(F32)
        factor = lax.rsqrt(jnp.mean(mid * mid, axis=-1, keepdims=True) + EPSILON)
        mid_ref[here, :] = mid
        second_ref[here, :] = (mid * factor * mlp_gain).astype(BF16)
        return carry

    lax.fori_loop(0, tok // chunk, mid_step, 0)

    for d in others:
        upstream_z[d].wait_recv()
        upstream_pair[d] = send(33 + d, upstream_all.at[d, 0], upstream_all.at[d, 1], sibling)
    keep_upstream.wait()
    for d in range(4):
        upstream_pair[d].wait_recv()
        upstream_pair[d].wait_send()
        input_pairs[d].wait_send()
    head_pair.wait_recv()
    for copy in (head_pair, attended_pair, out_sibling, *kv_pair):
        copy.wait_send()
    for d in others:
        down_chips[d].wait_recv()
        for copies in (input_chips, head_z, out_z, down_z, branch, down_chips, upstream_z):
            copies[d].wait_send()
        remote(9 + d, mine, head_rows, over_chips[d]).wait_send()


def front_of(
    inputs, attn_gain, mlp_gain, cosine, sine, code, low_code, key_code,
    w_query, w_key, w_value, w_out, w_down, upstream,
):
    tok, width = inputs.shape
    seq = 8 * tok
    hidden = w_down.shape[0] // 8
    vmem = pl.BlockSpec(memory_space=pltpu.VMEM)
    hbm = pl.BlockSpec(memory_space=pl.ANY)
    return pl.pallas_call(
        front_kernel,
        in_specs=[vmem] * 8 + [hbm] * 6,
        out_specs=[vmem] * 8 + [hbm] + [vmem] + [hbm] * 2,
        out_shape=[
            jax.ShapeDtypeStruct((tok, width), BF16),
            jax.ShapeDtypeStruct((tok, width), F32),
            jax.ShapeDtypeStruct((seq, width), BF16),
            jax.ShapeDtypeStruct((seq, HD), BF16),
            jax.ShapeDtypeStruct((2, seq, HD), BF16),
            jax.ShapeDtypeStruct((seq, HD), BF16),
            jax.ShapeDtypeStruct((seq, 1), F32),
            jax.ShapeDtypeStruct((2, width, HD), BF16),
            jax.ShapeDtypeStruct((2, width, HD), BF16),
            jax.ShapeDtypeStruct((2, HD, width), BF16),
            jax.ShapeDtypeStruct((hidden, width), BF16),
            jax.ShapeDtypeStruct((4, 2, tok, width), BF16),
        ],
        scratch_shapes=[
            pltpu.VMEM((2, 4, tok, width), BF16),
            pltpu.VMEM((4, 2, width // 4, HD), BF16),
            pltpu.VMEM((4 * tok, HD), BF16),
            pltpu.VMEM((tok, width), F32),
            pltpu.VMEM((3, tok, width), BF16),
            pltpu.VMEM((3, tok, width), BF16),
            pltpu.SemaphoreType.DMA((7,)),
            pltpu.SemaphoreType.DMA((37,)),
            pltpu.SemaphoreType.DMA((37,)),
        ],
        compiler_params=pltpu.CompilerParams(
            collective_id=2, has_side_effects=True, vmem_limit_bytes=56 << 20
        ),
        cost_estimate=pl.CostEstimate(
            flops=2 * seq * width * 3 * HD + 4 * seq * seq * HD,
            bytes_accessed=20 * seq * width,
            transcendentals=seq * seq,
        ),
    )(
        inputs, attn_gain, mlp_gain, cosine, sine, code, low_code, key_code,
        w_query, w_key, w_value, w_out, w_down, upstream,
    )


def back_kernel(
    input_ref,
    mid_grad_ref,
    attn_gain_ref,
    mlp_gain_grad_ref,
    cosine_ref,
    sine_ref,
    code_ref,
    low_code_ref,
    key_code_ref,
    normed_ref,
    query_ref,
    kv_ref,
    attended_ref,
    log_total_ref,
    w_head,
    w_sibling,
    out_rows_ref,
    branch_hbm,
    gate_up_terms,
    gate_up_near,
    down_terms,
    grad_input_ref,
    gain_total_ref,
    grad_out_ref,
    head_in,
    gate_up_in,
    down_in,
    branch_all,
    d_attended,
    d_head,
    d_other,
    d_kv,
    d_kv_other,
    out_send,
    out_recv,
    head_terms,
    head_recv,
    own_sum,
    chip_send,
    chip_recv,
    gate_up_parts,
    gate_up_sum,
    down_parts,
    down_sum,
    down_planes,
    gains,
    gains_z,
    gains_ctx,
    local_sem,
    send_sem,
    recv_sem,
):
    tok, width = input_ref.shape
    seq = 8 * tok
    half_seq = 4 * tok
    share = out_send.shape[1]
    ctx, plane = lax.axis_index("ctx"), lax.axis_index("shard")
    chip, core = ctx // 2, ctx % 2
    other_core = 1 - core
    sibling = (2 * chip + other_core, plane)
    over_z = [(ctx, flip(plane, d)) for d in range(4)]
    over_chips = [(2 * flip(chip, d) + core, plane) for d in range(4)]
    over_chips_cross = [(2 * flip(chip, d) + other_core, plane) for d in range(4)]
    over_z_cross = [(2 * chip + other_core, flip(plane, d)) for d in range(4)]
    others = (1, 2, 3)

    def at(i, size):
        return pl.ds(pl.multiple_of(i * size, size), size)

    def remote(slot, source, target, device):
        return pltpu.make_async_remote_copy(
            src_ref=source,
            dst_ref=target,
            send_sem=send_sem.at[slot],
            recv_sem=recv_sem.at[slot],
            device_id=device,
            device_id_type=MESH,
        )

    def send(slot, source, target, device):
        copy = remote(slot, source, target, device)
        copy.start()
        return copy

    def local(slot, source, target):
        return pltpu.make_async_copy(source, target, local_sem.at[slot])

    loads = [
        local(0, branch_hbm, branch_all),
        local(1, gate_up_terms.at[0], gate_up_parts.at[0]),
        local(2, gate_up_near, gate_up_parts.at[pl.ds(1, 2)]),
        local(3, down_terms.at[:, chip], down_parts.at[0]),
    ]
    for load in loads:
        load.start()

    barrier = pltpu.get_barrier_semaphore()
    partners = (
        over_z[1:] + over_z_cross + over_chips[1:] + over_chips_cross[1:]
    )
    for partner in partners:
        pl.semaphore_signal(barrier, inc=1, device_id=partner, device_id_type=MESH)
    pl.semaphore_wait(barrier, len(partners))

    gate_up_far = send(0, gate_up_terms.at[3], gate_up_parts.at[3], over_chips[3])
    down_chips = {
        d: send(d, down_terms.at[:, flip(chip, d)], down_parts.at[d], over_chips[d])
        for d in others
    }

    loads[0].wait()

    def out_step(t, carry):
        here = at(t, TILE)
        made = dot_tn(attended_ref[...], branch_all[:, here])
        out_send[:, :, here] = made.reshape(4, share, TILE).astype(BF16)
        return carry

    lax.fori_loop(0, width // TILE, out_step, 0)
    out_z = {
        d: send(3 + d, out_send.at[flip(plane, d)], out_recv.at[d - 1], over_z[d]) for d in others
    }

    def attended_step(t, carry):
        here = at(t, TILE)
        d_attended[here, :] = dot_nt(branch_all[here, :], out_rows_ref[...]).astype(BF16)
        return carry

    lax.fori_loop(0, seq // TILE, attended_step, 0)
    d_kv[...] = jnp.zeros_like(d_kv)

    def attend_step(t, carry):
        here = at(t, TILE)
        query, outgrad = query_ref[here, :], d_attended[here, :]
        scores = scores_of(
            query, kv_ref[0], code_ref[here, :], low_code_ref[here, :], key_code_ref[...]
        )
        probs = jnp.exp(scores - log_total_ref[here, :])
        prob_grad = dot_nt(outgrad, kv_ref[1])
        delta = jnp.sum(probs * prob_grad, axis=-1, keepdims=True)
        score_grad = (probs * (prob_grad - delta)).astype(BF16)
        d_query = dot_nn(score_grad, kv_ref[0]) * SCORE_SCALE
        d_head[here, :HD] = rotated(d_query, cosine_ref[here, :], -sine_ref[here, :]).astype(BF16)
        d_kv[0] += dot_tn(score_grad, query)
        d_kv[1] += dot_tn(probs.astype(BF16), outgrad)
        return carry

    lax.fori_loop(0, seq // TILE, attend_step, 0)

    give = d_kv.at[other_core]
    kv_pair = [
        send(
            7 + e,
            give.at[pl.ds(e * half_seq, half_seq)],
            d_kv_other.at[pl.ds((1 - e) * half_seq, half_seq)],
            sibling,
        )
        for e in range(2)
    ]
    for copy in kv_pair:
        copy.wait_recv()

    def kv_step(t, carry):
        here = at(t, TILE)
        total = d_kv[core, here, :] + d_kv_other[here, :]
        total = total * jnp.where(core == 0, SCORE_SCALE, 1.0)
        cosine = jnp.where(core == 0, cosine_ref[here, :], 1.0)
        sine = jnp.where(core == 0, sine_ref[here, :], 0.0)
        d_head[here, HD:] = rotated(total, cosine, -sine).astype(BF16)
        return carry

    lax.fori_loop(0, seq // TILE, kv_step, 0)
    head_pair = send(9, d_head.at[pl.ds(half_seq, half_seq)], d_other, sibling)

    def head_step(t, carry):
        made = dot_tn(normed_ref[:, at(t, TILE)], d_head[...])
        head_terms[:, t] = made.reshape(4, share, 2 * HD).astype(BF16)
        return carry

    lax.fori_loop(0, width // TILE, head_step, 0)
    head_z = {
        d: send(9 + d, head_terms.at[flip(plane, d)], head_recv.at[d - 1], over_z[d])
        for d in others
    }

    head_pair.wait_recv()

    def normed_step(t, carry):
        here = at(t, TILE)
        made = (
            dot_nt(d_head[:half_seq, :HD], w_head[0, here, :])
            + dot_nt(d_head[:half_seq, HD:], w_head[1, here, :])
            + dot_nt(d_other[:, :HD], w_sibling[0, here, :])
            + dot_nt(d_other[:, HD:], w_sibling[1, here, :])
        )
        own_sum[:, here] = made[:tok]
        for d in others:
            chip_send[d - 1, :, here] = made[d * tok : (d + 1) * tok].astype(BF16)
        return carry

    lax.fori_loop(0, width // TILE, normed_step, 0)
    normed_chips = {
        d: send(12 + d, chip_send.at[d - 1], chip_recv.at[d - 1], over_chips[d]) for d in others
    }

    loads[3].wait()
    for d in others:
        down_chips[d].wait_recv()

    def down_step(p, carry):
        total = down_parts[0, p].astype(F32)
        for d in others:
            total = total + down_parts[d, p].astype(F32)
        down_sum[p] = total.astype(BF16)
        return carry

    lax.fori_loop(0, 4, down_step, 0)
    down_z = {
        d: send(15 + d, down_sum.at[flip(plane, d)], down_planes.at[plane], over_z[d])
        for d in others
    }
    keep_down = local(3, down_sum.at[plane], down_planes.at[plane])
    keep_down.start()

    loads[1].wait()
    loads[2].wait()
    gate_up_far.wait_recv()

    def gate_up_step(i, carry):
        here = at(i, share)
        total = gate_up_parts[0, here, :].astype(F32)
        for d in others:
            total = total + gate_up_parts[d, here, :].astype(F32)
        gate_up_sum[i // 4, i % 4] = total.astype(BF16)
        return carry

    lax.fori_loop(0, 8, gate_up_step, 0)
    place = gate_up_in.at[plane, core]
    gate_up_z = {
        d: send(18 + d, gate_up_sum.at[core, flip(plane, d)], place, over_z[d]) for d in others
    }
    gate_up_cross = {
        d: send(22 + d, gate_up_sum.at[other_core, flip(plane, d)], place, over_z_cross[d])
        for d in range(4)
    }
    keep_gate_up = local(1, gate_up_sum.at[core, plane], place)
    keep_gate_up.start()

    for d in others:
        normed_chips[d].wait_recv()
    chunk = 32
    gain = attn_gain_ref[...]

    def input_step(i, carry):
        here = at(i, chunk)
        grad = own_sum[here, :]
        for d in range(3):
            grad = grad + chip_recv[d, here, :].astype(F32)
        block = input_ref[here, :].astype(F32)
        factor = lax.rsqrt(jnp.mean(block * block, axis=-1, keepdims=True) + EPSILON)
        scaled = grad * gain
        grad_input_ref[here, :] = (
            mid_grad_ref[here, :]
            + factor * scaled
            - block * (factor * factor * factor * jnp.mean(scaled * block, axis=-1, keepdims=True))
        ).astype(BF16)
        return carry + jnp.sum(grad * block * factor, axis=0, keepdims=True)

    gain_grad = lax.fori_loop(0, tok // chunk, input_step, jnp.zeros((1, width), F32))
    gains[...] = jnp.concatenate(
        [gain_grad, mlp_gain_grad_ref[...], jnp.zeros((6, width), F32)], axis=0
    )
    gains_planes = {d: send(25 + d, gains, gains_z.at[d - 1], over_z[d]) for d in others}

    for d in others:
        out_z[d].wait_recv()
    total = out_send[plane].astype(F32)
    for d in range(3):
        total = total + out_recv[d].astype(F32)
    grad_out_ref[...] = total

    for d in others:
        head_z[d].wait_recv()

    def head_sum(i, carry):
        total = head_terms[plane, i].astype(F32)
        for d in range(3):
            total = total + head_recv[d, i].astype(F32)
        head_terms[plane, i] = total.astype(BF16)
        return carry

    lax.fori_loop(0, 8, head_sum, 0)
    head_place = head_in.at[ctx]
    head_chips = {
        d: send(28 + d, head_terms.at[plane, 2 * flip(chip, d) + core], head_place, over_chips[d])
        for d in others
    }
    head_cross = {
        d: send(
            32 + d, head_terms.at[plane, 2 * flip(chip, d) + other_core], head_place,
            over_chips_cross[d],
        )
        for d in range(4)
    }
    keep_head = local(0, head_terms.at[plane, ctx], head_place)
    keep_head.start()

    for d in others:
        gains_planes[d].wait_recv()
        gains_planes[d].wait_send()
    gains[...] = gains[...] + gains_z[0] + gains_z[1] + gains_z[2]
    gains_chips = {
        d: send(35 + d, gains, gains_ctx.at[0, d], over_chips[d]) for d in others
    }
    gains_cross = {
        d: send(39 + d, gains, gains_ctx.at[1, d], over_chips_cross[d]) for d in range(4)
    }

    keep_down.wait()
    down_place = down_in.at[chip]
    for d in range(4):
        if d:
            down_z[d].wait_recv()
        source = flip(plane, d)
        apart = xor4(chip, source)
        block = down_planes.at[source]

        @pl.when(apart == 0)
        def _(block=block):
            local(4, block, down_place).start()

        @pl.when(apart != 0)
        def _(block=block, source=source, apart=apart):
            remote(42 + apart, block, down_place, (2 * source + core, plane)).start()

    for d in others:
        gains_chips[d].wait_recv()
    for d in range(4):
        gains_cross[d].wait_recv()
    total = gains[...] + gains_ctx[1, 0]
    for d in others:
        total = total + gains_ctx[0, d] + gains_ctx[1, d]
    gain_total_ref[...] = total

    local(4, down_sum.at[plane], down_place).wait()
    keep_gate_up.wait()
    keep_head.wait()
    for d in others:
        remote(42 + d, down_sum.at[plane], down_place, over_chips[d]).wait()
        gate_up_z[d].wait_recv()
        head_chips[d].wait_recv()
        for copies in (
            down_chips, out_z, head_z, normed_chips, down_z, gate_up_z, head_chips, gains_chips
        ):
            copies[d].wait_send()
    for d in range(4):
        for copies in (gate_up_cross, head_cross):
            copies[d].wait()
        gains_cross[d].wait_send()
    for copy in (gate_up_far, head_pair, *kv_pair):
        copy.wait_send()


def back_of(*operands):
    inputs, query, out_rows = operands[0], operands[10], operands[16]
    tok, width = inputs.shape
    seq = query.shape[0]
    hidden = operands[20].shape[0] * operands[20].shape[1] * operands[20].shape[2]
    share = HD // 4
    vmem = pl.BlockSpec(memory_space=pltpu.VMEM)
    hbm = pl.BlockSpec(memory_space=pl.ANY)
    return pl.pallas_call(
        back_kernel,
        in_specs=[vmem] * 17 + [hbm] * 4,
        out_specs=[vmem] * 6,
        out_shape=[
            jax.ShapeDtypeStruct((tok, width), BF16),
            jax.ShapeDtypeStruct((8, width), F32),
            jax.ShapeDtypeStruct((share, width), F32),
            jax.ShapeDtypeStruct((8, share, 2 * HD), BF16),
            jax.ShapeDtypeStruct((4, 2, share, 2 * hidden), BF16),
            jax.ShapeDtypeStruct((4, share, width), BF16),
        ],
        scratch_shapes=[
            pltpu.VMEM((seq, width), BF16),
            pltpu.VMEM((seq, HD), BF16),
            pltpu.VMEM((seq, 2 * HD), BF16),
            pltpu.VMEM((4 * tok, 2 * HD), BF16),
            pltpu.VMEM((2, seq, HD), F32),
            pltpu.VMEM((seq, HD), F32),
            pltpu.VMEM((4, share, width), BF16),
            pltpu.VMEM((3, share, width), BF16),
            pltpu.VMEM((4, 8, share, 2 * HD), BF16),
            pltpu.VMEM((3, 8, share, 2 * HD), BF16),
            pltpu.VMEM((tok, width), F32),
            pltpu.VMEM((3, tok, width), BF16),
            pltpu.VMEM((3, tok, width), BF16),
            pltpu.VMEM((4, 2 * TILE, 2 * hidden), BF16),
            pltpu.VMEM((2, 4, share, 2 * hidden), BF16),
            pltpu.VMEM((4, 4, share, width), BF16),
            pltpu.VMEM((4, share, width), BF16),
            pltpu.VMEM((4, share, width), BF16),
            pltpu.VMEM((8, width), F32),
            pltpu.VMEM((3, 8, width), F32),
            pltpu.VMEM((2, 4, 8, width), F32),
            pltpu.SemaphoreType.DMA((5,)),
            pltpu.SemaphoreType.DMA((46,)),
            pltpu.SemaphoreType.DMA((46,)),
        ],
        compiler_params=pltpu.CompilerParams(
            collective_id=3, has_side_effects=True, vmem_limit_bytes=60 << 20
        ),
        cost_estimate=pl.CostEstimate(
            flops=2 * seq * width * 6 * HD + 10 * seq * seq * HD,
            bytes_accessed=20 * seq * width,
            transcendentals=seq * seq,
        ),
    )(*operands)


def on_device_by_head(
    layer_input,
    w_query,
    w_key,
    w_value,
    w_out,
    w_gate,
    w_up,
    w_down,
    attn_gain,
    mlp_gain,
    block_pairs,
    doc_ids,
    cotangent,
):
    tok_rows, width = layer_input.shape[1:]
    planes = lax.axis_size("shard")
    ctx_count = lax.axis_size("ctx")
    chips = ctx_count // 2
    ctx, plane = lax.axis_index("ctx"), lax.axis_index("shard")
    chip, core = ctx // 2, ctx % 2
    seq_rows = tok_rows * ctx_count
    own_share = width // (planes * ctx_count)

    inputs_low = layer_input[0]
    pairs, documents = block_pairs[0], doc_ids[0]
    order = jnp.stack([(chip ^ d) * 2 + (core ^ e) for e in range(2) for d in range(chips)])
    rows = (order[:, None] * tok_rows + jnp.arange(tok_rows, dtype=jnp.int32)[None, :]).reshape(-1)
    positions = position_of(rows, pairs, tok_rows, 2 * ctx_count).astype(jnp.int32)
    span = 2 * seq_rows
    doc_first = jnp.take(documents, positions).astype(jnp.int32) * span
    code = doc_first + positions
    low_code = jnp.maximum(doc_first, code - (WINDOW - 1))
    code_column, low_column, code_row = code[:, None], low_code[:, None], code[None, :]
    cosine, sine = rope_tables(positions, HD)

    upstream_low = cotangent[0]
    (
        normed_two,
        mid,
        normed_all,
        query,
        key_value,
        attended,
        log_total,
        w_head,
        w_sibling,
        out_pair,
        down_rows,
        upstream_group,
    ) = front_of(
        inputs_low,
        attn_gain[None],
        mlp_gain[None],
        cosine,
        sine,
        code_column,
        low_column,
        code_row,
        w_query,
        w_key,
        w_value,
        w_out,
        w_down,
        upstream_low,
    )
    output, mid_grad, mlp_gain_grad, branch_all, gate_up_terms, gate_up_near, down_terms = mlp_of(
        normed_two,
        mid,
        upstream_low,
        mlp_gain[None],
        upstream_group.reshape(-1, width),
        w_gate,
        w_up,
        down_rows,
    )
    grad_input, gain_total, grad_out, head_in, gate_up_in, down_in = back_of(
        inputs_low,
        mid_grad,
        attn_gain[None],
        mlp_gain_grad,
        cosine,
        sine,
        code_column,
        low_column,
        code_row,
        normed_all,
        query,
        key_value,
        attended,
        log_total,
        w_head,
        w_sibling,
        out_pair[0],
        branch_all.reshape(seq_rows, width),
        gate_up_terms,
        gate_up_near,
        down_terms.reshape(planes, chips, -1, width),
    )
    hidden = gate_up_in.shape[-1] // 2
    gate_up = gate_up_in.astype(F32)
    columns = lambda parts: jnp.concatenate(parts, axis=1)
    grad_gate = columns([gate_up[p, e, :, :hidden] for p in range(planes) for e in range(2)])
    grad_up = columns([gate_up[p, e, :, hidden:] for p in range(planes) for e in range(2)])
    head = head_in.astype(F32)
    grad_query = columns([head[i, :, :HD] for i in range(ctx_count)])
    grad_key = columns([head[i, :, HD:] for i in range(0, ctx_count, 2)])
    grad_value = columns([head[i, :, HD:] for i in range(1, ctx_count, 2)])
    grad_down = down_in.astype(F32).reshape(-1, width)
    gains = lax.dynamic_slice(gain_total, (0, own_share * (planes * ctx + plane)), (2, own_share))
    return (
        output[None],
        grad_input[None],
        grad_query,
        grad_key,
        grad_value,
        grad_out,
        grad_gate,
        grad_up,
        grad_down,
        gains[0],
        gains[1],
    )


def plan_of(mesh):
    chips, planes = mesh.shape["ctx"] // 2, mesh.shape["shard"]
    if mesh.shape["ctx"] == HQ and HQ == 2 * HK and chips == planes == HK:
        return on_device_by_head
    return on_device


def solution(mesh):
    placed = (
        P("shard", "ctx", None),
        P(None, "shard"),
        P(None, "shard"),
        P(None, "shard"),
        P(None, "shard"),
        P(None, "shard"),
        P(None, "shard"),
        P(None, "shard"),
        P(),
        P(),
        P("shard", None),
        P("shard", None),
        P("shard", "ctx", None),
    )
    return jax.shard_map(
        plan_of(mesh),
        mesh=mesh,
        in_specs=placed,
        out_specs=(
            P("shard", "ctx", None),
            P("shard", "ctx", None),
            P(("ctx", "shard"), None),
            P(("ctx", "shard"), None),
            P(("ctx", "shard"), None),
            P(("ctx", "shard"), None),
            P(("ctx", "shard"), None),
            P(("ctx", "shard"), None),
            P(("ctx", "shard"), None),
            P(("ctx", "shard")),
            P(("ctx", "shard")),
        ),
        check_vma=False,
    )
```

```python
import math

import jax
import jax.numpy as jnp
from jax import lax
from jax.experimental import pallas as pl
from jax.experimental.pallas import tpu as pltpu
from jax.sharding import PartitionSpec as P

HQ = 8
HK = 4
HD = 256
WINDOW = 1024


EPSILON = 1e-06
SCORE_SCALE = 0.0625
MASKED = -1e30
ROPE_BASE = 1000042.0


def position_of(rows, pairs, per_device, blocks_total):
    device = rows // per_device
    within = rows % per_device
    half = per_device // 2
    chosen = jnp.take(pairs, device)
    first = chosen * half + within
    second = (blocks_total - 1 - chosen) * half + within - half
    return jnp.where(within < half, first, second)


def rope_tables(positions, head):
    half = head // 2
    freq = ROPE_BASE ** (-(jnp.arange(half, dtype=jnp.float32) * 2.0) / head)
    angle = positions.astype(jnp.float32)[:, None] * freq[None, :]
    return (jnp.cos(angle), jnp.sin(angle))


def rotate(values, cosine, sine):
    half = values.shape[-1] // 2
    first = values[..., :half]
    second = values[..., half:]
    cosine = cosine[:, None, :]
    sine = sine[:, None, :]
    return jnp.concatenate(
        [first * cosine - second * sine, second * cosine + first * sine], axis=-1
    )


def rotate_back(grads, cosine, sine):
    half = grads.shape[-1] // 2
    first = grads[..., :half]
    second = grads[..., half:]
    cosine = cosine[:, None, :]
    sine = sine[:, None, :]
    return jnp.concatenate(
        [first * cosine + second * sine, second * cosine - first * sine], axis=-1
    )


def visible(query_pos, query_doc, key_pos, key_doc):
    distance = query_pos[:, None] - key_pos[None, :]
    return (query_doc[:, None] == key_doc[None, :]) & (distance >= 0) & (distance < WINDOW)


def write_columns(left, piece):
    made = jnp.dot(left, piece, preferred_element_type=jnp.float32)
    return made


def contract_full(grads, weight):
    return lax.dot_general(
        grads, weight, (((1,), (1,)), ((), ())), preferred_element_type=jnp.float32
    )


def alternate(parts, shard_count, rows):
    return jnp.concatenate([part.reshape(rows, shard_count, -1) for part in parts], axis=2).reshape(
        rows, -1
    )


def outer_sum(left, right):
    return lax.dot_general(
        left, right, (((0,), (0,)), ((), ())), preferred_element_type=jnp.float32
    )


def term_rows(lefts, rights, gain_block, count):
    normed_all, attended_all, second_all, act_all = lefts
    query_g, key_g, value_g, branch_g, gate_g, up_g, upstream_g = rights
    down_part = outer_sum(act_all, upstream_g).reshape(count, -1)
    return jnp.concatenate(
        [
            outer_sum(normed_all, query_g),
            outer_sum(normed_all, key_g),
            outer_sum(normed_all, value_g),
            outer_sum(attended_all, branch_g),
            outer_sum(second_all, gate_g),
            outer_sum(second_all, up_g),
            down_part,
            gain_block,
        ],
        axis=1,
    )


def deal_columns(values, ctx_count, shard_count):
    rows = values.shape[0]
    return (
        values.reshape(rows, ctx_count, shard_count, -1)
        .transpose(0, 2, 1, 3)
        .reshape(rows, shard_count, -1)
    )


def on_device(
    layer_input,
    w_query,
    w_key,
    w_value,
    w_out,
    w_gate,
    w_up,
    w_down,
    attn_gain,
    mlp_gain,
    block_pairs,
    doc_ids,
    cotangent,
):
    tok_rows = layer_input.shape[1]
    model_width = layer_input.shape[2]
    shard_count = lax.axis_size("shard")
    ctx_count = lax.axis_size("ctx")
    device_count = lax.axis_size(("ctx", "shard"))
    group_size = HQ // HK
    blocks_total = 2 * ctx_count
    pairs = block_pairs[0]
    documents = doc_ids[0]
    own_rows = lax.axis_index("ctx") * tok_rows + jnp.arange(tok_rows, dtype=jnp.int32)
    own_pos = position_of(own_rows, pairs, tok_rows, blocks_total)
    own_doc = jnp.take(documents, own_pos)
    cosine, sine = rope_tables(own_pos, HD)
    stack_qkv = jnp.concatenate([w_query, w_key, w_value], axis=1)
    stack_mlp = jnp.concatenate([w_gate, w_up], axis=1)
    per_query = w_query.shape[1]
    per_key = w_key.shape[1]
    per_hidden = w_gate.shape[1]
    hidden_width = w_down.shape[0]
    inputs = layer_input.reshape(tok_rows, model_width).astype(jnp.float32)
    factor_one = lax.rsqrt(jnp.mean(inputs * inputs, axis=-1, keepdims=True) + EPSILON)
    normed = (inputs * factor_one * attn_gain).astype(jnp.bfloat16)
    projected = write_columns(normed, lax.all_gather(stack_qkv, "shard", axis=1, tiled=True))
    projected = projected.reshape(tok_rows, shard_count, -1)
    query_lin = projected[:, :, :per_query].reshape(tok_rows, HQ, HD)
    key_lin = projected[:, :, per_query : per_query + per_key].reshape(tok_rows, HK, HD)
    value_lin = projected[:, :, per_query + per_key :].reshape(tok_rows, HK * HD)
    query_rot = (
        rotate(query_lin, cosine, sine).astype(jnp.bfloat16).reshape(tok_rows, HK, group_size, HD)
    )
    key_rot = rotate(key_lin, cosine, sine).astype(jnp.bfloat16).reshape(tok_rows, HK * HD)
    value_low = value_lin.astype(jnp.bfloat16)

    def key_mask(first_row, count):
        key_pos = position_of(
            first_row + jnp.arange(count, dtype=jnp.int32), pairs, tok_rows, blocks_total
        )
        return visible(own_pos, own_doc, key_pos, jnp.take(documents, key_pos))[:, None, None, :]

    start_state = (
        jnp.full((tok_rows, HK, group_size), MASKED, jnp.float32),
        jnp.zeros((tok_rows, HK, group_size), jnp.float32),
        jnp.zeros((tok_rows, HK, group_size, HD), jnp.float32),
    )
    keys = lax.all_gather(key_rot, "ctx", axis=0, tiled=True)
    values = lax.all_gather(value_low, "ctx", axis=0, tiled=True)
    count = keys.shape[0]
    step = math.gcd(count, 4 * tok_rows)
    keys = keys.reshape(count // step, step, HK, HD)
    values = values.reshape(count // step, step, HK, HD)

    def attend_step(i, running):
        top, total, accum = running
        mask = key_mask(i * step, step)
        scores = (
            jnp.einsum("tkgd,skd->tkgs", query_rot, keys[i], preferred_element_type=jnp.float32)
            * SCORE_SCALE
        )
        scores = jnp.where(mask, scores, MASKED)
        new_top = jnp.maximum(top, jnp.max(scores, axis=-1))
        weights = jnp.where(mask, jnp.exp(scores - new_top[..., None]), 0.0)
        shrink = jnp.exp(top - new_top)
        total = total * shrink + jnp.sum(weights, axis=-1)
        accum = accum * shrink[..., None] + jnp.einsum(
            "tkgs,skd->tkgd",
            weights.astype(jnp.bfloat16),
            values[i],
            preferred_element_type=jnp.float32,
        )
        return (new_top, total, accum)

    top, total, accum = lax.fori_loop(0, count // step, attend_step, start_state)
    log_total = top + jnp.log(total)
    attended_full = accum / total[..., None]
    attended = attended_full.astype(jnp.bfloat16).reshape(tok_rows, HQ * HD)
    branch_one = write_columns(attended, lax.all_gather(w_out, "shard", axis=1, tiled=True))
    mid = inputs + branch_one
    factor_two = lax.rsqrt(jnp.mean(mid * mid, axis=-1, keepdims=True) + EPSILON)
    normed_two = (mid * factor_two * mlp_gain).astype(jnp.bfloat16)
    gate_up = write_columns(normed_two, lax.all_gather(stack_mlp, "shard", axis=1, tiled=True))
    gate_up = gate_up.reshape(tok_rows, shard_count, -1)
    gate = gate_up[:, :, :per_hidden].reshape(tok_rows, hidden_width)
    up_lin = gate_up[:, :, per_hidden:].reshape(tok_rows, hidden_width)
    sigma = jax.nn.sigmoid(gate)
    swish = gate * sigma
    act = (swish * up_lin).astype(jnp.bfloat16)
    branch_two = write_columns(act, lax.all_gather(w_down, "shard", axis=1, tiled=True))
    output = (mid + branch_two).astype(jnp.bfloat16).reshape(1, tok_rows, model_width)
    full_qkv, full_out, full_mlp, full_down = (
        lax.all_gather(stack_qkv, "shard", axis=1, tiled=True),
        lax.all_gather(w_out, "shard", axis=1, tiled=True),
        lax.all_gather(stack_mlp, "shard", axis=1, tiled=True),
        lax.all_gather(w_down, "shard", axis=1, tiled=True),
    )
    upstream_low = cotangent.reshape(tok_rows, model_width)
    upstream = upstream_low.astype(jnp.float32)
    act_grad = contract_full(upstream_low, full_down)
    gate_grad = (act_grad * up_lin * (sigma * (1.0 + gate * (1.0 - sigma)))).astype(jnp.bfloat16)
    up_grad = (act_grad * swish).astype(jnp.bfloat16)
    stacked_mlp_grad = alternate((gate_grad, up_grad), shard_count, tok_rows)
    norm_two_grad = contract_full(stacked_mlp_grad, full_mlp)
    mlp_gain_term = jnp.sum(norm_two_grad * mid * factor_two, axis=0)
    scaled_two = norm_two_grad * mlp_gain
    mid_grad = (
        upstream
        + factor_two * scaled_two
        - mid * factor_two**3 * jnp.mean(scaled_two * mid, axis=-1, keepdims=True)
    )
    branch_grad = mid_grad.astype(jnp.bfloat16)
    attended_grad = contract_full(branch_grad, full_out)
    attended_low = attended_grad.astype(jnp.bfloat16).reshape(tok_rows, HK, group_size, HD)
    delta = jnp.sum(attended_low.astype(jnp.float32) * attended_full, axis=-1)

    def query_grads(carry, piece):
        keys, values = piece
        count = keys.shape[0]
        step = math.gcd(count, 4 * tok_rows)
        keys = keys.reshape(count // step, step, HK, HD)
        values = values.reshape(count // step, step, HK, HD)

        def query_step(i, query_sum):
            mask = key_mask(i * step, step)
            scores = (
                jnp.einsum("tkgd,skd->tkgs", query_rot, keys[i], preferred_element_type=jnp.float32)
                * SCORE_SCALE
            )
            probs = jnp.where(mask, jnp.exp(scores - log_total[..., None]), 0.0)
            prob_grad = jnp.einsum(
                "tkgd,skd->tkgs", attended_low, values[i], preferred_element_type=jnp.float32
            )
            score_grad = (probs * (prob_grad - delta[..., None])).astype(jnp.bfloat16)
            return query_sum + jnp.einsum(
                "tkgs,skd->tkgd", score_grad, keys[i], preferred_element_type=jnp.float32
            )

        return lax.fori_loop(0, count // step, query_step, carry)

    query_sum = query_grads(
        jnp.zeros((tok_rows, HK, group_size, HD), jnp.float32),
        (
            lax.all_gather(key_rot, "ctx", axis=0, tiled=True),
            lax.all_gather(value_low, "ctx", axis=0, tiled=True),
        ),
    )
    all_log_total, all_delta = (
        lax.all_gather(log_total, "ctx", axis=0, tiled=True),
        lax.all_gather(delta, "ctx", axis=0, tiled=True),
    )
    key_three = key_rot.reshape(tok_rows, HK, HD)
    value_three = value_low.reshape(tok_rows, HK, HD)

    def key_grads(carry, piece):
        queries, outgrads = piece
        count = queries.shape[0]
        step = math.gcd(count, 4 * tok_rows)
        queries = queries.reshape(count // step, step, HK, group_size, HD)
        outgrads = outgrads.reshape(count // step, step, HK, group_size, HD)

        def key_step(i, running):
            key_sum, value_sum = running
            first_row = i * step
            query_pos = position_of(
                first_row + jnp.arange(step, dtype=jnp.int32), pairs, tok_rows, blocks_total
            )
            mask = visible(query_pos, jnp.take(documents, query_pos), own_pos, own_doc)[
                :, None, None, :
            ]
            lse_part = lax.dynamic_slice_in_dim(all_log_total, first_row, step, 0)
            delta_part = lax.dynamic_slice_in_dim(all_delta, first_row, step, 0)
            scores = (
                jnp.einsum(
                    "skgd,tkd->skgt", queries[i], key_three, preferred_element_type=jnp.float32
                )
                * SCORE_SCALE
            )
            probs = jnp.where(mask, jnp.exp(scores - lse_part[..., None]), 0.0)
            prob_grad = jnp.einsum(
                "skgd,tkd->skgt", outgrads[i], value_three, preferred_element_type=jnp.float32
            )
            score_grad = (probs * (prob_grad - delta_part[..., None])).astype(jnp.bfloat16)
            value_sum = value_sum + jnp.einsum(
                "skgt,skgd->tkd",
                probs.astype(jnp.bfloat16),
                outgrads[i],
                preferred_element_type=jnp.float32,
            )
            key_sum = key_sum + jnp.einsum(
                "skgt,skgd->tkd", score_grad, queries[i], preferred_element_type=jnp.float32
            )
            return (key_sum, value_sum)

        return lax.fori_loop(0, count // step, key_step, carry)

    key_sum, value_sum = key_grads(
        (jnp.zeros((tok_rows, HK, HD), jnp.float32), jnp.zeros((tok_rows, HK, HD), jnp.float32)),
        (
            lax.all_gather(query_rot.reshape(tok_rows, HQ * HD), "ctx", axis=0, tiled=True),
            lax.all_gather(attended_low.reshape(tok_rows, HQ * HD), "ctx", axis=0, tiled=True),
        ),
    )
    query_grad = (
        rotate_back(query_sum.reshape(tok_rows, HQ, HD) * SCORE_SCALE, cosine, sine)
        .astype(jnp.bfloat16)
        .reshape(tok_rows, HQ * HD)
    )
    key_grad = (
        rotate_back(key_sum * SCORE_SCALE, cosine, sine)
        .astype(jnp.bfloat16)
        .reshape(tok_rows, HK * HD)
    )
    value_grad = value_sum.astype(jnp.bfloat16).reshape(tok_rows, HK * HD)
    stacked_qkv_grad = alternate((query_grad, key_grad, value_grad), shard_count, tok_rows)
    normed_grad = contract_full(stacked_qkv_grad, full_qkv)
    attn_gain_term = jnp.sum(normed_grad * inputs * factor_one, axis=0)
    scaled_one = normed_grad * attn_gain
    input_grad = (
        mid_grad
        + factor_one * scaled_one
        - inputs * factor_one**3 * jnp.mean(scaled_one * inputs, axis=-1, keepdims=True)
    )
    grad_input = input_grad.astype(jnp.bfloat16).reshape(1, tok_rows, model_width)
    ratio = hidden_width // model_width
    own_share = model_width // device_count
    rights = (query_grad, key_grad, value_grad, branch_grad, gate_grad, up_grad, upstream_low)
    group_rights = (
        lax.all_gather(rights[0], "shard", axis=0, tiled=True),
        lax.all_gather(rights[1], "shard", axis=0, tiled=True),
        lax.all_gather(rights[2], "shard", axis=0, tiled=True),
        lax.all_gather(rights[3], "shard", axis=0, tiled=True),
        lax.all_gather(rights[4], "shard", axis=0, tiled=True),
        lax.all_gather(rights[5], "shard", axis=0, tiled=True),
        lax.all_gather(rights[6], "shard", axis=0, tiled=True),
    )
    dealt = (
        lax.all_to_all(
            deal_columns(normed, ctx_count, shard_count),
            "shard",
            split_axis=1,
            concat_axis=0,
            tiled=True,
        ),
        lax.all_to_all(
            deal_columns(attended, ctx_count, shard_count),
            "shard",
            split_axis=1,
            concat_axis=0,
            tiled=True,
        ),
        lax.all_to_all(
            deal_columns(normed_two, ctx_count, shard_count),
            "shard",
            split_axis=1,
            concat_axis=0,
            tiled=True,
        ),
        lax.all_to_all(
            deal_columns(act, ctx_count, shard_count),
            "shard",
            split_axis=1,
            concat_axis=0,
            tiled=True,
        ),
    )
    group_lefts = tuple((part.reshape(part.shape[0], -1) for part in dealt))
    gain_pair = lax.psum(jnp.stack([attn_gain_term, mlp_gain_term]), "shard")
    gain_mine = lax.dynamic_index_in_dim(
        gain_pair.reshape(2, ctx_count, shard_count, own_share),
        lax.axis_index("shard"),
        2,
        keepdims=False,
    ).reshape(2, ctx_count * own_share)
    gain_block = jnp.concatenate(
        [gain_mine.T, jnp.zeros((ctx_count * own_share, 126), jnp.float32)], axis=1
    )
    summed = lax.psum_scatter(
        term_rows(group_lefts, group_rights, gain_block, own_share * lax.axis_size("ctx")).astype(
            jnp.bfloat16
        ),
        "ctx",
        scatter_dimension=0,
        tiled=True,
    ).astype(jnp.float32)
    edge_one = HQ * HD
    edge_two = edge_one + HK * HD
    edge_three = edge_two + HK * HD
    edge_four = edge_three + model_width
    edge_five = edge_four + hidden_width
    edge_six = edge_five + hidden_width
    edge_seven = edge_six + ratio * model_width
    grad_query = summed[:, :edge_one]
    grad_key = summed[:, edge_one:edge_two]
    grad_value = summed[:, edge_two:edge_three]
    grad_out = summed[:, edge_three:edge_four]
    grad_gate = summed[:, edge_four:edge_five]
    grad_up = summed[:, edge_five:edge_six]
    grad_down = summed[:, edge_six:edge_seven].reshape(own_share * ratio, model_width)
    grad_attn_gain = summed[:, edge_seven]
    grad_mlp_gain = summed[:, edge_seven + 1]
    return (
        output,
        grad_input,
        grad_query,
        grad_key,
        grad_value,
        grad_out,
        grad_gate,
        grad_up,
        grad_down,
        grad_attn_gain,
        grad_mlp_gain,
    )


DOCS = 4
BF16 = jnp.bfloat16
F32 = jnp.float32
VISIBLE_ROWS = 256


def dot_nn(a, b):
    return jnp.dot(a, b, preferred_element_type=F32)


def dot_nt(a, b):
    return lax.dot_general(a, b, (((1,), (1,)), ((), ())), preferred_element_type=F32)


def dot_tn(a, b):
    return lax.dot_general(a, b, (((0,), (0,)), ((), ())), preferred_element_type=F32)


def scores_of(query, key, code, low_code, key_code):
    scores = dot_nt(query, key) * SCORE_SCALE
    mask = (key_code <= code) & (key_code >= low_code)
    return jnp.where(mask, scores, MASKED)


MESH = pl.DeviceIdType.MESH
TILE = 256


def flip(i, d):
    return (i, i + 1 - 2 * (i % 2), (i + 2) % 4, 3 - i)[d]


def line_gather(remote, ctx, plane, slot, own, place):
    def copy(i, way, block, source):
        to = plane + way
        return remote(
            slot + 2 * i + (way + 1) // 2, source, place(to, block), (ctx, to), slot + block
        )

    def sends(i):
        if i == 0:
            return [(plane < 3, lambda: copy(0, 1, plane, own)), (plane > 0, lambda: copy(0, -1, plane, own))]
        return [
            (
                jnp.logical_and(plane >= i, plane < 3),
                lambda: copy(i, 1, plane - i, place(plane, plane - i)),
            ),
            (
                jnp.logical_and(plane + i <= 3, plane > 0),
                lambda: copy(i, -1, plane + i, place(plane, plane + i)),
            ),
        ]

    def start(i):
        for whether, made in sends(i):

            @pl.when(whether)
            def _(made=made):
                made().start()

    def step(i, then=None):
        for whether, block in ((plane >= i, plane - i), (plane + i <= 3, plane + i)):

            @pl.when(whether)
            def _(block=block):
                remote(slot, own, place(plane, block), (ctx, plane), slot + block).wait_recv()
                if then is not None:
                    then(block)

        if i < 3:
            start(i)

    def finish():
        for i in range(3):
            for whether, made in sends(i):

                @pl.when(whether)
                def _(made=made):
                    made().wait_send()

    return start, step, finish


def xor4(a, b):
    return 2 * ((a // 2 + b // 2) % 2) + (a % 2 + b % 2) % 2


def mlp_kernel(
    second_ref,
    mid_ref,
    upstream_ref,
    gain_ref,
    upstream_hbm,
    gate_hbm,
    up_hbm,
    down_hbm,
    output_ref,
    mid_grad_ref,
    gain_grad_ref,
    branch_all,
    gate_up_terms,
    gate_up_near,
    down_terms,
    gate_w,
    up_w,
    down_w,
    upstream_all,
    second_all,
    act,
    gate_grad,
    up_grad,
    held,
    own_sum,
    pair_send,
    pair_recv,
    z_send,
    z_recv,
    branch_low,
    staged,
    local_sem,
    staged_sem,
    send_sem,
    recv_sem,
):
    tok = second_ref.shape[0]
    pair = 2 * tok
    hidden = gate_w.shape[1]
    width = second_ref.shape[1]
    ctx, plane = lax.axis_index("ctx"), lax.axis_index("shard")
    chip, core = ctx // 2, ctx % 2
    sibling = (ctx + 1 - 2 * core, plane)
    over_z = [(ctx, flip(plane, d)) for d in range(4)]
    over_chips = [(2 * flip(chip, d) + core, plane) for d in range(4)]

    half = pl.ds(pl.multiple_of(core * hidden, hidden), hidden)
    loads = [
        pltpu.make_async_copy(upstream_hbm, upstream_all, local_sem.at[0]),
        pltpu.make_async_copy(down_hbm, down_w, local_sem.at[1]),
        pltpu.make_async_copy(gate_hbm.at[:, half], gate_w, local_sem.at[2]),
        pltpu.make_async_copy(up_hbm.at[:, half], up_w, local_sem.at[3]),
        pltpu.make_async_copy(second_ref, second_all.at[0, 0], local_sem.at[4]),
    ]
    for load in loads:
        load.start()

    barrier = pltpu.get_barrier_semaphore()
    partners = [sibling] + over_z[1:] + over_chips[1:]
    for partner in partners:
        pl.semaphore_signal(barrier, inc=1, device_id=partner, device_id_type=MESH)
    pl.semaphore_wait(barrier, len(partners))

    def remote(slot, source, target, device, recv=None):
        return pltpu.make_async_remote_copy(
            src_ref=source,
            dst_ref=target,
            send_sem=send_sem.at[slot],
            recv_sem=recv_sem.at[slot if recv is None else recv],
            device_id=device,
            device_id_type=MESH,
        )

    def send(slot, source, target, device):
        copy = remote(slot, source, target, device)
        copy.start()
        return copy

    start_line, step_line, finish_line = line_gather(
        remote, ctx, plane, 30, second_ref, lambda r, b: second_all.at[xor4(r, b), 0]
    )
    start_line(0)
    gather_pair = {0: send(0, second_ref, second_all.at[0, 1], sibling)}
    for load in loads:
        load.wait()

    def rows_of(d):
        return pl.ds(d * pair, pair)

    def forward(d):
        rows = rows_of(d)
        second = lambda: second_all[d].reshape(pair, width)

        def step(t, carry):
            at = pl.ds(pl.multiple_of(t * TILE, TILE), TILE)
            act_grad = dot_nt(upstream_all[rows, :], down_w[at, :])
            gate = dot_nn(second(), gate_w[:, at])
            up_lin = dot_nn(second(), up_w[:, at])
            sigma = 1.0 / (1.0 + jnp.exp(-gate))
            swish = gate * sigma
            act[rows, at] = (swish * up_lin).astype(BF16)
            gate_grad[rows, at] = (
                act_grad * up_lin * (sigma * (1.0 + gate * (1.0 - sigma)))
            ).astype(BF16)
            up_grad[rows, at] = (act_grad * swish).astype(BF16)
            return carry

        lax.fori_loop(0, hidden // TILE, step, 0)

    def give_pair(d, base, product):
        which = 0 if base == 7 else 1

        def step(t, carry):
            at = pl.ds(pl.multiple_of(t * TILE, TILE), TILE)
            terms = product(at)
            held[d % 2, :, at] = terms[:tok]
            pair_send[which, d, :, at] = terms[tok:].astype(BF16)
            return carry

        lax.fori_loop(0, width // TILE, step, 0)
        return send(base + d, pair_send.at[which, d], pair_recv.at[which, d], sibling)

    def give_plane(d, base, copy):
        which = 0 if base == 7 else 1
        copy.wait_recv()
        total = held[d % 2] + pair_recv[which, d].astype(F32)
        if d == 0:
            own_sum[which] = total
            return None
        z_send[which, d - 1] = total.astype(BF16)
        copy = remote(
            base + 3 + d, z_send.at[which, d - 1], z_recv.at[which, d - 1], over_z[d]
        )
        if which == 0:
            copy.start()
        return copy

    def back(d):
        rows = rows_of(d)
        return lambda at: dot_nt(gate_grad[rows, :], gate_w[at, :]) + dot_nt(
            up_grad[rows, :], up_w[at, :]
        )

    def onward(d):
        rows = rows_of(d)
        return lambda at: dot_nn(act[rows, :], down_w[:, at])

    pairs, planes = {}, {}
    for d in range(4):
        if d:
            step_line(d)
            gather_pair[d] = send(
                3 + d, second_all.at[d, 0], second_all.at[d, 1], sibling
            )
        gather_pair[d].wait_recv()
        forward(d)
        pairs[d] = give_pair(d, 7, back(d))
        if d:
            planes[d - 1] = give_plane(d - 1, 7, pairs[d - 1])
    planes[3] = give_plane(3, 7, pairs[3])

    out_pairs, out_planes = {}, {}
    for d in range(4):
        out_pairs[d] = give_pair(d, 14, onward(d))
        if d:
            out_planes[d - 1] = give_plane(d - 1, 14, out_pairs[d - 1])
    out_planes[3] = give_plane(3, 14, out_pairs[3])

    second_rows = second_all.reshape(8 * tok, width)

    def to_hbm(slot, target):
        return pltpu.make_async_copy(staged.at[slot], target, staged_sem.at[slot])

    chunks = (1, 2, 3, 0)
    near = {}
    for i, d in enumerate(chunks):
        for h in range(2):
            first = flip(chip, d) * (2 * TILE) + h * TILE
            left = second_rows[:, pl.ds(pl.multiple_of(first, TILE), TILE)]
            target = gate_up_terms.at[d, pl.ds(h * TILE, TILE)]
            if i:
                to_hbm(h, target).wait()
            if h and 1 <= i <= 2:
                done = chunks[i - 1]
                near[done] = send(
                    27 + done, gate_up_terms.at[done], gate_up_near.at[done - 1], over_chips[done]
                )
            staged[h, :, :hidden] = dot_tn(left, gate_grad[...]).astype(BF16)
            staged[h, :, hidden:] = dot_tn(left, up_grad[...]).astype(BF16)
            to_hbm(h, target).start()

    for d in (1, 2, 3):
        planes[d].wait_recv()
    for d in (1, 2, 3):
        out_planes[d].start()
    chunk = 32
    gain = gain_ref[...]

    def mid_step(i, carry):
        at = pl.ds(pl.multiple_of(i * chunk, chunk), chunk)
        grad = own_sum[0, at, :]
        for d in range(3):
            grad = grad + z_recv[0, d, at, :].astype(F32)
        mid = mid_ref[at, :]
        factor = lax.rsqrt(jnp.mean(mid * mid, axis=-1, keepdims=True) + EPSILON)
        scaled = grad * gain
        mid_grad = (
            upstream_ref[at, :].astype(F32)
            + factor * scaled
            - mid * (factor * factor * factor * jnp.mean(scaled * mid, axis=-1, keepdims=True))
        )
        mid_grad_ref[at, :] = mid_grad
        branch_low[at, :] = mid_grad.astype(BF16)
        return carry + jnp.sum(grad * mid * factor, axis=0, keepdims=True)

    gain_grad_ref[...] = lax.fori_loop(0, tok // chunk, mid_step, jnp.zeros((1, width), F32))
    branch_chips = {
        d: send(20 + d, branch_low, branch_all.at[0, d], over_chips[d]) for d in (1, 2, 3)
    }
    branch_pairs = {0: send(24, branch_low, branch_all.at[1, 0], sibling)}
    keep = pltpu.make_async_copy(branch_low, branch_all.at[0, 0], local_sem.at[0])
    keep.start()

    def down_step(t):
        slot = t % 2
        target = down_terms.at[pl.ds(t * TILE, TILE)]
        to_hbm(slot, target).wait()
        left = act[:, pl.ds(t * TILE, TILE)]
        staged[slot] = dot_tn(left, upstream_all[...]).astype(BF16)
        to_hbm(slot, target).start()

    for t in range(hidden // TILE):
        down_step(t)
    for d in (1, 2, 3):
        branch_chips[d].wait_recv()
        branch_pairs[d] = send(24 + d, branch_all.at[0, d], branch_all.at[1, d], sibling)

    for d in (1, 2, 3):
        out_planes[d].wait_recv()

    def out_step(i, carry):
        at = pl.ds(pl.multiple_of(i * chunk, chunk), chunk)
        total = mid_ref[at, :] + own_sum[1, at, :]
        for d in range(3):
            total = total + z_recv[1, d, at, :].astype(F32)
        output_ref[at, :] = total.astype(BF16)
        return carry

    lax.fori_loop(0, tok // chunk, out_step, 0)

    for d in range(4):
        branch_pairs[d].wait_recv()
        for copy in (gather_pair[d], pairs[d], out_pairs[d], branch_pairs[d]):
            copy.wait_send()
    for d in (1, 2, 3):
        for copy in (planes[d], out_planes[d], branch_chips[d]):
            copy.wait_send()
    finish_line()
    keep.wait()
    for d in (1, 2):
        near[d].wait()
    for slot in range(2):
        to_hbm(slot, down_terms.at[pl.ds(0, TILE)]).wait()


def mlp_of(normed_two, mid, upstream, gain, upstream_group, w_gate, w_up, down_rows):
    tok, width = mid.shape
    hidden = down_rows.shape[0]
    rows = upstream_group.shape[0]
    vmem = pl.BlockSpec(memory_space=pltpu.VMEM)
    hbm = pl.BlockSpec(memory_space=pl.ANY)
    return pl.pallas_call(
        mlp_kernel,
        in_specs=[vmem] * 4 + [hbm] * 4,
        out_specs=[vmem] * 3 + [hbm] * 4,
        out_shape=[
            jax.ShapeDtypeStruct((tok, width), BF16),
            jax.ShapeDtypeStruct((tok, width), F32),
            jax.ShapeDtypeStruct((1, width), F32),
            jax.ShapeDtypeStruct((2, 4, tok, width), BF16),
            jax.ShapeDtypeStruct((4, 2 * TILE, 2 * hidden), BF16),
            jax.ShapeDtypeStruct((2, 2 * TILE, 2 * hidden), BF16),
            jax.ShapeDtypeStruct((hidden, width), BF16),
        ],
        scratch_shapes=[
            pltpu.VMEM((width, hidden), BF16),
            pltpu.VMEM((width, hidden), BF16),
            pltpu.VMEM((hidden, width), BF16),
            pltpu.VMEM((rows, width), BF16),
            pltpu.VMEM((4, 2, tok, width), BF16),
            pltpu.VMEM((rows, hidden), BF16),
            pltpu.VMEM((rows, hidden), BF16),
            pltpu.VMEM((rows, hidden), BF16),
            pltpu.VMEM((2, tok, width), F32),
            pltpu.VMEM((2, tok, width), F32),
            pltpu.VMEM((2, 4, tok, width), BF16),
            pltpu.VMEM((2, 4, tok, width), BF16),
            pltpu.VMEM((2, 3, tok, width), BF16),
            pltpu.VMEM((2, 3, tok, width), BF16),
            pltpu.VMEM((tok, width), BF16),
            pltpu.VMEM((2, TILE, width), BF16),
            pltpu.SemaphoreType.DMA((5,)),
            pltpu.SemaphoreType.DMA((2,)),
            pltpu.SemaphoreType.DMA((36,)),
            pltpu.SemaphoreType.DMA((36,)),
        ],
        compiler_params=pltpu.CompilerParams(
            collective_id=1, has_side_effects=True, vmem_limit_bytes=60 << 20
        ),
        cost_estimate=pl.CostEstimate(
            flops=18 * rows * width * hidden,
            bytes_accessed=2 * (5 * width * hidden + 4 * rows * width),
            transcendentals=rows * hidden,
        ),
    )(normed_two, mid, upstream, gain, upstream_group, w_gate, w_up, down_rows)


def rotated(values, cosine, sine):
    half = values.shape[1] // 2
    first, second = values[:, :half], values[:, half:]
    return jnp.concatenate([first * cosine - second * sine, second * cosine + first * sine], axis=1)


def front_kernel(
    input_ref,
    attn_gain_ref,
    mlp_gain_ref,
    cosine_ref,
    sine_ref,
    code_ref,
    low_code_ref,
    key_code_ref,
    query_hbm,
    key_hbm,
    value_hbm,
    out_hbm,
    down_hbm,
    upstream_hbm,
    second_ref,
    mid_ref,
    normed_ref,
    query_ref,
    kv_ref,
    attended_ref,
    log_total_ref,
    w_head,
    w_sibling,
    out_pair,
    down_rows,
    upstream_all,
    inputs_all,
    w_parts,
    attended_other,
    own_sum,
    chip_send,
    chip_recv,
    local_sem,
    send_sem,
    recv_sem,
):
    tok, width = input_ref.shape
    quarter = width // 4
    shard = out_hbm.shape[1]
    hidden = down_rows.shape[0]
    part = hidden // 4
    seq = 8 * tok
    half_seq = 4 * tok
    ctx, plane = lax.axis_index("ctx"), lax.axis_index("shard")
    chip, core = ctx // 2, ctx % 2
    sibling = (ctx + 1 - 2 * core, plane)
    over_z = [(ctx, flip(plane, d)) for d in range(4)]
    over_chips = [(2 * flip(chip, d) + core, plane) for d in range(4)]
    others = (1, 2, 3)

    def at(i, size):
        return pl.ds(pl.multiple_of(i * size, size), size)

    def remote(slot, source, target, device, recv=None):
        return pltpu.make_async_remote_copy(
            src_ref=source,
            dst_ref=target,
            send_sem=send_sem.at[slot],
            recv_sem=recv_sem.at[slot if recv is None else recv],
            device_id=device,
            device_id_type=MESH,
        )

    def send(slot, source, target, device):
        copy = remote(slot, source, target, device)
        copy.start()
        return copy

    def local(slot, source, target):
        return pltpu.make_async_copy(source, target, local_sem.at[slot])

    rows = at(chip, quarter)
    mine = w_parts.at[plane]
    load_query = local(0, query_hbm.at[rows, at(core, HD)], mine.at[0])
    load_key = local(1, key_hbm.at[rows], mine.at[1])
    load_value = local(1, value_hbm.at[rows], mine.at[1])
    load_query.start()

    @pl.when(core == 0)
    def _():
        load_key.start()

    @pl.when(core == 1)
    def _():
        load_value.start()

    keep_input = local(2, input_ref, inputs_all.at[0, 0])
    keep_input.start()
    out_own = out_hbm.at[at(ctx, HD), :]
    keep_out = local(3, out_own, out_pair.at[0, :, at(plane, shard)])
    keep_out.start()

    def down_block(to_plane):
        first = to_plane * (2 * hidden) + core * hidden + chip * part
        return down_hbm.at[pl.ds(pl.multiple_of(first, part), part), :]

    def down_place(column):
        return down_rows.at[at(chip, part), at(column, shard)]

    first_own = plane * (2 * hidden) + core * hidden
    keep_down = local(
        4,
        down_hbm.at[pl.ds(pl.multiple_of(first_own, hidden), hidden), :],
        down_rows.at[:, at(plane, shard)],
    )
    keep_down.start()
    keep_upstream = local(5, upstream_hbm, upstream_all.at[0, 0])
    keep_upstream.start()

    barrier = pltpu.get_barrier_semaphore()
    partners = [sibling] + over_z[1:] + over_chips[1:]
    for partner in partners:
        pl.semaphore_signal(barrier, inc=1, device_id=partner, device_id_type=MESH)
    pl.semaphore_wait(barrier, len(partners))

    input_chips = {
        d: send(d - 1, input_ref, inputs_all.at[0, d], over_chips[d]) for d in others
    }
    input_pairs = {0: send(3, input_ref, inputs_all.at[1, 0], sibling)}
    load_query.wait()
    load_key.wait()
    start_head, step_head, finish_head = line_gather(
        remote, ctx, plane, 37, mine, lambda r, b: w_parts.at[b]
    )
    start_out, step_out, finish_out = line_gather(
        remote, ctx, plane, 43, out_own, lambda r, b: out_pair.at[0, :, at(b, shard)]
    )
    start_up, step_up, finish_up = line_gather(
        remote, ctx, plane, 49, upstream_hbm, lambda r, b: upstream_all.at[xor4(r, b), 0]
    )
    start_head(0)

    head_rows = w_head.at[:, rows, :]

    def pass_head(source):
        apart = xor4(chip, source)
        block = w_parts.at[source]

        @pl.when(apart == 0)
        def _():
            local(6, block, head_rows).start()

        @pl.when(apart != 0)
        def _():
            remote(9 + apart, block, head_rows, (2 * source + core, plane)).start()

    pass_head(plane)
    chunk = 32
    attn_gain = attn_gain_ref[...]

    def norm(e, d):
        def step(i, carry):
            block = inputs_all[e, d, at(i, chunk), :].astype(F32)
            factor = lax.rsqrt(jnp.mean(block * block, axis=-1, keepdims=True) + EPSILON)
            first = (4 * e + d) * tok + i * chunk
            normed_ref[pl.ds(pl.multiple_of(first, chunk), chunk), :] = (
                block * factor * attn_gain
            ).astype(BF16)
            return carry

        lax.fori_loop(0, tok // chunk, step, 0)

    keep_input.wait()
    norm(0, 0)
    step_head(1, pass_head)
    input_pairs[0].wait_recv()
    norm(1, 0)
    for d in (1, 2):
        input_chips[d].wait_recv()
        input_pairs[d] = send(3 + d, inputs_all.at[0, d], inputs_all.at[1, d], sibling)
    norm(0, 1)
    norm(0, 2)
    step_head(2, pass_head)
    input_chips[3].wait_recv()
    input_pairs[3] = send(6, inputs_all.at[0, 3], inputs_all.at[1, 3], sibling)
    norm(0, 3)
    for d in others:
        input_pairs[d].wait_recv()
        norm(1, d)
    step_head(3, pass_head)

    down_z = {
        d: send(16 + d, down_block(flip(plane, d)), down_place(plane), over_z[d]) for d in others
    }
    start_out(0)
    local(6, mine, head_rows).wait()
    for d in others:
        remote(9 + d, mine, head_rows, over_chips[d]).wait_recv()
    head_pair = send(16, w_head, w_sibling, sibling)

    def project(which, target, flat):
        def step(t, carry):
            here = at(t, TILE)
            made = dot_nn(normed_ref[here, :], w_head[which])
            cosine, sine = cosine_ref[here, :], sine_ref[here, :]
            if flat:
                cosine = jnp.where(core == 0, cosine, 1.0)
                sine = jnp.where(core == 0, sine, 0.0)
            target[here, :] = rotated(made, cosine, sine).astype(BF16)
            return carry

        lax.fori_loop(0, seq // TILE, step, 0)

    mine_kv = kv_ref.at[core]
    project(1, mine_kv, True)
    kv_pair = [
        send(20 + e, mine_kv.at[pl.ds(e * half_seq, half_seq)],
             mine_kv.at[pl.ds((1 - e) * half_seq, half_seq)], sibling)
        for e in range(2)
    ]
    project(0, query_ref, False)
    step_out(1)
    for copy in kv_pair:
        copy.wait_recv()

    def attend_step(t, carry):
        here = at(t, TILE)
        scores = scores_of(
            query_ref[here, :], kv_ref[0], code_ref[here, :], low_code_ref[here, :], key_code_ref[...]
        )
        top = jnp.max(scores, axis=-1, keepdims=True)
        weights = jnp.exp(scores - top)
        total = jnp.sum(weights, axis=-1, keepdims=True)
        mixed = dot_nn(weights.astype(BF16), kv_ref[1])
        attended_ref[here, :] = (mixed / total).astype(BF16)
        log_total_ref[here, :] = top + jnp.log(total)
        return carry

    lax.fori_loop(0, seq // TILE, attend_step, 0)
    attended_pair = send(22, attended_ref.at[pl.ds(half_seq, half_seq)], attended_other, sibling)
    step_out(2)
    for d in others:
        down_z[d].wait_recv()
    down_chips = {}
    for e in others:
        for d in others:
            block = down_place(flip(plane, d))
            down_chips[e, d] = send(51 + 3 * e + d, block, block, over_chips[e])
    step_out(3)
    start_up(0)
    keep_out.wait()
    out_sibling = send(23, out_pair.at[0], out_pair.at[1], sibling)
    attended_pair.wait_recv()
    out_sibling.wait_recv()

    def out_step(t, carry):
        here = at(t, TILE)
        terms = dot_nn(attended_ref[:half_seq, :], out_pair[0, :, here]) + dot_nn(
            attended_other[...], out_pair[1, :, here]
        )
        own_sum[:, here] = terms[:tok]
        for d in others:
            chip_send[d - 1, :, here] = terms[d * tok : (d + 1) * tok].astype(BF16)
        return carry

    lax.fori_loop(0, width // TILE, out_step, 0)
    branch = {
        d: send(23 + d, chip_send.at[d - 1], chip_recv.at[d - 1], over_chips[d]) for d in others
    }

    upstream_pair = {0: send(33, upstream_hbm, upstream_all.at[0, 1], sibling)}

    def pass_up(d):
        step_up(d)
        upstream_pair[d] = send(33 + d, upstream_all.at[d, 0], upstream_all.at[d, 1], sibling)

    pass_up(1)
    pass_up(2)
    for d in others:
        branch[d].wait_recv()
    mlp_gain = mlp_gain_ref[...]

    def mid_step(i, carry):
        here = at(i, chunk)
        mid = input_ref[here, :].astype(F32) + own_sum[here, :]
        for d in range(3):
            mid = mid + chip_recv[d, here, :].astype(F32)
        factor = lax.rsqrt(jnp.mean(mid * mid, axis=-1, keepdims=True) + EPSILON)
        mid_ref[here, :] = mid
        second_ref[here, :] = (mid * factor * mlp_gain).astype(BF16)
        return carry

    lax.fori_loop(0, tok // chunk, mid_step, 0)

    pass_up(3)
    keep_upstream.wait()
    for d in range(4):
        upstream_pair[d].wait_recv()
        upstream_pair[d].wait_send()
        input_pairs[d].wait_send()
    head_pair.wait_recv()
    for copy in (head_pair, attended_pair, out_sibling, *kv_pair):
        copy.wait_send()
    keep_down.wait()
    for d in others:
        for e in others:
            down_chips[e, d].wait()
        for copies in (input_chips, down_z, branch):
            copies[d].wait_send()
        remote(9 + d, mine, head_rows, over_chips[d]).wait_send()
    finish_head()
    finish_out()
    finish_up()


def front_of(
    inputs, attn_gain, mlp_gain, cosine, sine, code, low_code, key_code,
    w_query, w_key, w_value, w_out, w_down, upstream,
):
    tok, width = inputs.shape
    seq = 8 * tok
    hidden = w_down.shape[0] // 8
    vmem = pl.BlockSpec(memory_space=pltpu.VMEM)
    hbm = pl.BlockSpec(memory_space=pl.ANY)
    return pl.pallas_call(
        front_kernel,
        in_specs=[vmem] * 8 + [hbm] * 6,
        out_specs=[vmem] * 8 + [hbm] + [vmem] + [hbm] * 2,
        out_shape=[
            jax.ShapeDtypeStruct((tok, width), BF16),
            jax.ShapeDtypeStruct((tok, width), F32),
            jax.ShapeDtypeStruct((seq, width), BF16),
            jax.ShapeDtypeStruct((seq, HD), BF16),
            jax.ShapeDtypeStruct((2, seq, HD), BF16),
            jax.ShapeDtypeStruct((seq, HD), BF16),
            jax.ShapeDtypeStruct((seq, 1), F32),
            jax.ShapeDtypeStruct((2, width, HD), BF16),
            jax.ShapeDtypeStruct((2, width, HD), BF16),
            jax.ShapeDtypeStruct((2, HD, width), BF16),
            jax.ShapeDtypeStruct((hidden, width), BF16),
            jax.ShapeDtypeStruct((4, 2, tok, width), BF16),
        ],
        scratch_shapes=[
            pltpu.VMEM((2, 4, tok, width), BF16),
            pltpu.VMEM((4, 2, width // 4, HD), BF16),
            pltpu.VMEM((4 * tok, HD), BF16),
            pltpu.VMEM((tok, width), F32),
            pltpu.VMEM((3, tok, width), BF16),
            pltpu.VMEM((3, tok, width), BF16),
            pltpu.SemaphoreType.DMA((7,)),
            pltpu.SemaphoreType.DMA((64,)),
            pltpu.SemaphoreType.DMA((64,)),
        ],
        compiler_params=pltpu.CompilerParams(
            collective_id=2, has_side_effects=True, vmem_limit_bytes=56 << 20
        ),
        cost_estimate=pl.CostEstimate(
            flops=2 * seq * width * 3 * HD + 4 * seq * seq * HD,
            bytes_accessed=20 * seq * width,
            transcendentals=seq * seq,
        ),
    )(
        inputs, attn_gain, mlp_gain, cosine, sine, code, low_code, key_code,
        w_query, w_key, w_value, w_out, w_down, upstream,
    )


def back_kernel(
    input_ref,
    mid_grad_ref,
    attn_gain_ref,
    mlp_gain_grad_ref,
    cosine_ref,
    sine_ref,
    code_ref,
    low_code_ref,
    key_code_ref,
    normed_ref,
    query_ref,
    kv_ref,
    attended_ref,
    log_total_ref,
    w_head,
    w_sibling,
    out_rows_ref,
    branch_hbm,
    gate_up_terms,
    gate_up_near,
    down_terms,
    grad_input_ref,
    gain_total_ref,
    grad_out_ref,
    head_in,
    gate_up_in,
    down_in,
    branch_all,
    d_attended,
    d_head,
    d_other,
    d_kv,
    d_kv_other,
    out_send,
    out_recv,
    head_terms,
    head_recv,
    own_sum,
    chip_send,
    chip_recv,
    gate_up_parts,
    gate_up_sum,
    down_parts,
    down_sum,
    down_planes,
    gains,
    gains_z,
    gains_ctx,
    local_sem,
    send_sem,
    recv_sem,
):
    tok, width = input_ref.shape
    seq = 8 * tok
    half_seq = 4 * tok
    share = out_send.shape[1]
    ctx, plane = lax.axis_index("ctx"), lax.axis_index("shard")
    chip, core = ctx // 2, ctx % 2
    other_core = 1 - core
    sibling = (2 * chip + other_core, plane)
    over_z = [(ctx, flip(plane, d)) for d in range(4)]
    over_chips = [(2 * flip(chip, d) + core, plane) for d in range(4)]
    over_chips_cross = [(2 * flip(chip, d) + other_core, plane) for d in range(4)]
    over_z_cross = [(2 * chip + other_core, flip(plane, d)) for d in range(4)]
    others = (1, 2, 3)

    def at(i, size):
        return pl.ds(pl.multiple_of(i * size, size), size)

    def remote(slot, source, target, device):
        return pltpu.make_async_remote_copy(
            src_ref=source,
            dst_ref=target,
            send_sem=send_sem.at[slot],
            recv_sem=recv_sem.at[slot],
            device_id=device,
            device_id_type=MESH,
        )

    def send(slot, source, target, device):
        copy = remote(slot, source, target, device)
        copy.start()
        return copy

    def local(slot, source, target):
        return pltpu.make_async_copy(source, target, local_sem.at[slot])

    loads = [
        local(0, branch_hbm, branch_all),
        local(1, gate_up_terms.at[0], gate_up_parts.at[0]),
        local(2, gate_up_near, gate_up_parts.at[pl.ds(1, 2)]),
        local(3, down_terms.at[:, chip], down_parts.at[0]),
    ]
    for load in loads:
        load.start()

    barrier = pltpu.get_barrier_semaphore()
    partners = (
        over_z[1:] + over_z_cross + over_chips[1:] + over_chips_cross[1:]
    )
    for partner in partners:
        pl.semaphore_signal(barrier, inc=1, device_id=partner, device_id_type=MESH)
    pl.semaphore_wait(barrier, len(partners))

    gate_up_far = send(0, gate_up_terms.at[3], gate_up_parts.at[3], over_chips[3])
    down_chips = {
        d: send(d, down_terms.at[:, flip(chip, d)], down_parts.at[d], over_chips[d])
        for d in others
    }

    loads[0].wait()

    def out_step(t, carry):
        here = at(t, TILE)
        made = dot_tn(attended_ref[...], branch_all[:, here])
        out_send[:, :, here] = made.reshape(4, share, TILE).astype(BF16)
        return carry

    lax.fori_loop(0, width // TILE, out_step, 0)
    out_z = {
        d: send(3 + d, out_send.at[flip(plane, d)], out_recv.at[d - 1], over_z[d]) for d in others
    }

    def attended_step(t, carry):
        here = at(t, TILE)
        d_attended[here, :] = dot_nt(branch_all[here, :], out_rows_ref[...]).astype(BF16)
        return carry

    lax.fori_loop(0, seq // TILE, attended_step, 0)
    d_kv[...] = jnp.zeros_like(d_kv)

    def attend_step(t, carry):
        here = at(t, TILE)
        query, outgrad = query_ref[here, :], d_attended[here, :]
        scores = scores_of(
            query, kv_ref[0], code_ref[here, :], low_code_ref[here, :], key_code_ref[...]
        )
        probs = jnp.exp(scores - log_total_ref[here, :])
        prob_grad = dot_nt(outgrad, kv_ref[1])
        delta = jnp.sum(probs * prob_grad, axis=-1, keepdims=True)
        score_grad = (probs * (prob_grad - delta)).astype(BF16)
        d_query = dot_nn(score_grad, kv_ref[0]) * SCORE_SCALE
        d_head[here, :HD] = rotated(d_query, cosine_ref[here, :], -sine_ref[here, :]).astype(BF16)
        d_kv[0] += dot_tn(score_grad, query)
        d_kv[1] += dot_tn(probs.astype(BF16), outgrad)
        return carry

    lax.fori_loop(0, seq // TILE, attend_step, 0)

    give = d_kv.at[other_core]
    kv_pair = [
        send(
            7 + e,
            give.at[pl.ds(e * half_seq, half_seq)],
            d_kv_other.at[pl.ds((1 - e) * half_seq, half_seq)],
            sibling,
        )
        for e in range(2)
    ]
    for copy in kv_pair:
        copy.wait_recv()

    def kv_step(t, carry):
        here = at(t, TILE)
        total = d_kv[core, here, :] + d_kv_other[here, :]
        total = total * jnp.where(core == 0, SCORE_SCALE, 1.0)
        cosine = jnp.where(core == 0, cosine_ref[here, :], 1.0)
        sine = jnp.where(core == 0, sine_ref[here, :], 0.0)
        d_head[here, HD:] = rotated(total, cosine, -sine).astype(BF16)
        return carry

    lax.fori_loop(0, seq // TILE, kv_step, 0)
    head_pair = send(9, d_head.at[pl.ds(half_seq, half_seq)], d_other, sibling)

    def head_step(t, carry):
        made = dot_tn(normed_ref[:, at(t, TILE)], d_head[...])
        head_terms[:, t] = made.reshape(4, share, 2 * HD).astype(BF16)
        return carry

    lax.fori_loop(0, width // TILE, head_step, 0)
    head_z = {
        d: send(9 + d, head_terms.at[flip(plane, d)], head_recv.at[d - 1], over_z[d])
        for d in others
    }

    head_pair.wait_recv()

    def normed_step(t, carry):
        here = at(t, TILE)
        made = (
            dot_nt(d_head[:half_seq, :HD], w_head[0, here, :])
            + dot_nt(d_head[:half_seq, HD:], w_head[1, here, :])
            + dot_nt(d_other[:, :HD], w_sibling[0, here, :])
            + dot_nt(d_other[:, HD:], w_sibling[1, here, :])
        )
        own_sum[:, here] = made[:tok]
        for d in others:
            chip_send[d - 1, :, here] = made[d * tok : (d + 1) * tok].astype(BF16)
        return carry

    lax.fori_loop(0, width // TILE, normed_step, 0)
    normed_chips = {
        d: send(12 + d, chip_send.at[d - 1], chip_recv.at[d - 1], over_chips[d]) for d in others
    }

    loads[3].wait()
    for d in others:
        down_chips[d].wait_recv()

    def down_step(p, carry):
        total = down_parts[0, p].astype(F32)
        for d in others:
            total = total + down_parts[d, p].astype(F32)
        down_sum[p] = total.astype(BF16)
        return carry

    lax.fori_loop(0, 4, down_step, 0)
    down_z = {
        d: send(15 + d, down_sum.at[flip(plane, d)], down_planes.at[plane], over_z[d])
        for d in others
    }
    keep_down = local(3, down_sum.at[plane], down_planes.at[plane])
    keep_down.start()

    loads[1].wait()
    loads[2].wait()
    gate_up_far.wait_recv()

    def gate_up_step(i, carry):
        here = at(i, share)
        total = gate_up_parts[0, here, :].astype(F32)
        for d in others:
            total = total + gate_up_parts[d, here, :].astype(F32)
        gate_up_sum[i // 4, i % 4] = total.astype(BF16)
        return carry

    lax.fori_loop(0, 8, gate_up_step, 0)
    place = gate_up_in.at[plane, core]
    gate_up_z = {
        d: send(18 + d, gate_up_sum.at[core, flip(plane, d)], place, over_z[d]) for d in others
    }
    gate_up_cross = {
        d: send(22 + d, gate_up_sum.at[other_core, flip(plane, d)], place, over_z_cross[d])
        for d in range(4)
    }
    keep_gate_up = local(1, gate_up_sum.at[core, plane], place)
    keep_gate_up.start()

    for d in others:
        normed_chips[d].wait_recv()
    chunk = 32
    gain = attn_gain_ref[...]

    def input_step(i, carry):
        here = at(i, chunk)
        grad = own_sum[here, :]
        for d in range(3):
            grad = grad + chip_recv[d, here, :].astype(F32)
        block = input_ref[here, :].astype(F32)
        factor = lax.rsqrt(jnp.mean(block * block, axis=-1, keepdims=True) + EPSILON)
        scaled = grad * gain
        grad_input_ref[here, :] = (
            mid_grad_ref[here, :]
            + factor * scaled
            - block * (factor * factor * factor * jnp.mean(scaled * block, axis=-1, keepdims=True))
        ).astype(BF16)
        return carry + jnp.sum(grad * block * factor, axis=0, keepdims=True)

    gain_grad = lax.fori_loop(0, tok // chunk, input_step, jnp.zeros((1, width), F32))
    gains[...] = jnp.concatenate(
        [gain_grad, mlp_gain_grad_ref[...], jnp.zeros((6, width), F32)], axis=0
    )
    gains_planes = {d: send(25 + d, gains, gains_z.at[d - 1], over_z[d]) for d in others}

    for d in others:
        out_z[d].wait_recv()
    total = out_send[plane].astype(F32)
    for d in range(3):
        total = total + out_recv[d].astype(F32)
    grad_out_ref[...] = total

    for d in others:
        head_z[d].wait_recv()

    def head_sum(i, carry):
        total = head_terms[plane, i].astype(F32)
        for d in range(3):
            total = total + head_recv[d, i].astype(F32)
        head_terms[plane, i] = total.astype(BF16)
        return carry

    lax.fori_loop(0, 8, head_sum, 0)
    head_place = head_in.at[ctx]
    head_chips = {
        d: send(28 + d, head_terms.at[plane, 2 * flip(chip, d) + core], head_place, over_chips[d])
        for d in others
    }
    head_cross = {
        d: send(
            32 + d, head_terms.at[plane, 2 * flip(chip, d) + other_core], head_place,
            over_chips_cross[d],
        )
        for d in range(4)
    }
    keep_head = local(0, head_terms.at[plane, ctx], head_place)
    keep_head.start()

    for d in others:
        gains_planes[d].wait_recv()
        gains_planes[d].wait_send()
    gains[...] = gains[...] + gains_z[0] + gains_z[1] + gains_z[2]
    gains_chips = {
        d: send(35 + d, gains, gains_ctx.at[0, d], over_chips[d]) for d in others
    }
    gains_cross = {
        d: send(39 + d, gains, gains_ctx.at[1, d], over_chips_cross[d]) for d in range(4)
    }

    keep_down.wait()
    down_place = down_in.at[chip]
    for d in range(4):
        if d:
            down_z[d].wait_recv()
        source = flip(plane, d)
        apart = xor4(chip, source)
        block = down_planes.at[source]

        @pl.when(apart == 0)
        def _(block=block):
            local(4, block, down_place).start()

        @pl.when(apart != 0)
        def _(block=block, source=source, apart=apart):
            remote(42 + apart, block, down_place, (2 * source + core, plane)).start()

    for d in others:
        gains_chips[d].wait_recv()
    for d in range(4):
        gains_cross[d].wait_recv()
    total = gains[...] + gains_ctx[1, 0]
    for d in others:
        total = total + gains_ctx[0, d] + gains_ctx[1, d]
    gain_total_ref[...] = total

    local(4, down_sum.at[plane], down_place).wait()
    keep_gate_up.wait()
    keep_head.wait()
    for d in others:
        remote(42 + d, down_sum.at[plane], down_place, over_chips[d]).wait()
        gate_up_z[d].wait_recv()
        head_chips[d].wait_recv()
        for copies in (
            down_chips, out_z, head_z, normed_chips, down_z, gate_up_z, head_chips, gains_chips
        ):
            copies[d].wait_send()
    for d in range(4):
        for copies in (gate_up_cross, head_cross):
            copies[d].wait()
        gains_cross[d].wait_send()
    for copy in (gate_up_far, head_pair, *kv_pair):
        copy.wait_send()


def back_of(*operands):
    inputs, query, out_rows = operands[0], operands[10], operands[16]
    tok, width = inputs.shape
    seq = query.shape[0]
    hidden = operands[20].shape[0] * operands[20].shape[1] * operands[20].shape[2]
    share = HD // 4
    vmem = pl.BlockSpec(memory_space=pltpu.VMEM)
    hbm = pl.BlockSpec(memory_space=pl.ANY)
    return pl.pallas_call(
        back_kernel,
        in_specs=[vmem] * 17 + [hbm] * 4,
        out_specs=[vmem] * 6,
        out_shape=[
            jax.ShapeDtypeStruct((tok, width), BF16),
            jax.ShapeDtypeStruct((8, width), F32),
            jax.ShapeDtypeStruct((share, width), F32),
            jax.ShapeDtypeStruct((8, share, 2 * HD), BF16),
            jax.ShapeDtypeStruct((4, 2, share, 2 * hidden), BF16),
            jax.ShapeDtypeStruct((4, share, width), BF16),
        ],
        scratch_shapes=[
            pltpu.VMEM((seq, width), BF16),
            pltpu.VMEM((seq, HD), BF16),
            pltpu.VMEM((seq, 2 * HD), BF16),
            pltpu.VMEM((4 * tok, 2 * HD), BF16),
            pltpu.VMEM((2, seq, HD), F32),
            pltpu.VMEM((seq, HD), F32),
            pltpu.VMEM((4, share, width), BF16),
            pltpu.VMEM((3, share, width), BF16),
            pltpu.VMEM((4, 8, share, 2 * HD), BF16),
            pltpu.VMEM((3, 8, share, 2 * HD), BF16),
            pltpu.VMEM((tok, width), F32),
            pltpu.VMEM((3, tok, width), BF16),
            pltpu.VMEM((3, tok, width), BF16),
            pltpu.VMEM((4, 2 * TILE, 2 * hidden), BF16),
            pltpu.VMEM((2, 4, share, 2 * hidden), BF16),
            pltpu.VMEM((4, 4, share, width), BF16),
            pltpu.VMEM((4, share, width), BF16),
            pltpu.VMEM((4, share, width), BF16),
            pltpu.VMEM((8, width), F32),
            pltpu.VMEM((3, 8, width), F32),
            pltpu.VMEM((2, 4, 8, width), F32),
            pltpu.SemaphoreType.DMA((5,)),
            pltpu.SemaphoreType.DMA((46,)),
            pltpu.SemaphoreType.DMA((46,)),
        ],
        compiler_params=pltpu.CompilerParams(
            collective_id=3, has_side_effects=True, vmem_limit_bytes=60 << 20
        ),
        cost_estimate=pl.CostEstimate(
            flops=2 * seq * width * 6 * HD + 10 * seq * seq * HD,
            bytes_accessed=20 * seq * width,
            transcendentals=seq * seq,
        ),
    )(*operands)


def on_device_by_head(
    layer_input,
    w_query,
    w_key,
    w_value,
    w_out,
    w_gate,
    w_up,
    w_down,
    attn_gain,
    mlp_gain,
    block_pairs,
    doc_ids,
    cotangent,
):
    tok_rows, width = layer_input.shape[1:]
    planes = lax.axis_size("shard")
    ctx_count = lax.axis_size("ctx")
    chips = ctx_count // 2
    ctx, plane = lax.axis_index("ctx"), lax.axis_index("shard")
    chip, core = ctx // 2, ctx % 2
    seq_rows = tok_rows * ctx_count
    own_share = width // (planes * ctx_count)

    inputs_low = layer_input[0]
    pairs, documents = block_pairs[0], doc_ids[0]
    order = jnp.stack([(chip ^ d) * 2 + (core ^ e) for e in range(2) for d in range(chips)])
    chosen = jnp.sum(
        jnp.where(order[:, None] == jnp.arange(ctx_count)[None, :], pairs[None, :], 0), axis=1
    )[:, None]
    within = jnp.arange(tok_rows, dtype=jnp.int32)[None, :]
    block = tok_rows // 2
    positions = jnp.where(
        within < block, chosen * block, (2 * ctx_count - 1 - chosen) * block - block
    )
    positions = (positions + within).reshape(-1)
    begins = jnp.sum(documents[None, :] < jnp.arange(1, DOCS)[:, None], axis=1)
    document = jnp.sum((positions[None, :] >= begins[:, None]).astype(jnp.int32), axis=0)
    span = 2 * seq_rows
    doc_first = document * span
    code = doc_first + positions
    low_code = jnp.maximum(doc_first, code - (WINDOW - 1))
    code_column, low_column, code_row = code[:, None], low_code[:, None], code[None, :]
    cosine, sine = rope_tables(positions, HD)

    upstream_low = cotangent[0]
    (
        normed_two,
        mid,
        normed_all,
        query,
        key_value,
        attended,
        log_total,
        w_head,
        w_sibling,
        out_pair,
        down_rows,
        upstream_group,
    ) = front_of(
        inputs_low,
        attn_gain[None],
        mlp_gain[None],
        cosine,
        sine,
        code_column,
        low_column,
        code_row,
        w_query,
        w_key,
        w_value,
        w_out,
        w_down,
        upstream_low,
    )
    output, mid_grad, mlp_gain_grad, branch_all, gate_up_terms, gate_up_near, down_terms = mlp_of(
        normed_two,
        mid,
        upstream_low,
        mlp_gain[None],
        upstream_group.reshape(-1, width),
        w_gate,
        w_up,
        down_rows,
    )
    grad_input, gain_total, grad_out, head_in, gate_up_in, down_in = back_of(
        inputs_low,
        mid_grad,
        attn_gain[None],
        mlp_gain_grad,
        cosine,
        sine,
        code_column,
        low_column,
        code_row,
        normed_all,
        query,
        key_value,
        attended,
        log_total,
        w_head,
        w_sibling,
        out_pair[0],
        branch_all.reshape(seq_rows, width),
        gate_up_terms,
        gate_up_near,
        down_terms.reshape(planes, chips, -1, width),
    )
    hidden = gate_up_in.shape[-1] // 2
    gate_up = gate_up_in.astype(F32)
    columns = lambda parts: jnp.concatenate(parts, axis=1)
    grad_gate = columns([gate_up[p, e, :, :hidden] for p in range(planes) for e in range(2)])
    grad_up = columns([gate_up[p, e, :, hidden:] for p in range(planes) for e in range(2)])
    head = head_in.astype(F32)
    grad_query = columns([head[i, :, :HD] for i in range(ctx_count)])
    grad_key = columns([head[i, :, HD:] for i in range(0, ctx_count, 2)])
    grad_value = columns([head[i, :, HD:] for i in range(1, ctx_count, 2)])
    grad_down = down_in.astype(F32).reshape(-1, width)
    gains = lax.dynamic_slice(gain_total, (0, own_share * (planes * ctx + plane)), (2, own_share))
    return (
        output[None],
        grad_input[None],
        grad_query,
        grad_key,
        grad_value,
        grad_out,
        grad_gate,
        grad_up,
        grad_down,
        gains[0],
        gains[1],
    )


def plan_of(mesh):
    chips, planes = mesh.shape["ctx"] // 2, mesh.shape["shard"]
    if mesh.shape["ctx"] == HQ and HQ == 2 * HK and chips == planes == HK:
        return on_device_by_head
    return on_device


def solution(mesh):
    placed = (
        P("shard", "ctx", None),
        P(None, "shard"),
        P(None, "shard"),
        P(None, "shard"),
        P(None, "shard"),
        P(None, "shard"),
        P(None, "shard"),
        P(None, "shard"),
        P(),
        P(),
        P("shard", None),
        P("shard", None),
        P("shard", "ctx", None),
    )
    return jax.shard_map(
        plan_of(mesh),
        mesh=mesh,
        in_specs=placed,
        out_specs=(
            P("shard", "ctx", None),
            P("shard", "ctx", None),
            P(("ctx", "shard"), None),
            P(("ctx", "shard"), None),
            P(("ctx", "shard"), None),
            P(("ctx", "shard"), None),
            P(("ctx", "shard"), None),
            P(("ctx", "shard"), None),
            P(("ctx", "shard"), None),
            P(("ctx", "shard")),
            P(("ctx", "shard")),
        ),
        check_vma=False,
    )
```

```python
import math

import jax
import jax.numpy as jnp
from jax import lax
from jax.experimental import pallas as pl
from jax.experimental.pallas import tpu as pltpu
from jax.sharding import PartitionSpec as P

HQ = 8
HK = 4
HD = 256
WINDOW = 1024


EPSILON = 1e-06
SCORE_SCALE = 0.0625
MASKED = -1e30
ROPE_BASE = 1000042.0


def position_of(rows, pairs, per_device, blocks_total):
    device = rows // per_device
    within = rows % per_device
    half = per_device // 2
    chosen = jnp.take(pairs, device)
    first = chosen * half + within
    second = (blocks_total - 1 - chosen) * half + within - half
    return jnp.where(within < half, first, second)


def rope_tables(positions, head):
    half = head // 2
    freq = ROPE_BASE ** (-(jnp.arange(half, dtype=jnp.float32) * 2.0) / head)
    angle = positions.astype(jnp.float32)[:, None] * freq[None, :]
    return (jnp.cos(angle), jnp.sin(angle))


def rotate(values, cosine, sine):
    half = values.shape[-1] // 2
    first = values[..., :half]
    second = values[..., half:]
    cosine = cosine[:, None, :]
    sine = sine[:, None, :]
    return jnp.concatenate(
        [first * cosine - second * sine, second * cosine + first * sine], axis=-1
    )


def rotate_back(grads, cosine, sine):
    half = grads.shape[-1] // 2
    first = grads[..., :half]
    second = grads[..., half:]
    cosine = cosine[:, None, :]
    sine = sine[:, None, :]
    return jnp.concatenate(
        [first * cosine + second * sine, second * cosine - first * sine], axis=-1
    )


def visible(query_pos, query_doc, key_pos, key_doc):
    distance = query_pos[:, None] - key_pos[None, :]
    return (query_doc[:, None] == key_doc[None, :]) & (distance >= 0) & (distance < WINDOW)


def write_columns(left, piece):
    made = jnp.dot(left, piece, preferred_element_type=jnp.float32)
    return made


def contract_full(grads, weight):
    return lax.dot_general(
        grads, weight, (((1,), (1,)), ((), ())), preferred_element_type=jnp.float32
    )


def alternate(parts, shard_count, rows):
    return jnp.concatenate([part.reshape(rows, shard_count, -1) for part in parts], axis=2).reshape(
        rows, -1
    )


def outer_sum(left, right):
    return lax.dot_general(
        left, right, (((0,), (0,)), ((), ())), preferred_element_type=jnp.float32
    )


def term_rows(lefts, rights, gain_block, count):
    normed_all, attended_all, second_all, act_all = lefts
    query_g, key_g, value_g, branch_g, gate_g, up_g, upstream_g = rights
    down_part = outer_sum(act_all, upstream_g).reshape(count, -1)
    return jnp.concatenate(
        [
            outer_sum(normed_all, query_g),
            outer_sum(normed_all, key_g),
            outer_sum(normed_all, value_g),
            outer_sum(attended_all, branch_g),
            outer_sum(second_all, gate_g),
            outer_sum(second_all, up_g),
            down_part,
            gain_block,
        ],
        axis=1,
    )


def deal_columns(values, ctx_count, shard_count):
    rows = values.shape[0]
    return (
        values.reshape(rows, ctx_count, shard_count, -1)
        .transpose(0, 2, 1, 3)
        .reshape(rows, shard_count, -1)
    )


def on_device(
    layer_input,
    w_query,
    w_key,
    w_value,
    w_out,
    w_gate,
    w_up,
    w_down,
    attn_gain,
    mlp_gain,
    block_pairs,
    doc_ids,
    cotangent,
):
    tok_rows = layer_input.shape[1]
    model_width = layer_input.shape[2]
    shard_count = lax.axis_size("shard")
    ctx_count = lax.axis_size("ctx")
    device_count = lax.axis_size(("ctx", "shard"))
    group_size = HQ // HK
    blocks_total = 2 * ctx_count
    pairs = block_pairs[0]
    documents = doc_ids[0]
    own_rows = lax.axis_index("ctx") * tok_rows + jnp.arange(tok_rows, dtype=jnp.int32)
    own_pos = position_of(own_rows, pairs, tok_rows, blocks_total)
    own_doc = jnp.take(documents, own_pos)
    cosine, sine = rope_tables(own_pos, HD)
    stack_qkv = jnp.concatenate([w_query, w_key, w_value], axis=1)
    stack_mlp = jnp.concatenate([w_gate, w_up], axis=1)
    per_query = w_query.shape[1]
    per_key = w_key.shape[1]
    per_hidden = w_gate.shape[1]
    hidden_width = w_down.shape[0]
    inputs = layer_input.reshape(tok_rows, model_width).astype(jnp.float32)
    factor_one = lax.rsqrt(jnp.mean(inputs * inputs, axis=-1, keepdims=True) + EPSILON)
    normed = (inputs * factor_one * attn_gain).astype(jnp.bfloat16)
    projected = write_columns(normed, lax.all_gather(stack_qkv, "shard", axis=1, tiled=True))
    projected = projected.reshape(tok_rows, shard_count, -1)
    query_lin = projected[:, :, :per_query].reshape(tok_rows, HQ, HD)
    key_lin = projected[:, :, per_query : per_query + per_key].reshape(tok_rows, HK, HD)
    value_lin = projected[:, :, per_query + per_key :].reshape(tok_rows, HK * HD)
    query_rot = (
        rotate(query_lin, cosine, sine).astype(jnp.bfloat16).reshape(tok_rows, HK, group_size, HD)
    )
    key_rot = rotate(key_lin, cosine, sine).astype(jnp.bfloat16).reshape(tok_rows, HK * HD)
    value_low = value_lin.astype(jnp.bfloat16)

    def key_mask(first_row, count):
        key_pos = position_of(
            first_row + jnp.arange(count, dtype=jnp.int32), pairs, tok_rows, blocks_total
        )
        return visible(own_pos, own_doc, key_pos, jnp.take(documents, key_pos))[:, None, None, :]

    start_state = (
        jnp.full((tok_rows, HK, group_size), MASKED, jnp.float32),
        jnp.zeros((tok_rows, HK, group_size), jnp.float32),
        jnp.zeros((tok_rows, HK, group_size, HD), jnp.float32),
    )
    keys = lax.all_gather(key_rot, "ctx", axis=0, tiled=True)
    values = lax.all_gather(value_low, "ctx", axis=0, tiled=True)
    count = keys.shape[0]
    step = math.gcd(count, 4 * tok_rows)
    keys = keys.reshape(count // step, step, HK, HD)
    values = values.reshape(count // step, step, HK, HD)

    def attend_step(i, running):
        top, total, accum = running
        mask = key_mask(i * step, step)
        scores = (
            jnp.einsum("tkgd,skd->tkgs", query_rot, keys[i], preferred_element_type=jnp.float32)
            * SCORE_SCALE
        )
        scores = jnp.where(mask, scores, MASKED)
        new_top = jnp.maximum(top, jnp.max(scores, axis=-1))
        weights = jnp.where(mask, jnp.exp(scores - new_top[..., None]), 0.0)
        shrink = jnp.exp(top - new_top)
        total = total * shrink + jnp.sum(weights, axis=-1)
        accum = accum * shrink[..., None] + jnp.einsum(
            "tkgs,skd->tkgd",
            weights.astype(jnp.bfloat16),
            values[i],
            preferred_element_type=jnp.float32,
        )
        return (new_top, total, accum)

    top, total, accum = lax.fori_loop(0, count // step, attend_step, start_state)
    log_total = top + jnp.log(total)
    attended_full = accum / total[..., None]
    attended = attended_full.astype(jnp.bfloat16).reshape(tok_rows, HQ * HD)
    branch_one = write_columns(attended, lax.all_gather(w_out, "shard", axis=1, tiled=True))
    mid = inputs + branch_one
    factor_two = lax.rsqrt(jnp.mean(mid * mid, axis=-1, keepdims=True) + EPSILON)
    normed_two = (mid * factor_two * mlp_gain).astype(jnp.bfloat16)
    gate_up = write_columns(normed_two, lax.all_gather(stack_mlp, "shard", axis=1, tiled=True))
    gate_up = gate_up.reshape(tok_rows, shard_count, -1)
    gate = gate_up[:, :, :per_hidden].reshape(tok_rows, hidden_width)
    up_lin = gate_up[:, :, per_hidden:].reshape(tok_rows, hidden_width)
    sigma = jax.nn.sigmoid(gate)
    swish = gate * sigma
    act = (swish * up_lin).astype(jnp.bfloat16)
    branch_two = write_columns(act, lax.all_gather(w_down, "shard", axis=1, tiled=True))
    output = (mid + branch_two).astype(jnp.bfloat16).reshape(1, tok_rows, model_width)
    full_qkv, full_out, full_mlp, full_down = (
        lax.all_gather(stack_qkv, "shard", axis=1, tiled=True),
        lax.all_gather(w_out, "shard", axis=1, tiled=True),
        lax.all_gather(stack_mlp, "shard", axis=1, tiled=True),
        lax.all_gather(w_down, "shard", axis=1, tiled=True),
    )
    upstream_low = cotangent.reshape(tok_rows, model_width)
    upstream = upstream_low.astype(jnp.float32)
    act_grad = contract_full(upstream_low, full_down)
    gate_grad = (act_grad * up_lin * (sigma * (1.0 + gate * (1.0 - sigma)))).astype(jnp.bfloat16)
    up_grad = (act_grad * swish).astype(jnp.bfloat16)
    stacked_mlp_grad = alternate((gate_grad, up_grad), shard_count, tok_rows)
    norm_two_grad = contract_full(stacked_mlp_grad, full_mlp)
    mlp_gain_term = jnp.sum(norm_two_grad * mid * factor_two, axis=0)
    scaled_two = norm_two_grad * mlp_gain
    mid_grad = (
        upstream
        + factor_two * scaled_two
        - mid * factor_two**3 * jnp.mean(scaled_two * mid, axis=-1, keepdims=True)
    )
    branch_grad = mid_grad.astype(jnp.bfloat16)
    attended_grad = contract_full(branch_grad, full_out)
    attended_low = attended_grad.astype(jnp.bfloat16).reshape(tok_rows, HK, group_size, HD)
    delta = jnp.sum(attended_low.astype(jnp.float32) * attended_full, axis=-1)

    def query_grads(carry, piece):
        keys, values = piece
        count = keys.shape[0]
        step = math.gcd(count, 4 * tok_rows)
        keys = keys.reshape(count // step, step, HK, HD)
        values = values.reshape(count // step, step, HK, HD)

        def query_step(i, query_sum):
            mask = key_mask(i * step, step)
            scores = (
                jnp.einsum("tkgd,skd->tkgs", query_rot, keys[i], preferred_element_type=jnp.float32)
                * SCORE_SCALE
            )
            probs = jnp.where(mask, jnp.exp(scores - log_total[..., None]), 0.0)
            prob_grad = jnp.einsum(
                "tkgd,skd->tkgs", attended_low, values[i], preferred_element_type=jnp.float32
            )
            score_grad = (probs * (prob_grad - delta[..., None])).astype(jnp.bfloat16)
            return query_sum + jnp.einsum(
                "tkgs,skd->tkgd", score_grad, keys[i], preferred_element_type=jnp.float32
            )

        return lax.fori_loop(0, count // step, query_step, carry)

    query_sum = query_grads(
        jnp.zeros((tok_rows, HK, group_size, HD), jnp.float32),
        (
            lax.all_gather(key_rot, "ctx", axis=0, tiled=True),
            lax.all_gather(value_low, "ctx", axis=0, tiled=True),
        ),
    )
    all_log_total, all_delta = (
        lax.all_gather(log_total, "ctx", axis=0, tiled=True),
        lax.all_gather(delta, "ctx", axis=0, tiled=True),
    )
    key_three = key_rot.reshape(tok_rows, HK, HD)
    value_three = value_low.reshape(tok_rows, HK, HD)

    def key_grads(carry, piece):
        queries, outgrads = piece
        count = queries.shape[0]
        step = math.gcd(count, 4 * tok_rows)
        queries = queries.reshape(count // step, step, HK, group_size, HD)
        outgrads = outgrads.reshape(count // step, step, HK, group_size, HD)

        def key_step(i, running):
            key_sum, value_sum = running
            first_row = i * step
            query_pos = position_of(
                first_row + jnp.arange(step, dtype=jnp.int32), pairs, tok_rows, blocks_total
            )
            mask = visible(query_pos, jnp.take(documents, query_pos), own_pos, own_doc)[
                :, None, None, :
            ]
            lse_part = lax.dynamic_slice_in_dim(all_log_total, first_row, step, 0)
            delta_part = lax.dynamic_slice_in_dim(all_delta, first_row, step, 0)
            scores = (
                jnp.einsum(
                    "skgd,tkd->skgt", queries[i], key_three, preferred_element_type=jnp.float32
                )
                * SCORE_SCALE
            )
            probs = jnp.where(mask, jnp.exp(scores - lse_part[..., None]), 0.0)
            prob_grad = jnp.einsum(
                "skgd,tkd->skgt", outgrads[i], value_three, preferred_element_type=jnp.float32
            )
            score_grad = (probs * (prob_grad - delta_part[..., None])).astype(jnp.bfloat16)
            value_sum = value_sum + jnp.einsum(
                "skgt,skgd->tkd",
                probs.astype(jnp.bfloat16),
                outgrads[i],
                preferred_element_type=jnp.float32,
            )
            key_sum = key_sum + jnp.einsum(
                "skgt,skgd->tkd", score_grad, queries[i], preferred_element_type=jnp.float32
            )
            return (key_sum, value_sum)

        return lax.fori_loop(0, count // step, key_step, carry)

    key_sum, value_sum = key_grads(
        (jnp.zeros((tok_rows, HK, HD), jnp.float32), jnp.zeros((tok_rows, HK, HD), jnp.float32)),
        (
            lax.all_gather(query_rot.reshape(tok_rows, HQ * HD), "ctx", axis=0, tiled=True),
            lax.all_gather(attended_low.reshape(tok_rows, HQ * HD), "ctx", axis=0, tiled=True),
        ),
    )
    query_grad = (
        rotate_back(query_sum.reshape(tok_rows, HQ, HD) * SCORE_SCALE, cosine, sine)
        .astype(jnp.bfloat16)
        .reshape(tok_rows, HQ * HD)
    )
    key_grad = (
        rotate_back(key_sum * SCORE_SCALE, cosine, sine)
        .astype(jnp.bfloat16)
        .reshape(tok_rows, HK * HD)
    )
    value_grad = value_sum.astype(jnp.bfloat16).reshape(tok_rows, HK * HD)
    stacked_qkv_grad = alternate((query_grad, key_grad, value_grad), shard_count, tok_rows)
    normed_grad = contract_full(stacked_qkv_grad, full_qkv)
    attn_gain_term = jnp.sum(normed_grad * inputs * factor_one, axis=0)
    scaled_one = normed_grad * attn_gain
    input_grad = (
        mid_grad
        + factor_one * scaled_one
        - inputs * factor_one**3 * jnp.mean(scaled_one * inputs, axis=-1, keepdims=True)
    )
    grad_input = input_grad.astype(jnp.bfloat16).reshape(1, tok_rows, model_width)
    ratio = hidden_width // model_width
    own_share = model_width // device_count
    rights = (query_grad, key_grad, value_grad, branch_grad, gate_grad, up_grad, upstream_low)
    group_rights = (
        lax.all_gather(rights[0], "shard", axis=0, tiled=True),
        lax.all_gather(rights[1], "shard", axis=0, tiled=True),
        lax.all_gather(rights[2], "shard", axis=0, tiled=True),
        lax.all_gather(rights[3], "shard", axis=0, tiled=True),
        lax.all_gather(rights[4], "shard", axis=0, tiled=True),
        lax.all_gather(rights[5], "shard", axis=0, tiled=True),
        lax.all_gather(rights[6], "shard", axis=0, tiled=True),
    )
    dealt = (
        lax.all_to_all(
            deal_columns(normed, ctx_count, shard_count),
            "shard",
            split_axis=1,
            concat_axis=0,
            tiled=True,
        ),
        lax.all_to_all(
            deal_columns(attended, ctx_count, shard_count),
            "shard",
            split_axis=1,
            concat_axis=0,
            tiled=True,
        ),
        lax.all_to_all(
            deal_columns(normed_two, ctx_count, shard_count),
            "shard",
            split_axis=1,
            concat_axis=0,
            tiled=True,
        ),
        lax.all_to_all(
            deal_columns(act, ctx_count, shard_count),
            "shard",
            split_axis=1,
            concat_axis=0,
            tiled=True,
        ),
    )
    group_lefts = tuple((part.reshape(part.shape[0], -1) for part in dealt))
    gain_pair = lax.psum(jnp.stack([attn_gain_term, mlp_gain_term]), "shard")
    gain_mine = lax.dynamic_index_in_dim(
        gain_pair.reshape(2, ctx_count, shard_count, own_share),
        lax.axis_index("shard"),
        2,
        keepdims=False,
    ).reshape(2, ctx_count * own_share)
    gain_block = jnp.concatenate(
        [gain_mine.T, jnp.zeros((ctx_count * own_share, 126), jnp.float32)], axis=1
    )
    summed = lax.psum_scatter(
        term_rows(group_lefts, group_rights, gain_block, own_share * lax.axis_size("ctx")).astype(
            jnp.bfloat16
        ),
        "ctx",
        scatter_dimension=0,
        tiled=True,
    ).astype(jnp.float32)
    edge_one = HQ * HD
    edge_two = edge_one + HK * HD
    edge_three = edge_two + HK * HD
    edge_four = edge_three + model_width
    edge_five = edge_four + hidden_width
    edge_six = edge_five + hidden_width
    edge_seven = edge_six + ratio * model_width
    grad_query = summed[:, :edge_one]
    grad_key = summed[:, edge_one:edge_two]
    grad_value = summed[:, edge_two:edge_three]
    grad_out = summed[:, edge_three:edge_four]
    grad_gate = summed[:, edge_four:edge_five]
    grad_up = summed[:, edge_five:edge_six]
    grad_down = summed[:, edge_six:edge_seven].reshape(own_share * ratio, model_width)
    grad_attn_gain = summed[:, edge_seven]
    grad_mlp_gain = summed[:, edge_seven + 1]
    return (
        output,
        grad_input,
        grad_query,
        grad_key,
        grad_value,
        grad_out,
        grad_gate,
        grad_up,
        grad_down,
        grad_attn_gain,
        grad_mlp_gain,
    )


DOCS = 4
BF16 = jnp.bfloat16
F32 = jnp.float32
VISIBLE_ROWS = 256


def dot_nn(a, b):
    return jnp.dot(a, b, preferred_element_type=F32)


def dot_nt(a, b):
    return lax.dot_general(a, b, (((1,), (1,)), ((), ())), preferred_element_type=F32)


def dot_tn(a, b):
    return lax.dot_general(a, b, (((0,), (0,)), ((), ())), preferred_element_type=F32)


def scores_of(query, key, code, low_code, key_code):
    scores = dot_nt(query, key) * SCORE_SCALE
    mask = (key_code <= code) & (key_code >= low_code)
    return jnp.where(mask, scores, MASKED)


MESH = pl.DeviceIdType.MESH
TILE = 256
WIDE = 512


def flip(i, d):
    return (i, i + 1 - 2 * (i % 2), (i + 2) % 4, 3 - i)[d]


def line_gather(remote, ctx, plane, slot, own, place):
    def copy(i, way, block, source):
        to = plane + way
        return remote(
            slot + 2 * i + (way + 1) // 2, source, place(to, block), (ctx, to), slot + block
        )

    def sends(i):
        if i == 0:
            return [(plane < 3, lambda: copy(0, 1, plane, own)), (plane > 0, lambda: copy(0, -1, plane, own))]
        return [
            (
                jnp.logical_and(plane >= i, plane < 3),
                lambda: copy(i, 1, plane - i, place(plane, plane - i)),
            ),
            (
                jnp.logical_and(plane + i <= 3, plane > 0),
                lambda: copy(i, -1, plane + i, place(plane, plane + i)),
            ),
        ]

    def start(i):
        for whether, made in sends(i):

            @pl.when(whether)
            def _(made=made):
                made().start()

    def step(i, then=None):
        for whether, block in ((plane >= i, plane - i), (plane + i <= 3, plane + i)):

            @pl.when(whether)
            def _(block=block):
                remote(slot, own, place(plane, block), (ctx, plane), slot + block).wait_recv()
                if then is not None:
                    then(block)

        if i < 3:
            start(i)

    def finish():
        for i in range(3):
            for whether, made in sends(i):

                @pl.when(whether)
                def _(made=made):
                    made().wait_send()

    return start, step, finish


def xor4(a, b):
    return 2 * ((a // 2 + b // 2) % 2) + (a % 2 + b % 2) % 2


def mlp_kernel(
    second_ref,
    mid_ref,
    upstream_ref,
    gain_ref,
    upstream_hbm,
    gate_hbm,
    up_hbm,
    down_hbm,
    output_ref,
    mid_grad_ref,
    gain_grad_ref,
    branch_all,
    gate_up_sum,
    gate_up_send,
    down_terms,
    gate_w,
    up_w,
    down_w,
    upstream_all,
    second_all,
    act,
    gate_grad,
    up_grad,
    held,
    own_sum,
    pair_send,
    pair_recv,
    z_send,
    z_recv,
    first_recv,
    branch_low,
    staged,
    local_sem,
    staged_sem,
    send_sem,
    recv_sem,
):
    tok = second_ref.shape[0]
    pair = 2 * tok
    hidden = gate_w.shape[1]
    width = second_ref.shape[1]
    ctx, plane = lax.axis_index("ctx"), lax.axis_index("shard")
    chip, core = ctx // 2, ctx % 2
    sibling = (ctx + 1 - 2 * core, plane)
    over_z = [(ctx, flip(plane, d)) for d in range(4)]
    over_chips = [(2 * flip(chip, d) + core, plane) for d in range(4)]

    half = pl.ds(pl.multiple_of(core * hidden, hidden), hidden)
    loads = [
        pltpu.make_async_copy(upstream_hbm, upstream_all, local_sem.at[0]),
        pltpu.make_async_copy(down_hbm, down_w, local_sem.at[1]),
        pltpu.make_async_copy(gate_hbm.at[:, half], gate_w, local_sem.at[2]),
        pltpu.make_async_copy(up_hbm.at[:, half], up_w, local_sem.at[3]),
        pltpu.make_async_copy(second_ref, second_all.at[0, 0], local_sem.at[4]),
    ]
    for load in loads:
        load.start()

    barrier = pltpu.get_barrier_semaphore()
    partners = [sibling] + over_z[1:] + over_chips[1:]
    for partner in partners:
        pl.semaphore_signal(barrier, inc=1, device_id=partner, device_id_type=MESH)
    pl.semaphore_wait(barrier, len(partners))

    def remote(slot, source, target, device, recv=None):
        return pltpu.make_async_remote_copy(
            src_ref=source,
            dst_ref=target,
            send_sem=send_sem.at[slot],
            recv_sem=recv_sem.at[slot if recv is None else recv],
            device_id=device,
            device_id_type=MESH,
        )

    def send(slot, source, target, device):
        copy = remote(slot, source, target, device)
        copy.start()
        return copy

    start_line, step_line, finish_line = line_gather(
        remote, ctx, plane, 32, second_ref, lambda r, b: second_all.at[xor4(r, b), 0]
    )
    start_line(0)
    gather_pair = {0: send(0, second_ref, second_all.at[0, 1], sibling)}
    for load in loads:
        load.wait()

    def rows_of(d):
        return pl.ds(d * pair, pair)

    def forward(d):
        rows = rows_of(d)
        second = lambda: second_all[d].reshape(pair, width)

        def step(t, carry):
            at = pl.ds(pl.multiple_of(t * WIDE, WIDE), WIDE)
            act_grad = dot_nt(upstream_all[rows, :], down_w[at, :])
            gate = dot_nn(second(), gate_w[:, at])
            up_lin = dot_nn(second(), up_w[:, at])
            sigma = 1.0 / (1.0 + jnp.exp(-gate))
            swish = gate * sigma
            act[rows, at] = (swish * up_lin).astype(BF16)
            gate_grad[rows, at] = (
                act_grad * up_lin * (sigma * (1.0 + gate * (1.0 - sigma)))
            ).astype(BF16)
            up_grad[rows, at] = (act_grad * swish).astype(BF16)
            return carry

        lax.fori_loop(0, hidden // WIDE, step, 0)

    def give_pair(d, base, product):
        which = 0 if base == 7 else 1

        def step(t, carry):
            at = pl.ds(pl.multiple_of(t * WIDE, WIDE), WIDE)
            terms = product(at)
            held[d % 2, :, at] = terms[:tok]
            pair_send[which, d, :, at] = terms[tok:].astype(BF16)
            return carry

        lax.fori_loop(0, width // WIDE, step, 0)
        return send(base + d, pair_send.at[which, d], pair_recv.at[which, d], sibling)

    def give_plane(d, base, copy):
        which = 0 if base == 7 else 1
        copy.wait_recv()
        total = held[d % 2] + pair_recv[which, d].astype(F32)
        if d == 0:
            own_sum[which] = total
            return None
        z_send[which, d - 1] = total.astype(BF16)
        copy = remote(
            base + 3 + d, z_send.at[which, d - 1], z_recv.at[which, d - 1], over_z[d]
        )
        if which == 0 or d == 1:
            copy.start()
        return copy

    def back(d):
        rows = rows_of(d)
        return lambda at: dot_nt(gate_grad[rows, :], gate_w[at, :]) + dot_nt(
            up_grad[rows, :], up_w[at, :]
        )

    def onward(d):
        rows = rows_of(d)
        return lambda at: dot_nn(act[rows, :], down_w[:, at])

    pairs, planes = {}, {}
    for d in range(4):
        if d:
            planes[d - 1] = give_plane(d - 1, 7, pairs[d - 1])
            step_line(d)
            gather_pair[d] = send(
                3 + d, second_all.at[d, 0], second_all.at[d, 1], sibling
            )
        gather_pair[d].wait_recv()
        forward(d)
        pairs[d] = give_pair(d, 7, back(d))
    planes[3] = give_plane(3, 7, pairs[3])

    second_rows = second_all.reshape(8 * tok, width)
    block = 2 * TILE

    def terms(grads, d, target, first):
        for h in range(2):
            column = flip(chip, d) * block + h * TILE
            left = second_rows[:, pl.ds(pl.multiple_of(column, TILE), TILE)]
            target[pl.ds(first + h * TILE, TILE), :] = dot_tn(left, grads[...]).astype(BF16)

    terms(gate_grad, 1, up_w, 0)
    terms(gate_grad, 3, up_w, block)
    first_gate = send(28, up_w.at[pl.ds(0, 2 * block)], first_recv.at[0], over_chips[1])
    terms(up_grad, 2, up_w, 2 * block)
    terms(up_grad, 3, up_w, 3 * block)
    first_up = send(29, up_w.at[pl.ds(2 * block, 2 * block)], first_recv.at[1], over_chips[2])

    out_pairs, out_planes = {}, {}
    for d in range(4):
        out_pairs[d] = give_pair(d, 14, onward(d))
        if d:
            out_planes[d - 1] = give_plane(d - 1, 14, out_pairs[d - 1])
    out_planes[3] = give_plane(3, 14, out_pairs[3])

    terms(gate_grad, 2, gate_w, 2 * block)
    terms(up_grad, 1, gate_w, 3 * block)

    for d in (1, 2, 3):
        planes[d].wait_recv()
    for d in (2, 3):
        out_planes[d].start()
    chunk = 32
    gain = gain_ref[...]

    def mid_step(i, carry):
        at = pl.ds(pl.multiple_of(i * chunk, chunk), chunk)
        grad = own_sum[0, at, :]
        for d in range(3):
            grad = grad + z_recv[0, d, at, :].astype(F32)
        mid = mid_ref[at, :]
        factor = lax.rsqrt(jnp.mean(mid * mid, axis=-1, keepdims=True) + EPSILON)
        scaled = grad * gain
        mid_grad = (
            upstream_ref[at, :].astype(F32)
            + factor * scaled
            - mid * (factor * factor * factor * jnp.mean(scaled * mid, axis=-1, keepdims=True))
        )
        mid_grad_ref[at, :] = mid_grad
        branch_low[at, :] = mid_grad.astype(BF16)
        return carry + jnp.sum(grad * mid * factor, axis=0, keepdims=True)

    gain_grad_ref[...] = lax.fori_loop(0, tok // chunk, mid_step, jnp.zeros((1, width), F32))
    branch_chips = {
        d: send(20 + d, branch_low, branch_all.at[0, d], over_chips[d]) for d in (1, 2, 3)
    }
    branch_pairs = {0: send(24, branch_low, branch_all.at[1, 0], sibling)}
    keep = pltpu.make_async_copy(branch_low, branch_all.at[0, 0], local_sem.at[0])
    keep.start()

    def to_hbm(slot, target):
        return pltpu.make_async_copy(staged.at[slot], target, staged_sem.at[slot])

    def down_step(t):
        slot = t % 2
        target = down_terms.at[pl.ds(t * TILE, TILE)]
        if t > 1:
            to_hbm(slot, target).wait()
        left = act[:, pl.ds(t * TILE, TILE)]
        staged[slot] = dot_tn(left, upstream_all[...]).astype(BF16)
        to_hbm(slot, target).start()

    for t in range(hidden // TILE):
        down_step(t)
    terms(gate_grad, 0, gate_w, 0)
    terms(up_grad, 0, gate_w, block)
    for d in (1, 2, 3):
        branch_chips[d].wait_recv()
        branch_pairs[d] = send(24 + d, branch_all.at[0, d], branch_all.at[1, d], sibling)

    keep_second = [
        pltpu.make_async_copy(
            gate_w.at[pl.ds((2 + e) * block, block)], gate_up_send.at[e], local_sem.at[2 + e]
        )
        for e in range(2)
    ]

    def add_first(i, carry):
        here = pl.ds(pl.multiple_of(i * 64, 64), 64)
        for e in range(2):
            mine = pl.ds(pl.multiple_of((2 + e) * block + i * 64, 64), 64)
            far = pl.ds(pl.multiple_of(block + i * 64, 64), 64)
            gate_w[mine, :] = (
                gate_w[mine, :].astype(F32) + first_recv[e, far, :].astype(F32)
            ).astype(BF16)
            own = gate_w[pl.ds(pl.multiple_of(e * block + i * 64, 64), 64), :].astype(F32)
            down_w[here, pl.ds(e * hidden, hidden)] = (
                own + first_recv[e, here, :].astype(F32)
            ).astype(BF16)
        return carry

    first_gate.wait_recv()
    first_up.wait_recv()
    lax.fori_loop(0, block // 64, add_first, 0)
    keep_sum = pltpu.make_async_copy(down_w.at[pl.ds(0, block)], gate_up_sum, local_sem.at[1])
    for copy in (keep_sum, *keep_second):
        copy.start()

    for d in (1, 2, 3):
        out_planes[d].wait_recv()

    def out_step(i, carry):
        at = pl.ds(pl.multiple_of(i * chunk, chunk), chunk)
        total = mid_ref[at, :] + own_sum[1, at, :]
        for d in range(3):
            total = total + z_recv[1, d, at, :].astype(F32)
        output_ref[at, :] = total.astype(BF16)
        return carry

    lax.fori_loop(0, tok // chunk, out_step, 0)

    for d in range(4):
        branch_pairs[d].wait_recv()
        for copy in (gather_pair[d], pairs[d], out_pairs[d], branch_pairs[d]):
            copy.wait_send()
    for d in (1, 2, 3):
        for copy in (planes[d], out_planes[d], branch_chips[d]):
            copy.wait_send()
    finish_line()
    keep.wait()
    for slot in range(2):
        to_hbm(slot, down_terms.at[pl.ds(0, TILE)]).wait()
    first_gate.wait_send()
    first_up.wait_send()
    for copy in (keep_sum, *keep_second):
        copy.wait()


def mlp_of(normed_two, mid, upstream, gain, upstream_group, w_gate, w_up, down_rows):
    tok, width = mid.shape
    hidden = down_rows.shape[0]
    rows = upstream_group.shape[0]
    vmem = pl.BlockSpec(memory_space=pltpu.VMEM)
    hbm = pl.BlockSpec(memory_space=pl.ANY)
    return pl.pallas_call(
        mlp_kernel,
        in_specs=[vmem] * 4 + [hbm] * 4,
        out_specs=[vmem] * 3 + [hbm] * 4,
        out_shape=[
            jax.ShapeDtypeStruct((tok, width), BF16),
            jax.ShapeDtypeStruct((tok, width), F32),
            jax.ShapeDtypeStruct((1, width), F32),
            jax.ShapeDtypeStruct((2, 4, tok, width), BF16),
            jax.ShapeDtypeStruct((2 * TILE, 2 * hidden), BF16),
            jax.ShapeDtypeStruct((2, 2 * TILE, hidden), BF16),
            jax.ShapeDtypeStruct((hidden, width), BF16),
        ],
        scratch_shapes=[
            pltpu.VMEM((width, hidden), BF16),
            pltpu.VMEM((width, hidden), BF16),
            pltpu.VMEM((hidden, width), BF16),
            pltpu.VMEM((rows, width), BF16),
            pltpu.VMEM((4, 2, tok, width), BF16),
            pltpu.VMEM((rows, hidden), BF16),
            pltpu.VMEM((rows, hidden), BF16),
            pltpu.VMEM((rows, hidden), BF16),
            pltpu.VMEM((2, tok, width), F32),
            pltpu.VMEM((2, tok, width), F32),
            pltpu.VMEM((2, 4, tok, width), BF16),
            pltpu.VMEM((2, 4, tok, width), BF16),
            pltpu.VMEM((2, 3, tok, width), BF16),
            pltpu.VMEM((2, 3, tok, width), BF16),
            pltpu.VMEM((2, 4 * TILE, hidden), BF16),
            pltpu.VMEM((tok, width), BF16),
            pltpu.VMEM((2, TILE, width), BF16),
            pltpu.SemaphoreType.DMA((5,)),
            pltpu.SemaphoreType.DMA((2,)),
            pltpu.SemaphoreType.DMA((38,)),
            pltpu.SemaphoreType.DMA((38,)),
        ],
        compiler_params=pltpu.CompilerParams(
            collective_id=1, has_side_effects=True, vmem_limit_bytes=60 << 20
        ),
        cost_estimate=pl.CostEstimate(
            flops=18 * rows * width * hidden,
            bytes_accessed=2 * (5 * width * hidden + 4 * rows * width),
            transcendentals=rows * hidden,
        ),
    )(normed_two, mid, upstream, gain, upstream_group, w_gate, w_up, down_rows)


def rotated(values, cosine, sine):
    half = values.shape[1] // 2
    first, second = values[:, :half], values[:, half:]
    return jnp.concatenate([first * cosine - second * sine, second * cosine + first * sine], axis=1)


def front_kernel(
    input_ref,
    attn_gain_ref,
    mlp_gain_ref,
    cosine_ref,
    sine_ref,
    code_ref,
    low_code_ref,
    key_code_ref,
    query_hbm,
    key_hbm,
    value_hbm,
    out_hbm,
    down_hbm,
    upstream_hbm,
    second_ref,
    mid_ref,
    normed_hbm,
    query_ref,
    kv_ref,
    attended_ref,
    log_total_ref,
    head_hbm,
    w_sibling,
    out_hbm_rows,
    down_rows,
    upstream_all,
    normed_ref,
    w_head,
    out_pair,
    inputs_all,
    w_parts,
    attended_other,
    own_sum,
    chip_send,
    chip_recv,
    local_sem,
    send_sem,
    recv_sem,
):
    tok, width = input_ref.shape
    quarter = width // 4
    shard = out_hbm.shape[1]
    hidden = down_rows.shape[0]
    part = hidden // 4
    seq = 8 * tok
    half_seq = 4 * tok
    ctx, plane = lax.axis_index("ctx"), lax.axis_index("shard")
    chip, core = ctx // 2, ctx % 2
    sibling = (ctx + 1 - 2 * core, plane)
    over_z = [(ctx, flip(plane, d)) for d in range(4)]
    over_chips = [(2 * flip(chip, d) + core, plane) for d in range(4)]
    others = (1, 2, 3)

    def at(i, size):
        return pl.ds(pl.multiple_of(i * size, size), size)

    def remote(slot, source, target, device, recv=None):
        return pltpu.make_async_remote_copy(
            src_ref=source,
            dst_ref=target,
            send_sem=send_sem.at[slot],
            recv_sem=recv_sem.at[slot if recv is None else recv],
            device_id=device,
            device_id_type=MESH,
        )

    def send(slot, source, target, device):
        copy = remote(slot, source, target, device)
        copy.start()
        return copy

    def local(slot, source, target):
        return pltpu.make_async_copy(source, target, local_sem.at[slot])

    rows = at(chip, quarter)
    mine = w_parts.at[plane]
    load_query = local(0, query_hbm.at[rows, at(core, HD)], mine.at[0])
    load_key = local(1, key_hbm.at[rows], mine.at[1])
    load_value = local(1, value_hbm.at[rows], mine.at[1])
    load_query.start()

    @pl.when(core == 0)
    def _():
        load_key.start()

    @pl.when(core == 1)
    def _():
        load_value.start()

    keep_input = local(2, input_ref, inputs_all.at[0, 0])
    keep_input.start()
    out_own = out_hbm.at[at(ctx, HD), :]
    keep_out = local(3, out_own, out_pair.at[0, :, at(plane, shard)])
    keep_out.start()

    def down_block(to_plane):
        first = to_plane * (2 * hidden) + core * hidden + chip * part
        return down_hbm.at[pl.ds(pl.multiple_of(first, part), part), :]

    def down_place(column):
        return down_rows.at[at(chip, part), at(column, shard)]

    first_own = plane * (2 * hidden) + core * hidden
    keep_down = local(
        4,
        down_hbm.at[pl.ds(pl.multiple_of(first_own, hidden), hidden), :],
        down_rows.at[:, at(plane, shard)],
    )
    keep_down.start()
    keep_upstream = local(5, upstream_hbm, upstream_all.at[0, 0])
    keep_upstream.start()

    barrier = pltpu.get_barrier_semaphore()
    partners = [sibling] + over_z[1:] + over_chips[1:]
    for partner in partners:
        pl.semaphore_signal(barrier, inc=1, device_id=partner, device_id_type=MESH)
    pl.semaphore_wait(barrier, len(partners))

    input_chips = {
        d: send(d - 1, input_ref, inputs_all.at[0, d], over_chips[d]) for d in others
    }
    input_pairs = {0: send(3, input_ref, inputs_all.at[1, 0], sibling)}
    load_query.wait()
    load_key.wait()
    start_head, step_head, finish_head = line_gather(
        remote, ctx, plane, 37, mine, lambda r, b: w_parts.at[b]
    )
    start_out, step_out, finish_out = line_gather(
        remote, ctx, plane, 43, out_own, lambda r, b: out_pair.at[0, :, at(b, shard)]
    )
    start_up, step_up, finish_up = line_gather(
        remote, ctx, plane, 49, upstream_hbm, lambda r, b: upstream_all.at[xor4(r, b), 0]
    )
    start_head(0)

    head_rows = w_head.at[:, rows, :]

    def pass_head(source):
        apart = xor4(chip, source)
        block = w_parts.at[source]

        @pl.when(apart == 0)
        def _():
            local(6, block, head_rows).start()

        @pl.when(apart != 0)
        def _():
            remote(9 + apart, block, head_rows, (2 * source + core, plane)).start()

    pass_head(plane)
    chunk = 32
    attn_gain = attn_gain_ref[...]

    def norm(e, d):
        def step(i, carry):
            block = inputs_all[e, d, at(i, chunk), :].astype(F32)
            factor = lax.rsqrt(jnp.mean(block * block, axis=-1, keepdims=True) + EPSILON)
            first = (4 * e + d) * tok + i * chunk
            normed_ref[pl.ds(pl.multiple_of(first, chunk), chunk), :] = (
                block * factor * attn_gain
            ).astype(BF16)
            return carry

        lax.fori_loop(0, tok // chunk, step, 0)

    keep_input.wait()
    norm(0, 0)
    step_head(1, pass_head)
    input_pairs[0].wait_recv()
    norm(1, 0)
    for d in (1, 2):
        input_chips[d].wait_recv()
        input_pairs[d] = send(3 + d, inputs_all.at[0, d], inputs_all.at[1, d], sibling)
    norm(0, 1)
    norm(0, 2)
    step_head(2, pass_head)
    input_chips[3].wait_recv()
    input_pairs[3] = send(6, inputs_all.at[0, 3], inputs_all.at[1, 3], sibling)
    norm(0, 3)
    for d in others:
        input_pairs[d].wait_recv()
        norm(1, d)
    step_head(3, pass_head)

    start_out(0)
    down_z = {
        d: send(16 + d, down_block(flip(plane, d)), down_place(plane), over_z[d]) for d in others
    }
    keep_normed = local(2, normed_ref, normed_hbm)
    keep_normed.start()
    local(6, mine, head_rows).wait()
    for d in others:
        remote(9 + d, mine, head_rows, over_chips[d]).wait_recv()

    def project(which, target, flat):
        def step(t, carry):
            here = at(t, TILE)
            made = dot_nn(normed_ref[here, :], w_head[which])
            cosine, sine = cosine_ref[here, :], sine_ref[here, :]
            if flat:
                cosine = jnp.where(core == 0, cosine, 1.0)
                sine = jnp.where(core == 0, sine, 0.0)
            target[here, :] = rotated(made, cosine, sine).astype(BF16)
            return carry

        lax.fori_loop(0, seq // TILE, step, 0)

    keep_out.wait()

    def pass_out(source):
        columns = out_pair.at[0, :, at(source, shard)]
        remote(23 + source, columns, out_pair.at[1, :, at(source, shard)], sibling).start()

    pass_out(plane)
    step_out(1, pass_out)
    mine_kv = kv_ref.at[core]
    project(1, mine_kv, True)
    kv_pair = [
        send(20 + e, mine_kv.at[pl.ds(e * half_seq, half_seq)],
             mine_kv.at[pl.ds((1 - e) * half_seq, half_seq)], sibling)
        for e in range(2)
    ]
    project(0, query_ref, False)
    step_out(2, pass_out)
    head_pair = send(16, w_head, w_sibling, sibling)
    keep_head = local(6, w_head, head_hbm)
    keep_head.start()
    down_chips = {}
    for d in others:
        down_z[d].wait_recv()
        block = down_place(flip(plane, d))
        for e in others:
            down_chips[e, d] = send(51 + 3 * e + d, block, block, over_chips[e])
    for copy in kv_pair:
        copy.wait_recv()

    def attend_step(t, carry):
        here = at(t, TILE)
        scores = scores_of(
            query_ref[here, :], kv_ref[0], code_ref[here, :], low_code_ref[here, :], key_code_ref[...]
        )
        top = jnp.max(scores, axis=-1, keepdims=True)
        weights = jnp.exp(scores - top)
        total = jnp.sum(weights, axis=-1, keepdims=True)
        mixed = dot_nn(weights.astype(BF16), kv_ref[1])
        attended_ref[here, :] = (mixed / total).astype(BF16)
        log_total_ref[here, :] = top + jnp.log(total)
        return carry

    lax.fori_loop(0, seq // TILE, attend_step, 0)
    attended_pair = send(22, attended_ref.at[pl.ds(half_seq, half_seq)], attended_other, sibling)
    step_out(3, pass_out)
    start_up(0)
    for d in range(4):
        columns = out_pair.at[1, :, pl.ds(d * shard, shard)]
        remote(23 + d, columns, columns, sibling).wait_recv()
    keep_rows = local(3, out_pair.at[0], out_hbm_rows)
    keep_rows.start()
    attended_pair.wait_recv()

    def out_step(t, carry):
        here = at(t, TILE)
        terms = dot_nn(attended_ref[:half_seq, :], out_pair[0, :, here]) + dot_nn(
            attended_other[...], out_pair[1, :, here]
        )
        own_sum[:, here] = terms[:tok]
        for d in others:
            chip_send[d - 1, :, here] = terms[d * tok : (d + 1) * tok].astype(BF16)
        return carry

    lax.fori_loop(0, width // TILE, out_step, 0)
    branch = {
        d: send(26 + d, chip_send.at[d - 1], chip_recv.at[d - 1], over_chips[d]) for d in others
    }

    upstream_pair = {0: send(33, upstream_hbm, upstream_all.at[0, 1], sibling)}

    def pass_up(d):
        step_up(d)
        upstream_pair[d] = send(33 + d, upstream_all.at[d, 0], upstream_all.at[d, 1], sibling)

    pass_up(1)
    pass_up(2)
    for d in others:
        branch[d].wait_recv()
    mlp_gain = mlp_gain_ref[...]

    def mid_step(i, carry):
        here = at(i, chunk)
        mid = input_ref[here, :].astype(F32) + own_sum[here, :]
        for d in range(3):
            mid = mid + chip_recv[d, here, :].astype(F32)
        factor = lax.rsqrt(jnp.mean(mid * mid, axis=-1, keepdims=True) + EPSILON)
        mid_ref[here, :] = mid
        second_ref[here, :] = (mid * factor * mlp_gain).astype(BF16)
        return carry

    lax.fori_loop(0, tok // chunk, mid_step, 0)

    pass_up(3)
    keep_upstream.wait()
    for d in range(4):
        upstream_pair[d].wait_recv()
        upstream_pair[d].wait_send()
        input_pairs[d].wait_send()
    head_pair.wait_recv()
    for copy in (head_pair, attended_pair, *kv_pair):
        copy.wait_send()
    for copy in (keep_normed, keep_head, keep_rows):
        copy.wait()
    for d in range(4):
        columns = out_pair.at[0, :, pl.ds(d * shard, shard)]
        remote(23 + d, columns, columns, sibling).wait_send()
    keep_down.wait()
    for d in others:
        for e in others:
            down_chips[e, d].wait()
        for copies in (input_chips, down_z, branch):
            copies[d].wait_send()
        remote(9 + d, mine, head_rows, over_chips[d]).wait_send()
    finish_head()
    finish_out()
    finish_up()


def front_of(
    inputs, attn_gain, mlp_gain, cosine, sine, code, low_code, key_code,
    w_query, w_key, w_value, w_out, w_down, upstream,
):
    tok, width = inputs.shape
    seq = 8 * tok
    hidden = w_down.shape[0] // 8
    vmem = pl.BlockSpec(memory_space=pltpu.VMEM)
    hbm = pl.BlockSpec(memory_space=pl.ANY)
    return pl.pallas_call(
        front_kernel,
        in_specs=[vmem] * 8 + [hbm] * 6,
        out_specs=[vmem] * 2 + [hbm] + [vmem] * 4 + [hbm] * 5,
        out_shape=[
            jax.ShapeDtypeStruct((tok, width), BF16),
            jax.ShapeDtypeStruct((tok, width), F32),
            jax.ShapeDtypeStruct((seq, width), BF16),
            jax.ShapeDtypeStruct((seq, HD), BF16),
            jax.ShapeDtypeStruct((2, seq, HD), BF16),
            jax.ShapeDtypeStruct((seq, HD), BF16),
            jax.ShapeDtypeStruct((seq, 1), F32),
            jax.ShapeDtypeStruct((2, width, HD), BF16),
            jax.ShapeDtypeStruct((2, width, HD), BF16),
            jax.ShapeDtypeStruct((HD, width), BF16),
            jax.ShapeDtypeStruct((hidden, width), BF16),
            jax.ShapeDtypeStruct((4, 2, tok, width), BF16),
        ],
        scratch_shapes=[
            pltpu.VMEM((seq, width), BF16),
            pltpu.VMEM((2, width, HD), BF16),
            pltpu.VMEM((2, HD, width), BF16),
            pltpu.VMEM((2, 4, tok, width), BF16),
            pltpu.VMEM((4, 2, width // 4, HD), BF16),
            pltpu.VMEM((4 * tok, HD), BF16),
            pltpu.VMEM((tok, width), F32),
            pltpu.VMEM((3, tok, width), BF16),
            pltpu.VMEM((3, tok, width), BF16),
            pltpu.SemaphoreType.DMA((7,)),
            pltpu.SemaphoreType.DMA((64,)),
            pltpu.SemaphoreType.DMA((64,)),
        ],
        compiler_params=pltpu.CompilerParams(
            collective_id=2, has_side_effects=True, vmem_limit_bytes=56 << 20
        ),
        cost_estimate=pl.CostEstimate(
            flops=2 * seq * width * 3 * HD + 4 * seq * seq * HD,
            bytes_accessed=20 * seq * width,
            transcendentals=seq * seq,
        ),
    )(
        inputs, attn_gain, mlp_gain, cosine, sine, code, low_code, key_code,
        w_query, w_key, w_value, w_out, w_down, upstream,
    )


def back_kernel(
    input_ref,
    mid_grad_ref,
    attn_gain_ref,
    mlp_gain_grad_ref,
    cosine_ref,
    sine_ref,
    code_ref,
    low_code_ref,
    key_code_ref,
    query_ref,
    kv_ref,
    attended_ref,
    log_total_ref,
    normed_hbm,
    head_hbm,
    sibling_hbm,
    out_rows_hbm,
    branch_hbm,
    gate_up_hbm,
    gate_up_send,
    down_terms,
    grad_input_ref,
    gain_total_ref,
    grad_out_ref,
    head_in,
    gate_up_in,
    down_in,
    normed_ref,
    w_head,
    w_sibling,
    out_rows_ref,
    branch_all,
    d_attended,
    d_head,
    d_other,
    d_kv,
    d_kv_other,
    out_send,
    out_recv,
    head_terms,
    head_recv,
    own_sum,
    chip_send,
    chip_recv,
    gate_up_sum,
    gate_up_recv,
    down_parts,
    down_sum,
    down_planes,
    gains,
    gains_z,
    gains_ctx,
    local_sem,
    send_sem,
    recv_sem,
):
    tok, width = input_ref.shape
    seq = 8 * tok
    half_seq = 4 * tok
    share = out_send.shape[1]
    ctx, plane = lax.axis_index("ctx"), lax.axis_index("shard")
    chip, core = ctx // 2, ctx % 2
    other_core = 1 - core
    sibling = (2 * chip + other_core, plane)
    over_z = [(ctx, flip(plane, d)) for d in range(4)]
    over_chips = [(2 * flip(chip, d) + core, plane) for d in range(4)]
    over_chips_cross = [(2 * flip(chip, d) + other_core, plane) for d in range(4)]
    over_z_cross = [(2 * chip + other_core, flip(plane, d)) for d in range(4)]
    others = (1, 2, 3)

    def at(i, size):
        return pl.ds(pl.multiple_of(i * size, size), size)

    def remote(slot, source, target, device):
        return pltpu.make_async_remote_copy(
            src_ref=source,
            dst_ref=target,
            send_sem=send_sem.at[slot],
            recv_sem=recv_sem.at[slot],
            device_id=device,
            device_id_type=MESH,
        )

    def send(slot, source, target, device):
        copy = remote(slot, source, target, device)
        copy.start()
        return copy

    def local(slot, source, target):
        return pltpu.make_async_copy(source, target, local_sem.at[slot])

    loads = [
        local(0, branch_hbm, branch_all),
        local(1, out_rows_hbm, out_rows_ref),
        local(2, normed_hbm, normed_ref),
        local(3, down_terms.at[:, chip], down_parts.at[0]),
        local(4, head_hbm, w_head),
        local(5, sibling_hbm, w_sibling),
        local(6, gate_up_hbm, gate_up_sum),
    ]
    for load in loads:
        load.start()

    barrier = pltpu.get_barrier_semaphore()
    partners = (
        over_z[1:] + over_z_cross + over_chips[1:] + over_chips_cross[1:]
    )
    for partner in partners:
        pl.semaphore_signal(barrier, inc=1, device_id=partner, device_id_type=MESH)
    pl.semaphore_wait(barrier, len(partners))

    down_chips = {
        d: send(d, down_terms.at[:, flip(chip, d)], down_parts.at[d], over_chips[d])
        for d in others
    }

    loads[0].wait()

    def out_step(t, carry):
        here = at(t, TILE)
        made = dot_tn(attended_ref[...], branch_all[:, here])
        out_send[:, :, here] = made.reshape(4, share, TILE).astype(BF16)
        return carry

    lax.fori_loop(0, width // TILE, out_step, 0)
    out_z = {
        d: send(3 + d, out_send.at[flip(plane, d)], out_recv.at[d - 1], over_z[d]) for d in others
    }

    loads[1].wait()

    def attended_step(t, carry):
        here = at(t, TILE)
        d_attended[here, :] = dot_nt(branch_all[here, :], out_rows_ref[...]).astype(BF16)
        return carry

    lax.fori_loop(0, seq // TILE, attended_step, 0)
    d_kv[...] = jnp.zeros_like(d_kv)

    def attend_step(t, carry):
        here = at(t, TILE)
        query, outgrad = query_ref[here, :], d_attended[here, :]
        scores = scores_of(
            query, kv_ref[0], code_ref[here, :], low_code_ref[here, :], key_code_ref[...]
        )
        probs = jnp.exp(scores - log_total_ref[here, :])
        prob_grad = dot_nt(outgrad, kv_ref[1])
        delta = jnp.sum(probs * prob_grad, axis=-1, keepdims=True)
        score_grad = (probs * (prob_grad - delta)).astype(BF16)
        d_query = dot_nn(score_grad, kv_ref[0]) * SCORE_SCALE
        d_head[here, :HD] = rotated(d_query, cosine_ref[here, :], -sine_ref[here, :]).astype(BF16)
        d_kv[0] += dot_tn(score_grad, query)
        d_kv[1] += dot_tn(probs.astype(BF16), outgrad)
        return carry

    lax.fori_loop(0, seq // TILE, attend_step, 0)

    give = d_kv.at[other_core]
    kv_pair = [
        send(
            7 + e,
            give.at[pl.ds(e * half_seq, half_seq)],
            d_kv_other.at[pl.ds((1 - e) * half_seq, half_seq)],
            sibling,
        )
        for e in range(2)
    ]
    for copy in kv_pair:
        copy.wait_recv()

    def kv_step(t, carry):
        here = at(t, TILE)
        total = d_kv[core, here, :] + d_kv_other[here, :]
        total = total * jnp.where(core == 0, SCORE_SCALE, 1.0)
        cosine = jnp.where(core == 0, cosine_ref[here, :], 1.0)
        sine = jnp.where(core == 0, sine_ref[here, :], 0.0)
        d_head[here, HD:] = rotated(total, cosine, -sine).astype(BF16)
        return carry

    lax.fori_loop(0, seq // TILE, kv_step, 0)
    head_pair = send(9, d_head.at[pl.ds(half_seq, half_seq)], d_other, sibling)

    loads[2].wait()

    def head_step(t, carry):
        made = dot_tn(normed_ref[:, at(t, TILE)], d_head[...])
        head_terms[:, t] = made.reshape(4, share, 2 * HD).astype(BF16)
        return carry

    lax.fori_loop(0, width // TILE, head_step, 0)
    head_z = {
        d: send(9 + d, head_terms.at[flip(plane, d)], head_recv.at[d - 1], over_z[d])
        for d in others
    }

    loads[4].wait()
    loads[5].wait()
    head_pair.wait_recv()

    def normed_step(t, carry):
        here = at(t, TILE)
        made = (
            dot_nt(d_head[:half_seq, :HD], w_head[0, here, :])
            + dot_nt(d_head[:half_seq, HD:], w_head[1, here, :])
            + dot_nt(d_other[:, :HD], w_sibling[0, here, :])
            + dot_nt(d_other[:, HD:], w_sibling[1, here, :])
        )
        own_sum[:, here] = made[:tok]
        for d in others:
            chip_send[d - 1, :, here] = made[d * tok : (d + 1) * tok].astype(BF16)
        return carry

    lax.fori_loop(0, width // TILE, normed_step, 0)
    normed_chips = {
        d: send(12 + d, chip_send.at[d - 1], chip_recv.at[d - 1], over_chips[d]) for d in others
    }

    loads[3].wait()
    for d in others:
        down_chips[d].wait_recv()

    def down_step(p, carry):
        total = down_parts[0, p].astype(F32)
        for d in others:
            total = total + down_parts[d, p].astype(F32)
        down_sum[p] = total.astype(BF16)
        return carry

    lax.fori_loop(0, 4, down_step, 0)
    for d in others:
        normed_chips[d].wait_recv()
    gate_second = send(0, gate_up_send.at[0], gate_up_recv.at[0], over_chips[2])
    up_second = send(46, gate_up_send.at[1], gate_up_recv.at[1], over_chips[1])
    chunk = 32
    gain = attn_gain_ref[...]

    def input_step(i, carry):
        here = at(i, chunk)
        grad = own_sum[here, :]
        for d in range(3):
            grad = grad + chip_recv[d, here, :].astype(F32)
        block = input_ref[here, :].astype(F32)
        factor = lax.rsqrt(jnp.mean(block * block, axis=-1, keepdims=True) + EPSILON)
        scaled = grad * gain
        grad_input_ref[here, :] = (
            mid_grad_ref[here, :]
            + factor * scaled
            - block * (factor * factor * factor * jnp.mean(scaled * block, axis=-1, keepdims=True))
        ).astype(BF16)
        return carry + jnp.sum(grad * block * factor, axis=0, keepdims=True)

    gain_grad = lax.fori_loop(0, tok // chunk, input_step, jnp.zeros((1, width), F32))
    gains[...] = jnp.concatenate(
        [gain_grad, mlp_gain_grad_ref[...], jnp.zeros((6, width), F32)], axis=0
    )
    gains_planes = {d: send(25 + d, gains, gains_z.at[d - 1], over_z[d]) for d in others}

    for d in others:
        head_z[d].wait_recv()
    down_z = {
        d: send(15 + d, down_sum.at[flip(plane, d)], down_planes.at[plane], over_z[d])
        for d in others
    }
    keep_down = local(3, down_sum.at[plane], down_planes.at[plane])
    keep_down.start()


    def head_sum(i, carry):
        total = head_terms[plane, i].astype(F32)
        for d in range(3):
            total = total + head_recv[d, i].astype(F32)
        head_terms[plane, i] = total.astype(BF16)
        return carry

    lax.fori_loop(0, 8, head_sum, 0)
    head_place = head_in.at[ctx]
    head_chips = {
        d: send(28 + d, head_terms.at[plane, 2 * flip(chip, d) + core], head_place, over_chips[d])
        for d in others
    }
    head_cross = {
        d: send(
            32 + d, head_terms.at[plane, 2 * flip(chip, d) + other_core], head_place,
            over_chips_cross[d],
        )
        for d in range(4)
    }
    keep_head = local(0, head_terms.at[plane, ctx], head_place)
    keep_head.start()

    for d in others:
        gains_planes[d].wait_recv()
        gains_planes[d].wait_send()
    gains[...] = gains[...] + gains_z[0] + gains_z[1] + gains_z[2]
    gains_chips = {
        d: send(35 + d, gains, gains_ctx.at[0, d], over_chips[d]) for d in others
    }
    gains_cross = {
        d: send(39 + d, gains, gains_ctx.at[1, d], over_chips_cross[d]) for d in range(4)
    }

    loads[6].wait()
    gate_second.wait_recv()
    up_second.wait_recv()
    hidden = gate_up_recv.shape[2]

    def gate_up_step(i, carry):
        here = at(i, share)
        for e in range(2):
            columns = pl.ds(e * hidden, hidden)
            gate_up_sum[here, columns] = (
                gate_up_sum[here, columns].astype(F32) + gate_up_recv[e, here, :].astype(F32)
            ).astype(BF16)
        return carry

    lax.fori_loop(0, 8, gate_up_step, 0)

    place = gate_up_in.at[plane, core]

    def gate_up_rows(to_core, to_plane):
        return gate_up_sum.at[at(4 * to_core + to_plane, share), :]

    gate_up_z = {
        d: send(18 + d, gate_up_rows(core, flip(plane, d)), place, over_z[d]) for d in others
    }
    gate_up_cross = {
        d: send(22 + d, gate_up_rows(other_core, flip(plane, d)), place, over_z_cross[d])
        for d in range(4)
    }
    keep_gate_up = local(1, gate_up_rows(core, plane), place)
    keep_gate_up.start()
    for d in others:
        out_z[d].wait_recv()
    total = out_send[plane].astype(F32)
    for d in range(3):
        total = total + out_recv[d].astype(F32)
    grad_out_ref[...] = total

    keep_down.wait()
    down_place = down_in.at[chip]
    for d in range(4):
        if d:
            down_z[d].wait_recv()
        source = flip(plane, d)
        apart = xor4(chip, source)
        block = down_planes.at[source]

        @pl.when(apart == 0)
        def _(block=block):
            local(4, block, down_place).start()

        @pl.when(apart != 0)
        def _(block=block, source=source, apart=apart):
            remote(42 + apart, block, down_place, (2 * source + core, plane)).start()

    for d in others:
        gains_chips[d].wait_recv()
    for d in range(4):
        gains_cross[d].wait_recv()
    total = gains[...] + gains_ctx[1, 0]
    for d in others:
        total = total + gains_ctx[0, d] + gains_ctx[1, d]
    gain_total_ref[...] = total

    local(4, down_sum.at[plane], down_place).wait()
    keep_gate_up.wait()
    keep_head.wait()
    for d in others:
        remote(42 + d, down_sum.at[plane], down_place, over_chips[d]).wait()
        gate_up_z[d].wait_recv()
        head_chips[d].wait_recv()
        for copies in (
            down_chips, out_z, head_z, normed_chips, down_z, gate_up_z, head_chips, gains_chips
        ):
            copies[d].wait_send()
    for d in range(4):
        for copies in (gate_up_cross, head_cross):
            copies[d].wait()
        gains_cross[d].wait_send()
    for copy in (gate_second, up_second, head_pair, *kv_pair):
        copy.wait_send()


def back_of(*operands):
    inputs, query = operands[0], operands[9]
    tok, width = inputs.shape
    seq = query.shape[0]
    hidden = operands[18].shape[-1] // 2
    share = HD // 4
    vmem = pl.BlockSpec(memory_space=pltpu.VMEM)
    hbm = pl.BlockSpec(memory_space=pl.ANY)
    return pl.pallas_call(
        back_kernel,
        in_specs=[vmem] * 13 + [hbm] * 8,
        out_specs=[vmem] * 6,
        out_shape=[
            jax.ShapeDtypeStruct((tok, width), BF16),
            jax.ShapeDtypeStruct((8, width), F32),
            jax.ShapeDtypeStruct((share, width), F32),
            jax.ShapeDtypeStruct((8, share, 2 * HD), BF16),
            jax.ShapeDtypeStruct((4, 2, share, 2 * hidden), BF16),
            jax.ShapeDtypeStruct((4, share, width), BF16),
        ],
        scratch_shapes=[
            pltpu.VMEM((seq, width), BF16),
            pltpu.VMEM((2, width, HD), BF16),
            pltpu.VMEM((2, width, HD), BF16),
            pltpu.VMEM((HD, width), BF16),
            pltpu.VMEM((seq, width), BF16),
            pltpu.VMEM((seq, HD), BF16),
            pltpu.VMEM((seq, 2 * HD), BF16),
            pltpu.VMEM((4 * tok, 2 * HD), BF16),
            pltpu.VMEM((2, seq, HD), F32),
            pltpu.VMEM((seq, HD), F32),
            pltpu.VMEM((4, share, width), BF16),
            pltpu.VMEM((3, share, width), BF16),
            pltpu.VMEM((4, 8, share, 2 * HD), BF16),
            pltpu.VMEM((3, 8, share, 2 * HD), BF16),
            pltpu.VMEM((tok, width), F32),
            pltpu.VMEM((3, tok, width), BF16),
            pltpu.VMEM((3, tok, width), BF16),
            pltpu.VMEM((8 * share, 2 * hidden), BF16),
            pltpu.VMEM((2, 8 * share, hidden), BF16),
            pltpu.VMEM((4, 4, share, width), BF16),
            pltpu.VMEM((4, share, width), BF16),
            pltpu.VMEM((4, share, width), BF16),
            pltpu.VMEM((8, width), F32),
            pltpu.VMEM((3, 8, width), F32),
            pltpu.VMEM((2, 4, 8, width), F32),
            pltpu.SemaphoreType.DMA((7,)),
            pltpu.SemaphoreType.DMA((47,)),
            pltpu.SemaphoreType.DMA((47,)),
        ],
        compiler_params=pltpu.CompilerParams(
            collective_id=3, has_side_effects=True, vmem_limit_bytes=60 << 20
        ),
        cost_estimate=pl.CostEstimate(
            flops=2 * seq * width * 6 * HD + 10 * seq * seq * HD,
            bytes_accessed=20 * seq * width,
            transcendentals=seq * seq,
        ),
    )(*operands)


def on_device_by_head(
    layer_input,
    w_query,
    w_key,
    w_value,
    w_out,
    w_gate,
    w_up,
    w_down,
    attn_gain,
    mlp_gain,
    block_pairs,
    doc_ids,
    cotangent,
):
    tok_rows, width = layer_input.shape[1:]
    planes = lax.axis_size("shard")
    ctx_count = lax.axis_size("ctx")
    chips = ctx_count // 2
    ctx, plane = lax.axis_index("ctx"), lax.axis_index("shard")
    chip, core = ctx // 2, ctx % 2
    seq_rows = tok_rows * ctx_count
    own_share = width // (planes * ctx_count)

    inputs_low = layer_input[0]
    pairs, documents = block_pairs[0], doc_ids[0]
    order = jnp.stack([(chip ^ d) * 2 + (core ^ e) for e in range(2) for d in range(chips)])
    chosen = jnp.sum(
        jnp.where(order[:, None] == jnp.arange(ctx_count)[None, :], pairs[None, :], 0), axis=1
    )[:, None]
    within = jnp.arange(tok_rows, dtype=jnp.int32)[None, :]
    block = tok_rows // 2
    positions = jnp.where(
        within < block, chosen * block, (2 * ctx_count - 1 - chosen) * block - block
    )
    positions = (positions + within).reshape(-1)
    begins = jnp.sum(documents[None, :] < jnp.arange(1, DOCS)[:, None], axis=1)
    document = jnp.sum((positions[None, :] >= begins[:, None]).astype(jnp.int32), axis=0)
    span = 2 * seq_rows
    doc_first = document * span
    code = doc_first + positions
    low_code = jnp.maximum(doc_first, code - (WINDOW - 1))
    code_column, low_column, code_row = code[:, None], low_code[:, None], code[None, :]
    cosine, sine = rope_tables(positions, HD)

    upstream_low = cotangent[0]
    (
        normed_two,
        mid,
        normed_all,
        query,
        key_value,
        attended,
        log_total,
        w_head,
        w_sibling,
        out_rows,
        down_rows,
        upstream_group,
    ) = front_of(
        inputs_low,
        attn_gain[None],
        mlp_gain[None],
        cosine,
        sine,
        code_column,
        low_column,
        code_row,
        w_query,
        w_key,
        w_value,
        w_out,
        w_down,
        upstream_low,
    )
    (
        output,
        mid_grad,
        mlp_gain_grad,
        branch_all,
        gate_up_sum,
        gate_up_send,
        down_terms,
    ) = mlp_of(
        normed_two,
        mid,
        upstream_low,
        mlp_gain[None],
        upstream_group.reshape(-1, width),
        w_gate,
        w_up,
        down_rows,
    )
    grad_input, gain_total, grad_out, head_in, gate_up_in, down_in = back_of(
        inputs_low,
        mid_grad,
        attn_gain[None],
        mlp_gain_grad,
        cosine,
        sine,
        code_column,
        low_column,
        code_row,
        query,
        key_value,
        attended,
        log_total,
        normed_all,
        w_head,
        w_sibling,
        out_rows,
        branch_all.reshape(seq_rows, width),
        gate_up_sum,
        gate_up_send,
        down_terms.reshape(planes, chips, -1, width),
    )
    hidden = gate_up_in.shape[-1] // 2
    gate_up = gate_up_in.astype(F32)
    columns = lambda parts: jnp.concatenate(parts, axis=1)
    grad_gate = columns([gate_up[p, e, :, :hidden] for p in range(planes) for e in range(2)])
    grad_up = columns([gate_up[p, e, :, hidden:] for p in range(planes) for e in range(2)])
    head = head_in.astype(F32)
    grad_query = columns([head[i, :, :HD] for i in range(ctx_count)])
    grad_key = columns([head[i, :, HD:] for i in range(0, ctx_count, 2)])
    grad_value = columns([head[i, :, HD:] for i in range(1, ctx_count, 2)])
    grad_down = down_in.astype(F32).reshape(-1, width)
    gains = lax.dynamic_slice(gain_total, (0, own_share * (planes * ctx + plane)), (2, own_share))
    return (
        output[None],
        grad_input[None],
        grad_query,
        grad_key,
        grad_value,
        grad_out,
        grad_gate,
        grad_up,
        grad_down,
        gains[0],
        gains[1],
    )


def plan_of(mesh):
    chips, planes = mesh.shape["ctx"] // 2, mesh.shape["shard"]
    if mesh.shape["ctx"] == HQ and HQ == 2 * HK and chips == planes == HK:
        return on_device_by_head
    return on_device


def solution(mesh):
    placed = (
        P("shard", "ctx", None),
        P(None, "shard"),
        P(None, "shard"),
        P(None, "shard"),
        P(None, "shard"),
        P(None, "shard"),
        P(None, "shard"),
        P(None, "shard"),
        P(),
        P(),
        P("shard", None),
        P("shard", None),
        P("shard", "ctx", None),
    )
    return jax.shard_map(
        plan_of(mesh),
        mesh=mesh,
        in_specs=placed,
        out_specs=(
            P("shard", "ctx", None),
            P("shard", "ctx", None),
            P(("ctx", "shard"), None),
            P(("ctx", "shard"), None),
            P(("ctx", "shard"), None),
            P(("ctx", "shard"), None),
            P(("ctx", "shard"), None),
            P(("ctx", "shard"), None),
            P(("ctx", "shard"), None),
            P(("ctx", "shard")),
            P(("ctx", "shard")),
        ),
        check_vma=False,
    )
```

```python
import math

import jax
import jax.numpy as jnp
from jax import lax
from jax.experimental import pallas as pl
from jax.experimental.pallas import tpu as pltpu
from jax.sharding import PartitionSpec as P

HQ = 8
HK = 4
HD = 256
WINDOW = 1024


EPSILON = 1e-06
SCORE_SCALE = 0.0625
MASKED = -1e30
ROPE_BASE = 1000042.0


def position_of(rows, pairs, per_device, blocks_total):
    device = rows // per_device
    within = rows % per_device
    half = per_device // 2
    chosen = jnp.take(pairs, device)
    first = chosen * half + within
    second = (blocks_total - 1 - chosen) * half + within - half
    return jnp.where(within < half, first, second)


def rope_tables(positions, head):
    half = head // 2
    freq = ROPE_BASE ** (-(jnp.arange(half, dtype=jnp.float32) * 2.0) / head)
    angle = positions.astype(jnp.float32)[:, None] * freq[None, :]
    return (jnp.cos(angle), jnp.sin(angle))


def rotate(values, cosine, sine):
    half = values.shape[-1] // 2
    first = values[..., :half]
    second = values[..., half:]
    cosine = cosine[:, None, :]
    sine = sine[:, None, :]
    return jnp.concatenate(
        [first * cosine - second * sine, second * cosine + first * sine], axis=-1
    )


def rotate_back(grads, cosine, sine):
    half = grads.shape[-1] // 2
    first = grads[..., :half]
    second = grads[..., half:]
    cosine = cosine[:, None, :]
    sine = sine[:, None, :]
    return jnp.concatenate(
        [first * cosine + second * sine, second * cosine - first * sine], axis=-1
    )


def visible(query_pos, query_doc, key_pos, key_doc):
    distance = query_pos[:, None] - key_pos[None, :]
    return (query_doc[:, None] == key_doc[None, :]) & (distance >= 0) & (distance < WINDOW)


def write_columns(left, piece):
    made = jnp.dot(left, piece, preferred_element_type=jnp.float32)
    return made


def contract_full(grads, weight):
    return lax.dot_general(
        grads, weight, (((1,), (1,)), ((), ())), preferred_element_type=jnp.float32
    )


def alternate(parts, shard_count, rows):
    return jnp.concatenate([part.reshape(rows, shard_count, -1) for part in parts], axis=2).reshape(
        rows, -1
    )


def outer_sum(left, right):
    return lax.dot_general(
        left, right, (((0,), (0,)), ((), ())), preferred_element_type=jnp.float32
    )


def term_rows(lefts, rights, gain_block, count):
    normed_all, attended_all, second_all, act_all = lefts
    query_g, key_g, value_g, branch_g, gate_g, up_g, upstream_g = rights
    down_part = outer_sum(act_all, upstream_g).reshape(count, -1)
    return jnp.concatenate(
        [
            outer_sum(normed_all, query_g),
            outer_sum(normed_all, key_g),
            outer_sum(normed_all, value_g),
            outer_sum(attended_all, branch_g),
            outer_sum(second_all, gate_g),
            outer_sum(second_all, up_g),
            down_part,
            gain_block,
        ],
        axis=1,
    )


def deal_columns(values, ctx_count, shard_count):
    rows = values.shape[0]
    return (
        values.reshape(rows, ctx_count, shard_count, -1)
        .transpose(0, 2, 1, 3)
        .reshape(rows, shard_count, -1)
    )


def on_device(
    layer_input,
    w_query,
    w_key,
    w_value,
    w_out,
    w_gate,
    w_up,
    w_down,
    attn_gain,
    mlp_gain,
    block_pairs,
    doc_ids,
    cotangent,
):
    tok_rows = layer_input.shape[1]
    model_width = layer_input.shape[2]
    shard_count = lax.axis_size("shard")
    ctx_count = lax.axis_size("ctx")
    device_count = lax.axis_size(("ctx", "shard"))
    group_size = HQ // HK
    blocks_total = 2 * ctx_count
    pairs = block_pairs[0]
    documents = doc_ids[0]
    own_rows = lax.axis_index("ctx") * tok_rows + jnp.arange(tok_rows, dtype=jnp.int32)
    own_pos = position_of(own_rows, pairs, tok_rows, blocks_total)
    own_doc = jnp.take(documents, own_pos)
    cosine, sine = rope_tables(own_pos, HD)
    stack_qkv = jnp.concatenate([w_query, w_key, w_value], axis=1)
    stack_mlp = jnp.concatenate([w_gate, w_up], axis=1)
    per_query = w_query.shape[1]
    per_key = w_key.shape[1]
    per_hidden = w_gate.shape[1]
    hidden_width = w_down.shape[0]
    inputs = layer_input.reshape(tok_rows, model_width).astype(jnp.float32)
    factor_one = lax.rsqrt(jnp.mean(inputs * inputs, axis=-1, keepdims=True) + EPSILON)
    normed = (inputs * factor_one * attn_gain).astype(jnp.bfloat16)
    projected = write_columns(normed, lax.all_gather(stack_qkv, "shard", axis=1, tiled=True))
    projected = projected.reshape(tok_rows, shard_count, -1)
    query_lin = projected[:, :, :per_query].reshape(tok_rows, HQ, HD)
    key_lin = projected[:, :, per_query : per_query + per_key].reshape(tok_rows, HK, HD)
    value_lin = projected[:, :, per_query + per_key :].reshape(tok_rows, HK * HD)
    query_rot = (
        rotate(query_lin, cosine, sine).astype(jnp.bfloat16).reshape(tok_rows, HK, group_size, HD)
    )
    key_rot = rotate(key_lin, cosine, sine).astype(jnp.bfloat16).reshape(tok_rows, HK * HD)
    value_low = value_lin.astype(jnp.bfloat16)

    def key_mask(first_row, count):
        key_pos = position_of(
            first_row + jnp.arange(count, dtype=jnp.int32), pairs, tok_rows, blocks_total
        )
        return visible(own_pos, own_doc, key_pos, jnp.take(documents, key_pos))[:, None, None, :]

    start_state = (
        jnp.full((tok_rows, HK, group_size), MASKED, jnp.float32),
        jnp.zeros((tok_rows, HK, group_size), jnp.float32),
        jnp.zeros((tok_rows, HK, group_size, HD), jnp.float32),
    )
    keys = lax.all_gather(key_rot, "ctx", axis=0, tiled=True)
    values = lax.all_gather(value_low, "ctx", axis=0, tiled=True)
    count = keys.shape[0]
    step = math.gcd(count, 4 * tok_rows)
    keys = keys.reshape(count // step, step, HK, HD)
    values = values.reshape(count // step, step, HK, HD)

    def attend_step(i, running):
        top, total, accum = running
        mask = key_mask(i * step, step)
        scores = (
            jnp.einsum("tkgd,skd->tkgs", query_rot, keys[i], preferred_element_type=jnp.float32)
            * SCORE_SCALE
        )
        scores = jnp.where(mask, scores, MASKED)
        new_top = jnp.maximum(top, jnp.max(scores, axis=-1))
        weights = jnp.where(mask, jnp.exp(scores - new_top[..., None]), 0.0)
        shrink = jnp.exp(top - new_top)
        total = total * shrink + jnp.sum(weights, axis=-1)
        accum = accum * shrink[..., None] + jnp.einsum(
            "tkgs,skd->tkgd",
            weights.astype(jnp.bfloat16),
            values[i],
            preferred_element_type=jnp.float32,
        )
        return (new_top, total, accum)

    top, total, accum = lax.fori_loop(0, count // step, attend_step, start_state)
    log_total = top + jnp.log(total)
    attended_full = accum / total[..., None]
    attended = attended_full.astype(jnp.bfloat16).reshape(tok_rows, HQ * HD)
    branch_one = write_columns(attended, lax.all_gather(w_out, "shard", axis=1, tiled=True))
    mid = inputs + branch_one
    factor_two = lax.rsqrt(jnp.mean(mid * mid, axis=-1, keepdims=True) + EPSILON)
    normed_two = (mid * factor_two * mlp_gain).astype(jnp.bfloat16)
    gate_up = write_columns(normed_two, lax.all_gather(stack_mlp, "shard", axis=1, tiled=True))
    gate_up = gate_up.reshape(tok_rows, shard_count, -1)
    gate = gate_up[:, :, :per_hidden].reshape(tok_rows, hidden_width)
    up_lin = gate_up[:, :, per_hidden:].reshape(tok_rows, hidden_width)
    sigma = jax.nn.sigmoid(gate)
    swish = gate * sigma
    act = (swish * up_lin).astype(jnp.bfloat16)
    branch_two = write_columns(act, lax.all_gather(w_down, "shard", axis=1, tiled=True))
    output = (mid + branch_two).astype(jnp.bfloat16).reshape(1, tok_rows, model_width)
    full_qkv, full_out, full_mlp, full_down = (
        lax.all_gather(stack_qkv, "shard", axis=1, tiled=True),
        lax.all_gather(w_out, "shard", axis=1, tiled=True),
        lax.all_gather(stack_mlp, "shard", axis=1, tiled=True),
        lax.all_gather(w_down, "shard", axis=1, tiled=True),
    )
    upstream_low = cotangent.reshape(tok_rows, model_width)
    upstream = upstream_low.astype(jnp.float32)
    act_grad = contract_full(upstream_low, full_down)
    gate_grad = (act_grad * up_lin * (sigma * (1.0 + gate * (1.0 - sigma)))).astype(jnp.bfloat16)
    up_grad = (act_grad * swish).astype(jnp.bfloat16)
    stacked_mlp_grad = alternate((gate_grad, up_grad), shard_count, tok_rows)
    norm_two_grad = contract_full(stacked_mlp_grad, full_mlp)
    mlp_gain_term = jnp.sum(norm_two_grad * mid * factor_two, axis=0)
    scaled_two = norm_two_grad * mlp_gain
    mid_grad = (
        upstream
        + factor_two * scaled_two
        - mid * factor_two**3 * jnp.mean(scaled_two * mid, axis=-1, keepdims=True)
    )
    branch_grad = mid_grad.astype(jnp.bfloat16)
    attended_grad = contract_full(branch_grad, full_out)
    attended_low = attended_grad.astype(jnp.bfloat16).reshape(tok_rows, HK, group_size, HD)
    delta = jnp.sum(attended_low.astype(jnp.float32) * attended_full, axis=-1)

    def query_grads(carry, piece):
        keys, values = piece
        count = keys.shape[0]
        step = math.gcd(count, 4 * tok_rows)
        keys = keys.reshape(count // step, step, HK, HD)
        values = values.reshape(count // step, step, HK, HD)

        def query_step(i, query_sum):
            mask = key_mask(i * step, step)
            scores = (
                jnp.einsum("tkgd,skd->tkgs", query_rot, keys[i], preferred_element_type=jnp.float32)
                * SCORE_SCALE
            )
            probs = jnp.where(mask, jnp.exp(scores - log_total[..., None]), 0.0)
            prob_grad = jnp.einsum(
                "tkgd,skd->tkgs", attended_low, values[i], preferred_element_type=jnp.float32
            )
            score_grad = (probs * (prob_grad - delta[..., None])).astype(jnp.bfloat16)
            return query_sum + jnp.einsum(
                "tkgs,skd->tkgd", score_grad, keys[i], preferred_element_type=jnp.float32
            )

        return lax.fori_loop(0, count // step, query_step, carry)

    query_sum = query_grads(
        jnp.zeros((tok_rows, HK, group_size, HD), jnp.float32),
        (
            lax.all_gather(key_rot, "ctx", axis=0, tiled=True),
            lax.all_gather(value_low, "ctx", axis=0, tiled=True),
        ),
    )
    all_log_total, all_delta = (
        lax.all_gather(log_total, "ctx", axis=0, tiled=True),
        lax.all_gather(delta, "ctx", axis=0, tiled=True),
    )
    key_three = key_rot.reshape(tok_rows, HK, HD)
    value_three = value_low.reshape(tok_rows, HK, HD)

    def key_grads(carry, piece):
        queries, outgrads = piece
        count = queries.shape[0]
        step = math.gcd(count, 4 * tok_rows)
        queries = queries.reshape(count // step, step, HK, group_size, HD)
        outgrads = outgrads.reshape(count // step, step, HK, group_size, HD)

        def key_step(i, running):
            key_sum, value_sum = running
            first_row = i * step
            query_pos = position_of(
                first_row + jnp.arange(step, dtype=jnp.int32), pairs, tok_rows, blocks_total
            )
            mask = visible(query_pos, jnp.take(documents, query_pos), own_pos, own_doc)[
                :, None, None, :
            ]
            lse_part = lax.dynamic_slice_in_dim(all_log_total, first_row, step, 0)
            delta_part = lax.dynamic_slice_in_dim(all_delta, first_row, step, 0)
            scores = (
                jnp.einsum(
                    "skgd,tkd->skgt", queries[i], key_three, preferred_element_type=jnp.float32
                )
                * SCORE_SCALE
            )
            probs = jnp.where(mask, jnp.exp(scores - lse_part[..., None]), 0.0)
            prob_grad = jnp.einsum(
                "skgd,tkd->skgt", outgrads[i], value_three, preferred_element_type=jnp.float32
            )
            score_grad = (probs * (prob_grad - delta_part[..., None])).astype(jnp.bfloat16)
            value_sum = value_sum + jnp.einsum(
                "skgt,skgd->tkd",
                probs.astype(jnp.bfloat16),
                outgrads[i],
                preferred_element_type=jnp.float32,
            )
            key_sum = key_sum + jnp.einsum(
                "skgt,skgd->tkd", score_grad, queries[i], preferred_element_type=jnp.float32
            )
            return (key_sum, value_sum)

        return lax.fori_loop(0, count // step, key_step, carry)

    key_sum, value_sum = key_grads(
        (jnp.zeros((tok_rows, HK, HD), jnp.float32), jnp.zeros((tok_rows, HK, HD), jnp.float32)),
        (
            lax.all_gather(query_rot.reshape(tok_rows, HQ * HD), "ctx", axis=0, tiled=True),
            lax.all_gather(attended_low.reshape(tok_rows, HQ * HD), "ctx", axis=0, tiled=True),
        ),
    )
    query_grad = (
        rotate_back(query_sum.reshape(tok_rows, HQ, HD) * SCORE_SCALE, cosine, sine)
        .astype(jnp.bfloat16)
        .reshape(tok_rows, HQ * HD)
    )
    key_grad = (
        rotate_back(key_sum * SCORE_SCALE, cosine, sine)
        .astype(jnp.bfloat16)
        .reshape(tok_rows, HK * HD)
    )
    value_grad = value_sum.astype(jnp.bfloat16).reshape(tok_rows, HK * HD)
    stacked_qkv_grad = alternate((query_grad, key_grad, value_grad), shard_count, tok_rows)
    normed_grad = contract_full(stacked_qkv_grad, full_qkv)
    attn_gain_term = jnp.sum(normed_grad * inputs * factor_one, axis=0)
    scaled_one = normed_grad * attn_gain
    input_grad = (
        mid_grad
        + factor_one * scaled_one
        - inputs * factor_one**3 * jnp.mean(scaled_one * inputs, axis=-1, keepdims=True)
    )
    grad_input = input_grad.astype(jnp.bfloat16).reshape(1, tok_rows, model_width)
    ratio = hidden_width // model_width
    own_share = model_width // device_count
    rights = (query_grad, key_grad, value_grad, branch_grad, gate_grad, up_grad, upstream_low)
    group_rights = (
        lax.all_gather(rights[0], "shard", axis=0, tiled=True),
        lax.all_gather(rights[1], "shard", axis=0, tiled=True),
        lax.all_gather(rights[2], "shard", axis=0, tiled=True),
        lax.all_gather(rights[3], "shard", axis=0, tiled=True),
        lax.all_gather(rights[4], "shard", axis=0, tiled=True),
        lax.all_gather(rights[5], "shard", axis=0, tiled=True),
        lax.all_gather(rights[6], "shard", axis=0, tiled=True),
    )
    dealt = (
        lax.all_to_all(
            deal_columns(normed, ctx_count, shard_count),
            "shard",
            split_axis=1,
            concat_axis=0,
            tiled=True,
        ),
        lax.all_to_all(
            deal_columns(attended, ctx_count, shard_count),
            "shard",
            split_axis=1,
            concat_axis=0,
            tiled=True,
        ),
        lax.all_to_all(
            deal_columns(normed_two, ctx_count, shard_count),
            "shard",
            split_axis=1,
            concat_axis=0,
            tiled=True,
        ),
        lax.all_to_all(
            deal_columns(act, ctx_count, shard_count),
            "shard",
            split_axis=1,
            concat_axis=0,
            tiled=True,
        ),
    )
    group_lefts = tuple((part.reshape(part.shape[0], -1) for part in dealt))
    gain_pair = lax.psum(jnp.stack([attn_gain_term, mlp_gain_term]), "shard")
    gain_mine = lax.dynamic_index_in_dim(
        gain_pair.reshape(2, ctx_count, shard_count, own_share),
        lax.axis_index("shard"),
        2,
        keepdims=False,
    ).reshape(2, ctx_count * own_share)
    gain_block = jnp.concatenate(
        [gain_mine.T, jnp.zeros((ctx_count * own_share, 126), jnp.float32)], axis=1
    )
    summed = lax.psum_scatter(
        term_rows(group_lefts, group_rights, gain_block, own_share * lax.axis_size("ctx")).astype(
            jnp.bfloat16
        ),
        "ctx",
        scatter_dimension=0,
        tiled=True,
    ).astype(jnp.float32)
    edge_one = HQ * HD
    edge_two = edge_one + HK * HD
    edge_three = edge_two + HK * HD
    edge_four = edge_three + model_width
    edge_five = edge_four + hidden_width
    edge_six = edge_five + hidden_width
    edge_seven = edge_six + ratio * model_width
    grad_query = summed[:, :edge_one]
    grad_key = summed[:, edge_one:edge_two]
    grad_value = summed[:, edge_two:edge_three]
    grad_out = summed[:, edge_three:edge_four]
    grad_gate = summed[:, edge_four:edge_five]
    grad_up = summed[:, edge_five:edge_six]
    grad_down = summed[:, edge_six:edge_seven].reshape(own_share * ratio, model_width)
    grad_attn_gain = summed[:, edge_seven]
    grad_mlp_gain = summed[:, edge_seven + 1]
    return (
        output,
        grad_input,
        grad_query,
        grad_key,
        grad_value,
        grad_out,
        grad_gate,
        grad_up,
        grad_down,
        grad_attn_gain,
        grad_mlp_gain,
    )


DOCS = 4
BF16 = jnp.bfloat16
F32 = jnp.float32
VISIBLE_ROWS = 256


def dot_nn(a, b):
    return jnp.dot(a, b, preferred_element_type=F32)


def dot_nt(a, b):
    return lax.dot_general(a, b, (((1,), (1,)), ((), ())), preferred_element_type=F32)


def dot_tn(a, b):
    return lax.dot_general(a, b, (((0,), (0,)), ((), ())), preferred_element_type=F32)


def scores_of(query, key, code, low_code, key_code):
    scores = dot_nt(query, key) * SCORE_SCALE
    mask = (key_code <= code) & (key_code >= low_code)
    return jnp.where(mask, scores, MASKED)


MESH = pl.DeviceIdType.MESH
TILE = 256
WIDE = 512


def flip(i, d):
    return (i, i + 1 - 2 * (i % 2), (i + 2) % 4, 3 - i)[d]


def line_gather(remote, ctx, plane, slot, own, place):
    def copy(i, way, block, source):
        to = plane + way
        return remote(
            slot + 2 * i + (way + 1) // 2, source, place(to, block), (ctx, to), slot + block
        )

    def sends(i):
        if i == 0:
            return [(plane < 3, lambda: copy(0, 1, plane, own)), (plane > 0, lambda: copy(0, -1, plane, own))]
        return [
            (
                jnp.logical_and(plane >= i, plane < 3),
                lambda: copy(i, 1, plane - i, place(plane, plane - i)),
            ),
            (
                jnp.logical_and(plane + i <= 3, plane > 0),
                lambda: copy(i, -1, plane + i, place(plane, plane + i)),
            ),
        ]

    def start(i):
        for whether, made in sends(i):

            @pl.when(whether)
            def _(made=made):
                made().start()

    def step(i, then=None):
        for whether, block in ((plane >= i, plane - i), (plane + i <= 3, plane + i)):

            @pl.when(whether)
            def _(block=block):
                remote(slot, own, place(plane, block), (ctx, plane), slot + block).wait_recv()
                if then is not None:
                    then(block)

        if i < 3:
            start(i)

    def finish():
        for i in range(3):
            for whether, made in sends(i):

                @pl.when(whether)
                def _(made=made):
                    made().wait_send()

    return start, step, finish


def line_sum(remote, over_z, plane, slot, own, recv, add):
    is_end = jnp.logical_or(plane == 0, plane == 3)
    is_inner = jnp.logical_and(plane > 0, plane < 3)

    def near():
        return remote(slot, own(1), recv.at[0], over_z[1])

    def through(u):
        return remote(slot + 1 + u, own(2 + u), recv.at[2 + u], over_z[1])

    def far(u):
        return remote(slot + 3 + u, own(3 - u), recv.at[1], over_z[3 - u], slot + 3)

    def start():
        @pl.when(is_end)
        def _():
            for u in range(2):
                through(u).start()

        near().start()

    def pass_on():
        @pl.when(is_inner)
        def _():
            for u in range(2):
                through(u).wait_recv()
                add(3 - u, 2 + u)
                far(u).start()

    def wait():
        near().wait_recv()
        far(0).wait_recv()

    def finish():
        near().wait_send()

        @pl.when(is_end)
        def _():
            for u in range(2):
                through(u).wait_send()

        @pl.when(is_inner)
        def _():
            for u in range(2):
                far(u).wait_send()

    return start, pass_on, wait, finish


def xor4(a, b):
    return 2 * ((a // 2 + b // 2) % 2) + (a % 2 + b % 2) % 2


def mlp_kernel(
    second_ref,
    mid_ref,
    upstream_ref,
    gain_ref,
    upstream_hbm,
    gate_hbm,
    up_hbm,
    down_hbm,
    output_ref,
    mid_grad_ref,
    gain_grad_ref,
    branch_all,
    gate_up_sum,
    gate_up_send,
    down_terms,
    gate_w,
    up_w,
    down_w,
    upstream_all,
    second_all,
    act,
    gate_grad,
    up_grad,
    held,
    own_sum,
    pair_send,
    pair_recv,
    z_send,
    z_recv,
    first_recv,
    branch_low,
    staged,
    local_sem,
    staged_sem,
    send_sem,
    recv_sem,
):
    tok = second_ref.shape[0]
    pair = 2 * tok
    hidden = gate_w.shape[1]
    width = second_ref.shape[1]
    ctx, plane = lax.axis_index("ctx"), lax.axis_index("shard")
    chip, core = ctx // 2, ctx % 2
    sibling = (ctx + 1 - 2 * core, plane)
    over_z = [(ctx, flip(plane, d)) for d in range(4)]
    over_chips = [(2 * flip(chip, d) + core, plane) for d in range(4)]

    half = pl.ds(pl.multiple_of(core * hidden, hidden), hidden)
    loads = [
        pltpu.make_async_copy(upstream_hbm, upstream_all, local_sem.at[0]),
        pltpu.make_async_copy(down_hbm, down_w, local_sem.at[1]),
        pltpu.make_async_copy(gate_hbm.at[:, half], gate_w, local_sem.at[2]),
        pltpu.make_async_copy(up_hbm.at[:, half], up_w, local_sem.at[3]),
        pltpu.make_async_copy(second_ref, second_all.at[0, 0], local_sem.at[4]),
    ]
    for load in loads:
        load.start()

    barrier = pltpu.get_barrier_semaphore()
    partners = [sibling] + over_z[1:] + over_chips[1:]
    for partner in partners:
        pl.semaphore_signal(barrier, inc=1, device_id=partner, device_id_type=MESH)
    pl.semaphore_wait(barrier, len(partners))

    def remote(slot, source, target, device, recv=None):
        return pltpu.make_async_remote_copy(
            src_ref=source,
            dst_ref=target,
            send_sem=send_sem.at[slot],
            recv_sem=recv_sem.at[slot if recv is None else recv],
            device_id=device,
            device_id_type=MESH,
        )

    def send(slot, source, target, device):
        copy = remote(slot, source, target, device)
        copy.start()
        return copy

    start_line, step_line, finish_line = line_gather(
        remote, ctx, plane, 32, second_ref, lambda r, b: second_all.at[xor4(r, b), 0]
    )
    start_line(0)
    gather_pair = {0: send(0, second_ref, second_all.at[0, 1], sibling)}
    for load in loads:
        load.wait()

    def rows_of(d):
        return pl.ds(d * pair, pair)

    def forward(d):
        rows = rows_of(d)
        second = lambda: second_all[d].reshape(pair, width)

        def step(t, carry):
            at = pl.ds(pl.multiple_of(t * WIDE, WIDE), WIDE)
            act_grad = dot_nt(upstream_all[rows, :], down_w[at, :])
            gate = dot_nn(second(), gate_w[:, at])
            up_lin = dot_nn(second(), up_w[:, at])
            sigma = 1.0 / (1.0 + jnp.exp(-gate))
            swish = gate * sigma
            act[rows, at] = (swish * up_lin).astype(BF16)
            gate_grad[rows, at] = (
                act_grad * up_lin * (sigma * (1.0 + gate * (1.0 - sigma)))
            ).astype(BF16)
            up_grad[rows, at] = (act_grad * swish).astype(BF16)
            return carry

        lax.fori_loop(0, hidden // WIDE, step, 0)

    def give_pair(d, base, product):
        which = 0 if base == 7 else 1

        def step(t, carry):
            at = pl.ds(pl.multiple_of(t * WIDE, WIDE), WIDE)
            terms = product(at)
            held[d % 2, :, at] = terms[:tok]
            pair_send[which, d, :, at] = terms[tok:].astype(BF16)
            return carry

        lax.fori_loop(0, width // WIDE, step, 0)
        return send(base + d, pair_send.at[which, d], pair_recv.at[which, d], sibling)

    def give_plane(d, base, copy):
        which = 0 if base == 7 else 1
        copy.wait_recv()
        total = held[d % 2] + pair_recv[which, d].astype(F32)
        if d == 0:
            own_sum[which] = total
            return None
        z_send[which, d - 1] = total.astype(BF16)
        copy = remote(
            base + 3 + d, z_send.at[which, d - 1], z_recv.at[which, d - 1], over_z[d]
        )
        if which == 0:
            copy.start()
        return copy

    def back(d):
        rows = rows_of(d)
        return lambda at: dot_nt(gate_grad[rows, :], gate_w[at, :]) + dot_nt(
            up_grad[rows, :], up_w[at, :]
        )

    def onward(d):
        rows = rows_of(d)
        return lambda at: dot_nn(act[rows, :], down_w[:, at])

    pairs, planes = {}, {}
    for d in range(4):
        if d:
            planes[d - 1] = give_plane(d - 1, 7, pairs[d - 1])
            step_line(d)
            gather_pair[d] = send(
                3 + d, second_all.at[d, 0], second_all.at[d, 1], sibling
            )
        gather_pair[d].wait_recv()
        forward(d)
        pairs[d] = give_pair(d, 7, back(d))
    planes[3] = give_plane(3, 7, pairs[3])

    second_rows = second_all.reshape(8 * tok, width)
    block = 2 * TILE

    def terms(grads, d, target, first):
        for h in range(2):
            column = flip(chip, d) * block + h * TILE
            left = second_rows[:, pl.ds(pl.multiple_of(column, TILE), TILE)]
            target[pl.ds(first + h * TILE, TILE), :] = dot_tn(left, grads[...]).astype(BF16)

    terms(gate_grad, 1, up_w, 0)
    terms(gate_grad, 3, up_w, block)
    first_gate = send(28, up_w.at[pl.ds(0, 2 * block)], first_recv.at[0], over_chips[1])
    terms(up_grad, 2, up_w, 2 * block)
    terms(up_grad, 3, up_w, 3 * block)
    first_up = send(29, up_w.at[pl.ds(2 * block, 2 * block)], first_recv.at[1], over_chips[2])

    out_pairs, out_planes = {}, {}
    for d in range(4):
        out_pairs[d] = give_pair(d, 14, onward(d))
        if d:
            out_planes[d - 1] = give_plane(d - 1, 14, out_pairs[d - 1])
    out_planes[3] = give_plane(3, 14, out_pairs[3])

    def add_out(d, i):
        def step(t, carry):
            at = pl.ds(pl.multiple_of(t * 32, 32), 32)
            z_send[1, d - 1, at, :] = (
                z_send[1, d - 1, at, :].astype(F32) + z_recv[1, i, at, :].astype(F32)
            ).astype(BF16)
            return carry

        lax.fori_loop(0, tok // 32, step, 0)

    start_sum, pass_sum, wait_sum, finish_sum = line_sum(
        remote, over_z, plane, 38, lambda d: z_send.at[1, d - 1], z_recv.at[1], add_out
    )
    start_sum()

    terms(gate_grad, 2, gate_w, 2 * block)
    terms(up_grad, 1, gate_w, 3 * block)

    for d in (1, 2, 3):
        planes[d].wait_recv()
    chunk = 32
    gain = gain_ref[...]

    def mid_step(i, carry):
        at = pl.ds(pl.multiple_of(i * chunk, chunk), chunk)
        grad = own_sum[0, at, :]
        for d in range(3):
            grad = grad + z_recv[0, d, at, :].astype(F32)
        mid = mid_ref[at, :]
        factor = lax.rsqrt(jnp.mean(mid * mid, axis=-1, keepdims=True) + EPSILON)
        scaled = grad * gain
        mid_grad = (
            upstream_ref[at, :].astype(F32)
            + factor * scaled
            - mid * (factor * factor * factor * jnp.mean(scaled * mid, axis=-1, keepdims=True))
        )
        mid_grad_ref[at, :] = mid_grad
        branch_low[at, :] = mid_grad.astype(BF16)
        return carry + jnp.sum(grad * mid * factor, axis=0, keepdims=True)

    gain_grad_ref[...] = lax.fori_loop(0, tok // chunk, mid_step, jnp.zeros((1, width), F32))
    branch_chips = {
        d: send(20 + d, branch_low, branch_all.at[0, d], over_chips[d]) for d in (1, 2)
    }
    branch_pairs = {0: send(24, branch_low, branch_all.at[1, 0], sibling)}
    keep = pltpu.make_async_copy(branch_low, branch_all.at[0, 0], local_sem.at[0])
    keep.start()

    def to_hbm(slot, target):
        return pltpu.make_async_copy(staged.at[slot], target, staged_sem.at[slot])

    def down_step(t):
        slot = t % 2
        target = down_terms.at[pl.ds(t * TILE, TILE)]
        if t > 1:
            to_hbm(slot, target).wait()
        left = act[:, pl.ds(t * TILE, TILE)]
        staged[slot] = dot_tn(left, upstream_all[...]).astype(BF16)
        to_hbm(slot, target).start()

    for t in range(hidden // TILE):
        down_step(t)
    terms(gate_grad, 0, gate_w, 0)
    terms(up_grad, 0, gate_w, block)
    branch_far = {}
    for d in (1, 2):
        branch_chips[d].wait_recv()
        part = pl.ds((d - 1) * (tok // 2), tok // 2)
        branch_far[d] = send(
            23 + 20 * (d - 1), branch_all.at[0, d, part], branch_all.at[0, 3, part], over_chips[3 - d]
        )
        branch_pairs[d] = send(24 + d, branch_all.at[0, d], branch_all.at[1, d], sibling)
    pass_sum()
    for d in (1, 2):
        branch_far[d].wait_recv()
    branch_pairs[3] = send(27, branch_all.at[0, 3], branch_all.at[1, 3], sibling)

    keep_second = [
        pltpu.make_async_copy(
            gate_w.at[pl.ds((2 + e) * block, block)], gate_up_send.at[e], local_sem.at[2 + e]
        )
        for e in range(2)
    ]

    def add_first(i, carry):
        here = pl.ds(pl.multiple_of(i * 64, 64), 64)
        for e in range(2):
            mine = pl.ds(pl.multiple_of((2 + e) * block + i * 64, 64), 64)
            far = pl.ds(pl.multiple_of(block + i * 64, 64), 64)
            gate_w[mine, :] = (
                gate_w[mine, :].astype(F32) + first_recv[e, far, :].astype(F32)
            ).astype(BF16)
            own = gate_w[pl.ds(pl.multiple_of(e * block + i * 64, 64), 64), :].astype(F32)
            down_w[here, pl.ds(e * hidden, hidden)] = (
                own + first_recv[e, here, :].astype(F32)
            ).astype(BF16)
        return carry

    first_gate.wait_recv()
    first_up.wait_recv()
    lax.fori_loop(0, block // 64, add_first, 0)
    keep_sum = pltpu.make_async_copy(down_w.at[pl.ds(0, block)], gate_up_sum, local_sem.at[1])
    for copy in (keep_sum, *keep_second):
        copy.start()

    wait_sum()

    def out_step(i, carry):
        at = pl.ds(pl.multiple_of(i * chunk, chunk), chunk)
        total = mid_ref[at, :] + own_sum[1, at, :]
        for d in range(2):
            total = total + z_recv[1, d, at, :].astype(F32)
        output_ref[at, :] = total.astype(BF16)
        return carry

    lax.fori_loop(0, tok // chunk, out_step, 0)

    for d in range(4):
        branch_pairs[d].wait_recv()
        for copy in (gather_pair[d], pairs[d], out_pairs[d], branch_pairs[d]):
            copy.wait_send()
    for d in (1, 2, 3):
        planes[d].wait_send()
    for d in (1, 2):
        branch_chips[d].wait_send()
        branch_far[d].wait_send()
    finish_sum()
    finish_line()
    keep.wait()
    for slot in range(2):
        to_hbm(slot, down_terms.at[pl.ds(0, TILE)]).wait()
    first_gate.wait_send()
    first_up.wait_send()
    for copy in (keep_sum, *keep_second):
        copy.wait()


def mlp_of(normed_two, mid, upstream, gain, upstream_group, w_gate, w_up, down_rows):
    tok, width = mid.shape
    hidden = down_rows.shape[0]
    rows = upstream_group.shape[0]
    vmem = pl.BlockSpec(memory_space=pltpu.VMEM)
    hbm = pl.BlockSpec(memory_space=pl.ANY)
    return pl.pallas_call(
        mlp_kernel,
        in_specs=[vmem] * 4 + [hbm] * 4,
        out_specs=[vmem] * 3 + [hbm] * 4,
        out_shape=[
            jax.ShapeDtypeStruct((tok, width), BF16),
            jax.ShapeDtypeStruct((tok, width), F32),
            jax.ShapeDtypeStruct((1, width), F32),
            jax.ShapeDtypeStruct((2, 4, tok, width), BF16),
            jax.ShapeDtypeStruct((2 * TILE, 2 * hidden), BF16),
            jax.ShapeDtypeStruct((2, 2 * TILE, hidden), BF16),
            jax.ShapeDtypeStruct((hidden, width), BF16),
        ],
        scratch_shapes=[
            pltpu.VMEM((width, hidden), BF16),
            pltpu.VMEM((width, hidden), BF16),
            pltpu.VMEM((hidden, width), BF16),
            pltpu.VMEM((rows, width), BF16),
            pltpu.VMEM((4, 2, tok, width), BF16),
            pltpu.VMEM((rows, hidden), BF16),
            pltpu.VMEM((rows, hidden), BF16),
            pltpu.VMEM((rows, hidden), BF16),
            pltpu.VMEM((2, tok, width), F32),
            pltpu.VMEM((2, tok, width), F32),
            pltpu.VMEM((2, 4, tok, width), BF16),
            pltpu.VMEM((2, 4, tok, width), BF16),
            pltpu.VMEM((2, 3, tok, width), BF16),
            pltpu.VMEM((2, 4, tok, width), BF16),
            pltpu.VMEM((2, 4 * TILE, hidden), BF16),
            pltpu.VMEM((tok, width), BF16),
            pltpu.VMEM((2, TILE, width), BF16),
            pltpu.SemaphoreType.DMA((5,)),
            pltpu.SemaphoreType.DMA((2,)),
            pltpu.SemaphoreType.DMA((44,)),
            pltpu.SemaphoreType.DMA((44,)),
        ],
        compiler_params=pltpu.CompilerParams(
            collective_id=1, has_side_effects=True, vmem_limit_bytes=60 << 20
        ),
        cost_estimate=pl.CostEstimate(
            flops=18 * rows * width * hidden,
            bytes_accessed=2 * (5 * width * hidden + 4 * rows * width),
            transcendentals=rows * hidden,
        ),
    )(normed_two, mid, upstream, gain, upstream_group, w_gate, w_up, down_rows)


def rotated(values, cosine, sine):
    half = values.shape[1] // 2
    first, second = values[:, :half], values[:, half:]
    return jnp.concatenate([first * cosine - second * sine, second * cosine + first * sine], axis=1)


def front_kernel(
    input_ref,
    attn_gain_ref,
    mlp_gain_ref,
    cosine_ref,
    sine_ref,
    code_ref,
    low_code_ref,
    key_code_ref,
    query_hbm,
    key_hbm,
    value_hbm,
    out_hbm,
    down_hbm,
    upstream_hbm,
    second_ref,
    mid_ref,
    normed_hbm,
    query_ref,
    kv_ref,
    attended_ref,
    log_total_ref,
    head_hbm,
    w_sibling,
    out_hbm_rows,
    down_rows,
    upstream_all,
    normed_ref,
    w_head,
    out_pair,
    inputs_all,
    w_parts,
    attended_other,
    own_sum,
    chip_send,
    chip_recv,
    local_sem,
    send_sem,
    recv_sem,
):
    tok, width = input_ref.shape
    quarter = width // 4
    shard = out_hbm.shape[1]
    hidden = down_rows.shape[0]
    part = hidden // 4
    seq = 8 * tok
    half_seq = 4 * tok
    ctx, plane = lax.axis_index("ctx"), lax.axis_index("shard")
    chip, core = ctx // 2, ctx % 2
    sibling = (ctx + 1 - 2 * core, plane)
    over_z = [(ctx, flip(plane, d)) for d in range(4)]
    over_chips = [(2 * flip(chip, d) + core, plane) for d in range(4)]
    others = (1, 2, 3)

    def at(i, size):
        return pl.ds(pl.multiple_of(i * size, size), size)

    def remote(slot, source, target, device, recv=None):
        return pltpu.make_async_remote_copy(
            src_ref=source,
            dst_ref=target,
            send_sem=send_sem.at[slot],
            recv_sem=recv_sem.at[slot if recv is None else recv],
            device_id=device,
            device_id_type=MESH,
        )

    def send(slot, source, target, device):
        copy = remote(slot, source, target, device)
        copy.start()
        return copy

    def local(slot, source, target):
        return pltpu.make_async_copy(source, target, local_sem.at[slot])

    rows = at(chip, quarter)
    mine = w_parts.at[plane]
    load_query = local(0, query_hbm.at[rows, at(core, HD)], mine.at[0])
    load_key = local(1, key_hbm.at[rows], mine.at[1])
    load_value = local(1, value_hbm.at[rows], mine.at[1])
    load_query.start()

    @pl.when(core == 0)
    def _():
        load_key.start()

    @pl.when(core == 1)
    def _():
        load_value.start()

    keep_input = local(2, input_ref, inputs_all.at[0, 0])
    keep_input.start()
    out_own = out_hbm.at[at(ctx, HD), :]
    keep_out = local(3, out_own, out_pair.at[0, :, at(plane, shard)])
    keep_out.start()

    def down_block(to_plane):
        first = to_plane * (2 * hidden) + core * hidden + chip * part
        return down_hbm.at[pl.ds(pl.multiple_of(first, part), part), :]

    def down_place(column):
        return down_rows.at[at(chip, part), at(column, shard)]

    first_own = plane * (2 * hidden) + core * hidden
    keep_down = local(
        4,
        down_hbm.at[pl.ds(pl.multiple_of(first_own, hidden), hidden), :],
        down_rows.at[:, at(plane, shard)],
    )
    keep_down.start()
    keep_upstream = local(5, upstream_hbm, upstream_all.at[0, 0])
    keep_upstream.start()

    barrier = pltpu.get_barrier_semaphore()
    partners = [sibling] + over_z[1:] + over_chips[1:]
    for partner in partners:
        pl.semaphore_signal(barrier, inc=1, device_id=partner, device_id_type=MESH)
    pl.semaphore_wait(barrier, len(partners))

    input_chips = {
        d: send(d - 1, input_ref, inputs_all.at[0, d], over_chips[d]) for d in others
    }
    input_pairs = {0: send(3, input_ref, inputs_all.at[1, 0], sibling)}
    load_query.wait()
    load_key.wait()
    start_head, step_head, finish_head = line_gather(
        remote, ctx, plane, 37, mine, lambda r, b: w_parts.at[b]
    )
    start_out, step_out, finish_out = line_gather(
        remote, ctx, plane, 43, out_own, lambda r, b: out_pair.at[0, :, at(b, shard)]
    )
    start_up, step_up, finish_up = line_gather(
        remote, ctx, plane, 49, upstream_hbm, lambda r, b: upstream_all.at[xor4(r, b), 0]
    )
    start_head(0)

    head_rows = w_head.at[:, rows, :]

    def pass_head(source):
        apart = xor4(chip, source)
        block = w_parts.at[source]

        @pl.when(apart == 0)
        def _():
            local(6, block, head_rows).start()

        @pl.when(apart != 0)
        def _():
            remote(9 + apart, block, head_rows, (2 * source + core, plane)).start()

    pass_head(plane)
    chunk = 32
    attn_gain = attn_gain_ref[...]

    def norm(e, d):
        def step(i, carry):
            block = inputs_all[e, d, at(i, chunk), :].astype(F32)
            factor = lax.rsqrt(jnp.mean(block * block, axis=-1, keepdims=True) + EPSILON)
            first = (4 * e + d) * tok + i * chunk
            normed_ref[pl.ds(pl.multiple_of(first, chunk), chunk), :] = (
                block * factor * attn_gain
            ).astype(BF16)
            return carry

        lax.fori_loop(0, tok // chunk, step, 0)

    keep_input.wait()
    norm(0, 0)
    step_head(1, pass_head)
    input_pairs[0].wait_recv()
    norm(1, 0)
    for d in (1, 2):
        input_chips[d].wait_recv()
        input_pairs[d] = send(3 + d, inputs_all.at[0, d], inputs_all.at[1, d], sibling)
    norm(0, 1)
    norm(0, 2)
    step_head(2, pass_head)
    down_z = {
        d: send(16 + d, down_block(flip(plane, d)), down_place(plane), over_z[d]) for d in others
    }
    input_chips[3].wait_recv()
    input_pairs[3] = send(6, inputs_all.at[0, 3], inputs_all.at[1, 3], sibling)
    norm(0, 3)
    for d in others:
        input_pairs[d].wait_recv()
        norm(1, d)
    step_head(3, pass_head)

    start_out(0)
    keep_normed = local(2, normed_ref, normed_hbm)
    keep_normed.start()
    local(6, mine, head_rows).wait()
    for d in others:
        remote(9 + d, mine, head_rows, over_chips[d]).wait_recv()

    def project(which, target, flat):
        def step(t, carry):
            here = at(t, TILE)
            made = dot_nn(normed_ref[here, :], w_head[which])
            cosine, sine = cosine_ref[here, :], sine_ref[here, :]
            if flat:
                cosine = jnp.where(core == 0, cosine, 1.0)
                sine = jnp.where(core == 0, sine, 0.0)
            target[here, :] = rotated(made, cosine, sine).astype(BF16)
            return carry

        lax.fori_loop(0, seq // TILE, step, 0)

    keep_out.wait()

    def pass_out(source):
        columns = out_pair.at[0, :, at(source, shard)]
        remote(23 + source, columns, out_pair.at[1, :, at(source, shard)], sibling).start()

    pass_out(plane)
    step_out(1, pass_out)
    mine_kv = kv_ref.at[core]
    project(1, mine_kv, True)
    kv_pair = [
        send(20 + e, mine_kv.at[pl.ds(e * half_seq, half_seq)],
             mine_kv.at[pl.ds((1 - e) * half_seq, half_seq)], sibling)
        for e in range(2)
    ]
    project(0, query_ref, False)
    step_out(2, pass_out)
    head_pair = send(16, w_head, w_sibling, sibling)
    keep_head = local(6, w_head, head_hbm)
    keep_head.start()
    down_near, down_far = {}, {}
    half_part = part // 2

    def down_half(of_chip, column, second):
        first = of_chip * part + second * half_part
        return down_rows.at[
            pl.ds(pl.multiple_of(first, half_part), half_part), at(column, shard)
        ]

    for d in others:
        down_z[d].wait_recv()
        block = down_place(flip(plane, d))
        for e in (1, 2):
            down_near[e, d] = send(51 + 3 * e + d, block, block, over_chips[e])
    start_up(0)
    for copy in kv_pair:
        copy.wait_recv()

    def attend_step(t, carry):
        here = at(t, TILE)
        scores = scores_of(
            query_ref[here, :], kv_ref[0], code_ref[here, :], low_code_ref[here, :], key_code_ref[...]
        )
        top = jnp.max(scores, axis=-1, keepdims=True)
        weights = jnp.exp(scores - top)
        total = jnp.sum(weights, axis=-1, keepdims=True)
        mixed = dot_nn(weights.astype(BF16), kv_ref[1])
        attended_ref[here, :] = (mixed / total).astype(BF16)
        log_total_ref[here, :] = top + jnp.log(total)
        return carry

    lax.fori_loop(0, seq // TILE, attend_step, 0)
    attended_pair = send(22, attended_ref.at[pl.ds(half_seq, half_seq)], attended_other, sibling)
    step_out(3, pass_out)
    for d in range(4):
        columns = out_pair.at[1, :, pl.ds(d * shard, shard)]
        remote(23 + d, columns, columns, sibling).wait_recv()
    keep_rows = local(3, out_pair.at[0], out_hbm_rows)
    keep_rows.start()
    attended_pair.wait_recv()

    def out_step(t, carry):
        here = at(t, TILE)
        terms = dot_nn(attended_ref[:half_seq, :], out_pair[0, :, here]) + dot_nn(
            attended_other[...], out_pair[1, :, here]
        )
        own_sum[:, here] = terms[:tok]
        for d in others:
            chip_send[d - 1, :, here] = terms[d * tok : (d + 1) * tok].astype(BF16)
        return carry

    lax.fori_loop(0, width // TILE, out_step, 0)
    branch = {
        d: send(26 + d, chip_send.at[d - 1], chip_recv.at[d - 1], over_chips[d]) for d in others
    }

    for d in others:
        column = flip(plane, d)
        for e in (1, 2):
            down_near[e, d].wait_recv()
            block = down_half(flip(chip, e), column, e - 1)
            down_far[e, d] = send(57 + 3 * e + d, block, block, over_chips[3 - e])
    upstream_pair = {0: send(33, upstream_hbm, upstream_all.at[0, 1], sibling)}

    def pass_up(d):
        step_up(d)
        upstream_pair[d] = send(33 + d, upstream_all.at[d, 0], upstream_all.at[d, 1], sibling)

    pass_up(1)
    pass_up(2)
    for d in others:
        branch[d].wait_recv()
    mlp_gain = mlp_gain_ref[...]

    def mid_step(i, carry):
        here = at(i, chunk)
        mid = input_ref[here, :].astype(F32) + own_sum[here, :]
        for d in range(3):
            mid = mid + chip_recv[d, here, :].astype(F32)
        factor = lax.rsqrt(jnp.mean(mid * mid, axis=-1, keepdims=True) + EPSILON)
        mid_ref[here, :] = mid
        second_ref[here, :] = (mid * factor * mlp_gain).astype(BF16)
        return carry

    lax.fori_loop(0, tok // chunk, mid_step, 0)

    pass_up(3)
    keep_upstream.wait()
    for d in range(4):
        upstream_pair[d].wait_recv()
        upstream_pair[d].wait_send()
        input_pairs[d].wait_send()
    head_pair.wait_recv()
    for copy in (head_pair, attended_pair, *kv_pair):
        copy.wait_send()
    for copy in (keep_normed, keep_head, keep_rows):
        copy.wait()
    for d in range(4):
        columns = out_pair.at[0, :, pl.ds(d * shard, shard)]
        remote(23 + d, columns, columns, sibling).wait_send()
    keep_down.wait()
    for d in others:
        for e in (1, 2):
            down_near[e, d].wait_send()
            down_far[e, d].wait()
        for copies in (input_chips, down_z, branch):
            copies[d].wait_send()
        remote(9 + d, mine, head_rows, over_chips[d]).wait_send()
    finish_head()
    finish_out()
    finish_up()


def front_of(
    inputs, attn_gain, mlp_gain, cosine, sine, code, low_code, key_code,
    w_query, w_key, w_value, w_out, w_down, upstream,
):
    tok, width = inputs.shape
    seq = 8 * tok
    hidden = w_down.shape[0] // 8
    vmem = pl.BlockSpec(memory_space=pltpu.VMEM)
    hbm = pl.BlockSpec(memory_space=pl.ANY)
    return pl.pallas_call(
        front_kernel,
        in_specs=[vmem] * 8 + [hbm] * 6,
        out_specs=[vmem] * 2 + [hbm] + [vmem] * 4 + [hbm] * 5,
        out_shape=[
            jax.ShapeDtypeStruct((tok, width), BF16),
            jax.ShapeDtypeStruct((tok, width), F32),
            jax.ShapeDtypeStruct((seq, width), BF16),
            jax.ShapeDtypeStruct((seq, HD), BF16),
            jax.ShapeDtypeStruct((2, seq, HD), BF16),
            jax.ShapeDtypeStruct((seq, HD), BF16),
            jax.ShapeDtypeStruct((seq, 1), F32),
            jax.ShapeDtypeStruct((2, width, HD), BF16),
            jax.ShapeDtypeStruct((2, width, HD), BF16),
            jax.ShapeDtypeStruct((HD, width), BF16),
            jax.ShapeDtypeStruct((hidden, width), BF16),
            jax.ShapeDtypeStruct((4, 2, tok, width), BF16),
        ],
        scratch_shapes=[
            pltpu.VMEM((seq, width), BF16),
            pltpu.VMEM((2, width, HD), BF16),
            pltpu.VMEM((2, HD, width), BF16),
            pltpu.VMEM((2, 4, tok, width), BF16),
            pltpu.VMEM((4, 2, width // 4, HD), BF16),
            pltpu.VMEM((4 * tok, HD), BF16),
            pltpu.VMEM((tok, width), F32),
            pltpu.VMEM((3, tok, width), BF16),
            pltpu.VMEM((3, tok, width), BF16),
            pltpu.SemaphoreType.DMA((7,)),
            pltpu.SemaphoreType.DMA((67,)),
            pltpu.SemaphoreType.DMA((67,)),
        ],
        compiler_params=pltpu.CompilerParams(
            collective_id=2, has_side_effects=True, vmem_limit_bytes=56 << 20
        ),
        cost_estimate=pl.CostEstimate(
            flops=2 * seq * width * 3 * HD + 4 * seq * seq * HD,
            bytes_accessed=20 * seq * width,
            transcendentals=seq * seq,
        ),
    )(
        inputs, attn_gain, mlp_gain, cosine, sine, code, low_code, key_code,
        w_query, w_key, w_value, w_out, w_down, upstream,
    )


def back_kernel(
    input_ref,
    mid_grad_ref,
    attn_gain_ref,
    mlp_gain_grad_ref,
    cosine_ref,
    sine_ref,
    code_ref,
    low_code_ref,
    key_code_ref,
    query_ref,
    kv_ref,
    attended_ref,
    log_total_ref,
    normed_hbm,
    head_hbm,
    sibling_hbm,
    out_rows_hbm,
    branch_hbm,
    gate_up_hbm,
    gate_up_send,
    down_terms,
    grad_input_ref,
    gain_total_ref,
    grad_out_ref,
    head_in,
    gate_up_in,
    down_in,
    normed_ref,
    w_head,
    w_sibling,
    out_rows_ref,
    branch_all,
    d_attended,
    d_head,
    d_other,
    d_kv,
    d_kv_other,
    out_send,
    out_recv,
    head_terms,
    head_recv,
    own_sum,
    chip_send,
    chip_recv,
    gate_up_sum,
    gate_up_recv,
    down_parts,
    down_first,
    down_mid,
    down_second,
    down_sum,
    down_planes,
    gains,
    gains_z,
    gains_ctx,
    local_sem,
    send_sem,
    recv_sem,
):
    tok, width = input_ref.shape
    seq = 8 * tok
    half_seq = 4 * tok
    share = out_send.shape[1]
    ctx, plane = lax.axis_index("ctx"), lax.axis_index("shard")
    chip, core = ctx // 2, ctx % 2
    other_core = 1 - core
    sibling = (2 * chip + other_core, plane)
    over_z = [(ctx, flip(plane, d)) for d in range(4)]
    over_chips = [(2 * flip(chip, d) + core, plane) for d in range(4)]
    over_chips_cross = [(2 * flip(chip, d) + other_core, plane) for d in range(4)]
    over_z_cross = [(2 * chip + other_core, flip(plane, d)) for d in range(4)]
    others = (1, 2, 3)

    def at(i, size):
        return pl.ds(pl.multiple_of(i * size, size), size)

    def remote(slot, source, target, device, recv=None):
        return pltpu.make_async_remote_copy(
            src_ref=source,
            dst_ref=target,
            send_sem=send_sem.at[slot],
            recv_sem=recv_sem.at[slot if recv is None else recv],
            device_id=device,
            device_id_type=MESH,
        )

    def send(slot, source, target, device):
        copy = remote(slot, source, target, device)
        copy.start()
        return copy

    def local(slot, source, target):
        return pltpu.make_async_copy(source, target, local_sem.at[slot])

    loads = [
        local(0, branch_hbm, branch_all),
        local(1, out_rows_hbm, out_rows_ref),
        local(2, normed_hbm, normed_ref),
        local(3, down_terms.at[:, chip], down_parts),
        local(7, down_terms.at[:, flip(chip, 2), :, pl.ds(0, width // 2)], down_mid.at[0]),
        local(8, down_terms.at[:, flip(chip, 1), :, pl.ds(width // 2, width // 2)], down_mid.at[1]),
        local(4, head_hbm, w_head),
        local(5, sibling_hbm, w_sibling),
        local(6, gate_up_hbm, gate_up_sum),
    ]
    for load in loads:
        load.start()

    barrier = pltpu.get_barrier_semaphore()
    partners = (
        over_z[1:] + over_z_cross + over_chips[1:] + over_chips_cross[1:]
    )
    for partner in partners:
        pl.semaphore_signal(barrier, inc=1, device_id=partner, device_id_type=MESH)
    pl.semaphore_wait(barrier, len(partners))

    gate_second = send(0, gate_up_send.at[0], gate_up_recv.at[0], over_chips[2])
    up_second = send(46, gate_up_send.at[1], gate_up_recv.at[1], over_chips[1])

    half_width = width // 2
    down_sent = [
        send(
            1 + 2 * e + u,
            down_terms.at[:, flip(chip, (1 + e, 3)[u]), :, pl.ds(e * half_width, half_width)],
            down_first.at[e, u],
            over_chips[1 + e],
        )
        for e in range(2)
        for u in range(2)
    ]

    loads[0].wait()

    def out_step(t, carry):
        here = at(t, TILE)
        made = dot_tn(attended_ref[...], branch_all[:, here])
        out_send[:, :, here] = made.reshape(4, share, TILE).astype(BF16)
        return carry

    lax.fori_loop(0, width // TILE, out_step, 0)

    def add_out(d, i):
        here = flip(plane, d)
        out_send[here] = (out_send[here].astype(F32) + out_recv[i].astype(F32)).astype(BF16)

    start_out, pass_out, wait_out, finish_out = line_sum(
        remote, over_z, plane, 52, lambda d: out_send.at[flip(plane, d)], out_recv, add_out
    )
    start_out()

    loads[1].wait()

    def attended_step(t, carry):
        here = at(t, TILE)
        d_attended[here, :] = dot_nt(branch_all[here, :], out_rows_ref[...]).astype(BF16)
        return carry

    lax.fori_loop(0, seq // TILE, attended_step, 0)
    d_kv[...] = jnp.zeros_like(d_kv)

    def attend_step(t, carry):
        here = at(t, TILE)
        query, outgrad = query_ref[here, :], d_attended[here, :]
        scores = scores_of(
            query, kv_ref[0], code_ref[here, :], low_code_ref[here, :], key_code_ref[...]
        )
        probs = jnp.exp(scores - log_total_ref[here, :])
        prob_grad = dot_nt(outgrad, kv_ref[1])
        delta = jnp.sum(probs * prob_grad, axis=-1, keepdims=True)
        score_grad = (probs * (prob_grad - delta)).astype(BF16)
        d_query = dot_nn(score_grad, kv_ref[0]) * SCORE_SCALE
        d_head[here, :HD] = rotated(d_query, cosine_ref[here, :], -sine_ref[here, :]).astype(BF16)
        d_kv[0] += dot_tn(score_grad, query)
        d_kv[1] += dot_tn(probs.astype(BF16), outgrad)
        return carry

    lax.fori_loop(0, seq // TILE, attend_step, 0)

    give = d_kv.at[other_core]
    kv_pair = [
        send(
            7 + e,
            give.at[pl.ds(e * half_seq, half_seq)],
            d_kv_other.at[pl.ds((1 - e) * half_seq, half_seq)],
            sibling,
        )
        for e in range(2)
    ]
    loads[8].wait()
    gate_second.wait_recv()
    up_second.wait_recv()
    hidden = gate_up_recv.shape[2]

    def gate_up_step(i, carry):
        here = at(i, share)
        for e in range(2):
            columns = pl.ds(e * hidden, hidden)
            gate_up_sum[here, columns] = (
                gate_up_sum[here, columns].astype(F32) + gate_up_recv[e, here, :].astype(F32)
            ).astype(BF16)
        return carry

    lax.fori_loop(0, 8, gate_up_step, 0)

    place = gate_up_in.at[plane, core]

    def gate_up_rows(to_core, to_plane):
        return gate_up_sum.at[at(4 * to_core + to_plane, share), :]

    gate_up_z = {
        d: send(18 + d, gate_up_rows(core, flip(plane, d)), place, over_z[d]) for d in others
    }
    gate_up_cross = {
        d: send(22 + d, gate_up_rows(other_core, flip(plane, d)), place, over_z_cross[d])
        for d in range(4)
    }
    keep_gate_up = local(1, gate_up_rows(core, plane), place)
    keep_gate_up.start()
    for copy in kv_pair:
        copy.wait_recv()

    def kv_step(t, carry):
        here = at(t, TILE)
        total = d_kv[core, here, :] + d_kv_other[here, :]
        total = total * jnp.where(core == 0, SCORE_SCALE, 1.0)
        cosine = jnp.where(core == 0, cosine_ref[here, :], 1.0)
        sine = jnp.where(core == 0, sine_ref[here, :], 0.0)
        d_head[here, HD:] = rotated(total, cosine, -sine).astype(BF16)
        return carry

    lax.fori_loop(0, seq // TILE, kv_step, 0)
    head_pair = send(9, d_head.at[pl.ds(half_seq, half_seq)], d_other, sibling)

    loads[2].wait()

    def head_step(t, carry):
        made = dot_tn(normed_ref[:, at(t, TILE)], d_head[...])
        head_terms[:, t] = made.reshape(4, share, 2 * HD).astype(BF16)
        return carry

    lax.fori_loop(0, width // TILE, head_step, 0)

    def add_head(d, i):
        here = flip(plane, d)

        def step(t, carry):
            head_terms[here, t] = (
                head_terms[here, t].astype(F32) + head_recv[i, t].astype(F32)
            ).astype(BF16)
            return carry

        lax.fori_loop(0, 8, step, 0)

    start_head, pass_head, wait_head, finish_head = line_sum(
        remote, over_z, plane, 47, lambda d: head_terms.at[flip(plane, d)], head_recv, add_head
    )
    start_head()

    loads[6].wait()
    loads[7].wait()
    head_pair.wait_recv()

    def normed_step(t, carry):
        here = at(t, TILE)
        made = (
            dot_nt(d_head[:half_seq, :HD], w_head[0, here, :])
            + dot_nt(d_head[:half_seq, HD:], w_head[1, here, :])
            + dot_nt(d_other[:, :HD], w_sibling[0, here, :])
            + dot_nt(d_other[:, HD:], w_sibling[1, here, :])
        )
        own_sum[:, here] = made[:tok]
        for d in others:
            chip_send[d - 1, :, here] = made[d * tok : (d + 1) * tok].astype(BF16)
        return carry

    lax.fori_loop(0, width // TILE, normed_step, 0)
    normed_chips = {
        d: send(12 + d, chip_send.at[d - 1], chip_recv.at[d - 1], over_chips[d]) for d in others
    }

    loads[4].wait()
    loads[5].wait()

    def down_mid_step(p, carry):
        for e in range(2):
            down_mid[e, p] = (
                down_mid[e, p].astype(F32) + down_first[e, 1, p].astype(F32)
            ).astype(BF16)
        return carry

    for copy in down_sent:
        copy.wait_recv()
    lax.fori_loop(0, 4, down_mid_step, 0)
    down_last = [
        send(5 + e, down_mid.at[e], down_second.at[e], over_chips[2 - e]) for e in range(2)
    ]
    pass_out()
    pass_head()
    for d in others:
        normed_chips[d].wait_recv()
    chunk = 32
    gain = attn_gain_ref[...]

    def input_step(i, carry):
        here = at(i, chunk)
        grad = own_sum[here, :]
        for d in range(3):
            grad = grad + chip_recv[d, here, :].astype(F32)
        block = input_ref[here, :].astype(F32)
        factor = lax.rsqrt(jnp.mean(block * block, axis=-1, keepdims=True) + EPSILON)
        scaled = grad * gain
        grad_input_ref[here, :] = (
            mid_grad_ref[here, :]
            + factor * scaled
            - block * (factor * factor * factor * jnp.mean(scaled * block, axis=-1, keepdims=True))
        ).astype(BF16)
        return carry + jnp.sum(grad * block * factor, axis=0, keepdims=True)

    gain_grad = lax.fori_loop(0, tok // chunk, input_step, jnp.zeros((1, width), F32))
    gains[...] = jnp.concatenate(
        [gain_grad, mlp_gain_grad_ref[...]], axis=0
    )
    gains_planes = {d: send(25 + d, gains, gains_z.at[d - 1], over_z[d]) for d in others}

    loads[3].wait()
    for copy in down_last:
        copy.wait_recv()

    def down_step(p, carry):
        for e in range(2):
            columns = pl.ds(e * half_width, half_width)
            down_sum[p, :, columns] = (
                down_parts[p, :, columns].astype(F32)
                + down_first[e, 0, p].astype(F32)
                + down_second[e, p].astype(F32)
            ).astype(BF16)
        return carry

    lax.fori_loop(0, 4, down_step, 0)
    down_z = {
        d: send(15 + d, down_sum.at[flip(plane, d)], down_planes.at[plane], over_z[d])
        for d in others
    }
    keep_down = local(3, down_sum.at[plane], down_planes.at[plane])
    keep_down.start()


    wait_head()
    def head_sum(i, carry):
        total = head_terms[plane, i].astype(F32)
        for d in range(2):
            total = total + head_recv[d, i].astype(F32)
        head_terms[plane, i] = total.astype(BF16)
        return carry

    lax.fori_loop(0, 8, head_sum, 0)
    head_place = head_in.at[ctx]
    head_chips = {
        d: send(28 + d, head_terms.at[plane, 2 * flip(chip, d) + core], head_place, over_chips[d])
        for d in others
    }
    head_cross = {
        d: send(
            32 + d, head_terms.at[plane, 2 * flip(chip, d) + other_core], head_place,
            over_chips_cross[d],
        )
        for d in range(4)
    }
    keep_head = local(0, head_terms.at[plane, ctx], head_place)
    keep_head.start()

    for d in others:
        gains_planes[d].wait_recv()
        gains_planes[d].wait_send()
    gains[...] = gains[...] + gains_z[0] + gains_z[1] + gains_z[2]
    gains_chips = {
        d: send(35 + d, gains, gains_ctx.at[0, d], over_chips[d]) for d in others
    }
    gains_cross = {
        d: send(39 + d, gains, gains_ctx.at[1, d], over_chips_cross[d]) for d in range(4)
    }

    wait_out()
    total = out_send[plane].astype(F32)
    for d in range(2):
        total = total + out_recv[d].astype(F32)
    grad_out_ref[...] = total

    keep_down.wait()
    down_place = down_in.at[chip]
    for d in range(4):
        if d:
            down_z[d].wait_recv()
        source = flip(plane, d)
        apart = xor4(chip, source)
        block = down_planes.at[source]

        @pl.when(apart == 0)
        def _(block=block):
            local(4, block, down_place).start()

        @pl.when(apart != 0)
        def _(block=block, source=source, apart=apart):
            remote(42 + apart, block, down_place, (2 * source + core, plane)).start()

    for d in others:
        gains_chips[d].wait_recv()
    for d in range(4):
        gains_cross[d].wait_recv()
    total = gains[...] + gains_ctx[1, 0]
    for d in others:
        total = total + gains_ctx[0, d] + gains_ctx[1, d]
    gain_total_ref[...] = total

    local(4, down_sum.at[plane], down_place).wait()
    keep_gate_up.wait()
    keep_head.wait()
    for d in others:
        remote(42 + d, down_sum.at[plane], down_place, over_chips[d]).wait()
        gate_up_z[d].wait_recv()
        head_chips[d].wait_recv()
        for copies in (
            normed_chips, down_z, gate_up_z, head_chips, gains_chips
        ):
            copies[d].wait_send()
    finish_out()
    finish_head()
    for d in range(4):
        for copies in (gate_up_cross, head_cross):
            copies[d].wait()
        gains_cross[d].wait_send()
    for copy in (gate_second, up_second, head_pair, *kv_pair, *down_sent, *down_last):
        copy.wait_send()


def back_of(*operands):
    inputs, query = operands[0], operands[9]
    tok, width = inputs.shape
    seq = query.shape[0]
    hidden = operands[18].shape[-1] // 2
    share = HD // 4
    vmem = pl.BlockSpec(memory_space=pltpu.VMEM)
    hbm = pl.BlockSpec(memory_space=pl.ANY)
    return pl.pallas_call(
        back_kernel,
        in_specs=[vmem] * 13 + [hbm] * 8,
        out_specs=[vmem] * 6,
        out_shape=[
            jax.ShapeDtypeStruct((tok, width), BF16),
            jax.ShapeDtypeStruct((2, width), F32),
            jax.ShapeDtypeStruct((share, width), F32),
            jax.ShapeDtypeStruct((8, share, 2 * HD), BF16),
            jax.ShapeDtypeStruct((4, 2, share, 2 * hidden), BF16),
            jax.ShapeDtypeStruct((4, share, width), BF16),
        ],
        scratch_shapes=[
            pltpu.VMEM((seq, width), BF16),
            pltpu.VMEM((2, width, HD), BF16),
            pltpu.VMEM((2, width, HD), BF16),
            pltpu.VMEM((HD, width), BF16),
            pltpu.VMEM((seq, width), BF16),
            pltpu.VMEM((seq, HD), BF16),
            pltpu.VMEM((seq, 2 * HD), BF16),
            pltpu.VMEM((4 * tok, 2 * HD), BF16),
            pltpu.VMEM((2, seq, HD), F32),
            pltpu.VMEM((seq, HD), F32),
            pltpu.VMEM((4, share, width), BF16),
            pltpu.VMEM((4, share, width), BF16),
            pltpu.VMEM((4, 8, share, 2 * HD), BF16),
            pltpu.VMEM((4, 8, share, 2 * HD), BF16),
            pltpu.VMEM((tok, width), F32),
            pltpu.VMEM((3, tok, width), BF16),
            pltpu.VMEM((3, tok, width), BF16),
            pltpu.VMEM((8 * share, 2 * hidden), BF16),
            pltpu.VMEM((2, 8 * share, hidden), BF16),
            pltpu.VMEM((4, share, width), BF16),
            pltpu.VMEM((2, 2, 4, share, width // 2), BF16),
            pltpu.VMEM((2, 4, share, width // 2), BF16),
            pltpu.VMEM((2, 4, share, width // 2), BF16),
            pltpu.VMEM((4, share, width), BF16),
            pltpu.VMEM((4, share, width), BF16),
            pltpu.VMEM((2, width), F32),
            pltpu.VMEM((3, 2, width), F32),
            pltpu.VMEM((2, 4, 2, width), F32),
            pltpu.SemaphoreType.DMA((9,)),
            pltpu.SemaphoreType.DMA((57,)),
            pltpu.SemaphoreType.DMA((57,)),
        ],
        compiler_params=pltpu.CompilerParams(
            collective_id=3, has_side_effects=True, vmem_limit_bytes=60 << 20
        ),
        cost_estimate=pl.CostEstimate(
            flops=2 * seq * width * 6 * HD + 10 * seq * seq * HD,
            bytes_accessed=20 * seq * width,
            transcendentals=seq * seq,
        ),
    )(*operands)


def on_device_by_head(
    layer_input,
    w_query,
    w_key,
    w_value,
    w_out,
    w_gate,
    w_up,
    w_down,
    attn_gain,
    mlp_gain,
    block_pairs,
    doc_ids,
    cotangent,
):
    tok_rows, width = layer_input.shape[1:]
    planes = lax.axis_size("shard")
    ctx_count = lax.axis_size("ctx")
    chips = ctx_count // 2
    ctx, plane = lax.axis_index("ctx"), lax.axis_index("shard")
    chip, core = ctx // 2, ctx % 2
    seq_rows = tok_rows * ctx_count
    own_share = width // (planes * ctx_count)

    inputs_low = layer_input[0]
    pairs, documents = block_pairs[0], doc_ids[0]
    order = jnp.stack([(chip ^ d) * 2 + (core ^ e) for e in range(2) for d in range(chips)])
    chosen = jnp.sum(
        jnp.where(order[:, None] == jnp.arange(ctx_count)[None, :], pairs[None, :], 0), axis=1
    )[:, None]
    within = jnp.arange(tok_rows, dtype=jnp.int32)[None, :]
    block = tok_rows // 2
    positions = jnp.where(
        within < block, chosen * block, (2 * ctx_count - 1 - chosen) * block - block
    )
    positions = (positions + within).reshape(-1)
    begins = jnp.sum(documents[None, :] < jnp.arange(1, DOCS)[:, None], axis=1)
    document = jnp.sum((positions[None, :] >= begins[:, None]).astype(jnp.int32), axis=0)
    span = 2 * seq_rows
    doc_first = document * span
    code = doc_first + positions
    low_code = jnp.maximum(doc_first, code - (WINDOW - 1))
    code_column, low_column, code_row = code[:, None], low_code[:, None], code[None, :]
    cosine, sine = rope_tables(positions, HD)

    upstream_low = cotangent[0]
    (
        normed_two,
        mid,
        normed_all,
        query,
        key_value,
        attended,
        log_total,
        w_head,
        w_sibling,
        out_rows,
        down_rows,
        upstream_group,
    ) = front_of(
        inputs_low,
        attn_gain[None],
        mlp_gain[None],
        cosine,
        sine,
        code_column,
        low_column,
        code_row,
        w_query,
        w_key,
        w_value,
        w_out,
        w_down,
        upstream_low,
    )
    (
        output,
        mid_grad,
        mlp_gain_grad,
        branch_all,
        gate_up_sum,
        gate_up_send,
        down_terms,
    ) = mlp_of(
        normed_two,
        mid,
        upstream_low,
        mlp_gain[None],
        upstream_group.reshape(-1, width),
        w_gate,
        w_up,
        down_rows,
    )
    grad_input, gain_total, grad_out, head_in, gate_up_in, down_in = back_of(
        inputs_low,
        mid_grad,
        attn_gain[None],
        mlp_gain_grad,
        cosine,
        sine,
        code_column,
        low_column,
        code_row,
        query,
        key_value,
        attended,
        log_total,
        normed_all,
        w_head,
        w_sibling,
        out_rows,
        branch_all.reshape(seq_rows, width),
        gate_up_sum,
        gate_up_send,
        down_terms.reshape(planes, chips, -1, width),
    )
    hidden = gate_up_in.shape[-1] // 2
    gate_up = gate_up_in.astype(F32)
    columns = lambda parts: jnp.concatenate(parts, axis=1)
    grad_gate = columns([gate_up[p, e, :, :hidden] for p in range(planes) for e in range(2)])
    grad_up = columns([gate_up[p, e, :, hidden:] for p in range(planes) for e in range(2)])
    head = head_in.astype(F32)
    grad_query = columns([head[i, :, :HD] for i in range(ctx_count)])
    grad_key = columns([head[i, :, HD:] for i in range(0, ctx_count, 2)])
    grad_value = columns([head[i, :, HD:] for i in range(1, ctx_count, 2)])
    grad_down = down_in.astype(F32).reshape(-1, width)
    gains = lax.dynamic_slice(gain_total, (0, own_share * (planes * ctx + plane)), (2, own_share))
    return (
        output[None],
        grad_input[None],
        grad_query,
        grad_key,
        grad_value,
        grad_out,
        grad_gate,
        grad_up,
        grad_down,
        gains[0],
        gains[1],
    )


def plan_of(mesh):
    chips, planes = mesh.shape["ctx"] // 2, mesh.shape["shard"]
    if mesh.shape["ctx"] == HQ and HQ == 2 * HK and chips == planes == HK:
        return on_device_by_head
    return on_device


def solution(mesh):
    placed = (
        P("shard", "ctx", None),
        P(None, "shard"),
        P(None, "shard"),
        P(None, "shard"),
        P(None, "shard"),
        P(None, "shard"),
        P(None, "shard"),
        P(None, "shard"),
        P(),
        P(),
        P("shard", None),
        P("shard", None),
        P("shard", "ctx", None),
    )
    return jax.shard_map(
        plan_of(mesh),
        mesh=mesh,
        in_specs=placed,
        out_specs=(
            P("shard", "ctx", None),
            P("shard", "ctx", None),
            P(("ctx", "shard"), None),
            P(("ctx", "shard"), None),
            P(("ctx", "shard"), None),
            P(("ctx", "shard"), None),
            P(("ctx", "shard"), None),
            P(("ctx", "shard"), None),
            P(("ctx", "shard"), None),
            P(("ctx", "shard")),
            P(("ctx", "shard")),
        ),
        check_vma=False,
    )
```

```python
import math

import jax
import jax.numpy as jnp
from jax import lax
from jax.experimental import pallas as pl
from jax.experimental.pallas import tpu as pltpu
from jax.sharding import PartitionSpec as P

HQ = 8
HK = 4
HD = 256
WINDOW = 1024


EPSILON = 1e-06
SCORE_SCALE = 0.0625
MASKED = -1e30
ROPE_BASE = 1000042.0


def position_of(rows, pairs, per_device, blocks_total):
    device = rows // per_device
    within = rows % per_device
    half = per_device // 2
    chosen = jnp.take(pairs, device)
    first = chosen * half + within
    second = (blocks_total - 1 - chosen) * half + within - half
    return jnp.where(within < half, first, second)


def rope_tables(positions, head):
    half = head // 2
    freq = ROPE_BASE ** (-(jnp.arange(half, dtype=jnp.float32) * 2.0) / head)
    angle = positions.astype(jnp.float32)[:, None] * freq[None, :]
    return (jnp.cos(angle), jnp.sin(angle))


def rotate(values, cosine, sine):
    half = values.shape[-1] // 2
    first = values[..., :half]
    second = values[..., half:]
    cosine = cosine[:, None, :]
    sine = sine[:, None, :]
    return jnp.concatenate(
        [first * cosine - second * sine, second * cosine + first * sine], axis=-1
    )


def rotate_back(grads, cosine, sine):
    half = grads.shape[-1] // 2
    first = grads[..., :half]
    second = grads[..., half:]
    cosine = cosine[:, None, :]
    sine = sine[:, None, :]
    return jnp.concatenate(
        [first * cosine + second * sine, second * cosine - first * sine], axis=-1
    )


def visible(query_pos, query_doc, key_pos, key_doc):
    distance = query_pos[:, None] - key_pos[None, :]
    return (query_doc[:, None] == key_doc[None, :]) & (distance >= 0) & (distance < WINDOW)


def write_columns(left, piece):
    made = jnp.dot(left, piece, preferred_element_type=jnp.float32)
    return made


def contract_full(grads, weight):
    return lax.dot_general(
        grads, weight, (((1,), (1,)), ((), ())), preferred_element_type=jnp.float32
    )


def alternate(parts, shard_count, rows):
    return jnp.concatenate([part.reshape(rows, shard_count, -1) for part in parts], axis=2).reshape(
        rows, -1
    )


def outer_sum(left, right):
    return lax.dot_general(
        left, right, (((0,), (0,)), ((), ())), preferred_element_type=jnp.float32
    )


def term_rows(lefts, rights, gain_block, count):
    normed_all, attended_all, second_all, act_all = lefts
    query_g, key_g, value_g, branch_g, gate_g, up_g, upstream_g = rights
    down_part = outer_sum(act_all, upstream_g).reshape(count, -1)
    return jnp.concatenate(
        [
            outer_sum(normed_all, query_g),
            outer_sum(normed_all, key_g),
            outer_sum(normed_all, value_g),
            outer_sum(attended_all, branch_g),
            outer_sum(second_all, gate_g),
            outer_sum(second_all, up_g),
            down_part,
            gain_block,
        ],
        axis=1,
    )


def deal_columns(values, ctx_count, shard_count):
    rows = values.shape[0]
    return (
        values.reshape(rows, ctx_count, shard_count, -1)
        .transpose(0, 2, 1, 3)
        .reshape(rows, shard_count, -1)
    )


def on_device(
    layer_input,
    w_query,
    w_key,
    w_value,
    w_out,
    w_gate,
    w_up,
    w_down,
    attn_gain,
    mlp_gain,
    block_pairs,
    doc_ids,
    cotangent,
):
    tok_rows = layer_input.shape[1]
    model_width = layer_input.shape[2]
    shard_count = lax.axis_size("shard")
    ctx_count = lax.axis_size("ctx")
    device_count = lax.axis_size(("ctx", "shard"))
    group_size = HQ // HK
    blocks_total = 2 * ctx_count
    pairs = block_pairs[0]
    documents = doc_ids[0]
    own_rows = lax.axis_index("ctx") * tok_rows + jnp.arange(tok_rows, dtype=jnp.int32)
    own_pos = position_of(own_rows, pairs, tok_rows, blocks_total)
    own_doc = jnp.take(documents, own_pos)
    cosine, sine = rope_tables(own_pos, HD)
    stack_qkv = jnp.concatenate([w_query, w_key, w_value], axis=1)
    stack_mlp = jnp.concatenate([w_gate, w_up], axis=1)
    per_query = w_query.shape[1]
    per_key = w_key.shape[1]
    per_hidden = w_gate.shape[1]
    hidden_width = w_down.shape[0]
    inputs = layer_input.reshape(tok_rows, model_width).astype(jnp.float32)
    factor_one = lax.rsqrt(jnp.mean(inputs * inputs, axis=-1, keepdims=True) + EPSILON)
    normed = (inputs * factor_one * attn_gain).astype(jnp.bfloat16)
    projected = write_columns(normed, lax.all_gather(stack_qkv, "shard", axis=1, tiled=True))
    projected = projected.reshape(tok_rows, shard_count, -1)
    query_lin = projected[:, :, :per_query].reshape(tok_rows, HQ, HD)
    key_lin = projected[:, :, per_query : per_query + per_key].reshape(tok_rows, HK, HD)
    value_lin = projected[:, :, per_query + per_key :].reshape(tok_rows, HK * HD)
    query_rot = (
        rotate(query_lin, cosine, sine).astype(jnp.bfloat16).reshape(tok_rows, HK, group_size, HD)
    )
    key_rot = rotate(key_lin, cosine, sine).astype(jnp.bfloat16).reshape(tok_rows, HK * HD)
    value_low = value_lin.astype(jnp.bfloat16)

    def key_mask(first_row, count):
        key_pos = position_of(
            first_row + jnp.arange(count, dtype=jnp.int32), pairs, tok_rows, blocks_total
        )
        return visible(own_pos, own_doc, key_pos, jnp.take(documents, key_pos))[:, None, None, :]

    start_state = (
        jnp.full((tok_rows, HK, group_size), MASKED, jnp.float32),
        jnp.zeros((tok_rows, HK, group_size), jnp.float32),
        jnp.zeros((tok_rows, HK, group_size, HD), jnp.float32),
    )
    keys = lax.all_gather(key_rot, "ctx", axis=0, tiled=True)
    values = lax.all_gather(value_low, "ctx", axis=0, tiled=True)
    count = keys.shape[0]
    step = math.gcd(count, 4 * tok_rows)
    keys = keys.reshape(count // step, step, HK, HD)
    values = values.reshape(count // step, step, HK, HD)

    def attend_step(i, running):
        top, total, accum = running
        mask = key_mask(i * step, step)
        scores = (
            jnp.einsum("tkgd,skd->tkgs", query_rot, keys[i], preferred_element_type=jnp.float32)
            * SCORE_SCALE
        )
        scores = jnp.where(mask, scores, MASKED)
        new_top = jnp.maximum(top, jnp.max(scores, axis=-1))
        weights = jnp.where(mask, jnp.exp(scores - new_top[..., None]), 0.0)
        shrink = jnp.exp(top - new_top)
        total = total * shrink + jnp.sum(weights, axis=-1)
        accum = accum * shrink[..., None] + jnp.einsum(
            "tkgs,skd->tkgd",
            weights.astype(jnp.bfloat16),
            values[i],
            preferred_element_type=jnp.float32,
        )
        return (new_top, total, accum)

    top, total, accum = lax.fori_loop(0, count // step, attend_step, start_state)
    log_total = top + jnp.log(total)
    attended_full = accum / total[..., None]
    attended = attended_full.astype(jnp.bfloat16).reshape(tok_rows, HQ * HD)
    branch_one = write_columns(attended, lax.all_gather(w_out, "shard", axis=1, tiled=True))
    mid = inputs + branch_one
    factor_two = lax.rsqrt(jnp.mean(mid * mid, axis=-1, keepdims=True) + EPSILON)
    normed_two = (mid * factor_two * mlp_gain).astype(jnp.bfloat16)
    gate_up = write_columns(normed_two, lax.all_gather(stack_mlp, "shard", axis=1, tiled=True))
    gate_up = gate_up.reshape(tok_rows, shard_count, -1)
    gate = gate_up[:, :, :per_hidden].reshape(tok_rows, hidden_width)
    up_lin = gate_up[:, :, per_hidden:].reshape(tok_rows, hidden_width)
    sigma = jax.nn.sigmoid(gate)
    swish = gate * sigma
    act = (swish * up_lin).astype(jnp.bfloat16)
    branch_two = write_columns(act, lax.all_gather(w_down, "shard", axis=1, tiled=True))
    output = (mid + branch_two).astype(jnp.bfloat16).reshape(1, tok_rows, model_width)
    full_qkv, full_out, full_mlp, full_down = (
        lax.all_gather(stack_qkv, "shard", axis=1, tiled=True),
        lax.all_gather(w_out, "shard", axis=1, tiled=True),
        lax.all_gather(stack_mlp, "shard", axis=1, tiled=True),
        lax.all_gather(w_down, "shard", axis=1, tiled=True),
    )
    upstream_low = cotangent.reshape(tok_rows, model_width)
    upstream = upstream_low.astype(jnp.float32)
    act_grad = contract_full(upstream_low, full_down)
    gate_grad = (act_grad * up_lin * (sigma * (1.0 + gate * (1.0 - sigma)))).astype(jnp.bfloat16)
    up_grad = (act_grad * swish).astype(jnp.bfloat16)
    stacked_mlp_grad = alternate((gate_grad, up_grad), shard_count, tok_rows)
    norm_two_grad = contract_full(stacked_mlp_grad, full_mlp)
    mlp_gain_term = jnp.sum(norm_two_grad * mid * factor_two, axis=0)
    scaled_two = norm_two_grad * mlp_gain
    mid_grad = (
        upstream
        + factor_two * scaled_two
        - mid * factor_two**3 * jnp.mean(scaled_two * mid, axis=-1, keepdims=True)
    )
    branch_grad = mid_grad.astype(jnp.bfloat16)
    attended_grad = contract_full(branch_grad, full_out)
    attended_low = attended_grad.astype(jnp.bfloat16).reshape(tok_rows, HK, group_size, HD)
    delta = jnp.sum(attended_low.astype(jnp.float32) * attended_full, axis=-1)

    def query_grads(carry, piece):
        keys, values = piece
        count = keys.shape[0]
        step = math.gcd(count, 4 * tok_rows)
        keys = keys.reshape(count // step, step, HK, HD)
        values = values.reshape(count // step, step, HK, HD)

        def query_step(i, query_sum):
            mask = key_mask(i * step, step)
            scores = (
                jnp.einsum("tkgd,skd->tkgs", query_rot, keys[i], preferred_element_type=jnp.float32)
                * SCORE_SCALE
            )
            probs = jnp.where(mask, jnp.exp(scores - log_total[..., None]), 0.0)
            prob_grad = jnp.einsum(
                "tkgd,skd->tkgs", attended_low, values[i], preferred_element_type=jnp.float32
            )
            score_grad = (probs * (prob_grad - delta[..., None])).astype(jnp.bfloat16)
            return query_sum + jnp.einsum(
                "tkgs,skd->tkgd", score_grad, keys[i], preferred_element_type=jnp.float32
            )

        return lax.fori_loop(0, count // step, query_step, carry)

    query_sum = query_grads(
        jnp.zeros((tok_rows, HK, group_size, HD), jnp.float32),
        (
            lax.all_gather(key_rot, "ctx", axis=0, tiled=True),
            lax.all_gather(value_low, "ctx", axis=0, tiled=True),
        ),
    )
    all_log_total, all_delta = (
        lax.all_gather(log_total, "ctx", axis=0, tiled=True),
        lax.all_gather(delta, "ctx", axis=0, tiled=True),
    )
    key_three = key_rot.reshape(tok_rows, HK, HD)
    value_three = value_low.reshape(tok_rows, HK, HD)

    def key_grads(carry, piece):
        queries, outgrads = piece
        count = queries.shape[0]
        step = math.gcd(count, 4 * tok_rows)
        queries = queries.reshape(count // step, step, HK, group_size, HD)
        outgrads = outgrads.reshape(count // step, step, HK, group_size, HD)

        def key_step(i, running):
            key_sum, value_sum = running
            first_row = i * step
            query_pos = position_of(
                first_row + jnp.arange(step, dtype=jnp.int32), pairs, tok_rows, blocks_total
            )
            mask = visible(query_pos, jnp.take(documents, query_pos), own_pos, own_doc)[
                :, None, None, :
            ]
            lse_part = lax.dynamic_slice_in_dim(all_log_total, first_row, step, 0)
            delta_part = lax.dynamic_slice_in_dim(all_delta, first_row, step, 0)
            scores = (
                jnp.einsum(
                    "skgd,tkd->skgt", queries[i], key_three, preferred_element_type=jnp.float32
                )
                * SCORE_SCALE
            )
            probs = jnp.where(mask, jnp.exp(scores - lse_part[..., None]), 0.0)
            prob_grad = jnp.einsum(
                "skgd,tkd->skgt", outgrads[i], value_three, preferred_element_type=jnp.float32
            )
            score_grad = (probs * (prob_grad - delta_part[..., None])).astype(jnp.bfloat16)
            value_sum = value_sum + jnp.einsum(
                "skgt,skgd->tkd",
                probs.astype(jnp.bfloat16),
                outgrads[i],
                preferred_element_type=jnp.float32,
            )
            key_sum = key_sum + jnp.einsum(
                "skgt,skgd->tkd", score_grad, queries[i], preferred_element_type=jnp.float32
            )
            return (key_sum, value_sum)

        return lax.fori_loop(0, count // step, key_step, carry)

    key_sum, value_sum = key_grads(
        (jnp.zeros((tok_rows, HK, HD), jnp.float32), jnp.zeros((tok_rows, HK, HD), jnp.float32)),
        (
            lax.all_gather(query_rot.reshape(tok_rows, HQ * HD), "ctx", axis=0, tiled=True),
            lax.all_gather(attended_low.reshape(tok_rows, HQ * HD), "ctx", axis=0, tiled=True),
        ),
    )
    query_grad = (
        rotate_back(query_sum.reshape(tok_rows, HQ, HD) * SCORE_SCALE, cosine, sine)
        .astype(jnp.bfloat16)
        .reshape(tok_rows, HQ * HD)
    )
    key_grad = (
        rotate_back(key_sum * SCORE_SCALE, cosine, sine)
        .astype(jnp.bfloat16)
        .reshape(tok_rows, HK * HD)
    )
    value_grad = value_sum.astype(jnp.bfloat16).reshape(tok_rows, HK * HD)
    stacked_qkv_grad = alternate((query_grad, key_grad, value_grad), shard_count, tok_rows)
    normed_grad = contract_full(stacked_qkv_grad, full_qkv)
    attn_gain_term = jnp.sum(normed_grad * inputs * factor_one, axis=0)
    scaled_one = normed_grad * attn_gain
    input_grad = (
        mid_grad
        + factor_one * scaled_one
        - inputs * factor_one**3 * jnp.mean(scaled_one * inputs, axis=-1, keepdims=True)
    )
    grad_input = input_grad.astype(jnp.bfloat16).reshape(1, tok_rows, model_width)
    ratio = hidden_width // model_width
    own_share = model_width // device_count
    rights = (query_grad, key_grad, value_grad, branch_grad, gate_grad, up_grad, upstream_low)
    group_rights = (
        lax.all_gather(rights[0], "shard", axis=0, tiled=True),
        lax.all_gather(rights[1], "shard", axis=0, tiled=True),
        lax.all_gather(rights[2], "shard", axis=0, tiled=True),
        lax.all_gather(rights[3], "shard", axis=0, tiled=True),
        lax.all_gather(rights[4], "shard", axis=0, tiled=True),
        lax.all_gather(rights[5], "shard", axis=0, tiled=True),
        lax.all_gather(rights[6], "shard", axis=0, tiled=True),
    )
    dealt = (
        lax.all_to_all(
            deal_columns(normed, ctx_count, shard_count),
            "shard",
            split_axis=1,
            concat_axis=0,
            tiled=True,
        ),
        lax.all_to_all(
            deal_columns(attended, ctx_count, shard_count),
            "shard",
            split_axis=1,
            concat_axis=0,
            tiled=True,
        ),
        lax.all_to_all(
            deal_columns(normed_two, ctx_count, shard_count),
            "shard",
            split_axis=1,
            concat_axis=0,
            tiled=True,
        ),
        lax.all_to_all(
            deal_columns(act, ctx_count, shard_count),
            "shard",
            split_axis=1,
            concat_axis=0,
            tiled=True,
        ),
    )
    group_lefts = tuple((part.reshape(part.shape[0], -1) for part in dealt))
    gain_pair = lax.psum(jnp.stack([attn_gain_term, mlp_gain_term]), "shard")
    gain_mine = lax.dynamic_index_in_dim(
        gain_pair.reshape(2, ctx_count, shard_count, own_share),
        lax.axis_index("shard"),
        2,
        keepdims=False,
    ).reshape(2, ctx_count * own_share)
    gain_block = jnp.concatenate(
        [gain_mine.T, jnp.zeros((ctx_count * own_share, 126), jnp.float32)], axis=1
    )
    summed = lax.psum_scatter(
        term_rows(group_lefts, group_rights, gain_block, own_share * lax.axis_size("ctx")).astype(
            jnp.bfloat16
        ),
        "ctx",
        scatter_dimension=0,
        tiled=True,
    ).astype(jnp.float32)
    edge_one = HQ * HD
    edge_two = edge_one + HK * HD
    edge_three = edge_two + HK * HD
    edge_four = edge_three + model_width
    edge_five = edge_four + hidden_width
    edge_six = edge_five + hidden_width
    edge_seven = edge_six + ratio * model_width
    grad_query = summed[:, :edge_one]
    grad_key = summed[:, edge_one:edge_two]
    grad_value = summed[:, edge_two:edge_three]
    grad_out = summed[:, edge_three:edge_four]
    grad_gate = summed[:, edge_four:edge_five]
    grad_up = summed[:, edge_five:edge_six]
    grad_down = summed[:, edge_six:edge_seven].reshape(own_share * ratio, model_width)
    grad_attn_gain = summed[:, edge_seven]
    grad_mlp_gain = summed[:, edge_seven + 1]
    return (
        output,
        grad_input,
        grad_query,
        grad_key,
        grad_value,
        grad_out,
        grad_gate,
        grad_up,
        grad_down,
        grad_attn_gain,
        grad_mlp_gain,
    )


DOCS = 4
BF16 = jnp.bfloat16
F32 = jnp.float32
VISIBLE_ROWS = 256


def dot_nn(a, b):
    return jnp.dot(a, b, preferred_element_type=F32)


def dot_nt(a, b):
    return lax.dot_general(a, b, (((1,), (1,)), ((), ())), preferred_element_type=F32)


def dot_tn(a, b):
    return lax.dot_general(a, b, (((0,), (0,)), ((), ())), preferred_element_type=F32)


def scores_of(query, key, code, low_code, key_code):
    scores = dot_nt(query, key) * SCORE_SCALE
    mask = (key_code <= code) & (key_code >= low_code)
    return jnp.where(mask, scores, MASKED)


MESH = pl.DeviceIdType.MESH
TILE = 256
WIDE = 512


def flip(i, d):
    return (i, i + 1 - 2 * (i % 2), (i + 2) % 4, 3 - i)[d]


def line_gather(remote, ctx, plane, slot, own, place):
    def copy(i, way, block, source):
        to = plane + way
        return remote(
            slot + 2 * i + (way + 1) // 2, source, place(to, block), (ctx, to), slot + block
        )

    def sends(i):
        if i == 0:
            return [(plane < 3, lambda: copy(0, 1, plane, own)), (plane > 0, lambda: copy(0, -1, plane, own))]
        return [
            (
                jnp.logical_and(plane >= i, plane < 3),
                lambda: copy(i, 1, plane - i, place(plane, plane - i)),
            ),
            (
                jnp.logical_and(plane + i <= 3, plane > 0),
                lambda: copy(i, -1, plane + i, place(plane, plane + i)),
            ),
        ]

    def start(i):
        for whether, made in sends(i):

            @pl.when(whether)
            def _(made=made):
                made().start()

    def step(i, then=None):
        for whether, block in ((plane >= i, plane - i), (plane + i <= 3, plane + i)):

            @pl.when(whether)
            def _(block=block):
                remote(slot, own, place(plane, block), (ctx, plane), slot + block).wait_recv()
                if then is not None:
                    then(block)

        if i < 3:
            start(i)

    def finish():
        for i in range(3):
            for whether, made in sends(i):

                @pl.when(whether)
                def _(made=made):
                    made().wait_send()

    return start, step, finish


def line_sum(remote, over_z, plane, slot, own, recv, add):
    is_end = jnp.logical_or(plane == 0, plane == 3)
    is_inner = jnp.logical_and(plane > 0, plane < 3)

    def near():
        return remote(slot, own(1), recv.at[0], over_z[1])

    def through(u):
        return remote(slot + 1 + u, own(2 + u), recv.at[2 + u], over_z[1])

    def far(u):
        return remote(slot + 3 + u, own(3 - u), recv.at[1], over_z[3 - u], slot + 3)

    def start():
        @pl.when(is_end)
        def _():
            for u in range(2):
                through(u).start()

        near().start()

    def pass_on():
        @pl.when(is_inner)
        def _():
            for u in range(2):
                through(u).wait_recv()
                add(3 - u, 2 + u)
                far(u).start()

    def wait():
        near().wait_recv()
        far(0).wait_recv()

    def finish():
        near().wait_send()

        @pl.when(is_end)
        def _():
            for u in range(2):
                through(u).wait_send()

        @pl.when(is_inner)
        def _():
            for u in range(2):
                far(u).wait_send()

    return start, pass_on, wait, finish


def xor4(a, b):
    return 2 * ((a // 2 + b // 2) % 2) + (a % 2 + b % 2) % 2


def mlp_kernel(
    second_ref,
    mid_ref,
    upstream_ref,
    gain_ref,
    upstream_hbm,
    gate_hbm,
    up_hbm,
    down_hbm,
    output_ref,
    mid_grad_ref,
    gain_grad_ref,
    branch_all,
    gate_up_sum,
    gate_up_send,
    down_terms,
    gate_w,
    up_w,
    down_w,
    upstream_all,
    second_all,
    act,
    gate_grad,
    up_grad,
    held,
    own_sum,
    pair_send,
    pair_recv,
    z_send,
    z_recv,
    first_recv,
    branch_low,
    staged,
    local_sem,
    staged_sem,
    send_sem,
    recv_sem,
):
    tok = second_ref.shape[0]
    pair = 2 * tok
    hidden = gate_w.shape[1]
    width = second_ref.shape[1]
    ctx, plane = lax.axis_index("ctx"), lax.axis_index("shard")
    chip, core = ctx // 2, ctx % 2
    sibling = (ctx + 1 - 2 * core, plane)
    over_z = [(ctx, flip(plane, d)) for d in range(4)]
    over_chips = [(2 * flip(chip, d) + core, plane) for d in range(4)]

    half = pl.ds(pl.multiple_of(core * hidden, hidden), hidden)
    loads = [
        pltpu.make_async_copy(upstream_hbm, upstream_all, local_sem.at[0]),
        pltpu.make_async_copy(down_hbm, down_w, local_sem.at[1]),
        pltpu.make_async_copy(gate_hbm.at[:, half], gate_w, local_sem.at[2]),
        pltpu.make_async_copy(up_hbm.at[:, half], up_w, local_sem.at[3]),
        pltpu.make_async_copy(second_ref, second_all.at[0, 0], local_sem.at[4]),
    ]
    for load in loads:
        load.start()

    barrier = pltpu.get_barrier_semaphore()
    partners = [sibling] + over_z[1:] + over_chips[1:]
    for partner in partners:
        pl.semaphore_signal(barrier, inc=1, device_id=partner, device_id_type=MESH)
    pl.semaphore_wait(barrier, len(partners))

    def remote(slot, source, target, device, recv=None):
        return pltpu.make_async_remote_copy(
            src_ref=source,
            dst_ref=target,
            send_sem=send_sem.at[slot],
            recv_sem=recv_sem.at[slot if recv is None else recv],
            device_id=device,
            device_id_type=MESH,
        )

    def send(slot, source, target, device):
        copy = remote(slot, source, target, device)
        copy.start()
        return copy

    start_line, step_line, finish_line = line_gather(
        remote, ctx, plane, 32, second_ref, lambda r, b: second_all.at[xor4(r, b), 0]
    )
    start_line(0)
    gather_pair = {0: send(0, second_ref, second_all.at[0, 1], sibling)}
    for load in loads:
        load.wait()

    def rows_of(d):
        return pl.ds(d * pair, pair)

    def forward(d):
        rows = rows_of(d)
        second = lambda: second_all[d].reshape(pair, width)

        def step(t, carry):
            at = pl.ds(pl.multiple_of(t * WIDE, WIDE), WIDE)
            act_grad = dot_nt(upstream_all[rows, :], down_w[at, :])
            gate = dot_nn(second(), gate_w[:, at])
            up_lin = dot_nn(second(), up_w[:, at])
            sigma = 1.0 / (1.0 + jnp.exp(-gate))
            swish = gate * sigma
            act[rows, at] = (swish * up_lin).astype(BF16)
            gate_grad[rows, at] = (
                act_grad * up_lin * (sigma * (1.0 + gate * (1.0 - sigma)))
            ).astype(BF16)
            up_grad[rows, at] = (act_grad * swish).astype(BF16)
            return carry

        lax.fori_loop(0, hidden // WIDE, step, 0)

    def give_pair(d, base, product):
        which = 0 if base == 7 else 1

        def step(t, carry):
            at = pl.ds(pl.multiple_of(t * WIDE, WIDE), WIDE)
            terms = product(at)
            held[d % 2, :, at] = terms[:tok]
            pair_send[which, d, :, at] = terms[tok:].astype(BF16)
            return carry

        copies = []
        half_width = width // 2
        for h in range(2):
            lax.fori_loop(h * half_width // WIDE, (h + 1) * half_width // WIDE, step, 0)
            columns = pl.ds(h * half_width, half_width)
            copies.append(
                send(
                    (base + d) if h == 0 else (44 + 4 * which + d),
                    pair_send.at[which, d, :, columns],
                    pair_recv.at[which, d, :, columns],
                    sibling,
                )
            )
        return copies

    def give_plane(d, base, copies):
        which = 0 if base == 7 else 1
        for copy in copies:
            copy.wait_recv()
        total = held[d % 2] + pair_recv[which, d].astype(F32)
        if d == 0:
            own_sum[which] = total
            return None
        z_send[which, d - 1] = total.astype(BF16)
        copy = remote(
            base + 3 + d, z_send.at[which, d - 1], z_recv.at[which, d - 1], over_z[d]
        )
        if which == 0:
            copy.start()
        return copy

    def back(d):
        rows = rows_of(d)
        return lambda at: dot_nt(gate_grad[rows, :], gate_w[at, :]) + dot_nt(
            up_grad[rows, :], up_w[at, :]
        )

    def onward(d):
        rows = rows_of(d)
        return lambda at: dot_nn(act[rows, :], down_w[:, at])

    def receive(d):
        step_line(d)
        gather_pair[d] = send(3 + d, second_all.at[d, 0], second_all.at[d, 1], sibling)

    pairs, planes = {}, {}
    for d in range(4):
        gather_pair[d].wait_recv()
        forward(d)
        if d == 0:
            receive(1)
        pairs[d] = give_pair(d, 7, back(d))
        if d == 1:
            receive(2)
        planes[d] = give_plane(d, 7, pairs[d])
        if d == 2:
            receive(3)

    second_rows = second_all.reshape(8 * tok, width)
    block = 2 * TILE

    def terms(grads, d, target, first):
        for h in range(2):
            column = flip(chip, d) * block + h * TILE
            left = second_rows[:, pl.ds(pl.multiple_of(column, TILE), TILE)]
            target[pl.ds(first + h * TILE, TILE), :] = dot_tn(left, grads[...]).astype(BF16)

    terms(gate_grad, 1, up_w, 0)
    terms(gate_grad, 3, up_w, block)
    first_gate = send(28, up_w.at[pl.ds(0, 2 * block)], first_recv.at[0], over_chips[1])
    terms(up_grad, 2, up_w, 2 * block)
    terms(up_grad, 3, up_w, 3 * block)
    first_up = send(29, up_w.at[pl.ds(2 * block, 2 * block)], first_recv.at[1], over_chips[2])

    out_pairs, out_planes = {}, {}
    for d in range(4):
        out_pairs[d] = give_pair(d, 14, onward(d))
        if d:
            out_planes[d - 1] = give_plane(d - 1, 14, out_pairs[d - 1])
    out_planes[3] = give_plane(3, 14, out_pairs[3])

    def add_out(d, i):
        def step(t, carry):
            at = pl.ds(pl.multiple_of(t * 32, 32), 32)
            z_send[1, d - 1, at, :] = (
                z_send[1, d - 1, at, :].astype(F32) + z_recv[1, i, at, :].astype(F32)
            ).astype(BF16)
            return carry

        lax.fori_loop(0, tok // 32, step, 0)

    start_sum, pass_sum, wait_sum, finish_sum = line_sum(
        remote, over_z, plane, 38, lambda d: z_send.at[1, d - 1], z_recv.at[1], add_out
    )
    start_sum()

    terms(gate_grad, 2, gate_w, 2 * block)
    terms(up_grad, 1, gate_w, 3 * block)

    for d in (1, 2, 3):
        planes[d].wait_recv()
    chunk = 32
    gain = gain_ref[...]

    def mid_step(i, carry):
        at = pl.ds(pl.multiple_of(i * chunk, chunk), chunk)
        grad = own_sum[0, at, :]
        for d in range(3):
            grad = grad + z_recv[0, d, at, :].astype(F32)
        mid = mid_ref[at, :]
        factor = lax.rsqrt(jnp.mean(mid * mid, axis=-1, keepdims=True) + EPSILON)
        scaled = grad * gain
        mid_grad = (
            upstream_ref[at, :].astype(F32)
            + factor * scaled
            - mid * (factor * factor * factor * jnp.mean(scaled * mid, axis=-1, keepdims=True))
        )
        mid_grad_ref[at, :] = mid_grad
        branch_low[at, :] = mid_grad.astype(BF16)
        return carry + jnp.sum(grad * mid * factor, axis=0, keepdims=True)

    gain_grad_ref[...] = lax.fori_loop(0, tok // chunk, mid_step, jnp.zeros((1, width), F32))
    branch_chips = {
        d: send(20 + d, branch_low, branch_all.at[0, d], over_chips[d]) for d in (1, 2)
    }
    branch_pairs = {0: send(24, branch_low, branch_all.at[1, 0], sibling)}
    keep = pltpu.make_async_copy(branch_low, branch_all.at[0, 0], local_sem.at[0])
    keep.start()

    def to_hbm(slot, target):
        return pltpu.make_async_copy(staged.at[slot], target, staged_sem.at[slot])

    def down_step(t):
        slot = t % 2
        target = down_terms.at[pl.ds(t * TILE, TILE)]
        if t > 1:
            to_hbm(slot, target).wait()
        left = act[:, pl.ds(t * TILE, TILE)]
        staged[slot] = dot_tn(left, upstream_all[...]).astype(BF16)
        to_hbm(slot, target).start()

    for t in range(hidden // TILE):
        down_step(t)
    terms(gate_grad, 0, gate_w, 0)
    terms(up_grad, 0, gate_w, block)
    pass_sum()
    branch_far = {}
    for d in (1, 2):
        branch_chips[d].wait_recv()
        part = pl.ds((d - 1) * (tok // 2), tok // 2)
        branch_far[d] = send(
            23 + 20 * (d - 1), branch_all.at[0, d, part], branch_all.at[0, 3, part], over_chips[3 - d]
        )
        branch_pairs[d] = send(24 + d, branch_all.at[0, d], branch_all.at[1, d], sibling)
    for d in (1, 2):
        branch_far[d].wait_recv()
    branch_pairs[3] = send(27, branch_all.at[0, 3], branch_all.at[1, 3], sibling)

    keep_second = [
        pltpu.make_async_copy(
            gate_w.at[pl.ds((2 + e) * block, block)], gate_up_send.at[e], local_sem.at[2 + e]
        )
        for e in range(2)
    ]

    def add_first(i, carry):
        here = pl.ds(pl.multiple_of(i * 64, 64), 64)
        for e in range(2):
            mine = pl.ds(pl.multiple_of((2 + e) * block + i * 64, 64), 64)
            far = pl.ds(pl.multiple_of(block + i * 64, 64), 64)
            gate_w[mine, :] = (
                gate_w[mine, :].astype(F32) + first_recv[e, far, :].astype(F32)
            ).astype(BF16)
            own = gate_w[pl.ds(pl.multiple_of(e * block + i * 64, 64), 64), :].astype(F32)
            down_w[here, pl.ds(e * hidden, hidden)] = (
                own + first_recv[e, here, :].astype(F32)
            ).astype(BF16)
        return carry

    first_gate.wait_recv()
    first_up.wait_recv()
    lax.fori_loop(0, block // 64, add_first, 0)
    keep_sum = pltpu.make_async_copy(down_w.at[pl.ds(0, block)], gate_up_sum, local_sem.at[1])
    for copy in (keep_sum, *keep_second):
        copy.start()

    wait_sum()

    def out_step(i, carry):
        at = pl.ds(pl.multiple_of(i * chunk, chunk), chunk)
        total = mid_ref[at, :] + own_sum[1, at, :]
        for d in range(2):
            total = total + z_recv[1, d, at, :].astype(F32)
        output_ref[at, :] = total.astype(BF16)
        return carry

    lax.fori_loop(0, tok // chunk, out_step, 0)

    for d in range(4):
        branch_pairs[d].wait_recv()
        for copy in (gather_pair[d], *pairs[d], *out_pairs[d], branch_pairs[d]):
            copy.wait_send()
    for d in (1, 2, 3):
        planes[d].wait_send()
    for d in (1, 2):
        branch_chips[d].wait_send()
        branch_far[d].wait_send()
    finish_sum()
    finish_line()
    keep.wait()
    for slot in range(2):
        to_hbm(slot, down_terms.at[pl.ds(0, TILE)]).wait()
    first_gate.wait_send()
    first_up.wait_send()
    for copy in (keep_sum, *keep_second):
        copy.wait()


def mlp_of(normed_two, mid, upstream, gain, upstream_group, w_gate, w_up, down_rows):
    tok, width = mid.shape
    hidden = down_rows.shape[0]
    rows = upstream_group.shape[0]
    vmem = pl.BlockSpec(memory_space=pltpu.VMEM)
    hbm = pl.BlockSpec(memory_space=pl.ANY)
    return pl.pallas_call(
        mlp_kernel,
        in_specs=[vmem] * 4 + [hbm] * 4,
        out_specs=[vmem] * 3 + [hbm] * 4,
        out_shape=[
            jax.ShapeDtypeStruct((tok, width), BF16),
            jax.ShapeDtypeStruct((tok, width), F32),
            jax.ShapeDtypeStruct((1, width), F32),
            jax.ShapeDtypeStruct((2, 4, tok, width), BF16),
            jax.ShapeDtypeStruct((2 * TILE, 2 * hidden), BF16),
            jax.ShapeDtypeStruct((2, 2 * TILE, hidden), BF16),
            jax.ShapeDtypeStruct((hidden, width), BF16),
        ],
        scratch_shapes=[
            pltpu.VMEM((width, hidden), BF16),
            pltpu.VMEM((width, hidden), BF16),
            pltpu.VMEM((hidden, width), BF16),
            pltpu.VMEM((rows, width), BF16),
            pltpu.VMEM((4, 2, tok, width), BF16),
            pltpu.VMEM((rows, hidden), BF16),
            pltpu.VMEM((rows, hidden), BF16),
            pltpu.VMEM((rows, hidden), BF16),
            pltpu.VMEM((2, tok, width), F32),
            pltpu.VMEM((2, tok, width), F32),
            pltpu.VMEM((2, 4, tok, width), BF16),
            pltpu.VMEM((2, 4, tok, width), BF16),
            pltpu.VMEM((2, 3, tok, width), BF16),
            pltpu.VMEM((2, 4, tok, width), BF16),
            pltpu.VMEM((2, 4 * TILE, hidden), BF16),
            pltpu.VMEM((tok, width), BF16),
            pltpu.VMEM((2, TILE, width), BF16),
            pltpu.SemaphoreType.DMA((5,)),
            pltpu.SemaphoreType.DMA((2,)),
            pltpu.SemaphoreType.DMA((52,)),
            pltpu.SemaphoreType.DMA((52,)),
        ],
        compiler_params=pltpu.CompilerParams(
            collective_id=1, has_side_effects=True, vmem_limit_bytes=60 << 20
        ),
        cost_estimate=pl.CostEstimate(
            flops=18 * rows * width * hidden,
            bytes_accessed=2 * (5 * width * hidden + 4 * rows * width),
            transcendentals=rows * hidden,
        ),
    )(normed_two, mid, upstream, gain, upstream_group, w_gate, w_up, down_rows)


def rotated(values, cosine, sine):
    half = values.shape[1] // 2
    first, second = values[:, :half], values[:, half:]
    return jnp.concatenate([first * cosine - second * sine, second * cosine + first * sine], axis=1)


def front_kernel(
    input_ref,
    attn_gain_ref,
    mlp_gain_ref,
    cosine_ref,
    sine_ref,
    code_ref,
    low_code_ref,
    key_code_ref,
    query_hbm,
    key_hbm,
    value_hbm,
    out_hbm,
    down_hbm,
    upstream_hbm,
    second_ref,
    mid_ref,
    normed_hbm,
    query_ref,
    kv_ref,
    attended_ref,
    log_total_ref,
    head_hbm,
    w_sibling,
    out_hbm_rows,
    down_rows,
    upstream_all,
    normed_ref,
    w_head,
    out_pair,
    inputs_all,
    w_parts,
    attended_other,
    own_sum,
    chip_send,
    chip_recv,
    local_sem,
    send_sem,
    recv_sem,
):
    tok, width = input_ref.shape
    quarter = width // 4
    shard = out_hbm.shape[1]
    hidden = down_rows.shape[0]
    part = hidden // 4
    seq = 8 * tok
    half_seq = 4 * tok
    ctx, plane = lax.axis_index("ctx"), lax.axis_index("shard")
    chip, core = ctx // 2, ctx % 2
    sibling = (ctx + 1 - 2 * core, plane)
    over_z = [(ctx, flip(plane, d)) for d in range(4)]
    over_chips = [(2 * flip(chip, d) + core, plane) for d in range(4)]
    others = (1, 2, 3)

    def at(i, size):
        return pl.ds(pl.multiple_of(i * size, size), size)

    def remote(slot, source, target, device, recv=None):
        return pltpu.make_async_remote_copy(
            src_ref=source,
            dst_ref=target,
            send_sem=send_sem.at[slot],
            recv_sem=recv_sem.at[slot if recv is None else recv],
            device_id=device,
            device_id_type=MESH,
        )

    def send(slot, source, target, device):
        copy = remote(slot, source, target, device)
        copy.start()
        return copy

    def local(slot, source, target):
        return pltpu.make_async_copy(source, target, local_sem.at[slot])

    rows = at(chip, quarter)
    mine = w_parts.at[plane]
    load_query = local(0, query_hbm.at[rows, at(core, HD)], mine.at[0])
    load_key = local(1, key_hbm.at[rows], mine.at[1])
    load_value = local(1, value_hbm.at[rows], mine.at[1])
    load_query.start()

    @pl.when(core == 0)
    def _():
        load_key.start()

    @pl.when(core == 1)
    def _():
        load_value.start()

    keep_input = local(2, input_ref, inputs_all.at[0, 0])
    keep_input.start()
    out_own = out_hbm.at[at(ctx, HD), :]
    keep_out = local(3, out_own, out_pair.at[0, :, at(plane, shard)])
    keep_out.start()

    def down_block(to_plane):
        first = to_plane * (2 * hidden) + core * hidden + chip * part
        return down_hbm.at[pl.ds(pl.multiple_of(first, part), part), :]

    def down_place(column):
        return down_rows.at[at(chip, part), at(column, shard)]

    first_own = plane * (2 * hidden) + core * hidden
    keep_down = local(
        4,
        down_hbm.at[pl.ds(pl.multiple_of(first_own, hidden), hidden), :],
        down_rows.at[:, at(plane, shard)],
    )
    keep_down.start()
    keep_upstream = local(5, upstream_hbm, upstream_all.at[0, 0])
    keep_upstream.start()

    barrier = pltpu.get_barrier_semaphore()
    partners = [sibling] + over_z[1:] + over_chips[1:]
    for partner in partners:
        pl.semaphore_signal(barrier, inc=1, device_id=partner, device_id_type=MESH)
    pl.semaphore_wait(barrier, len(partners))

    input_chips = {
        d: send(d - 1, input_ref, inputs_all.at[0, d], over_chips[d]) for d in others
    }
    input_pairs = {0: send(3, input_ref, inputs_all.at[1, 0], sibling)}
    load_query.wait()
    load_key.wait()
    start_head, step_head, finish_head = line_gather(
        remote, ctx, plane, 37, mine, lambda r, b: w_parts.at[b]
    )
    start_out, step_out, finish_out = line_gather(
        remote, ctx, plane, 43, out_own, lambda r, b: out_pair.at[0, :, at(b, shard)]
    )
    start_up, step_up, finish_up = line_gather(
        remote, ctx, plane, 49, upstream_hbm, lambda r, b: upstream_all.at[xor4(r, b), 0]
    )
    start_head(0)

    head_rows = w_head.at[:, rows, :]

    def pass_head(source):
        apart = xor4(chip, source)
        block = w_parts.at[source]

        @pl.when(apart == 0)
        def _():
            local(6, block, head_rows).start()

        @pl.when(apart != 0)
        def _():
            remote(9 + apart, block, head_rows, (2 * source + core, plane)).start()

    pass_head(plane)
    chunk = 32
    attn_gain = attn_gain_ref[...]

    def norm(e, d):
        def step(i, carry):
            block = inputs_all[e, d, at(i, chunk), :].astype(F32)
            factor = lax.rsqrt(jnp.mean(block * block, axis=-1, keepdims=True) + EPSILON)
            first = (4 * e + d) * tok + i * chunk
            normed_ref[pl.ds(pl.multiple_of(first, chunk), chunk), :] = (
                block * factor * attn_gain
            ).astype(BF16)
            return carry

        lax.fori_loop(0, tok // chunk, step, 0)

    keep_input.wait()
    norm(0, 0)
    step_head(1, pass_head)
    input_pairs[0].wait_recv()
    norm(1, 0)
    for d in (1, 2):
        input_chips[d].wait_recv()
        input_pairs[d] = send(3 + d, inputs_all.at[0, d], inputs_all.at[1, d], sibling)
    norm(0, 1)
    norm(0, 2)
    step_head(2, pass_head)
    down_z = {
        d: send(16 + d, down_block(flip(plane, d)), down_place(plane), over_z[d]) for d in others
    }
    input_chips[3].wait_recv()
    input_pairs[3] = send(6, inputs_all.at[0, 3], inputs_all.at[1, 3], sibling)
    norm(0, 3)
    for d in others:
        input_pairs[d].wait_recv()
        norm(1, d)
    step_head(3, pass_head)

    start_out(0)
    keep_normed = local(2, normed_ref, normed_hbm)
    keep_normed.start()
    local(6, mine, head_rows).wait()
    for d in others:
        remote(9 + d, mine, head_rows, over_chips[d]).wait_recv()

    def project(which, target, flat):
        def step(t, carry):
            here = at(t, TILE)
            made = dot_nn(normed_ref[here, :], w_head[which])
            cosine, sine = cosine_ref[here, :], sine_ref[here, :]
            if flat:
                cosine = jnp.where(core == 0, cosine, 1.0)
                sine = jnp.where(core == 0, sine, 0.0)
            target[here, :] = rotated(made, cosine, sine).astype(BF16)
            return carry

        lax.fori_loop(0, seq // TILE, step, 0)

    keep_out.wait()

    def pass_out(source):
        columns = out_pair.at[0, :, at(source, shard)]
        remote(23 + source, columns, out_pair.at[1, :, at(source, shard)], sibling).start()

    pass_out(plane)
    step_out(1, pass_out)
    mine_kv = kv_ref.at[core]
    project(1, mine_kv, True)
    kv_pair = [
        send(20 + e, mine_kv.at[pl.ds(e * half_seq, half_seq)],
             mine_kv.at[pl.ds((1 - e) * half_seq, half_seq)], sibling)
        for e in range(2)
    ]
    project(0, query_ref, False)
    step_out(2, pass_out)
    head_pair = send(16, w_head, w_sibling, sibling)
    keep_head = local(6, w_head, head_hbm)
    keep_head.start()
    down_near, down_far = {}, {}
    half_part = part // 2

    def down_half(of_chip, column, second):
        first = of_chip * part + second * half_part
        return down_rows.at[
            pl.ds(pl.multiple_of(first, half_part), half_part), at(column, shard)
        ]

    for d in others:
        down_z[d].wait_recv()
        block = down_place(flip(plane, d))
        for e in (1, 2):
            down_near[e, d] = send(51 + 3 * e + d, block, block, over_chips[e])
    start_up(0)
    for copy in kv_pair:
        copy.wait_recv()

    def attend_step(t, carry):
        here = at(t, TILE)
        scores = scores_of(
            query_ref[here, :], kv_ref[0], code_ref[here, :], low_code_ref[here, :], key_code_ref[...]
        )
        top = jnp.max(scores, axis=-1, keepdims=True)
        weights = jnp.exp(scores - top)
        total = jnp.sum(weights, axis=-1, keepdims=True)
        mixed = dot_nn(weights.astype(BF16), kv_ref[1])
        attended_ref[here, :] = (mixed / total).astype(BF16)
        log_total_ref[here, :] = top + jnp.log(total)
        return carry

    lax.fori_loop(0, seq // TILE, attend_step, 0)
    attended_pair = send(22, attended_ref.at[pl.ds(half_seq, half_seq)], attended_other, sibling)
    step_out(3, pass_out)
    for d in range(4):
        columns = out_pair.at[1, :, pl.ds(d * shard, shard)]
        remote(23 + d, columns, columns, sibling).wait_recv()
    keep_rows = local(3, out_pair.at[0], out_hbm_rows)
    keep_rows.start()
    attended_pair.wait_recv()

    def out_step(t, carry):
        here = at(t, TILE)
        terms = dot_nn(attended_ref[:half_seq, :], out_pair[0, :, here]) + dot_nn(
            attended_other[...], out_pair[1, :, here]
        )
        own_sum[:, here] = terms[:tok]
        for d in others:
            chip_send[d - 1, :, here] = terms[d * tok : (d + 1) * tok].astype(BF16)
        return carry

    lax.fori_loop(0, width // TILE, out_step, 0)
    branch = {
        d: send(26 + d, chip_send.at[d - 1], chip_recv.at[d - 1], over_chips[d]) for d in others
    }

    for d in others:
        column = flip(plane, d)
        for e in (1, 2):
            down_near[e, d].wait_recv()
            block = down_half(flip(chip, e), column, e - 1)
            down_far[e, d] = send(57 + 3 * e + d, block, block, over_chips[3 - e])
    upstream_pair = {0: send(33, upstream_hbm, upstream_all.at[0, 1], sibling)}

    def pass_up(d):
        step_up(d)
        upstream_pair[d] = send(33 + d, upstream_all.at[d, 0], upstream_all.at[d, 1], sibling)

    pass_up(1)
    pass_up(2)
    for d in others:
        branch[d].wait_recv()
    mlp_gain = mlp_gain_ref[...]

    def mid_step(i, carry):
        here = at(i, chunk)
        mid = input_ref[here, :].astype(F32) + own_sum[here, :]
        for d in range(3):
            mid = mid + chip_recv[d, here, :].astype(F32)
        factor = lax.rsqrt(jnp.mean(mid * mid, axis=-1, keepdims=True) + EPSILON)
        mid_ref[here, :] = mid
        second_ref[here, :] = (mid * factor * mlp_gain).astype(BF16)
        return carry

    lax.fori_loop(0, tok // chunk, mid_step, 0)

    pass_up(3)
    keep_upstream.wait()
    for d in range(4):
        upstream_pair[d].wait_recv()
        upstream_pair[d].wait_send()
        input_pairs[d].wait_send()
    head_pair.wait_recv()
    for copy in (head_pair, attended_pair, *kv_pair):
        copy.wait_send()
    for copy in (keep_normed, keep_head, keep_rows):
        copy.wait()
    for d in range(4):
        columns = out_pair.at[0, :, pl.ds(d * shard, shard)]
        remote(23 + d, columns, columns, sibling).wait_send()
    keep_down.wait()
    for d in others:
        for e in (1, 2):
            down_near[e, d].wait_send()
            down_far[e, d].wait()
        for copies in (input_chips, down_z, branch):
            copies[d].wait_send()
        remote(9 + d, mine, head_rows, over_chips[d]).wait_send()
    finish_head()
    finish_out()
    finish_up()


def front_of(
    inputs, attn_gain, mlp_gain, cosine, sine, code, low_code, key_code,
    w_query, w_key, w_value, w_out, w_down, upstream,
):
    tok, width = inputs.shape
    seq = 8 * tok
    hidden = w_down.shape[0] // 8
    vmem = pl.BlockSpec(memory_space=pltpu.VMEM)
    hbm = pl.BlockSpec(memory_space=pl.ANY)
    return pl.pallas_call(
        front_kernel,
        in_specs=[vmem] * 8 + [hbm] * 6,
        out_specs=[vmem] * 2 + [hbm] + [vmem] * 4 + [hbm] * 5,
        out_shape=[
            jax.ShapeDtypeStruct((tok, width), BF16),
            jax.ShapeDtypeStruct((tok, width), F32),
            jax.ShapeDtypeStruct((seq, width), BF16),
            jax.ShapeDtypeStruct((seq, HD), BF16),
            jax.ShapeDtypeStruct((2, seq, HD), BF16),
            jax.ShapeDtypeStruct((seq, HD), BF16),
            jax.ShapeDtypeStruct((seq, 1), F32),
            jax.ShapeDtypeStruct((2, width, HD), BF16),
            jax.ShapeDtypeStruct((2, width, HD), BF16),
            jax.ShapeDtypeStruct((HD, width), BF16),
            jax.ShapeDtypeStruct((hidden, width), BF16),
            jax.ShapeDtypeStruct((4, 2, tok, width), BF16),
        ],
        scratch_shapes=[
            pltpu.VMEM((seq, width), BF16),
            pltpu.VMEM((2, width, HD), BF16),
            pltpu.VMEM((2, HD, width), BF16),
            pltpu.VMEM((2, 4, tok, width), BF16),
            pltpu.VMEM((4, 2, width // 4, HD), BF16),
            pltpu.VMEM((4 * tok, HD), BF16),
            pltpu.VMEM((tok, width), F32),
            pltpu.VMEM((3, tok, width), BF16),
            pltpu.VMEM((3, tok, width), BF16),
            pltpu.SemaphoreType.DMA((7,)),
            pltpu.SemaphoreType.DMA((67,)),
            pltpu.SemaphoreType.DMA((67,)),
        ],
        compiler_params=pltpu.CompilerParams(
            collective_id=2, has_side_effects=True, vmem_limit_bytes=56 << 20
        ),
        cost_estimate=pl.CostEstimate(
            flops=2 * seq * width * 3 * HD + 4 * seq * seq * HD,
            bytes_accessed=20 * seq * width,
            transcendentals=seq * seq,
        ),
    )(
        inputs, attn_gain, mlp_gain, cosine, sine, code, low_code, key_code,
        w_query, w_key, w_value, w_out, w_down, upstream,
    )


def back_kernel(
    input_ref,
    mid_grad_ref,
    attn_gain_ref,
    mlp_gain_grad_ref,
    cosine_ref,
    sine_ref,
    code_ref,
    low_code_ref,
    key_code_ref,
    query_ref,
    kv_ref,
    attended_ref,
    log_total_ref,
    normed_hbm,
    head_hbm,
    sibling_hbm,
    out_rows_hbm,
    branch_hbm,
    gate_up_hbm,
    gate_up_send,
    down_terms,
    grad_input_ref,
    gain_total_ref,
    grad_out_ref,
    head_in,
    gate_up_in,
    down_in,
    normed_ref,
    w_head,
    w_sibling,
    out_rows_ref,
    branch_all,
    d_attended,
    d_head,
    d_other,
    d_kv,
    d_kv_other,
    out_send,
    out_recv,
    head_terms,
    head_recv,
    own_sum,
    chip_send,
    chip_recv,
    gate_up_sum,
    gate_up_recv,
    down_parts,
    down_first,
    down_mid,
    down_second,
    down_sum,
    down_planes,
    gains,
    gains_z,
    gains_ctx,
    local_sem,
    send_sem,
    recv_sem,
):
    tok, width = input_ref.shape
    seq = 8 * tok
    half_seq = 4 * tok
    share = out_send.shape[1]
    ctx, plane = lax.axis_index("ctx"), lax.axis_index("shard")
    chip, core = ctx // 2, ctx % 2
    other_core = 1 - core
    sibling = (2 * chip + other_core, plane)
    over_z = [(ctx, flip(plane, d)) for d in range(4)]
    over_chips = [(2 * flip(chip, d) + core, plane) for d in range(4)]
    over_chips_cross = [(2 * flip(chip, d) + other_core, plane) for d in range(4)]
    over_z_cross = [(2 * chip + other_core, flip(plane, d)) for d in range(4)]
    others = (1, 2, 3)

    def at(i, size):
        return pl.ds(pl.multiple_of(i * size, size), size)

    def remote(slot, source, target, device, recv=None):
        return pltpu.make_async_remote_copy(
            src_ref=source,
            dst_ref=target,
            send_sem=send_sem.at[slot],
            recv_sem=recv_sem.at[slot if recv is None else recv],
            device_id=device,
            device_id_type=MESH,
        )

    def send(slot, source, target, device):
        copy = remote(slot, source, target, device)
        copy.start()
        return copy

    def local(slot, source, target):
        return pltpu.make_async_copy(source, target, local_sem.at[slot])

    loads = [
        local(0, branch_hbm, branch_all),
        local(1, out_rows_hbm, out_rows_ref),
        local(2, normed_hbm, normed_ref),
        local(3, down_terms.at[:, chip], down_parts),
        local(7, down_terms.at[:, flip(chip, 2), :, pl.ds(0, width // 2)], down_mid.at[0]),
        local(8, down_terms.at[:, flip(chip, 1), :, pl.ds(width // 2, width // 2)], down_mid.at[1]),
        local(4, head_hbm, w_head),
        local(5, sibling_hbm, w_sibling),
        local(6, gate_up_hbm, gate_up_sum),
    ]
    for load in loads:
        load.start()

    barrier = pltpu.get_barrier_semaphore()
    partners = (
        over_z[1:] + over_z_cross + over_chips[1:] + over_chips_cross[1:]
    )
    for partner in partners:
        pl.semaphore_signal(barrier, inc=1, device_id=partner, device_id_type=MESH)
    pl.semaphore_wait(barrier, len(partners))

    gate_second = send(0, gate_up_send.at[0], gate_up_recv.at[0], over_chips[2])
    up_second = send(46, gate_up_send.at[1], gate_up_recv.at[1], over_chips[1])

    half_width = width // 2
    down_sent = [
        send(
            1 + 2 * e + u,
            down_terms.at[:, flip(chip, (1 + e, 3)[u]), :, pl.ds(e * half_width, half_width)],
            down_first.at[e, u],
            over_chips[1 + e],
        )
        for e in range(2)
        for u in range(2)
    ]

    loads[0].wait()

    def out_step(t, carry):
        here = at(t, TILE)
        made = dot_tn(attended_ref[...], branch_all[:, here])
        out_send[:, :, here] = made.reshape(4, share, TILE).astype(BF16)
        return carry

    lax.fori_loop(0, width // TILE, out_step, 0)

    def add_out(d, i):
        here = flip(plane, d)
        out_send[here] = (out_send[here].astype(F32) + out_recv[i].astype(F32)).astype(BF16)

    start_out, pass_out, wait_out, finish_out = line_sum(
        remote, over_z, plane, 52, lambda d: out_send.at[flip(plane, d)], out_recv, add_out
    )
    start_out()

    loads[1].wait()

    def attended_step(t, carry):
        here = at(t, TILE)
        d_attended[here, :] = dot_nt(branch_all[here, :], out_rows_ref[...]).astype(BF16)
        return carry

    lax.fori_loop(0, seq // TILE, attended_step, 0)
    d_kv[...] = jnp.zeros_like(d_kv)

    def attend_step(t, carry):
        here = at(t, TILE)
        query, outgrad = query_ref[here, :], d_attended[here, :]
        scores = scores_of(
            query, kv_ref[0], code_ref[here, :], low_code_ref[here, :], key_code_ref[...]
        )
        probs = jnp.exp(scores - log_total_ref[here, :])
        prob_grad = dot_nt(outgrad, kv_ref[1])
        delta = jnp.sum(probs * prob_grad, axis=-1, keepdims=True)
        score_grad = (probs * (prob_grad - delta)).astype(BF16)
        d_query = dot_nn(score_grad, kv_ref[0]) * SCORE_SCALE
        d_head[here, :HD] = rotated(d_query, cosine_ref[here, :], -sine_ref[here, :]).astype(BF16)
        d_kv[0] += dot_tn(score_grad, query)
        d_kv[1] += dot_tn(probs.astype(BF16), outgrad)
        return carry

    lax.fori_loop(0, seq // TILE, attend_step, 0)

    give = d_kv.at[other_core]
    kv_pair = [
        send(
            7 + e,
            give.at[pl.ds(e * half_seq, half_seq)],
            d_kv_other.at[pl.ds((1 - e) * half_seq, half_seq)],
            sibling,
        )
        for e in range(2)
    ]
    loads[8].wait()
    gate_second.wait_recv()
    up_second.wait_recv()
    hidden = gate_up_recv.shape[2]

    def gate_up_step(i, carry):
        here = at(i, share)
        for e in range(2):
            columns = pl.ds(e * hidden, hidden)
            gate_up_sum[here, columns] = (
                gate_up_sum[here, columns].astype(F32) + gate_up_recv[e, here, :].astype(F32)
            ).astype(BF16)
        return carry

    lax.fori_loop(0, 8, gate_up_step, 0)

    place = gate_up_in.at[plane, core]

    def gate_up_rows(to_core, to_plane):
        return gate_up_sum.at[at(4 * to_core + to_plane, share), :]

    gate_up_z = {
        d: send(18 + d, gate_up_rows(core, flip(plane, d)), place, over_z[d]) for d in others
    }
    gate_up_cross = {
        d: send(22 + d, gate_up_rows(other_core, flip(plane, d)), place, over_z_cross[d])
        for d in range(4)
    }
    keep_gate_up = local(1, gate_up_rows(core, plane), place)
    keep_gate_up.start()
    for copy in kv_pair:
        copy.wait_recv()

    def kv_step(t, carry):
        here = at(t, TILE)
        total = d_kv[core, here, :] + d_kv_other[here, :]
        total = total * jnp.where(core == 0, SCORE_SCALE, 1.0)
        cosine = jnp.where(core == 0, cosine_ref[here, :], 1.0)
        sine = jnp.where(core == 0, sine_ref[here, :], 0.0)
        d_head[here, HD:] = rotated(total, cosine, -sine).astype(BF16)
        return carry

    lax.fori_loop(0, seq // TILE, kv_step, 0)
    head_pair = send(9, d_head.at[pl.ds(half_seq, half_seq)], d_other, sibling)

    loads[2].wait()

    def head_step(t, carry):
        made = dot_tn(normed_ref[:, at(t, TILE)], d_head[...])
        head_terms[:, t] = made.reshape(4, share, 2 * HD).astype(BF16)
        return carry

    lax.fori_loop(0, width // TILE, head_step, 0)

    def add_head(d, i):
        here = flip(plane, d)

        def step(t, carry):
            head_terms[here, t] = (
                head_terms[here, t].astype(F32) + head_recv[i, t].astype(F32)
            ).astype(BF16)
            return carry

        lax.fori_loop(0, 8, step, 0)

    start_head, pass_head, wait_head, finish_head = line_sum(
        remote, over_z, plane, 47, lambda d: head_terms.at[flip(plane, d)], head_recv, add_head
    )
    start_head()

    loads[6].wait()
    loads[7].wait()
    head_pair.wait_recv()

    def normed_step(t, carry):
        here = at(t, TILE)
        made = (
            dot_nt(d_head[:half_seq, :HD], w_head[0, here, :])
            + dot_nt(d_head[:half_seq, HD:], w_head[1, here, :])
            + dot_nt(d_other[:, :HD], w_sibling[0, here, :])
            + dot_nt(d_other[:, HD:], w_sibling[1, here, :])
        )
        own_sum[:, here] = made[:tok]
        for d in others:
            chip_send[d - 1, :, here] = made[d * tok : (d + 1) * tok].astype(BF16)
        return carry

    lax.fori_loop(0, width // TILE, normed_step, 0)
    normed_chips = {
        d: send(12 + d, chip_send.at[d - 1], chip_recv.at[d - 1], over_chips[d]) for d in others
    }

    loads[4].wait()
    loads[5].wait()

    def down_mid_step(p, carry):
        for e in range(2):
            down_mid[e, p] = (
                down_mid[e, p].astype(F32) + down_first[e, 1, p].astype(F32)
            ).astype(BF16)
        return carry

    for copy in down_sent:
        copy.wait_recv()
    lax.fori_loop(0, 4, down_mid_step, 0)
    down_last = [
        send(5 + e, down_mid.at[e], down_second.at[e], over_chips[2 - e]) for e in range(2)
    ]
    pass_out()
    pass_head()
    for d in others:
        normed_chips[d].wait_recv()
    chunk = 32
    gain = attn_gain_ref[...]

    def input_step(i, carry):
        here = at(i, chunk)
        grad = own_sum[here, :]
        for d in range(3):
            grad = grad + chip_recv[d, here, :].astype(F32)
        block = input_ref[here, :].astype(F32)
        factor = lax.rsqrt(jnp.mean(block * block, axis=-1, keepdims=True) + EPSILON)
        scaled = grad * gain
        grad_input_ref[here, :] = (
            mid_grad_ref[here, :]
            + factor * scaled
            - block * (factor * factor * factor * jnp.mean(scaled * block, axis=-1, keepdims=True))
        ).astype(BF16)
        return carry + jnp.sum(grad * block * factor, axis=0, keepdims=True)

    gain_grad = lax.fori_loop(0, tok // chunk, input_step, jnp.zeros((1, width), F32))
    gains[...] = jnp.concatenate(
        [gain_grad, mlp_gain_grad_ref[...]], axis=0
    )
    gains_planes = {d: send(25 + d, gains, gains_z.at[d - 1], over_z[d]) for d in others}

    loads[3].wait()
    for copy in down_last:
        copy.wait_recv()

    def down_step(p, carry):
        for e in range(2):
            columns = pl.ds(e * half_width, half_width)
            down_sum[p, :, columns] = (
                down_parts[p, :, columns].astype(F32)
                + down_first[e, 0, p].astype(F32)
                + down_second[e, p].astype(F32)
            ).astype(BF16)
        return carry

    lax.fori_loop(0, 4, down_step, 0)
    down_z = {
        d: send(15 + d, down_sum.at[flip(plane, d)], down_planes.at[plane], over_z[d])
        for d in others
    }
    keep_down = local(3, down_sum.at[plane], down_planes.at[plane])
    keep_down.start()


    wait_head()
    def head_sum(i, carry):
        total = head_terms[plane, i].astype(F32)
        for d in range(2):
            total = total + head_recv[d, i].astype(F32)
        head_terms[plane, i] = total.astype(BF16)
        return carry

    lax.fori_loop(0, 8, head_sum, 0)
    head_place = head_in.at[ctx]
    head_chips = {
        d: send(28 + d, head_terms.at[plane, 2 * flip(chip, d) + core], head_place, over_chips[d])
        for d in others
    }
    head_cross = {
        d: send(
            32 + d, head_terms.at[plane, 2 * flip(chip, d) + other_core], head_place,
            over_chips_cross[d],
        )
        for d in range(4)
    }
    keep_head = local(0, head_terms.at[plane, ctx], head_place)
    keep_head.start()

    for d in others:
        gains_planes[d].wait_recv()
        gains_planes[d].wait_send()
    gains[...] = gains[...] + gains_z[0] + gains_z[1] + gains_z[2]
    gains_chips = {
        d: send(35 + d, gains, gains_ctx.at[0, d], over_chips[d]) for d in others
    }
    gains_cross = {
        d: send(39 + d, gains, gains_ctx.at[1, d], over_chips_cross[d]) for d in range(4)
    }

    wait_out()
    total = out_send[plane].astype(F32)
    for d in range(2):
        total = total + out_recv[d].astype(F32)
    grad_out_ref[...] = total

    keep_down.wait()
    down_place = down_in.at[chip]
    for d in range(4):
        if d:
            down_z[d].wait_recv()
        source = flip(plane, d)
        apart = xor4(chip, source)
        block = down_planes.at[source]

        @pl.when(apart == 0)
        def _(block=block):
            local(4, block, down_place).start()

        @pl.when(apart != 0)
        def _(block=block, source=source, apart=apart):
            remote(42 + apart, block, down_place, (2 * source + core, plane)).start()

    for d in others:
        gains_chips[d].wait_recv()
    for d in range(4):
        gains_cross[d].wait_recv()
    total = gains[...] + gains_ctx[1, 0]
    for d in others:
        total = total + gains_ctx[0, d] + gains_ctx[1, d]
    gain_total_ref[...] = total

    local(4, down_sum.at[plane], down_place).wait()
    keep_gate_up.wait()
    keep_head.wait()
    for d in others:
        remote(42 + d, down_sum.at[plane], down_place, over_chips[d]).wait()
        gate_up_z[d].wait_recv()
        head_chips[d].wait_recv()
        for copies in (
            normed_chips, down_z, gate_up_z, head_chips, gains_chips
        ):
            copies[d].wait_send()
    finish_out()
    finish_head()
    for d in range(4):
        for copies in (gate_up_cross, head_cross):
            copies[d].wait()
        gains_cross[d].wait_send()
    for copy in (gate_second, up_second, head_pair, *kv_pair, *down_sent, *down_last):
        copy.wait_send()


def back_of(*operands):
    inputs, query = operands[0], operands[9]
    tok, width = inputs.shape
    seq = query.shape[0]
    hidden = operands[18].shape[-1] // 2
    share = HD // 4
    vmem = pl.BlockSpec(memory_space=pltpu.VMEM)
    hbm = pl.BlockSpec(memory_space=pl.ANY)
    return pl.pallas_call(
        back_kernel,
        in_specs=[vmem] * 13 + [hbm] * 8,
        out_specs=[vmem] * 6,
        out_shape=[
            jax.ShapeDtypeStruct((tok, width), BF16),
            jax.ShapeDtypeStruct((2, width), F32),
            jax.ShapeDtypeStruct((share, width), F32),
            jax.ShapeDtypeStruct((8, share, 2 * HD), BF16),
            jax.ShapeDtypeStruct((4, 2, share, 2 * hidden), BF16),
            jax.ShapeDtypeStruct((4, share, width), BF16),
        ],
        scratch_shapes=[
            pltpu.VMEM((seq, width), BF16),
            pltpu.VMEM((2, width, HD), BF16),
            pltpu.VMEM((2, width, HD), BF16),
            pltpu.VMEM((HD, width), BF16),
            pltpu.VMEM((seq, width), BF16),
            pltpu.VMEM((seq, HD), BF16),
            pltpu.VMEM((seq, 2 * HD), BF16),
            pltpu.VMEM((4 * tok, 2 * HD), BF16),
            pltpu.VMEM((2, seq, HD), F32),
            pltpu.VMEM((seq, HD), F32),
            pltpu.VMEM((4, share, width), BF16),
            pltpu.VMEM((4, share, width), BF16),
            pltpu.VMEM((4, 8, share, 2 * HD), BF16),
            pltpu.VMEM((4, 8, share, 2 * HD), BF16),
            pltpu.VMEM((tok, width), F32),
            pltpu.VMEM((3, tok, width), BF16),
            pltpu.VMEM((3, tok, width), BF16),
            pltpu.VMEM((8 * share, 2 * hidden), BF16),
            pltpu.VMEM((2, 8 * share, hidden), BF16),
            pltpu.VMEM((4, share, width), BF16),
            pltpu.VMEM((2, 2, 4, share, width // 2), BF16),
            pltpu.VMEM((2, 4, share, width // 2), BF16),
            pltpu.VMEM((2, 4, share, width // 2), BF16),
            pltpu.VMEM((4, share, width), BF16),
            pltpu.VMEM((4, share, width), BF16),
            pltpu.VMEM((2, width), F32),
            pltpu.VMEM((3, 2, width), F32),
            pltpu.VMEM((2, 4, 2, width), F32),
            pltpu.SemaphoreType.DMA((9,)),
            pltpu.SemaphoreType.DMA((57,)),
            pltpu.SemaphoreType.DMA((57,)),
        ],
        compiler_params=pltpu.CompilerParams(
            collective_id=3, has_side_effects=True, vmem_limit_bytes=60 << 20
        ),
        cost_estimate=pl.CostEstimate(
            flops=2 * seq * width * 6 * HD + 10 * seq * seq * HD,
            bytes_accessed=20 * seq * width,
            transcendentals=seq * seq,
        ),
    )(*operands)


def on_device_by_head(
    layer_input,
    w_query,
    w_key,
    w_value,
    w_out,
    w_gate,
    w_up,
    w_down,
    attn_gain,
    mlp_gain,
    block_pairs,
    doc_ids,
    cotangent,
):
    tok_rows, width = layer_input.shape[1:]
    planes = lax.axis_size("shard")
    ctx_count = lax.axis_size("ctx")
    chips = ctx_count // 2
    ctx, plane = lax.axis_index("ctx"), lax.axis_index("shard")
    chip, core = ctx // 2, ctx % 2
    seq_rows = tok_rows * ctx_count
    own_share = width // (planes * ctx_count)

    inputs_low = layer_input[0]
    pairs, documents = block_pairs[0], doc_ids[0]
    order = jnp.stack([(chip ^ d) * 2 + (core ^ e) for e in range(2) for d in range(chips)])
    chosen = jnp.sum(
        jnp.where(order[:, None] == jnp.arange(ctx_count)[None, :], pairs[None, :], 0), axis=1
    )[:, None]
    within = jnp.arange(tok_rows, dtype=jnp.int32)[None, :]
    block = tok_rows // 2
    positions = jnp.where(
        within < block, chosen * block, (2 * ctx_count - 1 - chosen) * block - block
    )
    positions = (positions + within).reshape(-1)
    begins = jnp.sum(documents[None, :] < jnp.arange(1, DOCS)[:, None], axis=1)
    document = jnp.sum((positions[None, :] >= begins[:, None]).astype(jnp.int32), axis=0)
    span = 2 * seq_rows
    doc_first = document * span
    code = doc_first + positions
    low_code = jnp.maximum(doc_first, code - (WINDOW - 1))
    code_column, low_column, code_row = code[:, None], low_code[:, None], code[None, :]
    cosine, sine = rope_tables(positions, HD)

    upstream_low = cotangent[0]
    (
        normed_two,
        mid,
        normed_all,
        query,
        key_value,
        attended,
        log_total,
        w_head,
        w_sibling,
        out_rows,
        down_rows,
        upstream_group,
    ) = front_of(
        inputs_low,
        attn_gain[None],
        mlp_gain[None],
        cosine,
        sine,
        code_column,
        low_column,
        code_row,
        w_query,
        w_key,
        w_value,
        w_out,
        w_down,
        upstream_low,
    )
    (
        output,
        mid_grad,
        mlp_gain_grad,
        branch_all,
        gate_up_sum,
        gate_up_send,
        down_terms,
    ) = mlp_of(
        normed_two,
        mid,
        upstream_low,
        mlp_gain[None],
        upstream_group.reshape(-1, width),
        w_gate,
        w_up,
        down_rows,
    )
    grad_input, gain_total, grad_out, head_in, gate_up_in, down_in = back_of(
        inputs_low,
        mid_grad,
        attn_gain[None],
        mlp_gain_grad,
        cosine,
        sine,
        code_column,
        low_column,
        code_row,
        query,
        key_value,
        attended,
        log_total,
        normed_all,
        w_head,
        w_sibling,
        out_rows,
        branch_all.reshape(seq_rows, width),
        gate_up_sum,
        gate_up_send,
        down_terms.reshape(planes, chips, -1, width),
    )
    hidden = gate_up_in.shape[-1] // 2
    gate_up = gate_up_in.astype(F32)
    columns = lambda parts: jnp.concatenate(parts, axis=1)
    grad_gate = columns([gate_up[p, e, :, :hidden] for p in range(planes) for e in range(2)])
    grad_up = columns([gate_up[p, e, :, hidden:] for p in range(planes) for e in range(2)])
    head = head_in.astype(F32)
    grad_query = columns([head[i, :, :HD] for i in range(ctx_count)])
    grad_key = columns([head[i, :, HD:] for i in range(0, ctx_count, 2)])
    grad_value = columns([head[i, :, HD:] for i in range(1, ctx_count, 2)])
    grad_down = down_in.astype(F32).reshape(-1, width)
    gains = lax.dynamic_slice(gain_total, (0, own_share * (planes * ctx + plane)), (2, own_share))
    return (
        output[None],
        grad_input[None],
        grad_query,
        grad_key,
        grad_value,
        grad_out,
        grad_gate,
        grad_up,
        grad_down,
        gains[0],
        gains[1],
    )


def plan_of(mesh):
    chips, planes = mesh.shape["ctx"] // 2, mesh.shape["shard"]
    if mesh.shape["ctx"] == HQ and HQ == 2 * HK and chips == planes == HK:
        return on_device_by_head
    return on_device


def solution(mesh):
    placed = (
        P("shard", "ctx", None),
        P(None, "shard"),
        P(None, "shard"),
        P(None, "shard"),
        P(None, "shard"),
        P(None, "shard"),
        P(None, "shard"),
        P(None, "shard"),
        P(),
        P(),
        P("shard", None),
        P("shard", None),
        P("shard", "ctx", None),
    )
    return jax.shard_map(
        plan_of(mesh),
        mesh=mesh,
        in_specs=placed,
        out_specs=(
            P("shard", "ctx", None),
            P("shard", "ctx", None),
            P(("ctx", "shard"), None),
            P(("ctx", "shard"), None),
            P(("ctx", "shard"), None),
            P(("ctx", "shard"), None),
            P(("ctx", "shard"), None),
            P(("ctx", "shard"), None),
            P(("ctx", "shard"), None),
            P(("ctx", "shard")),
            P(("ctx", "shard")),
        ),
        check_vma=False,
    )
```

```python
import math

import jax
import jax.numpy as jnp
from jax import lax
from jax.experimental import pallas as pl
from jax.experimental.pallas import tpu as pltpu
from jax.sharding import PartitionSpec as P

HQ = 8
HK = 4
HD = 256
WINDOW = 1024


EPSILON = 1e-06
SCORE_SCALE = 0.0625
MASKED = -1e30
ROPE_BASE = 1000042.0


def position_of(rows, pairs, per_device, blocks_total):
    device = rows // per_device
    within = rows % per_device
    half = per_device // 2
    chosen = jnp.take(pairs, device)
    first = chosen * half + within
    second = (blocks_total - 1 - chosen) * half + within - half
    return jnp.where(within < half, first, second)


def rope_tables(positions, head):
    half = head // 2
    freq = ROPE_BASE ** (-(jnp.arange(half, dtype=jnp.float32) * 2.0) / head)
    angle = positions.astype(jnp.float32)[:, None] * freq[None, :]
    return (jnp.cos(angle), jnp.sin(angle))


def rotate(values, cosine, sine):
    half = values.shape[-1] // 2
    first = values[..., :half]
    second = values[..., half:]
    cosine = cosine[:, None, :]
    sine = sine[:, None, :]
    return jnp.concatenate(
        [first * cosine - second * sine, second * cosine + first * sine], axis=-1
    )


def rotate_back(grads, cosine, sine):
    half = grads.shape[-1] // 2
    first = grads[..., :half]
    second = grads[..., half:]
    cosine = cosine[:, None, :]
    sine = sine[:, None, :]
    return jnp.concatenate(
        [first * cosine + second * sine, second * cosine - first * sine], axis=-1
    )


def visible(query_pos, query_doc, key_pos, key_doc):
    distance = query_pos[:, None] - key_pos[None, :]
    return (query_doc[:, None] == key_doc[None, :]) & (distance >= 0) & (distance < WINDOW)


def write_columns(left, piece):
    made = jnp.dot(left, piece, preferred_element_type=jnp.float32)
    return made


def contract_full(grads, weight):
    return lax.dot_general(
        grads, weight, (((1,), (1,)), ((), ())), preferred_element_type=jnp.float32
    )


def alternate(parts, shard_count, rows):
    return jnp.concatenate([part.reshape(rows, shard_count, -1) for part in parts], axis=2).reshape(
        rows, -1
    )


def outer_sum(left, right):
    return lax.dot_general(
        left, right, (((0,), (0,)), ((), ())), preferred_element_type=jnp.float32
    )


def term_rows(lefts, rights, gain_block, count):
    normed_all, attended_all, second_all, act_all = lefts
    query_g, key_g, value_g, branch_g, gate_g, up_g, upstream_g = rights
    down_part = outer_sum(act_all, upstream_g).reshape(count, -1)
    return jnp.concatenate(
        [
            outer_sum(normed_all, query_g),
            outer_sum(normed_all, key_g),
            outer_sum(normed_all, value_g),
            outer_sum(attended_all, branch_g),
            outer_sum(second_all, gate_g),
            outer_sum(second_all, up_g),
            down_part,
            gain_block,
        ],
        axis=1,
    )


def deal_columns(values, ctx_count, shard_count):
    rows = values.shape[0]
    return (
        values.reshape(rows, ctx_count, shard_count, -1)
        .transpose(0, 2, 1, 3)
        .reshape(rows, shard_count, -1)
    )


def on_device(
    layer_input,
    w_query,
    w_key,
    w_value,
    w_out,
    w_gate,
    w_up,
    w_down,
    attn_gain,
    mlp_gain,
    block_pairs,
    doc_ids,
    cotangent,
):
    tok_rows = layer_input.shape[1]
    model_width = layer_input.shape[2]
    shard_count = lax.axis_size("shard")
    ctx_count = lax.axis_size("ctx")
    device_count = lax.axis_size(("ctx", "shard"))
    group_size = HQ // HK
    blocks_total = 2 * ctx_count
    pairs = block_pairs[0]
    documents = doc_ids[0]
    own_rows = lax.axis_index("ctx") * tok_rows + jnp.arange(tok_rows, dtype=jnp.int32)
    own_pos = position_of(own_rows, pairs, tok_rows, blocks_total)
    own_doc = jnp.take(documents, own_pos)
    cosine, sine = rope_tables(own_pos, HD)
    stack_qkv = jnp.concatenate([w_query, w_key, w_value], axis=1)
    stack_mlp = jnp.concatenate([w_gate, w_up], axis=1)
    per_query = w_query.shape[1]
    per_key = w_key.shape[1]
    per_hidden = w_gate.shape[1]
    hidden_width = w_down.shape[0]
    inputs = layer_input.reshape(tok_rows, model_width).astype(jnp.float32)
    factor_one = lax.rsqrt(jnp.mean(inputs * inputs, axis=-1, keepdims=True) + EPSILON)
    normed = (inputs * factor_one * attn_gain).astype(jnp.bfloat16)
    projected = write_columns(normed, lax.all_gather(stack_qkv, "shard", axis=1, tiled=True))
    projected = projected.reshape(tok_rows, shard_count, -1)
    query_lin = projected[:, :, :per_query].reshape(tok_rows, HQ, HD)
    key_lin = projected[:, :, per_query : per_query + per_key].reshape(tok_rows, HK, HD)
    value_lin = projected[:, :, per_query + per_key :].reshape(tok_rows, HK * HD)
    query_rot = (
        rotate(query_lin, cosine, sine).astype(jnp.bfloat16).reshape(tok_rows, HK, group_size, HD)
    )
    key_rot = rotate(key_lin, cosine, sine).astype(jnp.bfloat16).reshape(tok_rows, HK * HD)
    value_low = value_lin.astype(jnp.bfloat16)

    def key_mask(first_row, count):
        key_pos = position_of(
            first_row + jnp.arange(count, dtype=jnp.int32), pairs, tok_rows, blocks_total
        )
        return visible(own_pos, own_doc, key_pos, jnp.take(documents, key_pos))[:, None, None, :]

    start_state = (
        jnp.full((tok_rows, HK, group_size), MASKED, jnp.float32),
        jnp.zeros((tok_rows, HK, group_size), jnp.float32),
        jnp.zeros((tok_rows, HK, group_size, HD), jnp.float32),
    )
    keys = lax.all_gather(key_rot, "ctx", axis=0, tiled=True)
    values = lax.all_gather(value_low, "ctx", axis=0, tiled=True)
    count = keys.shape[0]
    step = math.gcd(count, 4 * tok_rows)
    keys = keys.reshape(count // step, step, HK, HD)
    values = values.reshape(count // step, step, HK, HD)

    def attend_step(i, running):
        top, total, accum = running
        mask = key_mask(i * step, step)
        scores = (
            jnp.einsum("tkgd,skd->tkgs", query_rot, keys[i], preferred_element_type=jnp.float32)
            * SCORE_SCALE
        )
        scores = jnp.where(mask, scores, MASKED)
        new_top = jnp.maximum(top, jnp.max(scores, axis=-1))
        weights = jnp.where(mask, jnp.exp(scores - new_top[..., None]), 0.0)
        shrink = jnp.exp(top - new_top)
        total = total * shrink + jnp.sum(weights, axis=-1)
        accum = accum * shrink[..., None] + jnp.einsum(
            "tkgs,skd->tkgd",
            weights.astype(jnp.bfloat16),
            values[i],
            preferred_element_type=jnp.float32,
        )
        return (new_top, total, accum)

    top, total, accum = lax.fori_loop(0, count // step, attend_step, start_state)
    log_total = top + jnp.log(total)
    attended_full = accum / total[..., None]
    attended = attended_full.astype(jnp.bfloat16).reshape(tok_rows, HQ * HD)
    branch_one = write_columns(attended, lax.all_gather(w_out, "shard", axis=1, tiled=True))
    mid = inputs + branch_one
    factor_two = lax.rsqrt(jnp.mean(mid * mid, axis=-1, keepdims=True) + EPSILON)
    normed_two = (mid * factor_two * mlp_gain).astype(jnp.bfloat16)
    gate_up = write_columns(normed_two, lax.all_gather(stack_mlp, "shard", axis=1, tiled=True))
    gate_up = gate_up.reshape(tok_rows, shard_count, -1)
    gate = gate_up[:, :, :per_hidden].reshape(tok_rows, hidden_width)
    up_lin = gate_up[:, :, per_hidden:].reshape(tok_rows, hidden_width)
    sigma = jax.nn.sigmoid(gate)
    swish = gate * sigma
    act = (swish * up_lin).astype(jnp.bfloat16)
    branch_two = write_columns(act, lax.all_gather(w_down, "shard", axis=1, tiled=True))
    output = (mid + branch_two).astype(jnp.bfloat16).reshape(1, tok_rows, model_width)
    full_qkv, full_out, full_mlp, full_down = (
        lax.all_gather(stack_qkv, "shard", axis=1, tiled=True),
        lax.all_gather(w_out, "shard", axis=1, tiled=True),
        lax.all_gather(stack_mlp, "shard", axis=1, tiled=True),
        lax.all_gather(w_down, "shard", axis=1, tiled=True),
    )
    upstream_low = cotangent.reshape(tok_rows, model_width)
    upstream = upstream_low.astype(jnp.float32)
    act_grad = contract_full(upstream_low, full_down)
    gate_grad = (act_grad * up_lin * (sigma * (1.0 + gate * (1.0 - sigma)))).astype(jnp.bfloat16)
    up_grad = (act_grad * swish).astype(jnp.bfloat16)
    stacked_mlp_grad = alternate((gate_grad, up_grad), shard_count, tok_rows)
    norm_two_grad = contract_full(stacked_mlp_grad, full_mlp)
    mlp_gain_term = jnp.sum(norm_two_grad * mid * factor_two, axis=0)
    scaled_two = norm_two_grad * mlp_gain
    mid_grad = (
        upstream
        + factor_two * scaled_two
        - mid * factor_two**3 * jnp.mean(scaled_two * mid, axis=-1, keepdims=True)
    )
    branch_grad = mid_grad.astype(jnp.bfloat16)
    attended_grad = contract_full(branch_grad, full_out)
    attended_low = attended_grad.astype(jnp.bfloat16).reshape(tok_rows, HK, group_size, HD)
    delta = jnp.sum(attended_low.astype(jnp.float32) * attended_full, axis=-1)

    def query_grads(carry, piece):
        keys, values = piece
        count = keys.shape[0]
        step = math.gcd(count, 4 * tok_rows)
        keys = keys.reshape(count // step, step, HK, HD)
        values = values.reshape(count // step, step, HK, HD)

        def query_step(i, query_sum):
            mask = key_mask(i * step, step)
            scores = (
                jnp.einsum("tkgd,skd->tkgs", query_rot, keys[i], preferred_element_type=jnp.float32)
                * SCORE_SCALE
            )
            probs = jnp.where(mask, jnp.exp(scores - log_total[..., None]), 0.0)
            prob_grad = jnp.einsum(
                "tkgd,skd->tkgs", attended_low, values[i], preferred_element_type=jnp.float32
            )
            score_grad = (probs * (prob_grad - delta[..., None])).astype(jnp.bfloat16)
            return query_sum + jnp.einsum(
                "tkgs,skd->tkgd", score_grad, keys[i], preferred_element_type=jnp.float32
            )

        return lax.fori_loop(0, count // step, query_step, carry)

    query_sum = query_grads(
        jnp.zeros((tok_rows, HK, group_size, HD), jnp.float32),
        (
            lax.all_gather(key_rot, "ctx", axis=0, tiled=True),
            lax.all_gather(value_low, "ctx", axis=0, tiled=True),
        ),
    )
    all_log_total, all_delta = (
        lax.all_gather(log_total, "ctx", axis=0, tiled=True),
        lax.all_gather(delta, "ctx", axis=0, tiled=True),
    )
    key_three = key_rot.reshape(tok_rows, HK, HD)
    value_three = value_low.reshape(tok_rows, HK, HD)

    def key_grads(carry, piece):
        queries, outgrads = piece
        count = queries.shape[0]
        step = math.gcd(count, 4 * tok_rows)
        queries = queries.reshape(count // step, step, HK, group_size, HD)
        outgrads = outgrads.reshape(count // step, step, HK, group_size, HD)

        def key_step(i, running):
            key_sum, value_sum = running
            first_row = i * step
            query_pos = position_of(
                first_row + jnp.arange(step, dtype=jnp.int32), pairs, tok_rows, blocks_total
            )
            mask = visible(query_pos, jnp.take(documents, query_pos), own_pos, own_doc)[
                :, None, None, :
            ]
            lse_part = lax.dynamic_slice_in_dim(all_log_total, first_row, step, 0)
            delta_part = lax.dynamic_slice_in_dim(all_delta, first_row, step, 0)
            scores = (
                jnp.einsum(
                    "skgd,tkd->skgt", queries[i], key_three, preferred_element_type=jnp.float32
                )
                * SCORE_SCALE
            )
            probs = jnp.where(mask, jnp.exp(scores - lse_part[..., None]), 0.0)
            prob_grad = jnp.einsum(
                "skgd,tkd->skgt", outgrads[i], value_three, preferred_element_type=jnp.float32
            )
            score_grad = (probs * (prob_grad - delta_part[..., None])).astype(jnp.bfloat16)
            value_sum = value_sum + jnp.einsum(
                "skgt,skgd->tkd",
                probs.astype(jnp.bfloat16),
                outgrads[i],
                preferred_element_type=jnp.float32,
            )
            key_sum = key_sum + jnp.einsum(
                "skgt,skgd->tkd", score_grad, queries[i], preferred_element_type=jnp.float32
            )
            return (key_sum, value_sum)

        return lax.fori_loop(0, count // step, key_step, carry)

    key_sum, value_sum = key_grads(
        (jnp.zeros((tok_rows, HK, HD), jnp.float32), jnp.zeros((tok_rows, HK, HD), jnp.float32)),
        (
            lax.all_gather(query_rot.reshape(tok_rows, HQ * HD), "ctx", axis=0, tiled=True),
            lax.all_gather(attended_low.reshape(tok_rows, HQ * HD), "ctx", axis=0, tiled=True),
        ),
    )
    query_grad = (
        rotate_back(query_sum.reshape(tok_rows, HQ, HD) * SCORE_SCALE, cosine, sine)
        .astype(jnp.bfloat16)
        .reshape(tok_rows, HQ * HD)
    )
    key_grad = (
        rotate_back(key_sum * SCORE_SCALE, cosine, sine)
        .astype(jnp.bfloat16)
        .reshape(tok_rows, HK * HD)
    )
    value_grad = value_sum.astype(jnp.bfloat16).reshape(tok_rows, HK * HD)
    stacked_qkv_grad = alternate((query_grad, key_grad, value_grad), shard_count, tok_rows)
    normed_grad = contract_full(stacked_qkv_grad, full_qkv)
    attn_gain_term = jnp.sum(normed_grad * inputs * factor_one, axis=0)
    scaled_one = normed_grad * attn_gain
    input_grad = (
        mid_grad
        + factor_one * scaled_one
        - inputs * factor_one**3 * jnp.mean(scaled_one * inputs, axis=-1, keepdims=True)
    )
    grad_input = input_grad.astype(jnp.bfloat16).reshape(1, tok_rows, model_width)
    ratio = hidden_width // model_width
    own_share = model_width // device_count
    rights = (query_grad, key_grad, value_grad, branch_grad, gate_grad, up_grad, upstream_low)
    group_rights = (
        lax.all_gather(rights[0], "shard", axis=0, tiled=True),
        lax.all_gather(rights[1], "shard", axis=0, tiled=True),
        lax.all_gather(rights[2], "shard", axis=0, tiled=True),
        lax.all_gather(rights[3], "shard", axis=0, tiled=True),
        lax.all_gather(rights[4], "shard", axis=0, tiled=True),
        lax.all_gather(rights[5], "shard", axis=0, tiled=True),
        lax.all_gather(rights[6], "shard", axis=0, tiled=True),
    )
    dealt = (
        lax.all_to_all(
            deal_columns(normed, ctx_count, shard_count),
            "shard",
            split_axis=1,
            concat_axis=0,
            tiled=True,
        ),
        lax.all_to_all(
            deal_columns(attended, ctx_count, shard_count),
            "shard",
            split_axis=1,
            concat_axis=0,
            tiled=True,
        ),
        lax.all_to_all(
            deal_columns(normed_two, ctx_count, shard_count),
            "shard",
            split_axis=1,
            concat_axis=0,
            tiled=True,
        ),
        lax.all_to_all(
            deal_columns(act, ctx_count, shard_count),
            "shard",
            split_axis=1,
            concat_axis=0,
            tiled=True,
        ),
    )
    group_lefts = tuple((part.reshape(part.shape[0], -1) for part in dealt))
    gain_pair = lax.psum(jnp.stack([attn_gain_term, mlp_gain_term]), "shard")
    gain_mine = lax.dynamic_index_in_dim(
        gain_pair.reshape(2, ctx_count, shard_count, own_share),
        lax.axis_index("shard"),
        2,
        keepdims=False,
    ).reshape(2, ctx_count * own_share)
    gain_block = jnp.concatenate(
        [gain_mine.T, jnp.zeros((ctx_count * own_share, 126), jnp.float32)], axis=1
    )
    summed = lax.psum_scatter(
        term_rows(group_lefts, group_rights, gain_block, own_share * lax.axis_size("ctx")).astype(
            jnp.bfloat16
        ),
        "ctx",
        scatter_dimension=0,
        tiled=True,
    ).astype(jnp.float32)
    edge_one = HQ * HD
    edge_two = edge_one + HK * HD
    edge_three = edge_two + HK * HD
    edge_four = edge_three + model_width
    edge_five = edge_four + hidden_width
    edge_six = edge_five + hidden_width
    edge_seven = edge_six + ratio * model_width
    grad_query = summed[:, :edge_one]
    grad_key = summed[:, edge_one:edge_two]
    grad_value = summed[:, edge_two:edge_three]
    grad_out = summed[:, edge_three:edge_four]
    grad_gate = summed[:, edge_four:edge_five]
    grad_up = summed[:, edge_five:edge_six]
    grad_down = summed[:, edge_six:edge_seven].reshape(own_share * ratio, model_width)
    grad_attn_gain = summed[:, edge_seven]
    grad_mlp_gain = summed[:, edge_seven + 1]
    return (
        output,
        grad_input,
        grad_query,
        grad_key,
        grad_value,
        grad_out,
        grad_gate,
        grad_up,
        grad_down,
        grad_attn_gain,
        grad_mlp_gain,
    )


DOCS = 4
BF16 = jnp.bfloat16
F32 = jnp.float32
VISIBLE_ROWS = 256


def dot_nn(a, b):
    return jnp.dot(a, b, preferred_element_type=F32)


def dot_nt(a, b):
    return lax.dot_general(a, b, (((1,), (1,)), ((), ())), preferred_element_type=F32)


def dot_tn(a, b):
    return lax.dot_general(a, b, (((0,), (0,)), ((), ())), preferred_element_type=F32)


def scores_of(query, key, code, low_code, key_code):
    scores = dot_nt(query, key) * SCORE_SCALE
    mask = (key_code <= code) & (key_code >= low_code)
    return jnp.where(mask, scores, MASKED)


MESH = pl.DeviceIdType.MESH
TILE = 256
WIDE = 512


def flip(i, d):
    return (i, i + 1 - 2 * (i % 2), (i + 2) % 4, 3 - i)[d]


def line_gather(remote, ctx, plane, slot, own, place):
    def copy(i, way, block, source):
        to = plane + way
        return remote(
            slot + 2 * i + (way + 1) // 2, source, place(to, block), (ctx, to), slot + block
        )

    def sends(i):
        if i == 0:
            return [(plane < 3, lambda: copy(0, 1, plane, own)), (plane > 0, lambda: copy(0, -1, plane, own))]
        return [
            (
                jnp.logical_and(plane >= i, plane < 3),
                lambda: copy(i, 1, plane - i, place(plane, plane - i)),
            ),
            (
                jnp.logical_and(plane + i <= 3, plane > 0),
                lambda: copy(i, -1, plane + i, place(plane, plane + i)),
            ),
        ]

    def start(i):
        for whether, made in sends(i):

            @pl.when(whether)
            def _(made=made):
                made().start()

    def step(i, then=None):
        for whether, block in ((plane >= i, plane - i), (plane + i <= 3, plane + i)):

            @pl.when(whether)
            def _(block=block):
                remote(slot, own, place(plane, block), (ctx, plane), slot + block).wait_recv()
                if then is not None:
                    then(block)

        if i < 3:
            start(i)

    def finish():
        for i in range(3):
            for whether, made in sends(i):

                @pl.when(whether)
                def _(made=made):
                    made().wait_send()

    return start, step, finish


def line_sum(remote, over_z, plane, slot, own, recv, add):
    is_end = jnp.logical_or(plane == 0, plane == 3)
    is_inner = jnp.logical_and(plane > 0, plane < 3)

    def near():
        return remote(slot, own(1), recv.at[0], over_z[1])

    def through(u):
        return remote(slot + 1 + u, own(2 + u), recv.at[2 + u], over_z[1])

    def far(u):
        return remote(slot + 3 + u, own(3 - u), recv.at[1], over_z[3 - u], slot + 3)

    def start():
        @pl.when(is_end)
        def _():
            for u in range(2):
                through(u).start()

        near().start()

    def pass_on():
        @pl.when(is_inner)
        def _():
            for u in range(2):
                through(u).wait_recv()
                add(3 - u, 2 + u)
                far(u).start()

    def wait():
        near().wait_recv()
        far(0).wait_recv()

    def finish():
        near().wait_send()

        @pl.when(is_end)
        def _():
            for u in range(2):
                through(u).wait_send()

        @pl.when(is_inner)
        def _():
            for u in range(2):
                far(u).wait_send()

    return start, pass_on, wait, finish


def xor4(a, b):
    return 2 * ((a // 2 + b // 2) % 2) + (a % 2 + b % 2) % 2


def mlp_kernel(
    second_ref,
    mid_ref,
    upstream_ref,
    gain_ref,
    upstream_hbm,
    gate_hbm,
    up_hbm,
    down_hbm,
    output_ref,
    mid_grad_ref,
    gain_grad_ref,
    branch_all,
    gate_up_sum,
    gate_up_send,
    down_terms,
    gate_w,
    up_w,
    down_w,
    upstream_all,
    second_all,
    act,
    gate_grad,
    up_grad,
    held,
    own_sum,
    pair_send,
    pair_recv,
    z_send,
    z_recv,
    first_recv,
    branch_low,
    staged,
    local_sem,
    staged_sem,
    send_sem,
    recv_sem,
):
    tok = second_ref.shape[0]
    pair = 2 * tok
    hidden = gate_w.shape[1]
    width = second_ref.shape[1]
    ctx, plane = lax.axis_index("ctx"), lax.axis_index("shard")
    chip, core = ctx // 2, ctx % 2
    sibling = (ctx + 1 - 2 * core, plane)
    over_z = [(ctx, flip(plane, d)) for d in range(4)]
    over_chips = [(2 * flip(chip, d) + core, plane) for d in range(4)]

    half = pl.ds(pl.multiple_of(core * hidden, hidden), hidden)
    loads = [
        pltpu.make_async_copy(upstream_hbm, upstream_all, local_sem.at[0]),
        pltpu.make_async_copy(down_hbm, down_w, local_sem.at[1]),
        pltpu.make_async_copy(gate_hbm.at[:, half], gate_w, local_sem.at[2]),
        pltpu.make_async_copy(up_hbm.at[:, half], up_w, local_sem.at[3]),
        pltpu.make_async_copy(second_ref, second_all.at[0, 0], local_sem.at[4]),
    ]
    for load in loads:
        load.start()

    barrier = pltpu.get_barrier_semaphore()
    partners = [sibling] + over_z[1:] + over_chips[1:]
    for partner in partners:
        pl.semaphore_signal(barrier, inc=1, device_id=partner, device_id_type=MESH)
    pl.semaphore_wait(barrier, len(partners))

    def remote(slot, source, target, device, recv=None):
        return pltpu.make_async_remote_copy(
            src_ref=source,
            dst_ref=target,
            send_sem=send_sem.at[slot],
            recv_sem=recv_sem.at[slot if recv is None else recv],
            device_id=device,
            device_id_type=MESH,
        )

    def send(slot, source, target, device):
        copy = remote(slot, source, target, device)
        copy.start()
        return copy

    start_line, step_line, finish_line = line_gather(
        remote, ctx, plane, 32, second_ref, lambda r, b: second_all.at[xor4(r, b), 0]
    )
    start_line(0)
    gather_pair = {0: send(0, second_ref, second_all.at[0, 1], sibling)}
    for load in loads:
        load.wait()

    def rows_of(d):
        return pl.ds(d * pair, pair)

    def forward(d):
        rows = rows_of(d)
        second = lambda: second_all[d].reshape(pair, width)

        def step(t, carry):
            at = pl.ds(pl.multiple_of(t * WIDE, WIDE), WIDE)
            act_grad = dot_nt(upstream_all[rows, :], down_w[at, :])
            gate = dot_nn(second(), gate_w[:, at])
            up_lin = dot_nn(second(), up_w[:, at])
            sigma = 1.0 / (1.0 + jnp.exp(-gate))
            swish = gate * sigma
            act[rows, at] = (swish * up_lin).astype(BF16)
            gate_grad[rows, at] = (
                act_grad * up_lin * (sigma * (1.0 + gate * (1.0 - sigma)))
            ).astype(BF16)
            up_grad[rows, at] = (act_grad * swish).astype(BF16)
            return carry

        lax.fori_loop(0, hidden // WIDE, step, 0)

    def give_pair(d, base, product):
        which = 0 if base == 7 else 1

        def step(t, carry):
            at = pl.ds(pl.multiple_of(t * WIDE, WIDE), WIDE)
            terms = product(at)
            held[d % 2, :, at] = terms[:tok]
            pair_send[which, d, :, at] = terms[tok:].astype(BF16)
            return carry

        copies = []
        half_width = width // 2
        for h in range(2):
            lax.fori_loop(h * half_width // WIDE, (h + 1) * half_width // WIDE, step, 0)
            columns = pl.ds(h * half_width, half_width)
            copies.append(
                send(
                    (base + d) if h == 0 else (44 + 4 * which + d),
                    pair_send.at[which, d, :, columns],
                    pair_recv.at[which, d, :, columns],
                    sibling,
                )
            )
        return copies

    def give_plane(d, base, copies):
        which = 0 if base == 7 else 1
        for copy in copies:
            copy.wait_recv()
        total = held[d % 2] + pair_recv[which, d].astype(F32)
        if d == 0:
            own_sum[which] = total
            return None
        z_send[which, d - 1] = total.astype(BF16)
        copy = remote(
            base + 3 + d, z_send.at[which, d - 1], z_recv.at[which, d - 1], over_z[d]
        )
        if which == 0:
            copy.start()
        return copy

    def back(d):
        rows = rows_of(d)
        return lambda at: dot_nt(gate_grad[rows, :], gate_w[at, :]) + dot_nt(
            up_grad[rows, :], up_w[at, :]
        )

    def onward(d):
        rows = rows_of(d)
        return lambda at: dot_nn(act[rows, :], down_w[:, at])

    def receive(d):
        step_line(d)
        gather_pair[d] = send(3 + d, second_all.at[d, 0], second_all.at[d, 1], sibling)

    pairs, planes = {}, {}
    for d in range(4):
        gather_pair[d].wait_recv()
        forward(d)
        if d == 0:
            receive(1)
        pairs[d] = give_pair(d, 7, back(d))
        if d == 1:
            receive(2)
        planes[d] = give_plane(d, 7, pairs[d])
        if d == 2:
            receive(3)

    second_rows = second_all.reshape(8 * tok, width)
    block = 2 * TILE

    def terms(grads, d, target, first):
        for h in range(2):
            column = flip(chip, d) * block + h * TILE
            left = second_rows[:, pl.ds(pl.multiple_of(column, TILE), TILE)]
            target[pl.ds(first + h * TILE, TILE), :] = dot_tn(left, grads[...]).astype(BF16)

    terms(gate_grad, 1, up_w, 0)
    terms(gate_grad, 3, up_w, block)
    first_gate = send(28, up_w.at[pl.ds(0, 2 * block)], first_recv.at[0], over_chips[1])
    terms(up_grad, 2, up_w, 2 * block)
    terms(up_grad, 3, up_w, 3 * block)
    first_up = send(29, up_w.at[pl.ds(2 * block, 2 * block)], first_recv.at[1], over_chips[2])

    out_pairs, out_planes = {}, {}
    for d in range(4):
        out_pairs[d] = give_pair(d, 14, onward(d))
        if d:
            out_planes[d - 1] = give_plane(d - 1, 14, out_pairs[d - 1])
    out_planes[3] = give_plane(3, 14, out_pairs[3])

    def add_out(d, i):
        def step(t, carry):
            at = pl.ds(pl.multiple_of(t * 32, 32), 32)
            z_send[1, d - 1, at, :] = (
                z_send[1, d - 1, at, :].astype(F32) + z_recv[1, i, at, :].astype(F32)
            ).astype(BF16)
            return carry

        lax.fori_loop(0, tok // 32, step, 0)

    start_sum, pass_sum, wait_sum, finish_sum = line_sum(
        remote, over_z, plane, 38, lambda d: z_send.at[1, d - 1], z_recv.at[1], add_out
    )
    start_sum()

    terms(gate_grad, 2, gate_w, 2 * block)
    terms(up_grad, 1, gate_w, 3 * block)

    for d in (1, 2, 3):
        planes[d].wait_recv()
    chunk = 32
    gain = gain_ref[...]

    def mid_step(i, carry):
        at = pl.ds(pl.multiple_of(i * chunk, chunk), chunk)
        grad = own_sum[0, at, :]
        for d in range(3):
            grad = grad + z_recv[0, d, at, :].astype(F32)
        mid = mid_ref[at, :]
        factor = lax.rsqrt(jnp.mean(mid * mid, axis=-1, keepdims=True) + EPSILON)
        scaled = grad * gain
        mid_grad = (
            upstream_ref[at, :].astype(F32)
            + factor * scaled
            - mid * (factor * factor * factor * jnp.mean(scaled * mid, axis=-1, keepdims=True))
        )
        mid_grad_ref[at, :] = mid_grad
        branch_low[at, :] = mid_grad.astype(BF16)
        return carry + jnp.sum(grad * mid * factor, axis=0, keepdims=True)

    gain_grad_ref[...] = lax.fori_loop(0, tok // chunk, mid_step, jnp.zeros((1, width), F32))
    branch_chips = {
        d: send(20 + d, branch_low, branch_all.at[0, d], over_chips[d]) for d in (1, 2)
    }
    branch_pairs = {0: send(24, branch_low, branch_all.at[1, 0], sibling)}
    keep = pltpu.make_async_copy(branch_low, branch_all.at[0, 0], local_sem.at[0])
    keep.start()

    def to_hbm(slot, target):
        return pltpu.make_async_copy(staged.at[slot], target, staged_sem.at[slot])

    def down_step(t):
        slot = t % 2
        target = down_terms.at[pl.ds(t * TILE, TILE)]
        if t > 1:
            to_hbm(slot, target).wait()
        left = act[:, pl.ds(t * TILE, TILE)]
        staged[slot] = dot_tn(left, upstream_all[...]).astype(BF16)
        to_hbm(slot, target).start()

    for t in range(hidden // TILE):
        down_step(t)
    terms(gate_grad, 0, gate_w, 0)
    terms(up_grad, 0, gate_w, block)
    pass_sum()
    branch_far = {}
    for d in (1, 2):
        branch_chips[d].wait_recv()
        part = pl.ds((d - 1) * (tok // 2), tok // 2)
        branch_far[d] = send(
            23 + 20 * (d - 1), branch_all.at[0, d, part], branch_all.at[0, 3, part], over_chips[3 - d]
        )
        branch_pairs[d] = send(24 + d, branch_all.at[0, d], branch_all.at[1, d], sibling)
    for d in (1, 2):
        branch_far[d].wait_recv()
    branch_pairs[3] = send(27, branch_all.at[0, 3], branch_all.at[1, 3], sibling)

    keep_second = [
        pltpu.make_async_copy(
            gate_w.at[pl.ds((2 + e) * block, block)], gate_up_send.at[e], local_sem.at[2 + e]
        )
        for e in range(2)
    ]

    def add_first(i, carry):
        here = pl.ds(pl.multiple_of(i * 64, 64), 64)
        for e in range(2):
            mine = pl.ds(pl.multiple_of((2 + e) * block + i * 64, 64), 64)
            far = pl.ds(pl.multiple_of(block + i * 64, 64), 64)
            gate_w[mine, :] = (
                gate_w[mine, :].astype(F32) + first_recv[e, far, :].astype(F32)
            ).astype(BF16)
            own = gate_w[pl.ds(pl.multiple_of(e * block + i * 64, 64), 64), :].astype(F32)
            down_w[here, pl.ds(e * hidden, hidden)] = (
                own + first_recv[e, here, :].astype(F32)
            ).astype(BF16)
        return carry

    first_gate.wait_recv()
    first_up.wait_recv()
    lax.fori_loop(0, block // 64, add_first, 0)
    keep_sum = pltpu.make_async_copy(down_w.at[pl.ds(0, block)], gate_up_sum, local_sem.at[1])
    for copy in (keep_sum, *keep_second):
        copy.start()

    wait_sum()

    def out_step(i, carry):
        at = pl.ds(pl.multiple_of(i * chunk, chunk), chunk)
        total = mid_ref[at, :] + own_sum[1, at, :]
        for d in range(2):
            total = total + z_recv[1, d, at, :].astype(F32)
        output_ref[at, :] = total.astype(BF16)
        return carry

    lax.fori_loop(0, tok // chunk, out_step, 0)

    for d in range(4):
        branch_pairs[d].wait_recv()
        for copy in (gather_pair[d], *pairs[d], *out_pairs[d], branch_pairs[d]):
            copy.wait_send()
    for d in (1, 2, 3):
        planes[d].wait_send()
    for d in (1, 2):
        branch_chips[d].wait_send()
        branch_far[d].wait_send()
    finish_sum()
    finish_line()
    keep.wait()
    for slot in range(2):
        to_hbm(slot, down_terms.at[pl.ds(0, TILE)]).wait()
    first_gate.wait_send()
    first_up.wait_send()
    for copy in (keep_sum, *keep_second):
        copy.wait()


def mlp_of(normed_two, mid, upstream, gain, upstream_group, w_gate, w_up, down_rows):
    tok, width = mid.shape
    hidden = down_rows.shape[0]
    rows = upstream_group.shape[0]
    vmem = pl.BlockSpec(memory_space=pltpu.VMEM)
    hbm = pl.BlockSpec(memory_space=pl.ANY)
    return pl.pallas_call(
        mlp_kernel,
        in_specs=[vmem] * 4 + [hbm] * 4,
        out_specs=[vmem] * 3 + [hbm] * 4,
        out_shape=[
            jax.ShapeDtypeStruct((tok, width), BF16),
            jax.ShapeDtypeStruct((tok, width), F32),
            jax.ShapeDtypeStruct((1, width), F32),
            jax.ShapeDtypeStruct((2, 4, tok, width), BF16),
            jax.ShapeDtypeStruct((2 * TILE, 2 * hidden), BF16),
            jax.ShapeDtypeStruct((2, 2 * TILE, hidden), BF16),
            jax.ShapeDtypeStruct((hidden, width), BF16),
        ],
        scratch_shapes=[
            pltpu.VMEM((width, hidden), BF16),
            pltpu.VMEM((width, hidden), BF16),
            pltpu.VMEM((hidden, width), BF16),
            pltpu.VMEM((rows, width), BF16),
            pltpu.VMEM((4, 2, tok, width), BF16),
            pltpu.VMEM((rows, hidden), BF16),
            pltpu.VMEM((rows, hidden), BF16),
            pltpu.VMEM((rows, hidden), BF16),
            pltpu.VMEM((2, tok, width), F32),
            pltpu.VMEM((2, tok, width), F32),
            pltpu.VMEM((2, 4, tok, width), BF16),
            pltpu.VMEM((2, 4, tok, width), BF16),
            pltpu.VMEM((2, 3, tok, width), BF16),
            pltpu.VMEM((2, 4, tok, width), BF16),
            pltpu.VMEM((2, 4 * TILE, hidden), BF16),
            pltpu.VMEM((tok, width), BF16),
            pltpu.VMEM((2, TILE, width), BF16),
            pltpu.SemaphoreType.DMA((5,)),
            pltpu.SemaphoreType.DMA((2,)),
            pltpu.SemaphoreType.DMA((52,)),
            pltpu.SemaphoreType.DMA((52,)),
        ],
        compiler_params=pltpu.CompilerParams(
            collective_id=1, has_side_effects=True, vmem_limit_bytes=60 << 20
        ),
        cost_estimate=pl.CostEstimate(
            flops=18 * rows * width * hidden,
            bytes_accessed=2 * (5 * width * hidden + 4 * rows * width),
            transcendentals=rows * hidden,
        ),
    )(normed_two, mid, upstream, gain, upstream_group, w_gate, w_up, down_rows)


def rotated(values, cosine, sine):
    half = values.shape[1] // 2
    first, second = values[:, :half], values[:, half:]
    return jnp.concatenate([first * cosine - second * sine, second * cosine + first * sine], axis=1)


def front_kernel(
    input_ref,
    attn_gain_ref,
    mlp_gain_ref,
    cosine_ref,
    sine_ref,
    code_ref,
    low_code_ref,
    key_code_ref,
    query_hbm,
    key_hbm,
    value_hbm,
    out_hbm,
    down_hbm,
    upstream_hbm,
    second_ref,
    mid_ref,
    normed_hbm,
    query_ref,
    kv_ref,
    attended_ref,
    log_total_ref,
    head_hbm,
    w_sibling,
    out_hbm_rows,
    down_rows,
    upstream_all,
    normed_ref,
    w_head,
    out_pair,
    inputs_all,
    w_parts,
    attended_other,
    own_sum,
    chip_send,
    chip_recv,
    local_sem,
    send_sem,
    recv_sem,
):
    tok, width = input_ref.shape
    quarter = width // 4
    shard = out_hbm.shape[1]
    hidden = down_rows.shape[0]
    part = hidden // 4
    seq = 8 * tok
    half_seq = 4 * tok
    ctx, plane = lax.axis_index("ctx"), lax.axis_index("shard")
    chip, core = ctx // 2, ctx % 2
    sibling = (ctx + 1 - 2 * core, plane)
    over_z = [(ctx, flip(plane, d)) for d in range(4)]
    over_chips = [(2 * flip(chip, d) + core, plane) for d in range(4)]
    others = (1, 2, 3)

    def at(i, size):
        return pl.ds(pl.multiple_of(i * size, size), size)

    def remote(slot, source, target, device, recv=None):
        return pltpu.make_async_remote_copy(
            src_ref=source,
            dst_ref=target,
            send_sem=send_sem.at[slot],
            recv_sem=recv_sem.at[slot if recv is None else recv],
            device_id=device,
            device_id_type=MESH,
        )

    def send(slot, source, target, device):
        copy = remote(slot, source, target, device)
        copy.start()
        return copy

    def local(slot, source, target):
        return pltpu.make_async_copy(source, target, local_sem.at[slot])

    rows = at(chip, quarter)
    mine = w_parts.at[plane]
    load_query = local(0, query_hbm.at[rows, at(core, HD)], mine.at[0])
    load_key = local(1, key_hbm.at[rows], mine.at[1])
    load_value = local(1, value_hbm.at[rows], mine.at[1])
    load_query.start()

    @pl.when(core == 0)
    def _():
        load_key.start()

    @pl.when(core == 1)
    def _():
        load_value.start()

    keep_input = local(2, input_ref, inputs_all.at[0, 0])
    keep_input.start()
    out_own = out_hbm.at[at(ctx, HD), :]
    keep_out = local(3, out_own, out_pair.at[0, :, at(plane, shard)])
    keep_out.start()

    def down_block(to_plane):
        first = to_plane * (2 * hidden) + core * hidden + chip * part
        return down_hbm.at[pl.ds(pl.multiple_of(first, part), part), :]

    def down_place(column):
        return down_rows.at[at(chip, part), at(column, shard)]

    first_own = plane * (2 * hidden) + core * hidden
    keep_down = local(
        4,
        down_hbm.at[pl.ds(pl.multiple_of(first_own, hidden), hidden), :],
        down_rows.at[:, at(plane, shard)],
    )
    keep_down.start()
    keep_upstream = local(5, upstream_hbm, upstream_all.at[0, 0])
    keep_upstream.start()

    barrier = pltpu.get_barrier_semaphore()
    partners = [sibling] + over_z[1:] + over_chips[1:]
    for partner in partners:
        pl.semaphore_signal(barrier, inc=1, device_id=partner, device_id_type=MESH)
    pl.semaphore_wait(barrier, len(partners))

    input_chips = {
        d: send(d - 1, input_ref, inputs_all.at[0, d], over_chips[d]) for d in others
    }
    input_pairs = {0: send(3, input_ref, inputs_all.at[1, 0], sibling)}
    load_query.wait()
    load_key.wait()
    start_head, step_head, finish_head = line_gather(
        remote, ctx, plane, 37, mine, lambda r, b: w_parts.at[b]
    )
    start_out, step_out, finish_out = line_gather(
        remote, ctx, plane, 43, out_own, lambda r, b: out_pair.at[0, :, at(b, shard)]
    )
    start_up, step_up, finish_up = line_gather(
        remote, ctx, plane, 49, upstream_hbm, lambda r, b: upstream_all.at[xor4(r, b), 0]
    )
    start_head(0)

    head_rows = w_head.at[:, rows, :]

    def pass_head(source):
        apart = xor4(chip, source)
        block = w_parts.at[source]

        @pl.when(apart == 0)
        def _():
            local(6, block, head_rows).start()

        @pl.when(apart != 0)
        def _():
            remote(9 + apart, block, head_rows, (2 * source + core, plane)).start()

    pass_head(plane)
    chunk = 32
    attn_gain = attn_gain_ref[...]

    def norm(e, d):
        def step(i, carry):
            block = inputs_all[e, d, at(i, chunk), :].astype(F32)
            factor = lax.rsqrt(jnp.mean(block * block, axis=-1, keepdims=True) + EPSILON)
            first = (4 * e + d) * tok + i * chunk
            normed_ref[pl.ds(pl.multiple_of(first, chunk), chunk), :] = (
                block * factor * attn_gain
            ).astype(BF16)
            return carry

        lax.fori_loop(0, tok // chunk, step, 0)

    keep_input.wait()
    norm(0, 0)
    step_head(1, pass_head)
    input_pairs[0].wait_recv()
    norm(1, 0)
    for d in (1, 2):
        input_chips[d].wait_recv()
        input_pairs[d] = send(3 + d, inputs_all.at[0, d], inputs_all.at[1, d], sibling)
    norm(0, 1)
    norm(0, 2)
    step_head(2, pass_head)
    down_z = {
        d: send(16 + d, down_block(flip(plane, d)), down_place(plane), over_z[d]) for d in others
    }
    input_chips[3].wait_recv()
    input_pairs[3] = send(6, inputs_all.at[0, 3], inputs_all.at[1, 3], sibling)
    norm(0, 3)
    for d in others:
        input_pairs[d].wait_recv()
        norm(1, d)
    step_head(3, pass_head)

    start_out(0)
    keep_normed = local(2, normed_ref, normed_hbm)
    keep_normed.start()
    local(6, mine, head_rows).wait()
    for d in others:
        remote(9 + d, mine, head_rows, over_chips[d]).wait_recv()

    def project(which, target, flat):
        def step(t, carry):
            here = at(t, TILE)
            made = dot_nn(normed_ref[here, :], w_head[which])
            cosine, sine = cosine_ref[here, :], sine_ref[here, :]
            if flat:
                cosine = jnp.where(core == 0, cosine, 1.0)
                sine = jnp.where(core == 0, sine, 0.0)
            target[here, :] = rotated(made, cosine, sine).astype(BF16)
            return carry

        lax.fori_loop(0, seq // TILE, step, 0)

    keep_out.wait()

    def pass_out(source):
        columns = out_pair.at[0, :, at(source, shard)]
        remote(23 + source, columns, out_pair.at[1, :, at(source, shard)], sibling).start()

    pass_out(plane)
    step_out(1, pass_out)
    mine_kv = kv_ref.at[core]
    project(1, mine_kv, True)
    kv_pair = [
        send(20 + e, mine_kv.at[pl.ds(e * half_seq, half_seq)],
             mine_kv.at[pl.ds((1 - e) * half_seq, half_seq)], sibling)
        for e in range(2)
    ]
    project(0, query_ref, False)
    step_out(2, pass_out)
    down_near, down_far = {}, {}
    half_part = part // 2

    def down_half(of_chip, column, second):
        first = of_chip * part + second * half_part
        return down_rows.at[
            pl.ds(pl.multiple_of(first, half_part), half_part), at(column, shard)
        ]

    for d in others:
        down_z[d].wait_recv()
        block = down_place(flip(plane, d))
        for e in (1, 2):
            down_near[e, d] = send(51 + 3 * e + d, block, block, over_chips[e])
    start_up(0)
    for copy in kv_pair:
        copy.wait_recv()

    def attend_step(t, carry):
        here = at(t, TILE)
        scores = scores_of(
            query_ref[here, :], kv_ref[0], code_ref[here, :], low_code_ref[here, :], key_code_ref[...]
        )
        top = jnp.max(scores, axis=-1, keepdims=True)
        weights = jnp.exp(scores - top)
        total = jnp.sum(weights, axis=-1, keepdims=True)
        mixed = dot_nn(weights.astype(BF16), kv_ref[1])
        attended_ref[here, :] = (mixed / total).astype(BF16)
        log_total_ref[here, :] = top + jnp.log(total)
        return carry

    lax.fori_loop(0, seq // TILE, attend_step, 0)
    attended_pair = send(22, attended_ref.at[pl.ds(half_seq, half_seq)], attended_other, sibling)
    step_out(3, pass_out)
    for d in range(4):
        columns = out_pair.at[1, :, pl.ds(d * shard, shard)]
        remote(23 + d, columns, columns, sibling).wait_recv()
    keep_rows = local(3, out_pair.at[0], out_hbm_rows)
    keep_rows.start()
    attended_pair.wait_recv()

    def out_step(t, carry):
        here = at(t, TILE)
        terms = dot_nn(attended_ref[:half_seq, :], out_pair[0, :, here]) + dot_nn(
            attended_other[...], out_pair[1, :, here]
        )
        own_sum[:, here] = terms[:tok]
        for d in others:
            chip_send[d - 1, :, here] = terms[d * tok : (d + 1) * tok].astype(BF16)
        return carry

    lax.fori_loop(0, width // TILE, out_step, 0)
    branch = {
        d: send(26 + d, chip_send.at[d - 1], chip_recv.at[d - 1], over_chips[d]) for d in others
    }
    head_pair = send(16, w_head, w_sibling, sibling)
    keep_head = local(6, w_head, head_hbm)
    keep_head.start()

    for d in others:
        column = flip(plane, d)
        for e in (1, 2):
            down_near[e, d].wait_recv()
            block = down_half(flip(chip, e), column, e - 1)
            down_far[e, d] = send(57 + 3 * e + d, block, block, over_chips[3 - e])
    upstream_pair = {0: send(33, upstream_hbm, upstream_all.at[0, 1], sibling)}

    def pass_up(d):
        step_up(d)
        upstream_pair[d] = send(33 + d, upstream_all.at[d, 0], upstream_all.at[d, 1], sibling)

    pass_up(1)
    pass_up(2)
    for d in others:
        branch[d].wait_recv()
    mlp_gain = mlp_gain_ref[...]

    def mid_step(i, carry):
        here = at(i, chunk)
        mid = input_ref[here, :].astype(F32) + own_sum[here, :]
        for d in range(3):
            mid = mid + chip_recv[d, here, :].astype(F32)
        factor = lax.rsqrt(jnp.mean(mid * mid, axis=-1, keepdims=True) + EPSILON)
        mid_ref[here, :] = mid
        second_ref[here, :] = (mid * factor * mlp_gain).astype(BF16)
        return carry

    lax.fori_loop(0, tok // chunk, mid_step, 0)

    pass_up(3)
    keep_upstream.wait()
    for d in range(4):
        upstream_pair[d].wait_recv()
        upstream_pair[d].wait_send()
        input_pairs[d].wait_send()
    head_pair.wait_recv()
    for copy in (head_pair, attended_pair, *kv_pair):
        copy.wait_send()
    for copy in (keep_normed, keep_head, keep_rows):
        copy.wait()
    for d in range(4):
        columns = out_pair.at[0, :, pl.ds(d * shard, shard)]
        remote(23 + d, columns, columns, sibling).wait_send()
    keep_down.wait()
    for d in others:
        for e in (1, 2):
            down_near[e, d].wait_send()
            down_far[e, d].wait()
        for copies in (input_chips, down_z, branch):
            copies[d].wait_send()
        remote(9 + d, mine, head_rows, over_chips[d]).wait_send()
    finish_head()
    finish_out()
    finish_up()


def front_of(
    inputs, attn_gain, mlp_gain, cosine, sine, code, low_code, key_code,
    w_query, w_key, w_value, w_out, w_down, upstream,
):
    tok, width = inputs.shape
    seq = 8 * tok
    hidden = w_down.shape[0] // 8
    vmem = pl.BlockSpec(memory_space=pltpu.VMEM)
    hbm = pl.BlockSpec(memory_space=pl.ANY)
    return pl.pallas_call(
        front_kernel,
        in_specs=[vmem] * 8 + [hbm] * 6,
        out_specs=[vmem] * 2 + [hbm] + [vmem] * 4 + [hbm] * 5,
        out_shape=[
            jax.ShapeDtypeStruct((tok, width), BF16),
            jax.ShapeDtypeStruct((tok, width), F32),
            jax.ShapeDtypeStruct((seq, width), BF16),
            jax.ShapeDtypeStruct((seq, HD), BF16),
            jax.ShapeDtypeStruct((2, seq, HD), BF16),
            jax.ShapeDtypeStruct((seq, HD), BF16),
            jax.ShapeDtypeStruct((seq, 1), F32),
            jax.ShapeDtypeStruct((2, width, HD), BF16),
            jax.ShapeDtypeStruct((2, width, HD), BF16),
            jax.ShapeDtypeStruct((HD, width), BF16),
            jax.ShapeDtypeStruct((hidden, width), BF16),
            jax.ShapeDtypeStruct((4, 2, tok, width), BF16),
        ],
        scratch_shapes=[
            pltpu.VMEM((seq, width), BF16),
            pltpu.VMEM((2, width, HD), BF16),
            pltpu.VMEM((2, HD, width), BF16),
            pltpu.VMEM((2, 4, tok, width), BF16),
            pltpu.VMEM((4, 2, width // 4, HD), BF16),
            pltpu.VMEM((4 * tok, HD), BF16),
            pltpu.VMEM((tok, width), F32),
            pltpu.VMEM((3, tok, width), BF16),
            pltpu.VMEM((3, tok, width), BF16),
            pltpu.SemaphoreType.DMA((7,)),
            pltpu.SemaphoreType.DMA((67,)),
            pltpu.SemaphoreType.DMA((67,)),
        ],
        compiler_params=pltpu.CompilerParams(
            collective_id=2, has_side_effects=True, vmem_limit_bytes=56 << 20
        ),
        cost_estimate=pl.CostEstimate(
            flops=2 * seq * width * 3 * HD + 4 * seq * seq * HD,
            bytes_accessed=20 * seq * width,
            transcendentals=seq * seq,
        ),
    )(
        inputs, attn_gain, mlp_gain, cosine, sine, code, low_code, key_code,
        w_query, w_key, w_value, w_out, w_down, upstream,
    )


def back_kernel(
    input_ref,
    mid_grad_ref,
    attn_gain_ref,
    mlp_gain_grad_ref,
    cosine_ref,
    sine_ref,
    code_ref,
    low_code_ref,
    key_code_ref,
    query_ref,
    kv_ref,
    attended_ref,
    log_total_ref,
    normed_hbm,
    head_hbm,
    sibling_hbm,
    out_rows_hbm,
    branch_hbm,
    gate_up_hbm,
    gate_up_send,
    down_terms,
    grad_input_ref,
    gain_total_ref,
    grad_out_ref,
    head_in,
    gate_up_in,
    down_in,
    normed_ref,
    w_head,
    w_sibling,
    out_rows_ref,
    branch_all,
    d_attended,
    d_head,
    d_other,
    d_kv,
    d_kv_other,
    out_send,
    out_recv,
    head_terms,
    head_recv,
    own_sum,
    chip_send,
    chip_recv,
    gate_up_sum,
    gate_up_recv,
    down_parts,
    down_first,
    down_mid,
    down_second,
    down_sum,
    down_planes,
    gains,
    gains_z,
    gains_ctx,
    local_sem,
    send_sem,
    recv_sem,
):
    tok, width = input_ref.shape
    seq = 8 * tok
    half_seq = 4 * tok
    share = out_send.shape[1]
    ctx, plane = lax.axis_index("ctx"), lax.axis_index("shard")
    chip, core = ctx // 2, ctx % 2
    other_core = 1 - core
    sibling = (2 * chip + other_core, plane)
    over_z = [(ctx, flip(plane, d)) for d in range(4)]
    over_chips = [(2 * flip(chip, d) + core, plane) for d in range(4)]
    over_chips_cross = [(2 * flip(chip, d) + other_core, plane) for d in range(4)]
    over_z_cross = [(2 * chip + other_core, flip(plane, d)) for d in range(4)]
    others = (1, 2, 3)

    def at(i, size):
        return pl.ds(pl.multiple_of(i * size, size), size)

    def remote(slot, source, target, device, recv=None):
        return pltpu.make_async_remote_copy(
            src_ref=source,
            dst_ref=target,
            send_sem=send_sem.at[slot],
            recv_sem=recv_sem.at[slot if recv is None else recv],
            device_id=device,
            device_id_type=MESH,
        )

    def send(slot, source, target, device):
        copy = remote(slot, source, target, device)
        copy.start()
        return copy

    def local(slot, source, target):
        return pltpu.make_async_copy(source, target, local_sem.at[slot])

    loads = [
        local(0, branch_hbm, branch_all),
        local(1, out_rows_hbm, out_rows_ref),
        local(2, normed_hbm, normed_ref),
        local(3, down_terms.at[:, chip], down_parts),
        local(7, down_terms.at[:, flip(chip, 2), :, pl.ds(0, width // 2)], down_mid.at[0]),
        local(8, down_terms.at[:, flip(chip, 1), :, pl.ds(width // 2, width // 2)], down_mid.at[1]),
        local(4, head_hbm, w_head),
        local(5, sibling_hbm, w_sibling),
        local(6, gate_up_hbm, gate_up_sum),
    ]
    for load in loads:
        load.start()

    barrier = pltpu.get_barrier_semaphore()
    partners = (
        over_z[1:] + over_z_cross + over_chips[1:] + over_chips_cross[1:]
    )
    for partner in partners:
        pl.semaphore_signal(barrier, inc=1, device_id=partner, device_id_type=MESH)
    pl.semaphore_wait(barrier, len(partners))

    gate_second = send(0, gate_up_send.at[0], gate_up_recv.at[0], over_chips[2])
    up_second = send(46, gate_up_send.at[1], gate_up_recv.at[1], over_chips[1])

    half_width = width // 2
    down_sent = [
        send(
            1 + 2 * e + u,
            down_terms.at[:, flip(chip, (1 + e, 3)[u]), :, pl.ds(e * half_width, half_width)],
            down_first.at[e, u],
            over_chips[1 + e],
        )
        for e in range(2)
        for u in range(2)
    ]

    loads[0].wait()

    def out_step(t, carry):
        here = at(t, TILE)
        made = dot_tn(attended_ref[...], branch_all[:, here])
        out_send[:, :, here] = made.reshape(4, share, TILE).astype(BF16)
        return carry

    lax.fori_loop(0, width // TILE, out_step, 0)

    def add_out(d, i):
        here = flip(plane, d)
        out_send[here] = (out_send[here].astype(F32) + out_recv[i].astype(F32)).astype(BF16)

    start_out, pass_out, wait_out, finish_out = line_sum(
        remote, over_z, plane, 52, lambda d: out_send.at[flip(plane, d)], out_recv, add_out
    )
    start_out()

    loads[1].wait()

    def attended_step(t, carry):
        here = at(t, TILE)
        d_attended[here, :] = dot_nt(branch_all[here, :], out_rows_ref[...]).astype(BF16)
        return carry

    lax.fori_loop(0, seq // TILE, attended_step, 0)
    d_kv[...] = jnp.zeros_like(d_kv)

    def attend_step(t, carry):
        here = at(t, TILE)
        query, outgrad = query_ref[here, :], d_attended[here, :]
        scores = scores_of(
            query, kv_ref[0], code_ref[here, :], low_code_ref[here, :], key_code_ref[...]
        )
        probs = jnp.exp(scores - log_total_ref[here, :])
        prob_grad = dot_nt(outgrad, kv_ref[1])
        delta = jnp.sum(probs * prob_grad, axis=-1, keepdims=True)
        score_grad = (probs * (prob_grad - delta)).astype(BF16)
        d_query = dot_nn(score_grad, kv_ref[0]) * SCORE_SCALE
        d_head[here, :HD] = rotated(d_query, cosine_ref[here, :], -sine_ref[here, :]).astype(BF16)
        d_kv[0] += dot_tn(score_grad, query)
        d_kv[1] += dot_tn(probs.astype(BF16), outgrad)
        return carry

    lax.fori_loop(0, seq // TILE, attend_step, 0)

    give = d_kv.at[other_core]
    kv_pair = [
        send(
            7 + e,
            give.at[pl.ds(e * half_seq, half_seq)],
            d_kv_other.at[pl.ds((1 - e) * half_seq, half_seq)],
            sibling,
        )
        for e in range(2)
    ]
    loads[8].wait()
    gate_second.wait_recv()
    up_second.wait_recv()
    hidden = gate_up_recv.shape[2]

    def gate_up_step(i, carry):
        here = at(i, share)
        for e in range(2):
            columns = pl.ds(e * hidden, hidden)
            gate_up_sum[here, columns] = (
                gate_up_sum[here, columns].astype(F32) + gate_up_recv[e, here, :].astype(F32)
            ).astype(BF16)
        return carry

    lax.fori_loop(0, 8, gate_up_step, 0)

    place = gate_up_in.at[plane, core]

    def gate_up_rows(to_core, to_plane):
        return gate_up_sum.at[at(4 * to_core + to_plane, share), :]

    gate_up_z = {
        d: send(18 + d, gate_up_rows(core, flip(plane, d)), place, over_z[d]) for d in others
    }
    gate_up_cross = {
        d: send(22 + d, gate_up_rows(other_core, flip(plane, d)), place, over_z_cross[d])
        for d in range(4)
    }
    keep_gate_up = local(1, gate_up_rows(core, plane), place)
    keep_gate_up.start()
    for copy in kv_pair:
        copy.wait_recv()

    def kv_step(t, carry):
        here = at(t, TILE)
        total = d_kv[core, here, :] + d_kv_other[here, :]
        total = total * jnp.where(core == 0, SCORE_SCALE, 1.0)
        cosine = jnp.where(core == 0, cosine_ref[here, :], 1.0)
        sine = jnp.where(core == 0, sine_ref[here, :], 0.0)
        d_head[here, HD:] = rotated(total, cosine, -sine).astype(BF16)
        return carry

    lax.fori_loop(0, seq // TILE, kv_step, 0)
    head_pair = send(9, d_head.at[pl.ds(half_seq, half_seq)], d_other, sibling)

    loads[2].wait()

    def head_step(t, carry):
        made = dot_tn(normed_ref[:, at(t, TILE)], d_head[...])
        head_terms[:, t] = made.reshape(4, share, 2 * HD).astype(BF16)
        return carry

    lax.fori_loop(0, width // TILE, head_step, 0)

    def add_head(d, i):
        here = flip(plane, d)

        def step(t, carry):
            head_terms[here, t] = (
                head_terms[here, t].astype(F32) + head_recv[i, t].astype(F32)
            ).astype(BF16)
            return carry

        lax.fori_loop(0, 8, step, 0)

    start_head, pass_head, wait_head, finish_head = line_sum(
        remote, over_z, plane, 47, lambda d: head_terms.at[flip(plane, d)], head_recv, add_head
    )
    start_head()

    loads[6].wait()
    loads[7].wait()
    head_pair.wait_recv()

    def normed_step(t, carry):
        here = at(t, TILE)
        made = (
            dot_nt(d_head[:half_seq, :HD], w_head[0, here, :])
            + dot_nt(d_head[:half_seq, HD:], w_head[1, here, :])
            + dot_nt(d_other[:, :HD], w_sibling[0, here, :])
            + dot_nt(d_other[:, HD:], w_sibling[1, here, :])
        )
        own_sum[:, here] = made[:tok]
        for d in others:
            chip_send[d - 1, :, here] = made[d * tok : (d + 1) * tok].astype(BF16)
        return carry

    lax.fori_loop(0, width // TILE, normed_step, 0)
    normed_chips = {
        d: send(12 + d, chip_send.at[d - 1], chip_recv.at[d - 1], over_chips[d]) for d in others
    }

    loads[4].wait()
    loads[5].wait()

    def down_mid_step(p, carry):
        for e in range(2):
            down_mid[e, p] = (
                down_mid[e, p].astype(F32) + down_first[e, 1, p].astype(F32)
            ).astype(BF16)
        return carry

    for copy in down_sent:
        copy.wait_recv()
    lax.fori_loop(0, 4, down_mid_step, 0)
    down_last = [
        send(5 + e, down_mid.at[e], down_second.at[e], over_chips[2 - e]) for e in range(2)
    ]
    pass_out()
    pass_head()
    for d in others:
        normed_chips[d].wait_recv()
    chunk = 32
    gain = attn_gain_ref[...]

    def input_step(i, carry):
        here = at(i, chunk)
        grad = own_sum[here, :]
        for d in range(3):
            grad = grad + chip_recv[d, here, :].astype(F32)
        block = input_ref[here, :].astype(F32)
        factor = lax.rsqrt(jnp.mean(block * block, axis=-1, keepdims=True) + EPSILON)
        scaled = grad * gain
        grad_input_ref[here, :] = (
            mid_grad_ref[here, :]
            + factor * scaled
            - block * (factor * factor * factor * jnp.mean(scaled * block, axis=-1, keepdims=True))
        ).astype(BF16)
        return carry + jnp.sum(grad * block * factor, axis=0, keepdims=True)

    gain_grad = lax.fori_loop(0, tok // chunk, input_step, jnp.zeros((1, width), F32))
    gains[...] = jnp.concatenate(
        [gain_grad, mlp_gain_grad_ref[...]], axis=0
    )
    gains_planes = {d: send(25 + d, gains, gains_z.at[d - 1], over_z[d]) for d in others}

    loads[3].wait()
    for copy in down_last:
        copy.wait_recv()

    def down_step(p, carry):
        for e in range(2):
            columns = pl.ds(e * half_width, half_width)
            down_sum[p, :, columns] = (
                down_parts[p, :, columns].astype(F32)
                + down_first[e, 0, p].astype(F32)
                + down_second[e, p].astype(F32)
            ).astype(BF16)
        return carry

    lax.fori_loop(0, 4, down_step, 0)
    down_z = {
        d: send(15 + d, down_sum.at[flip(plane, d)], down_planes.at[plane], over_z[d])
        for d in others
    }
    keep_down = local(3, down_sum.at[plane], down_planes.at[plane])
    keep_down.start()


    wait_head()
    def head_sum(i, carry):
        total = head_terms[plane, i].astype(F32)
        for d in range(2):
            total = total + head_recv[d, i].astype(F32)
        head_terms[plane, i] = total.astype(BF16)
        return carry

    lax.fori_loop(0, 8, head_sum, 0)
    head_place = head_in.at[ctx]
    head_chips = {
        d: send(28 + d, head_terms.at[plane, 2 * flip(chip, d) + core], head_place, over_chips[d])
        for d in others
    }
    head_cross = {
        d: send(
            32 + d, head_terms.at[plane, 2 * flip(chip, d) + other_core], head_place,
            over_chips_cross[d],
        )
        for d in range(4)
    }
    keep_head = local(0, head_terms.at[plane, ctx], head_place)
    keep_head.start()

    for d in others:
        gains_planes[d].wait_recv()
        gains_planes[d].wait_send()
    gains[...] = gains[...] + gains_z[0] + gains_z[1] + gains_z[2]
    gains_chips = {
        d: send(35 + d, gains, gains_ctx.at[0, d], over_chips[d]) for d in others
    }
    gains_cross = {
        d: send(39 + d, gains, gains_ctx.at[1, d], over_chips_cross[d]) for d in range(4)
    }

    wait_out()
    total = out_send[plane].astype(F32)
    for d in range(2):
        total = total + out_recv[d].astype(F32)
    grad_out_ref[...] = total

    keep_down.wait()
    down_place = down_in.at[chip]
    for d in range(4):
        if d:
            down_z[d].wait_recv()
        source = flip(plane, d)
        apart = xor4(chip, source)
        block = down_planes.at[source]

        @pl.when(apart == 0)
        def _(block=block):
            local(4, block, down_place).start()

        @pl.when(apart != 0)
        def _(block=block, source=source, apart=apart):
            remote(42 + apart, block, down_place, (2 * source + core, plane)).start()

    for d in others:
        gains_chips[d].wait_recv()
    for d in range(4):
        gains_cross[d].wait_recv()
    total = gains[...] + gains_ctx[1, 0]
    for d in others:
        total = total + gains_ctx[0, d] + gains_ctx[1, d]
    gain_total_ref[...] = total

    local(4, down_sum.at[plane], down_place).wait()
    keep_gate_up.wait()
    keep_head.wait()
    for d in others:
        remote(42 + d, down_sum.at[plane], down_place, over_chips[d]).wait()
        gate_up_z[d].wait_recv()
        head_chips[d].wait_recv()
        for copies in (
            normed_chips, down_z, gate_up_z, head_chips, gains_chips
        ):
            copies[d].wait_send()
    finish_out()
    finish_head()
    for d in range(4):
        for copies in (gate_up_cross, head_cross):
            copies[d].wait()
        gains_cross[d].wait_send()
    for copy in (gate_second, up_second, head_pair, *kv_pair, *down_sent, *down_last):
        copy.wait_send()


def back_of(*operands):
    inputs, query = operands[0], operands[9]
    tok, width = inputs.shape
    seq = query.shape[0]
    hidden = operands[18].shape[-1] // 2
    share = HD // 4
    vmem = pl.BlockSpec(memory_space=pltpu.VMEM)
    hbm = pl.BlockSpec(memory_space=pl.ANY)
    return pl.pallas_call(
        back_kernel,
        in_specs=[vmem] * 13 + [hbm] * 8,
        out_specs=[vmem] * 6,
        out_shape=[
            jax.ShapeDtypeStruct((tok, width), BF16),
            jax.ShapeDtypeStruct((2, width), F32),
            jax.ShapeDtypeStruct((share, width), F32),
            jax.ShapeDtypeStruct((8, share, 2 * HD), BF16),
            jax.ShapeDtypeStruct((4, 2, share, 2 * hidden), BF16),
            jax.ShapeDtypeStruct((4, share, width), BF16),
        ],
        scratch_shapes=[
            pltpu.VMEM((seq, width), BF16),
            pltpu.VMEM((2, width, HD), BF16),
            pltpu.VMEM((2, width, HD), BF16),
            pltpu.VMEM((HD, width), BF16),
            pltpu.VMEM((seq, width), BF16),
            pltpu.VMEM((seq, HD), BF16),
            pltpu.VMEM((seq, 2 * HD), BF16),
            pltpu.VMEM((4 * tok, 2 * HD), BF16),
            pltpu.VMEM((2, seq, HD), F32),
            pltpu.VMEM((seq, HD), F32),
            pltpu.VMEM((4, share, width), BF16),
            pltpu.VMEM((4, share, width), BF16),
            pltpu.VMEM((4, 8, share, 2 * HD), BF16),
            pltpu.VMEM((4, 8, share, 2 * HD), BF16),
            pltpu.VMEM((tok, width), F32),
            pltpu.VMEM((3, tok, width), BF16),
            pltpu.VMEM((3, tok, width), BF16),
            pltpu.VMEM((8 * share, 2 * hidden), BF16),
            pltpu.VMEM((2, 8 * share, hidden), BF16),
            pltpu.VMEM((4, share, width), BF16),
            pltpu.VMEM((2, 2, 4, share, width // 2), BF16),
            pltpu.VMEM((2, 4, share, width // 2), BF16),
            pltpu.VMEM((2, 4, share, width // 2), BF16),
            pltpu.VMEM((4, share, width), BF16),
            pltpu.VMEM((4, share, width), BF16),
            pltpu.VMEM((2, width), F32),
            pltpu.VMEM((3, 2, width), F32),
            pltpu.VMEM((2, 4, 2, width), F32),
            pltpu.SemaphoreType.DMA((9,)),
            pltpu.SemaphoreType.DMA((57,)),
            pltpu.SemaphoreType.DMA((57,)),
        ],
        compiler_params=pltpu.CompilerParams(
            collective_id=3, has_side_effects=True, vmem_limit_bytes=60 << 20
        ),
        cost_estimate=pl.CostEstimate(
            flops=2 * seq * width * 6 * HD + 10 * seq * seq * HD,
            bytes_accessed=20 * seq * width,
            transcendentals=seq * seq,
        ),
    )(*operands)


def on_device_by_head(
    layer_input,
    w_query,
    w_key,
    w_value,
    w_out,
    w_gate,
    w_up,
    w_down,
    attn_gain,
    mlp_gain,
    block_pairs,
    doc_ids,
    cotangent,
):
    tok_rows, width = layer_input.shape[1:]
    planes = lax.axis_size("shard")
    ctx_count = lax.axis_size("ctx")
    chips = ctx_count // 2
    ctx, plane = lax.axis_index("ctx"), lax.axis_index("shard")
    chip, core = ctx // 2, ctx % 2
    seq_rows = tok_rows * ctx_count
    own_share = width // (planes * ctx_count)

    inputs_low = layer_input[0]
    pairs, documents = block_pairs[0], doc_ids[0]
    order = jnp.stack([(chip ^ d) * 2 + (core ^ e) for e in range(2) for d in range(chips)])
    chosen = jnp.sum(
        jnp.where(order[:, None] == jnp.arange(ctx_count)[None, :], pairs[None, :], 0), axis=1
    )[:, None]
    within = jnp.arange(tok_rows, dtype=jnp.int32)[None, :]
    block = tok_rows // 2
    positions = jnp.where(
        within < block, chosen * block, (2 * ctx_count - 1 - chosen) * block - block
    )
    positions = (positions + within).reshape(-1)
    begins = jnp.sum(documents[None, :] < jnp.arange(1, DOCS)[:, None], axis=1)
    document = jnp.sum((positions[None, :] >= begins[:, None]).astype(jnp.int32), axis=0)
    span = 2 * seq_rows
    doc_first = document * span
    code = doc_first + positions
    low_code = jnp.maximum(doc_first, code - (WINDOW - 1))
    code_column, low_column, code_row = code[:, None], low_code[:, None], code[None, :]
    cosine, sine = rope_tables(positions, HD)

    upstream_low = cotangent[0]
    (
        normed_two,
        mid,
        normed_all,
        query,
        key_value,
        attended,
        log_total,
        w_head,
        w_sibling,
        out_rows,
        down_rows,
        upstream_group,
    ) = front_of(
        inputs_low,
        attn_gain[None],
        mlp_gain[None],
        cosine,
        sine,
        code_column,
        low_column,
        code_row,
        w_query,
        w_key,
        w_value,
        w_out,
        w_down,
        upstream_low,
    )
    (
        output,
        mid_grad,
        mlp_gain_grad,
        branch_all,
        gate_up_sum,
        gate_up_send,
        down_terms,
    ) = mlp_of(
        normed_two,
        mid,
        upstream_low,
        mlp_gain[None],
        upstream_group.reshape(-1, width),
        w_gate,
        w_up,
        down_rows,
    )
    grad_input, gain_total, grad_out, head_in, gate_up_in, down_in = back_of(
        inputs_low,
        mid_grad,
        attn_gain[None],
        mlp_gain_grad,
        cosine,
        sine,
        code_column,
        low_column,
        code_row,
        query,
        key_value,
        attended,
        log_total,
        normed_all,
        w_head,
        w_sibling,
        out_rows,
        branch_all.reshape(seq_rows, width),
        gate_up_sum,
        gate_up_send,
        down_terms.reshape(planes, chips, -1, width),
    )
    hidden = gate_up_in.shape[-1] // 2
    gate_up = gate_up_in.astype(F32)
    columns = lambda parts: jnp.concatenate(parts, axis=1)
    grad_gate = columns([gate_up[p, e, :, :hidden] for p in range(planes) for e in range(2)])
    grad_up = columns([gate_up[p, e, :, hidden:] for p in range(planes) for e in range(2)])
    head = head_in.astype(F32)
    grad_query = columns([head[i, :, :HD] for i in range(ctx_count)])
    grad_key = columns([head[i, :, HD:] for i in range(0, ctx_count, 2)])
    grad_value = columns([head[i, :, HD:] for i in range(1, ctx_count, 2)])
    grad_down = down_in.astype(F32).reshape(-1, width)
    gains = lax.dynamic_slice(gain_total, (0, own_share * (planes * ctx + plane)), (2, own_share))
    return (
        output[None],
        grad_input[None],
        grad_query,
        grad_key,
        grad_value,
        grad_out,
        grad_gate,
        grad_up,
        grad_down,
        gains[0],
        gains[1],
    )


def plan_of(mesh):
    chips, planes = mesh.shape["ctx"] // 2, mesh.shape["shard"]
    if mesh.shape["ctx"] == HQ and HQ == 2 * HK and chips == planes == HK:
        return on_device_by_head
    return on_device


def solution(mesh):
    placed = (
        P("shard", "ctx", None),
        P(None, "shard"),
        P(None, "shard"),
        P(None, "shard"),
        P(None, "shard"),
        P(None, "shard"),
        P(None, "shard"),
        P(None, "shard"),
        P(),
        P(),
        P("shard", None),
        P("shard", None),
        P("shard", "ctx", None),
    )
    return jax.shard_map(
        plan_of(mesh),
        mesh=mesh,
        in_specs=placed,
        out_specs=(
            P("shard", "ctx", None),
            P("shard", "ctx", None),
            P(("ctx", "shard"), None),
            P(("ctx", "shard"), None),
            P(("ctx", "shard"), None),
            P(("ctx", "shard"), None),
            P(("ctx", "shard"), None),
            P(("ctx", "shard"), None),
            P(("ctx", "shard"), None),
            P(("ctx", "shard")),
            P(("ctx", "shard")),
        ),
        check_vma=False,
    )
```
